32 devices in a mesh: amp: 32 (over z, y, x, core).
Axes of the slice: x: 2, y: 2, z: 4, core: 2. Of those that a mesh axis runs over, the one named last changes fastest.
Arguments:
- state: float32 [2, 4194304], P(None, 'amp'), may hold values from -6 to 6
- costate: float32 [2, 4194304], P(None, 'amp'), may hold values from -6 to 6
- gates: float32 [3, 2, 128, 128], replicated, may hold values from -1 to 1, as said below
Outputs:
- state_out: float32 [2, 4194304], P(None, 'amp')
- costate_out: float32 [2, 4194304], P(None, 'amp')
- gradients: float32 [3, 2, 128, 128], replicated
The draws below stay inside these ranges and needn't reach their ends.
Inputs may be any that keep to these rules, and one draw needn't show every extreme that they name: Each gates[l, 0] + i gates[l, 1] is a unitary matrix.
All inputs are finite; a program needn't handle non-finite values.
Results may differ from the reference program's by a relative error of at most 0.0001.
Values sent between devices are 32-bit elements; how exact they have to be, the bound alone decides.
No kernel may reach another device: no remote copies, remote signals or barrier semaphores. Data moves between devices by JAX's collectives and lax.ppermute only.
A program may use at most 64 MiB of HBM per device.

```python
import math
import jax
import jax.numpy as jnp
from jax import lax

GATE = 128
LAYERS = 3
AMP_DEV = 131072
STATE = 4194304
N_AMP = 32


def draw_gates(key, part):
    key_real, key_imag = jax.random.split(jax.random.fold_in(key, 17))
    real_part = jax.random.normal(key_real, (LAYERS, GATE, GATE), jnp.float32)
    imag_part = jax.random.normal(key_imag, (LAYERS, GATE, GATE), jnp.float32)
    matrix = lax.complex(real_part, imag_part)
    factor_q, factor_r = jnp.linalg.qr(matrix)
    diagonal = jnp.diagonal(factor_r, axis1=-2, axis2=-1)
    phases = diagonal / jnp.abs(diagonal)
    unitary = factor_q * phases[:, None, :]
    return jnp.stack([jnp.real(unitary), jnp.imag(unitary)], axis=1).astype(jnp.float32)


def block_scale(stream_key, dims, cuts, low, top_value):
    gain = 1.0
    for position, parts in cuts:
        heights = jax.random.uniform(jax.random.fold_in(jax.random.fold_in(stream_key, 6), position), (parts,), jnp.float32, low / len(cuts), top_value / len(cuts))
        gain = gain * jnp.repeat(jnp.exp(heights), dims[position] // parts).reshape((-1,) + (1,) * (len(dims) - 1 - position))
    return gain


def bell_draw(key, extent, width, reach, shards=(), kind=jnp.bfloat16):
    gain = block_scale(key, extent, shards, -0.22, 0.18) if shards else 1.0
    result = jax.random.normal(key, extent, jnp.float32) * width * gain
    return jnp.minimum(jnp.maximum(result, -reach), reach).astype(kind)


def setup_inputs(seed: int = 0) -> dict:
    seeds = jax.random.split(jax.random.key(seed), 4)
    state = bell_draw(seeds[0], (2, STATE), 1.0, 6.0, ((1, 32),), jnp.float32)
    costate = bell_draw(seeds[1], (2, STATE), 1.0, 6.0, ((1, 32),), jnp.float32)
    gates = draw_gates(jax.random.fold_in(seeds[3], 71), 0)
    return dict(state=state, costate=costate, gates=gates)


def undo_gate(field, gate_now):
    gate_real = gate_now[0]
    gate_imag = gate_now[1]
    high = lax.Precision.HIGHEST
    new_real = jnp.einsum('ts,dtc->dsc', gate_real, field[0], precision=high) + jnp.einsum('ts,dtc->dsc', gate_imag, field[1], precision=high)
    new_imag = jnp.einsum('ts,dtc->dsc', gate_real, field[1], precision=high) - jnp.einsum('ts,dtc->dsc', gate_imag, field[0], precision=high)
    return jnp.stack([new_real, new_imag], axis=0)

def gate_gradient(adjoint, amplitudes):
    high = lax.Precision.HIGHEST
    grad_real = jnp.einsum('dtc,dsc->ts', adjoint[0], amplitudes[0], precision=high) + jnp.einsum('dtc,dsc->ts', adjoint[1], amplitudes[1], precision=high)
    grad_imag = jnp.einsum('dtc,dsc->ts', adjoint[1], amplitudes[0], precision=high) - jnp.einsum('dtc,dsc->ts', adjoint[0], amplitudes[1], precision=high)
    return jnp.stack([grad_real, grad_imag], axis=0)

def swap_bits(field, dev_bit, gate_bit):
    shape_now = field.shape
    reshaped = field.reshape(2, shape_now[1] >> dev_bit + 1, 2, 1 << dev_bit, shape_now[2] >> gate_bit + 1, 2, (1 << gate_bit) * shape_now[3])
    return jnp.swapaxes(reshaped, 2, 5).reshape(shape_now)

def regroup_bits(field):
    shape_now = field.shape
    reshaped = field.reshape(2, shape_now[1], shape_now[2] // shape_now[1], shape_now[1], shape_now[3])
    return jnp.swapaxes(reshaped, 1, 3).reshape(shape_now)

def reference(state, costate, gates):
    columns = AMP_DEV // GATE
    amplitudes = state.reshape(2, N_AMP, GATE, columns)
    adjoint = costate.reshape(2, N_AMP, GATE, columns)
    device_bits = N_AMP.bit_length() - 1
    gate_bits = GATE.bit_length() - 1
    grad_scale = 1.0 / math.sqrt(STATE // GATE)
    gradient_list = []
    for layer_index in range(LAYERS):
        amplitudes = undo_gate(amplitudes, gates[layer_index])
        gradient_list.append(gate_gradient(adjoint, amplitudes) * grad_scale)
        adjoint = undo_gate(adjoint, gates[layer_index])
        if layer_index + 1 < LAYERS:
            if layer_index % 2 == 0:
                amplitudes = swap_bits(amplitudes, device_bits - 1, gate_bits - 1)
                adjoint = swap_bits(adjoint, device_bits - 1, gate_bits - 1)
                amplitudes = swap_bits(amplitudes, 0, gate_bits - 2)
                adjoint = swap_bits(adjoint, 0, gate_bits - 2)
            else:
                amplitudes = regroup_bits(amplitudes)
                adjoint = regroup_bits(adjoint)
    return (amplitudes.reshape(2, STATE), adjoint.reshape(2, STATE), jnp.stack(gradient_list, axis=0))
```

```python
import functools
import math

import jax
import jax.numpy as jnp
from jax import lax
from jax.experimental import pallas as pl
from jax.experimental.pallas import tpu as pltpu
from jax.sharding import PartitionSpec as P

VMEM_BYTES = 40 * 1024 * 1024
ROW_ROW = (((1,), (1,)), ((), ()))


def split(value):
    high = value.astype(jnp.bfloat16)
    low = (value - high.astype(jnp.float32)).astype(jnp.bfloat16)
    return high, low


def dot_parts(left_both, right, dims=None):
    dims = (((1,), (0,)), ((), ())) if dims is None else dims
    rows = left_both.shape[0] // 2
    high, low = split(right)
    first = lax.dot_general(left_both, high, dims, preferred_element_type=jnp.float32)
    second = lax.dot_general(left_both[:rows], low, dims, preferred_element_type=jnp.float32)
    return first[:rows] + first[rows:] + second


def both_parts(value):
    high, low = split(value)
    return jnp.concatenate([high, low], axis=0)


def lane_index(shape):
    return lax.broadcasted_iota(jnp.int32, shape, len(shape) - 1)


def turned(value):
    lanes = value.shape[-1]
    step = lanes // 4
    ahead = pltpu.roll(value, lanes - step, 1)
    back = pltpu.roll(value, step, 1)
    return jnp.where((lane_index(value.shape) // step) % 2 == 0, ahead, -back)


def swap_groups(values):
    lanes = values[0].shape[-1]
    group = lane_index(values[0].shape) // (lanes // 4)
    for bit in (2, 1):
        width = bit * (lanes // 4)
        fresh = list(values)
        for index in range(4):
            if index & bit == 0:
                low, high = values[index], values[index | bit]
                upper = group & bit != 0
                fresh[index] = jnp.where(upper, pltpu.roll(high, width, 1), low)
                fresh[index | bit] = jnp.where(upper, high, pltpu.roll(low, lanes - width, 1))
        values = fresh
    return values


def first_kernel(state_ref, costate_ref, gate_ref, out_ref, matrix_ref):
    block = pl.program_id(0)
    order = gate_ref.shape[1]
    stride = state_ref.shape[0] // order

    @pl.when(block == 0)
    def _():
        real, imag = gate_ref[0].T, gate_ref[1].T
        top = jnp.concatenate([real, imag], axis=1)
        low = jnp.concatenate([-imag, real], axis=1)
        matrix_ref[...] = both_parts(jnp.concatenate([top, low], axis=0))

    def column(ref):
        parts = [ref[pl.ds(block * 2 + part, order, stride=stride), :] for part in range(2)]
        return jnp.concatenate(parts, axis=0)

    lanes = state_ref.shape[1]
    field = jnp.concatenate([column(state_ref), column(costate_ref)], axis=1)
    undone = dot_parts(matrix_ref[...], field)
    pieces = [
        undone[part * order : (part + 1) * order, vector * lanes : (vector + 1) * lanes]
        for vector in range(2)
        for part in range(2)
    ]
    for index, piece in enumerate(swap_groups(pieces)):
        out_ref[index] = piece


def undo_matrix(real, imag):
    return both_parts(jnp.concatenate([real.T, imag.T], axis=1))


def middle_kernel(moved_ref, gates_ref, out_ref, matrix_ref, kept_ref, *, devices):
    phase = pl.program_id(0)
    step = pl.program_id(1)
    order, lanes = moved_ref.shape[3], moved_ref.shape[4]
    low_rows = order // 4

    @pl.when((phase == 0) & (step == 0))
    def _():
        matrix_ref[0] = undo_matrix(gates_ref[1, 0], gates_ref[1, 1])
        matrix_ref[1] = undo_matrix(gates_ref[2, 0], gates_ref[2, 1])

    def undo(which, fields):
        plain = jnp.concatenate(fields, axis=1)
        other = jnp.concatenate([turned(field) for field in fields], axis=1)
        result = dot_parts(matrix_ref[which], jnp.concatenate([plain, other], axis=0))
        return [result[:, index * lanes : (index + 1) * lanes] for index in range(len(fields))]

    @pl.when(phase == 0)
    def _():
        fields = []
        for group in range(4):
            rows = pl.ds(group * low_rows, low_rows)
            parts = [moved_ref[top, 0, low, rows, :] for top in range(2) for low in range(2)]
            fields.append(jnp.concatenate(parts, axis=0))
        for group, result in enumerate(undo(0, fields)):
            place = (group // 2 * (devices // 4) + step) * 2 + group % 2
            kept_ref[pl.ds(pl.multiple_of(place * order, order), order), :] = result

    @pl.when(phase == 1)
    def _():
        fields = []
        for index in range(4):
            batch = step * 4 + index
            parts = [
                kept_ref[pl.ds(high * devices + batch, devices, stride=order), :]
                for high in range(order // devices)
            ]
            fields.append(jnp.concatenate(parts, axis=0))
        for index, result in enumerate(undo(1, fields)):
            out_ref[index] = result


def outer_parts(fields):
    lanes = fields[0].shape[-1]
    lower = lane_index(fields[0].shape) < lanes // 2
    adjoint, plain, other = [], [], []
    for first, second in zip(fields[0::2], fields[1::2]):
        adjoint.append(jnp.where(lower, pltpu.roll(first, lanes // 2, 1), second))
        pair = jnp.where(lower, first, pltpu.roll(second, lanes // 2, 1))
        plain.append(pair)
        other.append(-turned(pair))
    right = jnp.concatenate(
        [jnp.concatenate(plain, axis=1), jnp.concatenate(other, axis=1)], axis=0
    )
    return dot_parts(both_parts(jnp.concatenate(adjoint, axis=1)), right, ROW_ROW)


def gradient_kernel(moved_ref, last_ref, gates_ref, out_ref, sum_ref, *, scale):
    step = pl.program_id(0)
    order = moved_ref.shape[3]
    low_rows = order // 4
    whole = [moved_ref[top, 0, low] for top in range(2) for low in range(2)]
    mixed = [
        jnp.concatenate([part[group * low_rows : (group + 1) * low_rows] for part in whole], axis=0)
        for group in range(4)
    ]
    terms = [outer_parts(whole), outer_parts(mixed), outer_parts([last_ref[i] for i in range(4)])]

    @pl.when(step == 0)
    def _():
        for index, term in enumerate(terms):
            sum_ref[index] = term

    @pl.when(step > 0)
    def _():
        for index, term in enumerate(terms):
            sum_ref[index] += term

    @pl.when(step == pl.num_programs(0) - 1)
    def _():
        def times(left, right):
            return jnp.dot(
                left, right, precision=lax.Precision.HIGHEST, preferred_element_type=jnp.float32
            )

        for index in range(3):
            total = (sum_ref[index, :, :order], sum_ref[index, :, order:])
            gate = (gates_ref[index, 0], gates_ref[index, 1])
            left, right = (total, gate) if index == 1 else (gate, total)
            out_ref[index, 0] = (times(left[0], right[0]) - times(left[1], right[1])) * scale
            out_ref[index, 1] = (times(left[0], right[1]) + times(left[1], right[0])) * scale


def last_kernel(moved_ref, state_ref, costate_ref):
    block = pl.program_id(0)
    order = moved_ref.shape[1]
    stride = state_ref.shape[0] // order
    pieces = swap_groups([moved_ref[index] for index in range(4)])
    for index, piece in enumerate(pieces):
        ref = (state_ref, costate_ref)[index // 2]
        ref[pl.ds(block * 2 + index % 2, order, stride=stride), :] = piece


def tree_sum(parts):
    while len(parts) > 1:
        parts = [parts[i] + parts[i + 1] for i in range(0, len(parts), 2)]
    return parts[0]


def sum_over_devices(value):
    devices = lax.axis_size("amp")
    inner = min(8, devices)
    place = lax.axis_index("amp") % inner
    blocks = value.reshape(inner, -1, value.shape[-1])

    def send(part, distance):
        return lax.ppermute(part, "amp", [(i, i ^ distance) for i in range(devices)])

    def pick(stack, index):
        return lax.dynamic_index_in_dim(stack, index, 0, keepdims=False)

    part = tree_sum(
        [pick(blocks, place)] + [send(pick(blocks, place ^ k), k) for k in range(1, inner)]
    )
    part = tree_sum([part] + [send(part, k) for k in range(inner, devices, inner)])
    found = jnp.stack([part] + [send(part, k) for k in range(1, inner)], axis=0)
    return jnp.stack([pick(found, place ^ k) for k in range(inner)], axis=0).reshape(value.shape)


def to_rows(field, lanes):
    return field.reshape(2, -1, lanes).swapaxes(0, 1).reshape(-1, lanes)


def from_rows(rows):
    return rows.reshape(-1, 2, rows.shape[-1]).swapaxes(0, 1).reshape(2, -1)


def whole_spec(shape):
    return pl.BlockSpec(shape, lambda *_: (0,) * len(shape))


def params(dimensions):
    return pltpu.CompilerParams(
        dimension_semantics=("arbitrary",) * dimensions, vmem_limit_bytes=VMEM_BYTES
    )


def on_device_lanes(state, costate, gates, devices, order, columns):
    lanes = 4 * columns // devices
    steps = devices // 4
    rows = 2 * order * columns // lanes
    half = pltpu.VMEM
    sent = pl.pallas_call(
        first_kernel,
        grid=(steps,),
        in_specs=[whole_spec((rows, lanes)), whole_spec((rows, lanes)), whole_spec((2, order, order))],
        out_specs=pl.BlockSpec((4, order, lanes), lambda i: (i, 0, 0)),
        out_shape=jax.ShapeDtypeStruct((devices, order, lanes), jnp.float32),
        scratch_shapes=[half((4 * order, 2 * order), jnp.bfloat16)],
        compiler_params=params(1),
    )(to_rows(state, lanes), to_rows(costate, lanes), gates[0])
    moved = lax.all_to_all(sent, "amp", 0, 0, tiled=True)
    moved = moved.reshape(2, steps, 2, order, lanes)
    last = pl.pallas_call(
        functools.partial(middle_kernel, devices=devices),
        grid=(2, steps),
        in_specs=[
            pl.BlockSpec(
                (2, 1, 2, order, lanes),
                lambda p, i: (0, i * (1 - p) + (steps - 1) * p, 0, 0, 0),
            ),
            whole_spec(gates.shape),
        ],
        out_specs=pl.BlockSpec((4, order, lanes), lambda p, i: (i * p, 0, 0)),
        out_shape=jax.ShapeDtypeStruct((devices, order, lanes), jnp.float32),
        scratch_shapes=[
            half((2, 2 * order, 2 * order), jnp.bfloat16),
            half((devices * order, lanes), jnp.float32),
        ],
        compiler_params=params(2),
    )(moved, gates)
    arrived = lax.all_to_all(last, "amp", 0, 0, tiled=True)
    gradients = pl.pallas_call(
        functools.partial(gradient_kernel, scale=1.0 / math.sqrt(devices * columns)),
        grid=(steps,),
        in_specs=[
            pl.BlockSpec((2, 1, 2, order, lanes), lambda i: (0, i, 0, 0, 0)),
            pl.BlockSpec((4, order, lanes), lambda i: (i, 0, 0)),
            whole_spec(gates.shape),
        ],
        out_specs=whole_spec(gates.shape),
        out_shape=jax.ShapeDtypeStruct(gates.shape, jnp.float32),
        scratch_shapes=[half((3, order, 2 * order), jnp.float32)],
        compiler_params=params(1),
    )(moved, last, gates)
    gradients = sum_over_devices(gradients)
    state_rows, costate_rows = pl.pallas_call(
        last_kernel,
        grid=(steps,),
        in_specs=[pl.BlockSpec((4, order, lanes), lambda i: (i, 0, 0))],
        out_specs=[whole_spec((rows, lanes)), whole_spec((rows, lanes))],
        out_shape=[jax.ShapeDtypeStruct((rows, lanes), jnp.float32)] * 2,
        compiler_params=params(1),
    )(arrived)
    return from_rows(state_rows), from_rows(costate_rows), gradients


def undo_gate(field, gate):
    high = lax.Precision.HIGHEST
    shape = field.shape
    parts = field.reshape(shape[:-1] + (2, 2, -1))
    real, imag = parts[..., 0, :], parts[..., 1, :]

    def contract(matrix, operand):
        return jnp.einsum("ts,btvc->bsvc", matrix, operand, precision=high)

    new_real = contract(gate[0], real) + contract(gate[1], imag)
    new_imag = contract(gate[0], imag) - contract(gate[1], real)
    return jnp.stack([new_real, new_imag], axis=-2).reshape(shape)


def gate_gradient(before, after):
    high = lax.Precision.HIGHEST
    lam = before.reshape(before.shape[:-1] + (2, 2, -1))[..., 1, :, :]
    psi = after.reshape(after.shape[:-1] + (2, 2, -1))[..., 0, :, :]
    real = jnp.einsum("btpc,bspc->ts", lam, psi, precision=high)
    imag = jnp.einsum("btc,bsc->ts", lam[..., 1, :], psi[..., 0, :], precision=high) - jnp.einsum(
        "btc,bsc->ts", lam[..., 0, :], psi[..., 1, :], precision=high
    )
    return jnp.stack([real, imag], axis=0)


def on_device_plain(state, costate, gates, devices, order, columns):
    own = columns // devices
    both = jnp.stack([state, costate], axis=0).reshape(2, 2, order, devices, own)
    field = both.transpose(3, 2, 0, 1, 4).reshape(devices, order, 4 * own)
    field = lax.all_to_all(field, "amp", 0, 0, tiled=True)
    after = undo_gate(field, gates[0])
    terms = [gate_gradient(field, after)]
    field = after.reshape(2, devices // 4, 2, 2, 2, order // 4, 4 * own)
    field = field.transpose(3, 1, 4, 0, 2, 5, 6).reshape(devices, order, 4 * own)
    after = undo_gate(field, gates[1])
    terms.append(gate_gradient(field, after))
    field = after.reshape(devices, order // devices, devices, 4 * own)
    field = field.transpose(2, 1, 0, 3).reshape(devices, order, 4 * own)
    after = undo_gate(field, gates[2])
    terms.append(gate_gradient(field, after))
    gradients = sum_over_devices(jnp.stack(terms, axis=0)) / math.sqrt(devices * columns)
    field = lax.all_to_all(after, "amp", 0, 0, tiled=True)
    field = field.reshape(devices, order, 2, 2, own).transpose(2, 3, 1, 0, 4)
    field = field.reshape(2, 2, order * columns)
    return field[0], field[1], gradients


def on_device(state, costate, gates):
    devices = lax.axis_size("amp")
    order = gates.shape[2]
    columns = state.shape[1] // order
    form = on_device_lanes if 4 * columns == 128 * devices else on_device_plain
    return form(state, costate, gates, devices, order, columns)


def solution(mesh):
    return jax.shard_map(
        on_device,
        mesh=mesh,
        in_specs=(P(None, "amp"), P(None, "amp"), P()),
        out_specs=(P(None, "amp"), P(None, "amp"), P()),
        check_vma=False,
    )
```

```python
import functools
import math

import jax
import jax.numpy as jnp
from jax import lax
from jax.experimental import pallas as pl
from jax.experimental.pallas import tpu as pltpu
from jax.sharding import PartitionSpec as P

VMEM_BYTES = 24 * 1024 * 1024
ROW_ROW = (((1,), (1,)), ((), ()))


def split(value):
    high = value.astype(jnp.bfloat16)
    low = (value - high.astype(jnp.float32)).astype(jnp.bfloat16)
    return high, low


def dot_parts(left_both, right, dims=None):
    dims = (((1,), (0,)), ((), ())) if dims is None else dims
    rows = left_both.shape[0] // 2
    high, low = split(right)
    first = lax.dot_general(left_both, high, dims, preferred_element_type=jnp.float32)
    second = lax.dot_general(left_both[:rows], low, dims, preferred_element_type=jnp.float32)
    return first[:rows] + first[rows:] + second


def both_parts(value):
    high, low = split(value)
    return jnp.concatenate([high, low], axis=0)


def lane_index(shape):
    return lax.broadcasted_iota(jnp.int32, shape, len(shape) - 1)


def turned(value):
    lanes = value.shape[-1]
    step = lanes // 4
    ahead = pltpu.roll(value, lanes - step, 1)
    back = pltpu.roll(value, step, 1)
    return jnp.where((lane_index(value.shape) // step) % 2 == 0, ahead, -back)


def swap_groups(values):
    lanes = values[0].shape[-1]
    group = lane_index(values[0].shape) // (lanes // 4)
    for bit in (2, 1):
        width = bit * (lanes // 4)
        fresh = list(values)
        for index in range(4):
            if index & bit == 0:
                low, high = values[index], values[index | bit]
                upper = group & bit != 0
                fresh[index] = jnp.where(upper, pltpu.roll(high, width, 1), low)
                fresh[index | bit] = jnp.where(upper, high, pltpu.roll(low, lanes - width, 1))
        values = fresh
    return values


def wait_all(copies):
    for copy in copies:
        copy.wait()


def first_kernel(state_ref, costate_ref, gates_ref, out_ref, state, costate, gate, copy_sems):
    order = gate.shape[1]
    lanes = state.shape[1]
    stride = state.shape[0] // order
    copies = [
        pltpu.make_async_copy(source, target, copy_sems.at[index])
        for index, (source, target) in enumerate(
            [(gates_ref.at[0], gate), (state_ref, state), (costate_ref, costate)]
        )
    ]
    for copy in copies:
        copy.start()
    copies[0].wait()
    real, imag = gate[0].T, gate[1].T
    top = jnp.concatenate([real, imag], axis=1)
    low = jnp.concatenate([-imag, real], axis=1)
    matrix = both_parts(jnp.concatenate([top, low], axis=0))
    wait_all(copies[1:])

    def column(ref, block):
        parts = [ref[pl.ds(block * 2 + part, order, stride=stride), :] for part in range(2)]
        return jnp.concatenate(parts, axis=0)

    for block in range(stride // 2):
        field = jnp.concatenate([column(state, block), column(costate, block)], axis=1)
        undone = dot_parts(matrix, field)
        pieces = [
            undone[part * order : (part + 1) * order, vector * lanes : (vector + 1) * lanes]
            for vector in range(2)
            for part in range(2)
        ]
        for index, piece in enumerate(swap_groups(pieces)):
            out_ref[block * 4 + index] = piece


def undo_matrix(real, imag):
    return both_parts(jnp.concatenate([real.T, imag.T], axis=1))


def middle_kernel(moved_ref, matrix_ref, out_ref, kept_ref):
    _, steps, _, order, lanes = moved_ref.shape
    devices = 4 * steps
    low_rows = order // 4

    def undo(which, fields):
        plain = jnp.concatenate(fields, axis=1)
        other = jnp.concatenate([turned(field) for field in fields], axis=1)
        result = dot_parts(matrix_ref[which], jnp.concatenate([plain, other], axis=0))
        return [result[:, index * lanes : (index + 1) * lanes] for index in range(len(fields))]

    @pl.loop(0, steps)
    def _(step):
        fields = []
        for group in range(4):
            rows = pl.ds(group * low_rows, low_rows)
            parts = [moved_ref[top, step, low, rows, :] for top in range(2) for low in range(2)]
            fields.append(jnp.concatenate(parts, axis=0))
        for group, result in enumerate(undo(0, fields)):
            place = (group // 2 * steps + step) * 2 + group % 2
            kept_ref[pl.ds(pl.multiple_of(place * order, order), order), :] = result

    @pl.loop(0, steps)
    def _(step):
        fields = []
        for index in range(4):
            batch = step * 4 + index
            parts = [
                kept_ref[pl.ds(high * devices + batch, devices, stride=order), :]
                for high in range(order // devices)
            ]
            fields.append(jnp.concatenate(parts, axis=0))
        for index, result in enumerate(undo(1, fields)):
            out_ref[step * 4 + index] = result


def outer_parts(fields):
    lanes = fields[0].shape[-1]
    lower = lane_index(fields[0].shape) < lanes // 2
    adjoint, plain, other = [], [], []
    for first, second in zip(fields[0::2], fields[1::2]):
        adjoint.append(jnp.where(lower, pltpu.roll(first, lanes // 2, 1), second))
        pair = jnp.where(lower, first, pltpu.roll(second, lanes // 2, 1))
        plain.append(pair)
        other.append(-turned(pair))
    right = jnp.concatenate(
        [jnp.concatenate(plain, axis=1), jnp.concatenate(other, axis=1)], axis=0
    )
    return dot_parts(both_parts(jnp.concatenate(adjoint, axis=1)), right, ROW_ROW)


def complex_product(left, right, scale):
    def times(first, second):
        return jnp.dot(
            first, second, precision=lax.Precision.HIGHEST, preferred_element_type=jnp.float32
        )

    real = times(left[0], right[0]) - times(left[1], right[1])
    imag = times(left[0], right[1]) + times(left[1], right[0])
    return real * scale, imag * scale


def early_kernel(sent_ref, gates_ref, out_ref, matrix_ref, sum_ref, *, scale):
    devices, order, _ = sent_ref.shape
    matrix_ref[0] = undo_matrix(gates_ref[1, 0], gates_ref[1, 1])
    matrix_ref[1] = undo_matrix(gates_ref[2, 0], gates_ref[2, 1])
    sum_ref[...] = jnp.zeros_like(sum_ref)

    @pl.loop(0, devices // 4)
    def _(step):
        sum_ref[...] += outer_parts([sent_ref[step * 4 + index] for index in range(4)])

    total = (sum_ref[:, :order], sum_ref[:, order:])
    out_ref[0], out_ref[1] = complex_product((gates_ref[0, 0], gates_ref[0, 1]), total, scale)


def late_kernel(moved_ref, last_ref, gates_ref, out_ref, sum_ref, *, scale):
    steps, order = moved_ref.shape[1], moved_ref.shape[3]
    low_rows = order // 4
    sum_ref[...] = jnp.zeros_like(sum_ref)

    @pl.loop(0, steps)
    def _(step):
        mixed = []
        for group in range(4):
            rows = pl.ds(group * low_rows, low_rows)
            parts = [moved_ref[top, step, low, rows, :] for top in range(2) for low in range(2)]
            mixed.append(jnp.concatenate(parts, axis=0))
        sum_ref[0] += outer_parts(mixed)
        sum_ref[1] += outer_parts([last_ref[step * 4 + index] for index in range(4)])

    for index in range(2):
        total = (sum_ref[index, :, :order], sum_ref[index, :, order:])
        gate = (gates_ref[index + 1, 0], gates_ref[index + 1, 1])
        left, right = (total, gate) if index == 0 else (gate, total)
        out_ref[index, 0], out_ref[index, 1] = complex_product(left, right, scale)


def last_kernel(moved_ref, state_ref, costate_ref, state, costate, copy_sems):
    order = moved_ref.shape[1]
    stride = state.shape[0] // order
    chunks = copy_sems.shape[1]
    rows = order // chunks
    copies = []
    for chunk in range(chunks):
        for block in range(stride // 2):
            pieces = [
                moved_ref[block * 4 + index, pl.ds(chunk * rows, rows), :] for index in range(4)
            ]
            for index, piece in enumerate(swap_groups(pieces)):
                place = chunk * rows * stride + block * 2 + index % 2
                (state, costate)[index // 2][pl.ds(place, rows, stride=stride), :] = piece
        part = pl.ds(chunk * rows * stride, rows * stride)
        for index, (source, target) in enumerate([(state, state_ref), (costate, costate_ref)]):
            copy = pltpu.make_async_copy(
                source.at[part], target.at[part], copy_sems.at[index, chunk]
            )
            copy.start()
            copies.append(copy)
    wait_all(copies)


def tree_sum(parts):
    while len(parts) > 1:
        parts = [parts[i] + parts[i + 1] for i in range(0, len(parts), 2)]
    return parts[0]


def sum_over_devices(value):
    devices = lax.axis_size("amp")
    inner = min(8, devices)
    place = lax.axis_index("amp")

    def send(part, distance):
        return lax.ppermute(part, "amp", [(i, i ^ distance) for i in range(devices)])

    def pick(stack, index):
        return lax.dynamic_index_in_dim(stack, index, 0, keepdims=False)

    def scatter(part, count, distance):
        own = place // distance % count
        blocks = part.reshape(count, -1, part.shape[-1])
        return tree_sum(
            [pick(blocks, own)] + [send(pick(blocks, own ^ k), k * distance) for k in range(1, count)]
        )

    def gather(part, count, distance):
        own = place // distance % count
        found = jnp.stack([part] + [send(part, k * distance) for k in range(1, count)], axis=0)
        return jnp.concatenate([pick(found, own ^ k) for k in range(count)], axis=0)

    part = scatter(value.reshape(-1, value.shape[-1]), inner, 1)
    part = scatter(part, devices // inner, inner)
    part = gather(part, devices // inner, inner)
    return gather(part, inner, 1).reshape(value.shape)


def to_rows(field, lanes):
    return field.reshape(2, -1, lanes).swapaxes(0, 1).reshape(-1, lanes)


def from_rows(rows):
    return rows.reshape(-1, 2, rows.shape[-1]).swapaxes(0, 1).reshape(2, -1)


IN_HBM = pl.BlockSpec(memory_space=pl.ANY)
IN_VMEM = pl.BlockSpec(memory_space=pltpu.VMEM)
PARAMS = pltpu.CompilerParams(vmem_limit_bytes=VMEM_BYTES)


def on_device_lanes(state, costate, gates, devices, order, columns):
    lanes = 4 * columns // devices
    rows = 2 * order * columns // lanes
    scale = 1.0 / math.sqrt(devices * columns)
    field_shape = jax.ShapeDtypeStruct((devices, order, lanes), jnp.float32)
    rows_shape = jax.ShapeDtypeStruct((rows, lanes), jnp.float32)
    rows_buffer = pltpu.VMEM((rows, lanes), jnp.float32)
    sum_buffer = pltpu.VMEM((order, 2 * order), jnp.float32)
    sent = pl.pallas_call(
        first_kernel,
        in_specs=[IN_HBM, IN_HBM, IN_HBM],
        out_specs=IN_VMEM,
        out_shape=field_shape,
        scratch_shapes=[
            rows_buffer,
            rows_buffer,
            pltpu.VMEM((2, order, order), jnp.float32),
            pltpu.SemaphoreType.DMA((3,)),
        ],
        compiler_params=PARAMS,
    )(to_rows(state, lanes), to_rows(costate, lanes), gates)
    moved = lax.all_to_all(sent, "amp", 0, 0, tiled=True)
    early, matrices = pl.pallas_call(
        functools.partial(early_kernel, scale=scale),
        in_specs=[IN_VMEM, IN_VMEM],
        out_specs=[IN_VMEM, IN_VMEM],
        out_shape=[
            jax.ShapeDtypeStruct(gates.shape[1:], jnp.float32),
            jax.ShapeDtypeStruct((2, 2 * order, 2 * order), jnp.bfloat16),
        ],
        scratch_shapes=[sum_buffer],
        compiler_params=PARAMS,
    )(sent, gates)
    early = sum_over_devices(early)
    moved = moved.reshape(2, devices // 4, 2, order, lanes)
    last = pl.pallas_call(
        middle_kernel,
        in_specs=[IN_VMEM, IN_VMEM],
        out_specs=IN_VMEM,
        out_shape=field_shape,
        scratch_shapes=[pltpu.VMEM((devices * order, lanes), jnp.float32)],
        compiler_params=PARAMS,
    )(moved, matrices)
    arrived = lax.all_to_all(last, "amp", 0, 0, tiled=True)
    late = pl.pallas_call(
        functools.partial(late_kernel, scale=scale),
        in_specs=[IN_VMEM, IN_VMEM, IN_VMEM],
        out_specs=IN_VMEM,
        out_shape=jax.ShapeDtypeStruct((2,) + gates.shape[1:], jnp.float32),
        scratch_shapes=[pltpu.VMEM((2, order, 2 * order), jnp.float32)],
        compiler_params=PARAMS,
    )(moved, last, gates)
    late = sum_over_devices(late)
    state_rows, costate_rows = pl.pallas_call(
        last_kernel,
        in_specs=[IN_VMEM],
        out_specs=[IN_HBM, IN_HBM],
        out_shape=[rows_shape, rows_shape],
        scratch_shapes=[rows_buffer, rows_buffer, pltpu.SemaphoreType.DMA((2, 8))],
        compiler_params=PARAMS,
    )(arrived)
    gradients = jnp.concatenate([early[None], late], axis=0)
    return from_rows(state_rows), from_rows(costate_rows), gradients


def undo_gate(field, gate):
    high = lax.Precision.HIGHEST
    shape = field.shape
    parts = field.reshape(shape[:-1] + (2, 2, -1))
    real, imag = parts[..., 0, :], parts[..., 1, :]

    def contract(matrix, operand):
        return jnp.einsum("ts,btvc->bsvc", matrix, operand, precision=high)

    new_real = contract(gate[0], real) + contract(gate[1], imag)
    new_imag = contract(gate[0], imag) - contract(gate[1], real)
    return jnp.stack([new_real, new_imag], axis=-2).reshape(shape)


def gate_gradient(before, after):
    high = lax.Precision.HIGHEST
    lam = before.reshape(before.shape[:-1] + (2, 2, -1))[..., 1, :, :]
    psi = after.reshape(after.shape[:-1] + (2, 2, -1))[..., 0, :, :]
    real = jnp.einsum("btpc,bspc->ts", lam, psi, precision=high)
    imag = jnp.einsum("btc,bsc->ts", lam[..., 1, :], psi[..., 0, :], precision=high) - jnp.einsum(
        "btc,bsc->ts", lam[..., 0, :], psi[..., 1, :], precision=high
    )
    return jnp.stack([real, imag], axis=0)


def on_device_plain(state, costate, gates, devices, order, columns):
    own = columns // devices
    both = jnp.stack([state, costate], axis=0).reshape(2, 2, order, devices, own)
    field = both.transpose(3, 2, 0, 1, 4).reshape(devices, order, 4 * own)
    field = lax.all_to_all(field, "amp", 0, 0, tiled=True)
    after = undo_gate(field, gates[0])
    terms = [gate_gradient(field, after)]
    field = after.reshape(2, devices // 4, 2, 2, 2, order // 4, 4 * own)
    field = field.transpose(3, 1, 4, 0, 2, 5, 6).reshape(devices, order, 4 * own)
    after = undo_gate(field, gates[1])
    terms.append(gate_gradient(field, after))
    field = after.reshape(devices, order // devices, devices, 4 * own)
    field = field.transpose(2, 1, 0, 3).reshape(devices, order, 4 * own)
    after = undo_gate(field, gates[2])
    terms.append(gate_gradient(field, after))
    gradients = sum_over_devices(jnp.stack(terms, axis=0)) / math.sqrt(devices * columns)
    field = lax.all_to_all(after, "amp", 0, 0, tiled=True)
    field = field.reshape(devices, order, 2, 2, own).transpose(2, 3, 1, 0, 4)
    field = field.reshape(2, 2, order * columns)
    return field[0], field[1], gradients


def on_device(state, costate, gates):
    devices = lax.axis_size("amp")
    order = gates.shape[2]
    columns = state.shape[1] // order
    form = on_device_lanes if 4 * columns == 128 * devices else on_device_plain
    return form(state, costate, gates, devices, order, columns)


def solution(mesh):
    return jax.shard_map(
        on_device,
        mesh=mesh,
        in_specs=(P(None, "amp"), P(None, "amp"), P()),
        out_specs=(P(None, "amp"), P(None, "amp"), P()),
        check_vma=False,
    )
```

```python
import functools
import math

import jax
import jax.numpy as jnp
from jax import lax
from jax.experimental import pallas as pl
from jax.experimental.pallas import tpu as pltpu
from jax.sharding import PartitionSpec as P

VMEM_BYTES = 24 * 1024 * 1024
ROW_ROW = (((1,), (1,)), ((), ()))


def split(value):
    high = value.astype(jnp.bfloat16)
    low = (value - high.astype(jnp.float32)).astype(jnp.bfloat16)
    return high, low


def dot_parts(left_both, right, dims=None):
    dims = (((1,), (0,)), ((), ())) if dims is None else dims
    rows = left_both.shape[0] // 2
    high, low = split(right)
    first = lax.dot_general(left_both, high, dims, preferred_element_type=jnp.float32)
    second = lax.dot_general(left_both[:rows], low, dims, preferred_element_type=jnp.float32)
    return first[:rows] + first[rows:] + second


def both_parts(value):
    high, low = split(value)
    return jnp.concatenate([high, low], axis=0)


def lane_index(shape):
    return lax.broadcasted_iota(jnp.int32, shape, len(shape) - 1)


def turned(value):
    lanes = value.shape[-1]
    step = lanes // 4
    ahead = pltpu.roll(value, lanes - step, 1)
    back = pltpu.roll(value, step, 1)
    return jnp.where((lane_index(value.shape) // step) % 2 == 0, ahead, -back)


def swap_groups(values):
    lanes = values[0].shape[-1]
    group = lane_index(values[0].shape) // (lanes // 4)
    for bit in (2, 1):
        width = bit * (lanes // 4)
        fresh = list(values)
        for index in range(4):
            if index & bit == 0:
                low, high = values[index], values[index | bit]
                upper = group & bit != 0
                fresh[index] = jnp.where(upper, pltpu.roll(high, width, 1), low)
                fresh[index | bit] = jnp.where(upper, high, pltpu.roll(low, lanes - width, 1))
        values = fresh
    return values


def wait_all(copies):
    for copy in copies:
        copy.wait()


def first_kernel(
    state_ref, costate_ref, gates_ref, out_ref, state, costate, gate, field_ref, copy_sems, out_sems
):
    order = gate.shape[1]
    lanes = state.shape[1]
    stride = state.shape[0] // order
    copies = [
        pltpu.make_async_copy(source, target, copy_sems.at[index])
        for index, (source, target) in enumerate(
            [(gates_ref.at[0], gate), (state_ref, state), (costate_ref, costate)]
        )
    ]
    for copy in copies:
        copy.start()
    copies[0].wait()
    real, imag = gate[0].T, gate[1].T
    top = jnp.concatenate([real, imag], axis=1)
    low = jnp.concatenate([-imag, real], axis=1)
    matrix = both_parts(jnp.concatenate([top, low], axis=0))
    wait_all(copies[1:])
    copies = []

    def column(ref, block):
        parts = [ref[pl.ds(block * 2 + part, order, stride=stride), :] for part in range(2)]
        return jnp.concatenate(parts, axis=0)

    for block in range(stride // 2):
        field = jnp.concatenate([column(state, block), column(costate, block)], axis=1)
        undone = dot_parts(matrix, field)
        pieces = [
            undone[part * order : (part + 1) * order, vector * lanes : (vector + 1) * lanes]
            for vector in range(2)
            for part in range(2)
        ]
        for index, piece in enumerate(swap_groups(pieces)):
            field_ref[block * 4 + index] = piece
        part = pl.ds(block * 4, 4)
        copy = pltpu.make_async_copy(field_ref.at[part], out_ref.at[part], out_sems.at[block])
        copy.start()
        copies.append(copy)
    wait_all(copies)


def undo_matrix(real, imag):
    return both_parts(jnp.concatenate([real.T, imag.T], axis=1))


def middle_kernel(moved_ref, matrix_ref, out_ref, kept_ref):
    _, steps, _, order, lanes = moved_ref.shape
    devices = 4 * steps
    low_rows = order // 4

    def undo(which, fields):
        plain = jnp.concatenate(fields, axis=1)
        other = jnp.concatenate([turned(field) for field in fields], axis=1)
        result = dot_parts(matrix_ref[which], jnp.concatenate([plain, other], axis=0))
        return [result[:, index * lanes : (index + 1) * lanes] for index in range(len(fields))]

    @pl.loop(0, steps)
    def _(step):
        fields = []
        for group in range(4):
            rows = pl.ds(group * low_rows, low_rows)
            parts = [moved_ref[top, step, low, rows, :] for top in range(2) for low in range(2)]
            fields.append(jnp.concatenate(parts, axis=0))
        for group, result in enumerate(undo(0, fields)):
            place = (group // 2 * steps + step) * 2 + group % 2
            kept_ref[pl.ds(pl.multiple_of(place * order, order), order), :] = result

    @pl.loop(0, steps)
    def _(step):
        fields = []
        for index in range(4):
            batch = step * 4 + index
            parts = [
                kept_ref[pl.ds(high * devices + batch, devices, stride=order), :]
                for high in range(order // devices)
            ]
            fields.append(jnp.concatenate(parts, axis=0))
        for index, result in enumerate(undo(1, fields)):
            out_ref[step * 4 + index] = result


def outer_parts(fields):
    lanes = fields[0].shape[-1]
    lower = lane_index(fields[0].shape) < lanes // 2
    adjoint, plain, other = [], [], []
    for first, second in zip(fields[0::2], fields[1::2]):
        adjoint.append(jnp.where(lower, pltpu.roll(first, lanes // 2, 1), second))
        pair = jnp.where(lower, first, pltpu.roll(second, lanes // 2, 1))
        plain.append(pair)
        other.append(-turned(pair))
    right = jnp.concatenate(
        [jnp.concatenate(plain, axis=1), jnp.concatenate(other, axis=1)], axis=0
    )
    return dot_parts(both_parts(jnp.concatenate(adjoint, axis=1)), right, ROW_ROW)


def complex_product(left, right, scale):
    def times(first, second):
        return jnp.dot(
            first, second, precision=lax.Precision.HIGHEST, preferred_element_type=jnp.float32
        )

    real = times(left[0], right[0]) - times(left[1], right[1])
    imag = times(left[0], right[1]) + times(left[1], right[0])
    return real * scale, imag * scale


def early_kernel(sent_ref, gates_ref, out_ref, matrix_ref):
    devices = sent_ref.shape[0]
    matrix_ref[0] = undo_matrix(gates_ref[1, 0], gates_ref[1, 1])
    matrix_ref[1] = undo_matrix(gates_ref[2, 0], gates_ref[2, 1])
    out_ref[...] = jnp.zeros_like(out_ref)

    @pl.loop(0, devices // 4)
    def _(step):
        out_ref[...] += outer_parts([sent_ref[step * 4 + index] for index in range(4)])


def late_kernel(moved_ref, last_ref, early_ref, gates_ref, out_ref, sum_ref, *, scale):
    steps, order = moved_ref.shape[1], moved_ref.shape[3]
    low_rows = order // 4
    sum_ref[0] = early_ref[...]
    sum_ref[1:3] = jnp.zeros((2,) + early_ref.shape, jnp.float32)

    @pl.loop(0, steps)
    def _(step):
        mixed = []
        for group in range(4):
            rows = pl.ds(group * low_rows, low_rows)
            parts = [moved_ref[top, step, low, rows, :] for top in range(2) for low in range(2)]
            mixed.append(jnp.concatenate(parts, axis=0))
        sum_ref[1] += outer_parts(mixed)
        sum_ref[2] += outer_parts([last_ref[step * 4 + index] for index in range(4)])

    for index in range(3):
        total = (sum_ref[index, :, :order], sum_ref[index, :, order:])
        gate = (gates_ref[index, 0], gates_ref[index, 1])
        left, right = (total, gate) if index == 1 else (gate, total)
        out_ref[index, 0], out_ref[index, 1] = complex_product(left, right, scale)


def last_kernel(moved_ref, state_ref, costate_ref, state, costate, copy_sems):
    order = moved_ref.shape[1]
    stride = state.shape[0] // order
    chunks = copy_sems.shape[1]
    rows = order // chunks
    copies = []
    for chunk in range(chunks):
        for block in range(stride // 2):
            pieces = [
                moved_ref[block * 4 + index, pl.ds(chunk * rows, rows), :] for index in range(4)
            ]
            for index, piece in enumerate(swap_groups(pieces)):
                place = chunk * rows * stride + block * 2 + index % 2
                (state, costate)[index // 2][pl.ds(place, rows, stride=stride), :] = piece
        part = pl.ds(chunk * rows * stride, rows * stride)
        for index, (source, target) in enumerate([(state, state_ref), (costate, costate_ref)]):
            copy = pltpu.make_async_copy(
                source.at[part], target.at[part], copy_sems.at[index, chunk]
            )
            copy.start()
            copies.append(copy)
    wait_all(copies)


def tree_sum(parts):
    while len(parts) > 1:
        parts = [parts[i] + parts[i + 1] for i in range(0, len(parts), 2)]
    return parts[0]


def exchange(part, distance):
    devices = lax.axis_size("amp")
    return lax.ppermute(part, "amp", [(i, i ^ distance) for i in range(devices)])


def scattered_sum(value):
    devices = lax.axis_size("amp")
    place = lax.axis_index("amp")
    half = devices // 2
    inner = min(8, half)

    def scatter(blocks, distance):
        count = blocks.shape[0]
        own = place // distance % count

        def pick(index):
            return lax.dynamic_index_in_dim(blocks, index, 0, keepdims=False)

        return tree_sum(
            [pick(own)] + [exchange(pick(own ^ k), k * distance) for k in range(1, count)]
        )

    blocks = value.reshape(half // inner, inner, -1, value.shape[-1])
    part = scatter(blocks.swapaxes(0, 1), 1)
    part = scatter(part, inner)
    return part + exchange(part, half)


def gathered(part):
    devices = lax.axis_size("amp")
    half = devices // 2
    groups = [list(range(half)), list(range(half, devices))]
    copies = jnp.broadcast_to(part[None], (half,) + part.shape)
    return lax.all_to_all(copies, "amp", 0, 0, axis_index_groups=groups, tiled=True)


def to_rows(field, lanes):
    return field.reshape(2, -1, lanes).swapaxes(0, 1).reshape(-1, lanes)


def from_rows(rows):
    return rows.reshape(-1, 2, rows.shape[-1]).swapaxes(0, 1).reshape(2, -1)


IN_HBM = pl.BlockSpec(memory_space=pltpu.HBM)
IN_VMEM = pl.BlockSpec(memory_space=pltpu.VMEM)
PARAMS = pltpu.CompilerParams(vmem_limit_bytes=VMEM_BYTES)
FIRST_PARAMS = pltpu.CompilerParams(vmem_limit_bytes=60 * 1024 * 1024)


def cost(layers, amplitudes, order):
    flops = layers * 3 * 8 * amplitudes * order
    return pl.CostEstimate(flops=flops, bytes_accessed=32 * amplitudes, transcendentals=0)


def on_device_lanes(state, costate, gates, devices, order, columns):
    lanes = 4 * columns // devices
    rows = 2 * order * columns // lanes
    scale = 1.0 / math.sqrt(devices * columns)
    field_shape = jax.ShapeDtypeStruct((devices, order, lanes), jnp.float32)
    rows_shape = jax.ShapeDtypeStruct((rows, lanes), jnp.float32)
    rows_buffer = pltpu.VMEM((rows, lanes), jnp.float32)
    sum_shape = (order, 2 * order)
    amplitudes = 2 * order * columns
    sent = pl.pallas_call(
        first_kernel,
        in_specs=[IN_HBM, IN_HBM, IN_HBM],
        out_specs=IN_HBM,
        out_shape=field_shape,
        scratch_shapes=[
            rows_buffer,
            rows_buffer,
            pltpu.VMEM((2, order, order), jnp.float32),
            pltpu.VMEM(field_shape.shape, jnp.float32),
            pltpu.SemaphoreType.DMA((3,)),
            pltpu.SemaphoreType.DMA((devices // 4,)),
        ],
        compiler_params=FIRST_PARAMS,
        cost_estimate=cost(1, amplitudes, order),
    )(to_rows(state, lanes), to_rows(costate, lanes), gates)
    moved = lax.all_to_all(sent, "amp", 0, 0, tiled=True)
    early, matrices = pl.pallas_call(
        early_kernel,
        in_specs=[IN_VMEM, IN_VMEM],
        out_specs=[IN_VMEM, IN_VMEM],
        out_shape=[
            jax.ShapeDtypeStruct(sum_shape, jnp.float32),
            jax.ShapeDtypeStruct((2, 2 * order, 2 * order), jnp.bfloat16),
        ],
        compiler_params=PARAMS,
        cost_estimate=cost(1, amplitudes, order),
    )(sent, gates)
    moved = moved.reshape(2, devices // 4, 2, order, lanes)
    last = pl.pallas_call(
        middle_kernel,
        in_specs=[IN_VMEM, IN_VMEM],
        out_specs=IN_VMEM,
        out_shape=field_shape,
        scratch_shapes=[pltpu.VMEM((devices * order, lanes), jnp.float32)],
        compiler_params=PARAMS,
        cost_estimate=cost(2, amplitudes, order),
    )(moved, matrices)
    arrived = lax.all_to_all(last, "amp", 0, 0, tiled=True)
    gradients = pl.pallas_call(
        functools.partial(late_kernel, scale=scale),
        in_specs=[IN_VMEM, IN_VMEM, IN_VMEM, IN_VMEM],
        out_specs=IN_VMEM,
        out_shape=jax.ShapeDtypeStruct(gates.shape, jnp.float32),
        scratch_shapes=[pltpu.VMEM((3,) + sum_shape, jnp.float32)],
        compiler_params=PARAMS,
        cost_estimate=cost(2, amplitudes, order),
    )(moved, last, early, gates)
    part = scattered_sum(gradients)
    part, arrived = lax.optimization_barrier((part, arrived))
    gradients = gathered(part).reshape(gates.shape)
    state_rows, costate_rows = pl.pallas_call(
        last_kernel,
        in_specs=[IN_VMEM],
        out_specs=[IN_HBM, IN_HBM],
        out_shape=[rows_shape, rows_shape],
        scratch_shapes=[rows_buffer, rows_buffer, pltpu.SemaphoreType.DMA((2, order // 16))],
        compiler_params=PARAMS,
        cost_estimate=cost(1, amplitudes, order),
    )(arrived)
    return from_rows(state_rows), from_rows(costate_rows), gradients


def undo_gate(field, gate):
    high = lax.Precision.HIGHEST
    shape = field.shape
    parts = field.reshape(shape[:-1] + (2, 2, -1))
    real, imag = parts[..., 0, :], parts[..., 1, :]

    def contract(matrix, operand):
        return jnp.einsum("ts,btvc->bsvc", matrix, operand, precision=high)

    new_real = contract(gate[0], real) + contract(gate[1], imag)
    new_imag = contract(gate[0], imag) - contract(gate[1], real)
    return jnp.stack([new_real, new_imag], axis=-2).reshape(shape)


def gate_gradient(before, after):
    high = lax.Precision.HIGHEST
    lam = before.reshape(before.shape[:-1] + (2, 2, -1))[..., 1, :, :]
    psi = after.reshape(after.shape[:-1] + (2, 2, -1))[..., 0, :, :]
    real = jnp.einsum("btpc,bspc->ts", lam, psi, precision=high)
    imag = jnp.einsum("btc,bsc->ts", lam[..., 1, :], psi[..., 0, :], precision=high) - jnp.einsum(
        "btc,bsc->ts", lam[..., 0, :], psi[..., 1, :], precision=high
    )
    return jnp.stack([real, imag], axis=0)


def on_device_plain(state, costate, gates, devices, order, columns):
    own = columns // devices
    both = jnp.stack([state, costate], axis=0).reshape(2, 2, order, devices, own)
    field = both.transpose(3, 2, 0, 1, 4).reshape(devices, order, 4 * own)
    field = lax.all_to_all(field, "amp", 0, 0, tiled=True)
    after = undo_gate(field, gates[0])
    terms = [gate_gradient(field, after)]
    field = after.reshape(2, devices // 4, 2, 2, 2, order // 4, 4 * own)
    field = field.transpose(3, 1, 4, 0, 2, 5, 6).reshape(devices, order, 4 * own)
    after = undo_gate(field, gates[1])
    terms.append(gate_gradient(field, after))
    field = after.reshape(devices, order // devices, devices, 4 * own)
    field = field.transpose(2, 1, 0, 3).reshape(devices, order, 4 * own)
    after = undo_gate(field, gates[2])
    terms.append(gate_gradient(field, after))
    terms = jnp.stack(terms, axis=0) / math.sqrt(devices * columns)
    gradients = gathered(scattered_sum(terms)).reshape(gates.shape)
    field = lax.all_to_all(after, "amp", 0, 0, tiled=True)
    field = field.reshape(devices, order, 2, 2, own).transpose(2, 3, 1, 0, 4)
    field = field.reshape(2, 2, order * columns)
    return field[0], field[1], gradients


def on_device(state, costate, gates):
    devices = lax.axis_size("amp")
    order = gates.shape[2]
    columns = state.shape[1] // order
    form = on_device_lanes if 4 * columns == 128 * devices else on_device_plain
    return form(state, costate, gates, devices, order, columns)


def solution(mesh):
    return jax.shard_map(
        on_device,
        mesh=mesh,
        in_specs=(P(None, "amp"), P(None, "amp"), P()),
        out_specs=(P(None, "amp"), P(None, "amp"), P()),
        check_vma=False,
    )
```

```python
import functools
import math

import jax
import jax.numpy as jnp
from jax import lax
from jax.experimental import pallas as pl
from jax.experimental.pallas import tpu as pltpu
from jax.sharding import PartitionSpec as P

VMEM_BYTES = 24 * 1024 * 1024
ROW_ROW = (((1,), (1,)), ((), ()))


def split(value):
    high = value.astype(jnp.bfloat16)
    low = (value - high.astype(jnp.float32)).astype(jnp.bfloat16)
    return high, low


def dot_parts(left_both, right, dims=None):
    dims = (((1,), (0,)), ((), ())) if dims is None else dims
    rows = left_both.shape[0] // 2
    high, low = split(right)
    first = lax.dot_general(left_both, high, dims, preferred_element_type=jnp.float32)
    second = lax.dot_general(left_both[:rows], low, dims, preferred_element_type=jnp.float32)
    return first[:rows] + first[rows:] + second


def both_parts(value):
    high, low = split(value)
    return jnp.concatenate([high, low], axis=0)


def lane_index(shape):
    return lax.broadcasted_iota(jnp.int32, shape, len(shape) - 1)


def turned(value):
    lanes = value.shape[-1]
    step = lanes // 4
    ahead = pltpu.roll(value, lanes - step, 1)
    back = pltpu.roll(value, step, 1)
    return jnp.where((lane_index(value.shape) // step) % 2 == 0, ahead, -back)


def swap_groups(values):
    lanes = values[0].shape[-1]
    group = lane_index(values[0].shape) // (lanes // 4)
    for bit in (2, 1):
        width = bit * (lanes // 4)
        fresh = list(values)
        for index in range(4):
            if index & bit == 0:
                low, high = values[index], values[index | bit]
                upper = group & bit != 0
                fresh[index] = jnp.where(upper, pltpu.roll(high, width, 1), low)
                fresh[index | bit] = jnp.where(upper, high, pltpu.roll(low, lanes - width, 1))
        values = fresh
    return values


def wait_all(copies):
    for copy in copies:
        copy.wait()


def first_kernel(
    state_ref, costate_ref, gates_ref, out_ref, gate, rows, field_ref, gate_sem, row_sems, out_sems
):
    order = gate.shape[1]
    lanes = rows.shape[-1]
    columns = rows.shape[1]
    gate_copy = pltpu.make_async_copy(gates_ref.at[0], gate, gate_sem)
    gate_copy.start()
    row_copies = [
        [
            pltpu.make_async_copy(
                ref.at[:, column, 0], rows.at[vector, column], row_sems.at[vector, column]
            )
            for vector, ref in enumerate((state_ref, costate_ref))
        ]
        for column in range(columns)
    ]
    for pair in row_copies:
        for copy in pair:
            copy.start()
    gate_copy.wait()
    real, imag = gate[0].T, gate[1].T
    top = jnp.concatenate([real, imag], axis=1)
    low = jnp.concatenate([-imag, real], axis=1)
    matrix = both_parts(jnp.concatenate([top, low], axis=0))
    out_copies = []
    for block in range(columns // 2):
        wait_all(row_copies[2 * block] + row_copies[2 * block + 1])
        field = jnp.concatenate(
            [
                jnp.concatenate([rows[vector, 2 * block], rows[vector, 2 * block + 1]], axis=0)
                for vector in range(2)
            ],
            axis=1,
        )
        undone = dot_parts(matrix, field)
        pieces = [
            undone[part * order : (part + 1) * order, vector * lanes : (vector + 1) * lanes]
            for vector in range(2)
            for part in range(2)
        ]
        for index, piece in enumerate(swap_groups(pieces)):
            field_ref[block * 4 + index] = piece
        part = pl.ds(block * 4, 4)
        copy = pltpu.make_async_copy(field_ref.at[part], out_ref.at[part], out_sems.at[block])
        copy.start()
        out_copies.append(copy)
    wait_all(out_copies)


def undo_matrix(real, imag):
    return both_parts(jnp.concatenate([real.T, imag.T], axis=1))


def middle_kernel(moved_ref, matrix_ref, kept_ref, *refs):
    *out_refs, moved, last, in_sems, out_sems = refs
    _, steps, _, order, lanes = moved.shape
    devices = 4 * steps
    low_rows = order // 4
    out_rows = order // len(out_refs)

    def in_copy(step):
        return pltpu.make_async_copy(moved_ref.at[:, step], moved.at[:, step], in_sems.at[step])

    def out_copies(step):
        batches = pl.ds(step * 4, 4)
        return [
            pltpu.make_async_copy(
                last.at[batches, pl.ds(index * out_rows, out_rows)],
                out_ref.at[batches],
                out_sems.at[index, step],
            )
            for index, out_ref in enumerate(out_refs)
        ]

    def undo(which, fields):
        plain = jnp.concatenate(fields, axis=1)
        other = jnp.concatenate([turned(field) for field in fields], axis=1)
        result = dot_parts(matrix_ref[which], jnp.concatenate([plain, other], axis=0))
        return [result[:, index * lanes : (index + 1) * lanes] for index in range(len(fields))]

    @pl.loop(0, steps)
    def _(step):
        in_copy(step).start()

    @pl.loop(0, steps, unroll=2)
    def _(step):
        in_copy(step).wait()
        fields = []
        for group in range(4):
            rows = pl.ds(group * low_rows, low_rows)
            parts = [moved[top, step, low, rows, :] for top in range(2) for low in range(2)]
            fields.append(jnp.concatenate(parts, axis=0))
        for group, result in enumerate(undo(0, fields)):
            place = (group // 2 * steps + step) * 2 + group % 2
            kept_ref[pl.ds(pl.multiple_of(place * order, order), order), :] = result

    @pl.loop(0, steps, unroll=2)
    def _(step):
        fields = [regrouped(kept_ref, step * 4 + index, order, devices) for index in range(4)]
        for index, result in enumerate(undo(1, fields)):
            last[step * 4 + index] = result
        for copy in out_copies(step):
            copy.start()

    @pl.loop(0, steps)
    def _(step):
        wait_all(out_copies(step))


def regrouped(kept_ref, batch, order, devices):
    parts = [
        kept_ref[pl.ds(high * devices + batch, devices, stride=order), :]
        for high in range(order // devices)
    ]
    return jnp.concatenate(parts, axis=0)


def outer_parts(fields):
    lanes = fields[0].shape[-1]
    lower = lane_index(fields[0].shape) < lanes // 2
    adjoint, plain, other = [], [], []
    for first, second in zip(fields[0::2], fields[1::2]):
        adjoint.append(jnp.where(lower, pltpu.roll(first, lanes // 2, 1), second))
        pair = jnp.where(lower, first, pltpu.roll(second, lanes // 2, 1))
        plain.append(pair)
        other.append(-turned(pair))
    right = jnp.concatenate(
        [jnp.concatenate(plain, axis=1), jnp.concatenate(other, axis=1)], axis=0
    )
    return dot_parts(both_parts(jnp.concatenate(adjoint, axis=1)), right, ROW_ROW)


def complex_product(left, right, scale):
    def times(first, second):
        return jnp.dot(
            first, second, precision=lax.Precision.HIGHEST, preferred_element_type=jnp.float32
        )

    real = times(left[0], right[0]) - times(left[1], right[1])
    imag = times(left[0], right[1]) + times(left[1], right[0])
    return real * scale, imag * scale


def early_kernel(sent_ref, gates_ref, out_ref, matrix_ref):
    devices = sent_ref.shape[0]
    matrix_ref[0] = undo_matrix(gates_ref[1, 0], gates_ref[1, 1])
    matrix_ref[1] = undo_matrix(gates_ref[2, 0], gates_ref[2, 1])
    out_ref[...] = jnp.zeros_like(out_ref)

    @pl.loop(0, devices // 4)
    def _(step):
        out_ref[...] += outer_parts([sent_ref[step * 4 + index] for index in range(4)])


def late_kernel(kept_ref, early_ref, gates_ref, out_ref, sum_ref, *, scale):
    order = early_ref.shape[0]
    devices = kept_ref.shape[0] // order
    sum_ref[0] = early_ref[...]
    sum_ref[1:3] = jnp.zeros((2,) + early_ref.shape, jnp.float32)

    @pl.loop(0, devices // 4)
    def _(step):
        batches = [step * 4 + index for index in range(4)]
        plain = [kept_ref[pl.ds(pl.multiple_of(b * order, order), order), :] for b in batches]
        sum_ref[1] += outer_parts(plain)
        sum_ref[2] += outer_parts([regrouped(kept_ref, b, order, devices) for b in batches])

    for index in range(3):
        total = (sum_ref[index, :, :order], sum_ref[index, :, order:])
        gate = (gates_ref[index, 0], gates_ref[index, 1])
        left, right = (total, gate) if index == 2 else (gate, total)
        out_ref[index, 0], out_ref[index, 1] = complex_product(left, right, scale)


def last_kernel(moved_ref, *refs, start):
    state_ref, costate_ref, rows, copy_sems = refs[-4:]
    count = moved_ref.shape[1]
    copies = []
    for block in range(rows.shape[1] // 2):
        pieces = [moved_ref[block * 4 + index] for index in range(4)]
        for index, piece in enumerate(swap_groups(pieces)):
            vector, column = index // 2, block * 2 + index % 2
            rows[vector, column] = piece
            copy = pltpu.make_async_copy(
                rows.at[vector, column],
                (state_ref, costate_ref)[vector].at[pl.ds(start, count), column, 0],
                copy_sems.at[vector, column],
            )
            copy.start()
            copies.append(copy)
    wait_all(copies)


def gather_kernel(*refs):
    *part_refs, out_ref, copy_sems = refs
    place = lax.rem(lax.axis_index("amp"), len(part_refs))
    copies = [
        pltpu.make_async_copy(ref, out_ref.at[place ^ index], copy_sems.at[index])
        for index, ref in enumerate(part_refs)
    ]
    for copy in copies:
        copy.start()
    wait_all(copies)


def tree_sum(parts):
    while len(parts) > 1:
        parts = [parts[i] + parts[i + 1] for i in range(0, len(parts), 2)]
    return parts[0]


def exchange(part, distance):
    devices = lax.axis_size("amp")
    return lax.ppermute(part, "amp", [(i, i ^ distance) for i in range(devices)])


def scattered_sum(value):
    devices = lax.axis_size("amp")
    inner = min(8, devices)
    own = lax.axis_index("amp") % inner
    blocks = value.reshape(inner, -1, value.shape[-1])

    def pick(index):
        return lax.dynamic_index_in_dim(blocks, index, 0, keepdims=False)

    part = tree_sum([pick(own)] + [exchange(pick(own ^ k), k) for k in range(1, inner)])
    distance = inner
    while distance < devices:
        part = part + exchange(part, distance)
        distance *= 2
    return part


def gathered(part, shape):
    inner = min(8, lax.axis_size("amp"))
    parts = [part] + [exchange(part, k) for k in range(1, inner)]
    out = pl.pallas_call(
        gather_kernel,
        in_specs=[pl.BlockSpec(memory_space=pl.ANY)] * inner,
        out_specs=IN_HBM,
        out_shape=jax.ShapeDtypeStruct((inner,) + part.shape, part.dtype),
        scratch_shapes=[pltpu.SemaphoreType.DMA((inner,))],
        compiler_params=PARAMS,
    )(*parts)
    return out.reshape(shape)


def to_rows(field, order, lanes):
    return field.reshape(2, -1, lanes).swapaxes(0, 1).reshape(order, -1, 1, lanes)


def from_rows(rows):
    return rows.reshape(-1, 2, rows.shape[-1]).swapaxes(0, 1).reshape(2, -1)


IN_HBM = pl.BlockSpec(memory_space=pltpu.HBM)
IN_VMEM = pl.BlockSpec(memory_space=pltpu.VMEM)
PARAMS = pltpu.CompilerParams(vmem_limit_bytes=VMEM_BYTES)
FIRST_PARAMS = pltpu.CompilerParams(vmem_limit_bytes=60 * 1024 * 1024)


def cost(layers, amplitudes, order):
    flops = layers * 3 * 8 * amplitudes * order
    return pl.CostEstimate(flops=flops, bytes_accessed=32 * amplitudes, transcendentals=0)


def on_device_lanes(state, costate, gates, devices, order, columns):
    lanes = 4 * columns // devices
    steps = devices // 4
    rows = 2 * columns // lanes
    halves = 2
    half = order // halves
    scale = 1.0 / math.sqrt(devices * columns)
    field_shape = (devices, order, lanes)
    sum_shape = (order, 2 * order)
    amplitudes = 2 * order * columns

    def array(shape, kind=jnp.float32):
        return jax.ShapeDtypeStruct(shape, kind)

    sent = pl.pallas_call(
        first_kernel,
        in_specs=[IN_HBM, IN_HBM, IN_HBM],
        out_specs=IN_HBM,
        out_shape=array(field_shape),
        scratch_shapes=[
            pltpu.VMEM((2, order, order), jnp.float32),
            pltpu.VMEM((2, rows, order, lanes), jnp.float32),
            pltpu.VMEM(field_shape, jnp.float32),
            pltpu.SemaphoreType.DMA,
            pltpu.SemaphoreType.DMA((2, rows)),
            pltpu.SemaphoreType.DMA((steps,)),
        ],
        compiler_params=FIRST_PARAMS,
        cost_estimate=cost(1, amplitudes, order),
    )(to_rows(state, order, lanes), to_rows(costate, order, lanes), gates)
    moved = lax.all_to_all(sent, "amp", 0, 0, tiled=True)
    early, matrices = pl.pallas_call(
        early_kernel,
        in_specs=[IN_VMEM, IN_VMEM],
        out_specs=[IN_VMEM, IN_VMEM],
        out_shape=[array(sum_shape), array((2, 2 * order, 2 * order), jnp.bfloat16)],
        compiler_params=PARAMS,
        cost_estimate=cost(1, amplitudes, order),
    )(sent, gates)
    kept, *last = pl.pallas_call(
        middle_kernel,
        in_specs=[IN_HBM, IN_VMEM],
        out_specs=[IN_VMEM] + [IN_HBM] * halves,
        out_shape=[array((devices * order, lanes))] + [array((devices, half, lanes))] * halves,
        scratch_shapes=[
            pltpu.VMEM((2, steps, 2, order, lanes), jnp.float32),
            pltpu.VMEM(field_shape, jnp.float32),
            pltpu.SemaphoreType.DMA((steps,)),
            pltpu.SemaphoreType.DMA((halves, steps)),
        ],
        compiler_params=PARAMS,
        cost_estimate=cost(2, amplitudes, order),
    )(moved.reshape(2, steps, 2, order, lanes), matrices)
    arrived = [lax.all_to_all(part, "amp", 0, 0, tiled=True) for part in last]
    gradients = pl.pallas_call(
        functools.partial(late_kernel, scale=scale),
        in_specs=[IN_VMEM, IN_VMEM, IN_VMEM],
        out_specs=IN_VMEM,
        out_shape=array(gates.shape),
        scratch_shapes=[pltpu.VMEM((3,) + sum_shape, jnp.float32)],
        compiler_params=PARAMS,
        cost_estimate=cost(2, amplitudes, order),
    )(kept, early, gates)
    part, arrived[0] = lax.optimization_barrier((scattered_sum(gradients), arrived[0]))
    gradients = gathered(part, gates.shape)
    results = []
    for index, field in enumerate(arrived):
        results = pl.pallas_call(
            functools.partial(last_kernel, start=index * half),
            in_specs=[IN_VMEM] + [IN_HBM] * len(results),
            out_specs=[IN_HBM, IN_HBM],
            out_shape=[array((order, rows, 1, lanes))] * 2,
            input_output_aliases={1 + i: i for i in range(len(results))},
            scratch_shapes=[
                pltpu.VMEM((2, rows, half, lanes), jnp.float32),
                pltpu.SemaphoreType.DMA((2, rows)),
            ],
            compiler_params=PARAMS,
            cost_estimate=cost(1, amplitudes, order),
        )(field, *results)
    return from_rows(results[0]), from_rows(results[1]), gradients


def undo_gate(field, gate):
    high = lax.Precision.HIGHEST
    shape = field.shape
    parts = field.reshape(shape[:-1] + (2, 2, -1))
    real, imag = parts[..., 0, :], parts[..., 1, :]

    def contract(matrix, operand):
        return jnp.einsum("ts,btvc->bsvc", matrix, operand, precision=high)

    new_real = contract(gate[0], real) + contract(gate[1], imag)
    new_imag = contract(gate[0], imag) - contract(gate[1], real)
    return jnp.stack([new_real, new_imag], axis=-2).reshape(shape)


def gate_gradient(before, after):
    high = lax.Precision.HIGHEST
    lam = before.reshape(before.shape[:-1] + (2, 2, -1))[..., 1, :, :]
    psi = after.reshape(after.shape[:-1] + (2, 2, -1))[..., 0, :, :]
    real = jnp.einsum("btpc,bspc->ts", lam, psi, precision=high)
    imag = jnp.einsum("btc,bsc->ts", lam[..., 1, :], psi[..., 0, :], precision=high) - jnp.einsum(
        "btc,bsc->ts", lam[..., 0, :], psi[..., 1, :], precision=high
    )
    return jnp.stack([real, imag], axis=0)


def on_device_plain(state, costate, gates, devices, order, columns):
    own = columns // devices
    both = jnp.stack([state, costate], axis=0).reshape(2, 2, order, devices, own)
    field = both.transpose(3, 2, 0, 1, 4).reshape(devices, order, 4 * own)
    field = lax.all_to_all(field, "amp", 0, 0, tiled=True)
    after = undo_gate(field, gates[0])
    terms = [gate_gradient(field, after)]
    field = after.reshape(2, devices // 4, 2, 2, 2, order // 4, 4 * own)
    field = field.transpose(3, 1, 4, 0, 2, 5, 6).reshape(devices, order, 4 * own)
    after = undo_gate(field, gates[1])
    terms.append(gate_gradient(field, after))
    field = after.reshape(devices, order // devices, devices, 4 * own)
    field = field.transpose(2, 1, 0, 3).reshape(devices, order, 4 * own)
    after = undo_gate(field, gates[2])
    terms.append(gate_gradient(field, after))
    terms = jnp.stack(terms, axis=0) / math.sqrt(devices * columns)
    gradients = gathered(scattered_sum(terms), gates.shape)
    field = lax.all_to_all(after, "amp", 0, 0, tiled=True)
    field = field.reshape(devices, order, 2, 2, own).transpose(2, 3, 1, 0, 4)
    field = field.reshape(2, 2, order * columns)
    return field[0], field[1], gradients


def on_device(state, costate, gates):
    devices = lax.axis_size("amp")
    order = gates.shape[2]
    columns = state.shape[1] // order
    form = on_device_lanes if 4 * columns == 128 * devices else on_device_plain
    return form(state, costate, gates, devices, order, columns)


def solution(mesh):
    return jax.shard_map(
        on_device,
        mesh=mesh,
        in_specs=(P(None, "amp"), P(None, "amp"), P()),
        out_specs=(P(None, "amp"), P(None, "amp"), P()),
        check_vma=False,
    )
```

```python
import functools
import math

import jax
import jax.numpy as jnp
from jax import lax
from jax.experimental import pallas as pl
from jax.experimental.pallas import tpu as pltpu
from jax.sharding import PartitionSpec as P

VMEM_BYTES = 24 * 1024 * 1024
ROW_ROW = (((1,), (1,)), ((), ()))


def split(value):
    high = value.astype(jnp.bfloat16)
    low = (value - high.astype(jnp.float32)).astype(jnp.bfloat16)
    return high, low


def dot_parts(left_both, right, dims=None):
    dims = (((1,), (0,)), ((), ())) if dims is None else dims
    rows = left_both.shape[0] // 2
    high, low = split(right)
    first = lax.dot_general(left_both, high, dims, preferred_element_type=jnp.float32)
    second = lax.dot_general(left_both[:rows], low, dims, preferred_element_type=jnp.float32)
    return first[:rows] + first[rows:] + second


def both_parts(value):
    high, low = split(value)
    return jnp.concatenate([high, low], axis=0)


def lane_index(shape):
    return lax.broadcasted_iota(jnp.int32, shape, len(shape) - 1)


def swap_groups(values):
    lanes = values[0].shape[-1]
    group = lane_index(values[0].shape) // (lanes // 4)
    for bit in (2, 1):
        width = bit * (lanes // 4)
        fresh = list(values)
        for index in range(4):
            if index & bit == 0:
                low, high = values[index], values[index | bit]
                upper = group & bit != 0
                fresh[index] = jnp.where(upper, pltpu.roll(high, width, 1), low)
                fresh[index | bit] = jnp.where(upper, high, pltpu.roll(low, lanes - width, 1))
        values = fresh
    return values


def swap_bit(low, high):
    lanes = low.shape[-1]
    width = lanes // 4
    upper = (lane_index(low.shape) // width) % 2 == 1
    first = jnp.where(upper, pltpu.roll(high, width, 1), low)
    second = jnp.where(upper, high, pltpu.roll(low, lanes - width, 1))
    return first, second


def row_halves(value, groups):
    rows, lanes = value.shape
    parts = value.reshape(groups, 2, rows // groups // 2, lanes)
    return parts[:, 0].reshape(rows // 2, lanes), parts[:, 1].reshape(rows // 2, lanes)


def wait_all(copies):
    for copy in copies:
        copy.wait()


def undo_matrix(gate):
    real, imag = gate[0].T, gate[1].T
    top = jnp.concatenate([real, imag], axis=1)
    low = jnp.concatenate([-imag, real], axis=1)
    return both_parts(jnp.concatenate([top, low], axis=0))


def first_kernel(
    state_ref, costate_ref, gates_ref, out_ref, gate, rows, field_ref, gate_sem, row_sems, out_sems
):
    order = gate.shape[1]
    lanes = rows.shape[2]
    stride = rows.shape[1] // order
    chunks = row_sems.shape[1]
    chunk = rows.shape[1] // chunks
    copies = [pltpu.make_async_copy(gates_ref.at[0], gate, gate_sem)]
    for index in range(chunks):
        part = pl.ds(index * chunk, chunk)
        for vector, ref in enumerate((state_ref, costate_ref)):
            copies.append(
                pltpu.make_async_copy(ref.at[part], rows.at[vector, part], row_sems.at[vector, index])
            )
    for copy in copies:
        copy.start()
    copies[0].wait()
    matrix = undo_matrix(gate)
    wait_all(copies[1:])

    def column(vector, block):
        parts = [rows[vector, pl.ds(block * 2 + part, order, stride=stride), :] for part in range(2)]
        return jnp.concatenate(parts, axis=0)

    out_copies = []
    for block in range(stride // 2):
        field = jnp.concatenate([column(0, block), column(1, block)], axis=1)
        undone = dot_parts(matrix, field)
        pieces = []
        for vector in range(2):
            pieces += row_halves(undone[:, vector * lanes : (vector + 1) * lanes], 2)
        for index, piece in enumerate(swap_groups(pieces)):
            field_ref[block * 4 + index] = piece
        part = pl.ds(block * 4, 4)
        copy = pltpu.make_async_copy(field_ref.at[part], out_ref.at[part], out_sems.at[block])
        copy.start()
        out_copies.append(copy)
    wait_all(out_copies)


def outer_product(lam, psi):
    order = lam.shape[0] // 2
    left = jnp.concatenate([lam[:order], lam[order:]], axis=1)
    plain = jnp.concatenate([psi[:order], psi[order:]], axis=1)
    other = jnp.concatenate([-psi[order:], psi[:order]], axis=1)
    return dot_parts(both_parts(left), jnp.concatenate([plain, other], axis=0), ROW_ROW)


def four_products(fields, groups):
    pieces = swap_groups(fields)
    rows, lanes = pieces[0].shape

    def joined(vector):
        parts = [
            piece.reshape(groups, 1, rows // groups, lanes)
            for piece in pieces[2 * vector : 2 * vector + 2]
        ]
        return jnp.concatenate(parts, axis=1).reshape(2 * rows, lanes)

    return outer_product(joined(1), joined(0))


def early_kernel(sent_ref, gates_ref, out_ref, matrix_ref):
    devices = sent_ref.shape[0]
    for index in range(2):
        matrix_ref[index] = undo_matrix(gates_ref[index + 1])
    out_ref[...] = jnp.zeros_like(out_ref)

    @pl.loop(0, devices // 4)
    def _(step):
        out_ref[...] += four_products([sent_ref[step * 4 + index] for index in range(4)], 2)


def middle_kernel(moved_ref, matrix_ref, kept_ref, out_ref, moved, last, in_sems, out_sems):
    _, steps, _, order, lanes = moved.shape
    batches = 2 * steps
    low_rows = order // 4

    def in_copy(step):
        return pltpu.make_async_copy(moved_ref.at[:, step], moved.at[:, step], in_sems.at[step])

    def out_copies(step):
        places = [pl.ds(bit * batches + step * 2, 2) for bit in range(2)]
        return [
            pltpu.make_async_copy(last.at[place], out_ref.at[place], out_sems.at[bit, step])
            for bit, place in enumerate(places)
        ]

    def undo(which, fields):
        result = dot_parts(matrix_ref[which], jnp.concatenate(fields, axis=1))
        return [result[:, index * lanes : (index + 1) * lanes] for index in range(len(fields))]

    @pl.loop(0, steps)
    def _(step):
        in_copy(step).start()

    @pl.loop(0, steps)
    def _(step):
        in_copy(step).wait()
        fields = []
        for bit in range(2):
            parts = [
                moved[top, step, low, pl.ds((part * 2 + bit) * low_rows, low_rows), :]
                for part in range(2)
                for top in range(2)
                for low in range(2)
            ]
            fields.append(jnp.concatenate(parts, axis=0))
        for bit, result in enumerate(undo(0, fields)):
            for top, piece in enumerate(swap_bit(*row_halves(result, 8))):
                place = (top * steps + step) * 2 + bit
                kept_ref[pl.ds(pl.multiple_of(place * order, order), order), :] = piece

    @pl.loop(0, steps)
    def _(step):
        fields = [regrouped(kept_ref, step * 2 + index, order) for index in range(2)]
        for index, result in enumerate(undo(1, fields)):
            for bit, piece in enumerate(swap_bit(*row_halves(result, 2))):
                last[bit * batches + step * 2 + index] = piece
        for copy in out_copies(step):
            copy.start()

    @pl.loop(0, steps)
    def _(step):
        wait_all(out_copies(step))


def regrouped(kept_ref, batch, order):
    devices = kept_ref.shape[0] // order
    parts = [
        kept_ref[pl.ds(row * (devices // 2) + batch, devices, stride=order), :] for row in range(8)
    ]
    return jnp.concatenate(parts, axis=0)


def late_kernel(kept_ref, early_ref, gates_ref, out_ref, sum_ref, *, scale):
    order = early_ref.shape[0]
    devices = kept_ref.shape[0] // order
    sum_ref[0] = early_ref[...]
    sum_ref[1:3] = jnp.zeros((2,) + early_ref.shape, jnp.float32)

    @pl.loop(0, devices // 4)
    def _(step):
        places = [pl.multiple_of((step * 4 + index) * order, order) for index in range(4)]
        sum_ref[1] += four_products([kept_ref[pl.ds(place, order), :] for place in places], 8)
        first, second = (regrouped(kept_ref, step * 2 + index, order) for index in range(2))
        half = first.shape[-1] // 2
        lower = lane_index(first.shape) < half
        psi = jnp.where(lower, first, pltpu.roll(second, half, 1))
        lam = jnp.where(lower, pltpu.roll(first, half, 1), second)
        sum_ref[2] += outer_product(lam, psi)

    for index in range(3):
        total = (sum_ref[index, :, :order], sum_ref[index, :, order:])
        gate = (gates_ref[index, 0], gates_ref[index, 1])
        left, right = (total, gate) if index == 2 else (gate, total)
        out_ref[index, 0], out_ref[index, 1] = complex_product(left, right, scale)


def complex_product(left, right, scale):
    def times(first, second):
        return jnp.dot(
            first, second, precision=lax.Precision.HIGHEST, preferred_element_type=jnp.float32
        )

    real = times(left[0], right[0]) - times(left[1], right[1])
    imag = times(left[0], right[1]) + times(left[1], right[0])
    return real * scale, imag * scale


def last_kernel(moved_ref, state_ref, costate_ref, rows, copy_sems):
    half = moved_ref.shape[1] // 2
    copies = []
    for block in range(rows.shape[1] // 2):
        pieces = swap_groups([moved_ref[block * 4 + index] for index in range(4)])
        for vector, ref in enumerate((state_ref, costate_ref)):
            for part in range(2):
                column = block * 2 + part
                for bit in range(2):
                    piece = pieces[2 * vector + bit][part * half : (part + 1) * half]
                    rows[vector, column, bit * half : (bit + 1) * half] = piece
                copy = pltpu.make_async_copy(
                    rows.at[vector, column], ref.at[:, column, 0], copy_sems.at[vector, column]
                )
                copy.start()
                copies.append(copy)
    wait_all(copies)


def gather_kernel(*refs, distance):
    *part_refs, out_ref, copy_sems = refs
    place = lax.rem(lax.axis_index("amp") // distance, len(part_refs))
    copies = [
        pltpu.make_async_copy(ref, out_ref.at[place ^ index], copy_sems.at[index])
        for index, ref in enumerate(part_refs)
    ]
    for copy in copies:
        copy.start()
    wait_all(copies)


def tree_sum(parts):
    while len(parts) > 1:
        parts = [parts[i] + parts[i + 1] for i in range(0, len(parts), 2)]
    return parts[0]


def exchange(part, distance):
    devices = lax.axis_size("amp")
    return lax.ppermute(part, "amp", [(i, i ^ distance) for i in range(devices)])


def scattered_sum(value):
    devices = lax.axis_size("amp")
    inner = min(8, devices)
    own = lax.axis_index("amp") % inner
    blocks = value.reshape(inner, -1, value.shape[-1])

    def pick(index):
        return lax.dynamic_index_in_dim(blocks, index, 0, keepdims=False)

    part = tree_sum([pick(own)] + [exchange(pick(own ^ k), k) for k in range(1, inner)])
    distance = inner
    while distance < devices:
        part = part + exchange(part, distance)
        distance *= 2
    return part


def gathered(part, shape):
    inner = min(8, lax.axis_size("amp"))
    other = exchange(part, 1)
    upper = lax.axis_index("amp") % 2 == 1
    pair = jnp.stack([jnp.where(upper, other, part), jnp.where(upper, part, other)], axis=0)
    pairs = [pair] + [exchange(pair, k) for k in range(2, inner, 2)]
    out = pl.pallas_call(
        functools.partial(gather_kernel, distance=2),
        in_specs=[pl.BlockSpec(memory_space=pl.ANY)] * len(pairs),
        out_specs=IN_HBM,
        out_shape=jax.ShapeDtypeStruct((len(pairs),) + pair.shape, part.dtype),
        scratch_shapes=[pltpu.SemaphoreType.DMA((len(pairs),))],
        compiler_params=PARAMS,
    )(*pairs)
    return out.reshape(shape)


def to_rows(field, lanes):
    return field.reshape(2, -1, lanes).swapaxes(0, 1).reshape(-1, lanes)


def from_rows(rows):
    return rows.reshape(-1, 2, rows.shape[-1]).swapaxes(0, 1).reshape(2, -1)


IN_HBM = pl.BlockSpec(memory_space=pltpu.HBM)
IN_VMEM = pl.BlockSpec(memory_space=pltpu.VMEM)
PARAMS = pltpu.CompilerParams(vmem_limit_bytes=VMEM_BYTES)
FIRST_PARAMS = pltpu.CompilerParams(vmem_limit_bytes=60 * 1024 * 1024)


def cost(layers, amplitudes, order):
    flops = layers * 3 * 8 * amplitudes * order
    return pl.CostEstimate(flops=flops, bytes_accessed=32 * amplitudes, transcendentals=0)


def on_device_lanes(state, costate, gates, devices, order, columns):
    lanes = 4 * columns // devices
    steps = devices // 4
    rows = 2 * columns // lanes
    scale = 1.0 / math.sqrt(devices * columns)
    field_shape = (devices, order, lanes)
    sum_shape = (order, 2 * order)
    amplitudes = 2 * order * columns

    def array(shape, kind=jnp.float32):
        return jax.ShapeDtypeStruct(shape, kind)

    sent = pl.pallas_call(
        first_kernel,
        in_specs=[IN_HBM, IN_HBM, IN_HBM],
        out_specs=IN_HBM,
        out_shape=array(field_shape),
        scratch_shapes=[
            pltpu.VMEM((2, order, order), jnp.float32),
            pltpu.VMEM((2, rows * order, lanes), jnp.float32),
            pltpu.VMEM(field_shape, jnp.float32),
            pltpu.SemaphoreType.DMA,
            pltpu.SemaphoreType.DMA((2, 4)),
            pltpu.SemaphoreType.DMA((steps,)),
        ],
        compiler_params=FIRST_PARAMS,
        cost_estimate=cost(1, amplitudes, order),
    )(to_rows(state, lanes), to_rows(costate, lanes), gates)
    moved = lax.all_to_all(sent, "amp", 0, 0, tiled=True)
    early, matrices = pl.pallas_call(
        early_kernel,
        in_specs=[IN_VMEM, IN_VMEM],
        out_specs=[IN_VMEM, IN_VMEM],
        out_shape=[array(sum_shape), array((2, 4 * order, 2 * order), jnp.bfloat16)],
        compiler_params=PARAMS,
        cost_estimate=cost(1, amplitudes, order),
    )(sent, gates)
    kept, last = pl.pallas_call(
        middle_kernel,
        in_specs=[IN_HBM, IN_VMEM],
        out_specs=[IN_VMEM, IN_HBM],
        out_shape=[array((devices * order, lanes)), array(field_shape)],
        scratch_shapes=[
            pltpu.VMEM((2, steps, 2, order, lanes), jnp.float32),
            pltpu.VMEM(field_shape, jnp.float32),
            pltpu.SemaphoreType.DMA((steps,)),
            pltpu.SemaphoreType.DMA((2, steps)),
        ],
        compiler_params=PARAMS,
        cost_estimate=cost(2, amplitudes, order),
    )(moved.reshape(2, steps, 2, order, lanes), matrices)
    arrived = lax.all_to_all(last, "amp", 0, 0, tiled=True)
    gradients = pl.pallas_call(
        functools.partial(late_kernel, scale=scale),
        in_specs=[IN_VMEM, IN_VMEM, IN_VMEM],
        out_specs=IN_VMEM,
        out_shape=array(gates.shape),
        scratch_shapes=[pltpu.VMEM((3,) + sum_shape, jnp.float32)],
        compiler_params=PARAMS,
        cost_estimate=cost(2, amplitudes, order),
    )(kept, early, gates)
    part, arrived = lax.optimization_barrier((scattered_sum(gradients), arrived))
    gradients = gathered(part, gates.shape)
    state_rows, costate_rows = pl.pallas_call(
        last_kernel,
        in_specs=[IN_VMEM],
        out_specs=[IN_HBM, IN_HBM],
        out_shape=[array((order, rows, 1, lanes))] * 2,
        scratch_shapes=[
            pltpu.VMEM((2, rows, order, lanes), jnp.float32),
            pltpu.SemaphoreType.DMA((2, rows)),
        ],
        compiler_params=PARAMS,
        cost_estimate=cost(1, amplitudes, order),
    )(arrived)
    return from_rows(state_rows), from_rows(costate_rows), gradients


def undo_gate(field, gate):
    high = lax.Precision.HIGHEST
    shape = field.shape
    parts = field.reshape(shape[:-1] + (2, 2, -1))
    real, imag = parts[..., 0, :], parts[..., 1, :]

    def contract(matrix, operand):
        return jnp.einsum("ts,btvc->bsvc", matrix, operand, precision=high)

    new_real = contract(gate[0], real) + contract(gate[1], imag)
    new_imag = contract(gate[0], imag) - contract(gate[1], real)
    return jnp.stack([new_real, new_imag], axis=-2).reshape(shape)


def gate_gradient(before, after):
    high = lax.Precision.HIGHEST
    lam = before.reshape(before.shape[:-1] + (2, 2, -1))[..., 1, :, :]
    psi = after.reshape(after.shape[:-1] + (2, 2, -1))[..., 0, :, :]
    real = jnp.einsum("btpc,bspc->ts", lam, psi, precision=high)
    imag = jnp.einsum("btc,bsc->ts", lam[..., 1, :], psi[..., 0, :], precision=high) - jnp.einsum(
        "btc,bsc->ts", lam[..., 0, :], psi[..., 1, :], precision=high
    )
    return jnp.stack([real, imag], axis=0)


def on_device_plain(state, costate, gates, devices, order, columns):
    own = columns // devices
    both = jnp.stack([state, costate], axis=0).reshape(2, 2, order, devices, own)
    field = both.transpose(3, 2, 0, 1, 4).reshape(devices, order, 4 * own)
    field = lax.all_to_all(field, "amp", 0, 0, tiled=True)
    after = undo_gate(field, gates[0])
    terms = [gate_gradient(field, after)]
    field = after.reshape(2, devices // 4, 2, 2, 2, order // 4, 4 * own)
    field = field.transpose(3, 1, 4, 0, 2, 5, 6).reshape(devices, order, 4 * own)
    after = undo_gate(field, gates[1])
    terms.append(gate_gradient(field, after))
    field = after.reshape(devices, order // devices, devices, 4 * own)
    field = field.transpose(2, 1, 0, 3).reshape(devices, order, 4 * own)
    after = undo_gate(field, gates[2])
    terms.append(gate_gradient(field, after))
    terms = jnp.stack(terms, axis=0) / math.sqrt(devices * columns)
    gradients = gathered(scattered_sum(terms), gates.shape)
    field = lax.all_to_all(after, "amp", 0, 0, tiled=True)
    field = field.reshape(devices, order, 2, 2, own).transpose(2, 3, 1, 0, 4)
    field = field.reshape(2, 2, order * columns)
    return field[0], field[1], gradients


def on_device(state, costate, gates):
    devices = lax.axis_size("amp")
    order = gates.shape[2]
    columns = state.shape[1] // order
    filled = 4 * columns == 128 * devices and order == 4 * devices
    form = on_device_lanes if filled else on_device_plain
    return form(state, costate, gates, devices, order, columns)


def solution(mesh):
    return jax.shard_map(
        on_device,
        mesh=mesh,
        in_specs=(P(None, "amp"), P(None, "amp"), P()),
        out_specs=(P(None, "amp"), P(None, "amp"), P()),
        check_vma=False,
    )
```

```python
import functools
import math

import jax
import jax.numpy as jnp
from jax import lax
from jax.experimental import pallas as pl
from jax.experimental.pallas import tpu as pltpu
from jax.sharding import PartitionSpec as P

VMEM_BYTES = 24 * 1024 * 1024
ROW_ROW = (((1,), (1,)), ((), ()))


def split(value):
    high = value.astype(jnp.bfloat16)
    low = (value - high.astype(jnp.float32)).astype(jnp.bfloat16)
    return high, low


def dot_parts(left_both, right, dims=None):
    dims = (((1,), (0,)), ((), ())) if dims is None else dims
    rows = left_both.shape[0] // 2
    high, low = split(right)
    first = lax.dot_general(left_both, high, dims, preferred_element_type=jnp.float32)
    second = lax.dot_general(left_both[:rows], low, dims, preferred_element_type=jnp.float32)
    return first[:rows] + first[rows:] + second


def both_parts(value):
    high, low = split(value)
    return jnp.concatenate([high, low], axis=0)


def lane_index(shape):
    return lax.broadcasted_iota(jnp.int32, shape, len(shape) - 1)


def swap_groups(values):
    lanes = values[0].shape[-1]
    group = lane_index(values[0].shape) // (lanes // 4)
    for bit in (2, 1):
        width = bit * (lanes // 4)
        fresh = list(values)
        for index in range(4):
            if index & bit == 0:
                low, high = values[index], values[index | bit]
                upper = group & bit != 0
                fresh[index] = jnp.where(upper, pltpu.roll(high, width, 1), low)
                fresh[index | bit] = jnp.where(upper, high, pltpu.roll(low, lanes - width, 1))
        values = fresh
    return values


def swap_bit(low, high):
    lanes = low.shape[-1]
    width = lanes // 4
    upper = (lane_index(low.shape) // width) % 2 == 1
    first = jnp.where(upper, pltpu.roll(high, width, 1), low)
    second = jnp.where(upper, high, pltpu.roll(low, lanes - width, 1))
    return first, second


def row_halves(value, groups):
    rows, lanes = value.shape
    parts = value.reshape(groups, 2, rows // groups // 2, lanes)
    return parts[:, 0].reshape(rows // 2, lanes), parts[:, 1].reshape(rows // 2, lanes)


def wait_all(copies):
    for copy in copies:
        copy.wait()


def undo_matrix(gate):
    real, imag = gate[0].T, gate[1].T
    top = jnp.concatenate([real, imag], axis=1)
    low = jnp.concatenate([-imag, real], axis=1)
    return both_parts(jnp.concatenate([top, low], axis=0))


def first_kernel(
    state_ref, costate_ref, gates_ref, out_ref, gate, rows, field_ref, gate_sem, row_sems, out_sems
):
    order = gate.shape[1]
    lanes = rows.shape[2]
    stride = rows.shape[1] // order
    chunks = row_sems.shape[1]
    chunk = rows.shape[1] // chunks
    copies = [pltpu.make_async_copy(gates_ref.at[0], gate, gate_sem)]
    for index in range(chunks):
        part = pl.ds(index * chunk, chunk)
        for vector, ref in enumerate((state_ref, costate_ref)):
            copies.append(
                pltpu.make_async_copy(ref.at[part], rows.at[vector, part], row_sems.at[vector, index])
            )
    for copy in copies:
        copy.start()
    copies[0].wait()
    matrix = undo_matrix(gate)
    wait_all(copies[1:])

    def column(vector, block):
        parts = [rows[vector, pl.ds(block * 2 + part, order, stride=stride), :] for part in range(2)]
        return jnp.concatenate(parts, axis=0)

    out_copies = []
    for block in range(stride // 2):
        field = jnp.concatenate([column(0, block), column(1, block)], axis=1)
        undone = dot_parts(matrix, field)
        pieces = []
        for vector in range(2):
            pieces += row_halves(undone[:, vector * lanes : (vector + 1) * lanes], 2)
        for index, piece in enumerate(swap_groups(pieces)):
            field_ref[block * 4 + index] = piece
        part = pl.ds(block * 4, 4)
        copy = pltpu.make_async_copy(field_ref.at[part], out_ref.at[part], out_sems.at[block])
        copy.start()
        out_copies.append(copy)
    wait_all(out_copies)


def outer_product(lam, psi):
    order = lam.shape[0] // 2
    left = jnp.concatenate([lam[:order], lam[order:]], axis=1)
    plain = jnp.concatenate([psi[:order], psi[order:]], axis=1)
    other = jnp.concatenate([-psi[order:], psi[:order]], axis=1)
    return dot_parts(both_parts(left), jnp.concatenate([plain, other], axis=0), ROW_ROW)


def four_products(fields, groups):
    pieces = swap_groups(fields)
    rows, lanes = pieces[0].shape

    def joined(vector):
        parts = [
            piece.reshape(groups, 1, rows // groups, lanes)
            for piece in pieces[2 * vector : 2 * vector + 2]
        ]
        return jnp.concatenate(parts, axis=1).reshape(2 * rows, lanes)

    return outer_product(joined(1), joined(0))


def early_kernel(sent_ref, gates_ref, out_ref, matrix_ref):
    devices = sent_ref.shape[0]
    for index in range(2):
        matrix_ref[index] = undo_matrix(gates_ref[index + 1])
    out_ref[...] = jnp.zeros_like(out_ref)

    @pl.loop(0, devices // 4)
    def _(step):
        out_ref[...] += four_products([sent_ref[step * 4 + index] for index in range(4)], 2)


def middle_kernel(
    moved_ref,
    matrix_ref,
    kept_out_ref,
    out_ref,
    moved,
    matrix,
    kept,
    last,
    matrix_sem,
    in_sems,
    kept_sems,
    out_sems,
):
    _, steps, _, order, lanes = moved.shape
    batches = 2 * steps
    low_rows = order // 4
    in_copies = [
        pltpu.make_async_copy(moved_ref.at[:, step], moved.at[:, step], in_sems.at[step])
        for step in range(steps)
    ]
    matrix_copy = pltpu.make_async_copy(matrix_ref, matrix, matrix_sem)
    matrix_copy.start()
    for copy in in_copies:
        copy.start()
    matrix_copy.wait()
    out_copies = []

    def undo(which, fields):
        result = dot_parts(matrix[which], jnp.concatenate(fields, axis=1))
        return [result[:, index * lanes : (index + 1) * lanes] for index in range(len(fields))]

    for step in range(steps):
        in_copies[step].wait()
        fields = []
        for bit in range(2):
            parts = [
                moved[top, step, low, pl.ds((part * 2 + bit) * low_rows, low_rows), :]
                for part in range(2)
                for top in range(2)
                for low in range(2)
            ]
            fields.append(jnp.concatenate(parts, axis=0))
        for bit, result in enumerate(undo(0, fields)):
            for top, piece in enumerate(swap_bit(*row_halves(result, 8))):
                place = (top * steps + step) * 2 + bit
                kept[pl.ds(place * order, order), :] = piece
        for top in range(2):
            part = pl.ds((top * steps + step) * 2 * order, 2 * order)
            copy = pltpu.make_async_copy(
                kept.at[part], kept_out_ref.at[part], kept_sems.at[top, step]
            )
            copy.start()
            out_copies.append(copy)

    for step in range(steps):
        fields = [regrouped(kept, step * 2 + index, order) for index in range(2)]
        for index, result in enumerate(undo(1, fields)):
            for bit, piece in enumerate(swap_bit(*row_halves(result, 2))):
                last[bit * batches + step * 2 + index] = piece
        for bit in range(2):
            part = pl.ds(bit * batches + step * 2, 2)
            copy = pltpu.make_async_copy(last.at[part], out_ref.at[part], out_sems.at[bit, step])
            copy.start()
            out_copies.append(copy)
    wait_all(out_copies)


def regrouped(kept_ref, batch, order):
    devices = kept_ref.shape[0] // order
    parts = [
        kept_ref[pl.ds(row * (devices // 2) + batch, devices, stride=order), :] for row in range(8)
    ]
    return jnp.concatenate(parts, axis=0)


def late_kernel(kept_ref, early_ref, gates_ref, out_ref, sum_ref, *, scale):
    order = early_ref.shape[0]
    devices = kept_ref.shape[0] // order
    sum_ref[0] = early_ref[...]
    sum_ref[1:3] = jnp.zeros((2,) + early_ref.shape, jnp.float32)

    @pl.loop(0, devices // 4)
    def _(step):
        places = [pl.multiple_of((step * 4 + index) * order, order) for index in range(4)]
        sum_ref[1] += four_products([kept_ref[pl.ds(place, order), :] for place in places], 8)
        first, second = (regrouped(kept_ref, step * 2 + index, order) for index in range(2))
        half = first.shape[-1] // 2
        lower = lane_index(first.shape) < half
        psi = jnp.where(lower, first, pltpu.roll(second, half, 1))
        lam = jnp.where(lower, pltpu.roll(first, half, 1), second)
        sum_ref[2] += outer_product(lam, psi)

    for index in range(3):
        total = (sum_ref[index, :, :order], sum_ref[index, :, order:])
        gate = (gates_ref[index, 0], gates_ref[index, 1])
        left, right = (total, gate) if index == 2 else (gate, total)
        out_ref[index, 0], out_ref[index, 1] = complex_product(left, right, scale)


def complex_product(left, right, scale):
    def times(first, second):
        return jnp.dot(
            first, second, precision=lax.Precision.HIGHEST, preferred_element_type=jnp.float32
        )

    real = times(left[0], right[0]) - times(left[1], right[1])
    imag = times(left[0], right[1]) + times(left[1], right[0])
    return real * scale, imag * scale


def last_kernel(moved_ref, state_ref, costate_ref, rows, copy_sems):
    half = moved_ref.shape[1] // 2
    copies = []
    for block in range(rows.shape[1] // 2):
        pieces = swap_groups([moved_ref[block * 4 + index] for index in range(4)])
        for vector, ref in enumerate((state_ref, costate_ref)):
            for part in range(2):
                column = block * 2 + part
                for bit in range(2):
                    piece = pieces[2 * vector + bit][part * half : (part + 1) * half]
                    rows[vector, column, bit * half : (bit + 1) * half] = piece
                copy = pltpu.make_async_copy(
                    rows.at[vector, column], ref.at[:, column, 0], copy_sems.at[vector, column]
                )
                copy.start()
                copies.append(copy)
    wait_all(copies)


def gather_kernel(*refs, distance):
    *part_refs, out_ref, copy_sems = refs
    place = lax.rem(lax.axis_index("amp") // distance, len(part_refs))
    copies = [
        pltpu.make_async_copy(ref, out_ref.at[place ^ index], copy_sems.at[index])
        for index, ref in enumerate(part_refs)
    ]
    for copy in copies:
        copy.start()
    wait_all(copies)


def tree_sum(parts):
    while len(parts) > 1:
        parts = [parts[i] + parts[i + 1] for i in range(0, len(parts), 2)]
    return parts[0]


def exchange(part, distance):
    devices = lax.axis_size("amp")
    return lax.ppermute(part, "amp", [(i, i ^ distance) for i in range(devices)])


def scattered_sum(value):
    devices = lax.axis_size("amp")
    inner = min(8, devices)
    own = lax.axis_index("amp") % inner
    blocks = value.reshape(inner, -1, value.shape[-1])

    def pick(index):
        return lax.dynamic_index_in_dim(blocks, index, 0, keepdims=False)

    part = tree_sum([pick(own)] + [exchange(pick(own ^ k), k) for k in range(1, inner)])
    distance = inner
    while distance < devices:
        part = part + exchange(part, distance)
        distance *= 2
    return part


def gathered(part, shape):
    inner = min(8, lax.axis_size("amp"))
    other = exchange(part, 1)
    upper = lax.axis_index("amp") % 2 == 1
    pair = jnp.stack([jnp.where(upper, other, part), jnp.where(upper, part, other)], axis=0)
    pairs = [pair] + [exchange(pair, k) for k in range(2, inner, 2)]
    out = pl.pallas_call(
        functools.partial(gather_kernel, distance=2),
        in_specs=[pl.BlockSpec(memory_space=pl.ANY)] * len(pairs),
        out_specs=IN_HBM,
        out_shape=jax.ShapeDtypeStruct((len(pairs),) + pair.shape, part.dtype),
        scratch_shapes=[pltpu.SemaphoreType.DMA((len(pairs),))],
        compiler_params=PARAMS,
    )(*pairs)
    return out.reshape(shape)


def to_rows(field, lanes):
    return field.reshape(2, -1, lanes).swapaxes(0, 1).reshape(-1, lanes)


def from_rows(rows):
    return rows.reshape(-1, 2, rows.shape[-1]).swapaxes(0, 1).reshape(2, -1)


IN_HBM = pl.BlockSpec(memory_space=pltpu.HBM)
IN_VMEM = pl.BlockSpec(memory_space=pltpu.VMEM)
PARAMS = pltpu.CompilerParams(vmem_limit_bytes=VMEM_BYTES)
HBM_PARAMS = pltpu.CompilerParams(vmem_limit_bytes=60 * 1024 * 1024)


def cost(layers, amplitudes, order):
    flops = layers * 3 * 8 * amplitudes * order
    return pl.CostEstimate(flops=flops, bytes_accessed=32 * amplitudes, transcendentals=0)


def on_device_lanes(state, costate, gates, devices, order, columns):
    lanes = 4 * columns // devices
    steps = devices // 4
    rows = 2 * columns // lanes
    scale = 1.0 / math.sqrt(devices * columns)
    field_shape = (devices, order, lanes)
    sum_shape = (order, 2 * order)
    amplitudes = 2 * order * columns

    def array(shape, kind=jnp.float32):
        return jax.ShapeDtypeStruct(shape, kind)

    sent = pl.pallas_call(
        first_kernel,
        in_specs=[IN_HBM, IN_HBM, IN_HBM],
        out_specs=IN_HBM,
        out_shape=array(field_shape),
        scratch_shapes=[
            pltpu.VMEM((2, order, order), jnp.float32),
            pltpu.VMEM((2, rows * order, lanes), jnp.float32),
            pltpu.VMEM(field_shape, jnp.float32),
            pltpu.SemaphoreType.DMA,
            pltpu.SemaphoreType.DMA((2, 4)),
            pltpu.SemaphoreType.DMA((steps,)),
        ],
        compiler_params=HBM_PARAMS,
        cost_estimate=cost(1, amplitudes, order),
    )(to_rows(state, lanes), to_rows(costate, lanes), gates)
    moved = lax.all_to_all(sent, "amp", 0, 0, tiled=True)
    early, matrices = pl.pallas_call(
        early_kernel,
        in_specs=[IN_VMEM, IN_VMEM],
        out_specs=[IN_VMEM, IN_VMEM],
        out_shape=[array(sum_shape), array((2, 4 * order, 2 * order), jnp.bfloat16)],
        compiler_params=PARAMS,
        cost_estimate=cost(1, amplitudes, order),
    )(sent, gates)
    kept, last = pl.pallas_call(
        middle_kernel,
        in_specs=[IN_HBM, IN_HBM],
        out_specs=[IN_HBM, IN_HBM],
        out_shape=[array((devices * order, lanes)), array(field_shape)],
        scratch_shapes=[
            pltpu.VMEM((2, steps, 2, order, lanes), jnp.float32),
            pltpu.VMEM(matrices.shape, jnp.bfloat16),
            pltpu.VMEM((devices * order, lanes), jnp.float32),
            pltpu.VMEM(field_shape, jnp.float32),
            pltpu.SemaphoreType.DMA,
            pltpu.SemaphoreType.DMA((steps,)),
            pltpu.SemaphoreType.DMA((2, steps)),
            pltpu.SemaphoreType.DMA((2, steps)),
        ],
        compiler_params=HBM_PARAMS,
        cost_estimate=cost(2, amplitudes, order),
    )(moved.reshape(2, steps, 2, order, lanes), matrices)
    arrived = lax.all_to_all(last, "amp", 0, 0, tiled=True)
    gradients = pl.pallas_call(
        functools.partial(late_kernel, scale=scale),
        in_specs=[IN_VMEM, IN_VMEM, IN_VMEM],
        out_specs=IN_VMEM,
        out_shape=array(gates.shape),
        scratch_shapes=[pltpu.VMEM((3,) + sum_shape, jnp.float32)],
        compiler_params=PARAMS,
        cost_estimate=cost(2, amplitudes, order),
    )(kept, early, gates)
    part, arrived = lax.optimization_barrier((scattered_sum(gradients), arrived))
    gradients = gathered(part, gates.shape)
    state_rows, costate_rows = pl.pallas_call(
        last_kernel,
        in_specs=[IN_VMEM],
        out_specs=[IN_HBM, IN_HBM],
        out_shape=[array((order, rows, 1, lanes))] * 2,
        scratch_shapes=[
            pltpu.VMEM((2, rows, order, lanes), jnp.float32),
            pltpu.SemaphoreType.DMA((2, rows)),
        ],
        compiler_params=PARAMS,
        cost_estimate=cost(1, amplitudes, order),
    )(arrived)
    return from_rows(state_rows), from_rows(costate_rows), gradients


def undo_gate(field, gate):
    high = lax.Precision.HIGHEST
    shape = field.shape
    parts = field.reshape(shape[:-1] + (2, 2, -1))
    real, imag = parts[..., 0, :], parts[..., 1, :]

    def contract(matrix, operand):
        return jnp.einsum("ts,btvc->bsvc", matrix, operand, precision=high)

    new_real = contract(gate[0], real) + contract(gate[1], imag)
    new_imag = contract(gate[0], imag) - contract(gate[1], real)
    return jnp.stack([new_real, new_imag], axis=-2).reshape(shape)


def gate_gradient(before, after):
    high = lax.Precision.HIGHEST
    lam = before.reshape(before.shape[:-1] + (2, 2, -1))[..., 1, :, :]
    psi = after.reshape(after.shape[:-1] + (2, 2, -1))[..., 0, :, :]
    real = jnp.einsum("btpc,bspc->ts", lam, psi, precision=high)
    imag = jnp.einsum("btc,bsc->ts", lam[..., 1, :], psi[..., 0, :], precision=high) - jnp.einsum(
        "btc,bsc->ts", lam[..., 0, :], psi[..., 1, :], precision=high
    )
    return jnp.stack([real, imag], axis=0)


def on_device_plain(state, costate, gates, devices, order, columns):
    own = columns // devices
    both = jnp.stack([state, costate], axis=0).reshape(2, 2, order, devices, own)
    field = both.transpose(3, 2, 0, 1, 4).reshape(devices, order, 4 * own)
    field = lax.all_to_all(field, "amp", 0, 0, tiled=True)
    after = undo_gate(field, gates[0])
    terms = [gate_gradient(field, after)]
    field = after.reshape(2, devices // 4, 2, 2, 2, order // 4, 4 * own)
    field = field.transpose(3, 1, 4, 0, 2, 5, 6).reshape(devices, order, 4 * own)
    after = undo_gate(field, gates[1])
    terms.append(gate_gradient(field, after))
    field = after.reshape(devices, order // devices, devices, 4 * own)
    field = field.transpose(2, 1, 0, 3).reshape(devices, order, 4 * own)
    after = undo_gate(field, gates[2])
    terms.append(gate_gradient(field, after))
    terms = jnp.stack(terms, axis=0) / math.sqrt(devices * columns)
    gradients = gathered(scattered_sum(terms), gates.shape)
    field = lax.all_to_all(after, "amp", 0, 0, tiled=True)
    field = field.reshape(devices, order, 2, 2, own).transpose(2, 3, 1, 0, 4)
    field = field.reshape(2, 2, order * columns)
    return field[0], field[1], gradients


def on_device(state, costate, gates):
    devices = lax.axis_size("amp")
    order = gates.shape[2]
    columns = state.shape[1] // order
    filled = 4 * columns == 128 * devices and order == 4 * devices
    form = on_device_lanes if filled else on_device_plain
    return form(state, costate, gates, devices, order, columns)


def solution(mesh):
    return jax.shard_map(
        on_device,
        mesh=mesh,
        in_specs=(P(None, "amp"), P(None, "amp"), P()),
        out_specs=(P(None, "amp"), P(None, "amp"), P()),
        check_vma=False,
    )
```

```python
import functools
import math

import jax
import jax.numpy as jnp
from jax import lax
from jax.experimental import pallas as pl
from jax.experimental.pallas import tpu as pltpu
from jax.sharding import PartitionSpec as P

VMEM_BYTES = 24 * 1024 * 1024
ROW_ROW = (((1,), (1,)), ((), ()))


def split(value):
    high = value.astype(jnp.bfloat16)
    low = (value - high.astype(jnp.float32)).astype(jnp.bfloat16)
    return high, low


def dot_parts(left_both, right, dims=None):
    dims = (((1,), (0,)), ((), ())) if dims is None else dims
    rows = left_both.shape[0] // 2
    high, low = split(right)
    first = lax.dot_general(left_both, high, dims, preferred_element_type=jnp.float32)
    second = lax.dot_general(left_both[:rows], low, dims, preferred_element_type=jnp.float32)
    return first[:rows] + first[rows:] + second


def both_parts(value):
    high, low = split(value)
    return jnp.concatenate([high, low], axis=0)


def lane_index(shape):
    return lax.broadcasted_iota(jnp.int32, shape, len(shape) - 1)


def swap_groups(values):
    lanes = values[0].shape[-1]
    group = lane_index(values[0].shape) // (lanes // 4)
    for bit in (2, 1):
        width = bit * (lanes // 4)
        fresh = list(values)
        for index in range(4):
            if index & bit == 0:
                low, high = values[index], values[index | bit]
                upper = group & bit != 0
                fresh[index] = jnp.where(upper, pltpu.roll(high, width, 1), low)
                fresh[index | bit] = jnp.where(upper, high, pltpu.roll(low, lanes - width, 1))
        values = fresh
    return values


def swap_bit(low, high):
    lanes = low.shape[-1]
    width = lanes // 4
    upper = (lane_index(low.shape) // width) % 2 == 1
    first = jnp.where(upper, pltpu.roll(high, width, 1), low)
    second = jnp.where(upper, high, pltpu.roll(low, lanes - width, 1))
    return first, second


def row_halves(value, groups):
    rows, lanes = value.shape
    parts = value.reshape(groups, 2, rows // groups // 2, lanes)
    return parts[:, 0].reshape(rows // 2, lanes), parts[:, 1].reshape(rows // 2, lanes)


def wait_all(copies):
    for copy in copies:
        copy.wait()


def undo_matrix(gate):
    real, imag = gate[0].T, gate[1].T
    top = jnp.concatenate([real, imag], axis=1)
    low = jnp.concatenate([-imag, real], axis=1)
    return both_parts(jnp.concatenate([top, low], axis=0))


def first_kernel(
    state_ref, costate_ref, gates_ref, out_ref, gate, rows, field_ref, gate_sem, row_sems, out_sems
):
    order = gate.shape[1]
    lanes = rows.shape[2]
    stride = rows.shape[1] // order
    chunks = row_sems.shape[1]
    chunk = rows.shape[1] // chunks
    copies = [pltpu.make_async_copy(gates_ref.at[0], gate, gate_sem)]
    for index in range(chunks):
        part = pl.ds(index * chunk, chunk)
        for vector, ref in enumerate((state_ref, costate_ref)):
            copies.append(
                pltpu.make_async_copy(ref.at[part], rows.at[vector, part], row_sems.at[vector, index])
            )
    for copy in copies:
        copy.start()
    copies[0].wait()
    matrix = undo_matrix(gate)
    wait_all(copies[1:])

    def column(vector, block):
        parts = [rows[vector, pl.ds(block * 2 + part, order, stride=stride), :] for part in range(2)]
        return jnp.concatenate(parts, axis=0)

    out_copies = []
    for block in range(stride // 2):
        field = jnp.concatenate([column(0, block), column(1, block)], axis=1)
        undone = dot_parts(matrix, field)
        pieces = []
        for vector in range(2):
            pieces += row_halves(undone[:, vector * lanes : (vector + 1) * lanes], 2)
        for index, piece in enumerate(swap_groups(pieces)):
            field_ref[block * 4 + index] = piece
        part = pl.ds(block * 4, 4)
        copy = pltpu.make_async_copy(field_ref.at[part], out_ref.at[part], out_sems.at[block])
        copy.start()
        out_copies.append(copy)
    wait_all(out_copies)


def outer_product(lam, psi):
    order = lam.shape[0] // 2
    left = jnp.concatenate([lam[:order], lam[order:]], axis=1)
    plain = jnp.concatenate([psi[:order], psi[order:]], axis=1)
    other = jnp.concatenate([-psi[order:], psi[:order]], axis=1)
    return dot_parts(both_parts(left), jnp.concatenate([plain, other], axis=0), ROW_ROW)


def four_products(fields, groups):
    pieces = swap_groups(fields)
    rows, lanes = pieces[0].shape

    def joined(vector):
        parts = [
            piece.reshape(groups, 1, rows // groups, lanes)
            for piece in pieces[2 * vector : 2 * vector + 2]
        ]
        return jnp.concatenate(parts, axis=1).reshape(2 * rows, lanes)

    return outer_product(joined(1), joined(0))


def early_kernel(sent_ref, gates_ref, out_ref, matrix_ref):
    devices = sent_ref.shape[0]
    for index in range(2):
        matrix_ref[index] = undo_matrix(gates_ref[index + 1])
    out_ref[...] = jnp.zeros_like(out_ref)

    @pl.loop(0, devices // 4)
    def _(step):
        out_ref[...] += four_products([sent_ref[step * 4 + index] for index in range(4)], 2)


def middle_kernel(
    moved_ref, matrix_ref, out_ref, moved, matrix, kept, last, matrix_sem, in_sems, out_sems
):
    _, steps, _, order, lanes = moved.shape
    batches = 2 * steps
    in_copies = [
        pltpu.make_async_copy(moved_ref.at[:, step], moved.at[:, step], in_sems.at[step])
        for step in range(steps)
    ]
    matrix_copy = pltpu.make_async_copy(matrix_ref, matrix, matrix_sem)
    matrix_copy.start()
    for copy in in_copies:
        copy.start()
    matrix_copy.wait()
    out_copies = []

    def undo(which, fields):
        result = dot_parts(matrix[which], jnp.concatenate(fields, axis=1))
        return [result[:, index * lanes : (index + 1) * lanes] for index in range(len(fields))]

    for step in range(steps):
        in_copies[step].wait()
        fields = [mixed_rows(moved, step, bit) for bit in range(2)]
        for bit, result in enumerate(undo(0, fields)):
            for top, piece in enumerate(swap_bit(*row_halves(result, 8))):
                place = (top * steps + reversed_bits(step, steps)) * 2 + bit
                kept[pl.ds(place * order, order), :] = piece

    for step in range(steps):
        pair = [reversed_bits(step * 2 + index, batches) for index in range(2)]
        fields = [regrouped(kept, batch, order) for batch in pair]
        for index, result in enumerate(undo(1, fields)):
            for bit, piece in enumerate(swap_bit(*row_halves(result, 2))):
                last[(step * 2 + index) * 2 + bit] = piece
        part = pl.ds(step * 4, 4)
        copy = pltpu.make_async_copy(last.at[part], out_ref.at[part], out_sems.at[step])
        copy.start()
        out_copies.append(copy)
    wait_all(out_copies)


def regrouped(kept_ref, batch, order):
    devices = kept_ref.shape[0] // order
    parts = [
        kept_ref[pl.ds(row * (devices // 2) + batch, devices, stride=order), :] for row in range(8)
    ]
    return jnp.concatenate(parts, axis=0)


def mixed_rows(moved_ref, step, bit):
    low_rows = moved_ref.shape[3] // 4
    parts = [
        moved_ref[low, step, top, pl.ds((part * 2 + bit) * low_rows, low_rows), :]
        for part in range(2)
        for top in range(2)
        for low in range(2)
    ]
    return jnp.concatenate(parts, axis=0)


def late_kernel(moved_ref, last_ref, early_ref, gates_ref, out_ref, sum_ref, *, scale):
    order = early_ref.shape[0]
    steps = moved_ref.shape[1]
    sum_ref[0] = early_ref[...]
    sum_ref[1:3] = jnp.zeros((2,) + early_ref.shape, jnp.float32)

    @pl.loop(0, steps)
    def _(step):
        first, second = (mixed_rows(moved_ref, step, bit) for bit in range(2))
        half = first.shape[-1] // 2
        lower = lane_index(first.shape) < half
        psi = jnp.where(lower, first, pltpu.roll(second, half, 1))
        lam = jnp.where(lower, pltpu.roll(first, half, 1), second)
        sum_ref[1] += outer_product(lam, psi)
        sum_ref[2] += four_products([last_ref[step * 4 + index] for index in range(4)], 2)

    for index in range(3):
        total = (sum_ref[index, :, :order], sum_ref[index, :, order:])
        gate = (gates_ref[index, 0], gates_ref[index, 1])
        left, right = (total, gate) if index == 1 else (gate, total)
        out_ref[index, 0], out_ref[index, 1] = complex_product(left, right, scale)


def complex_product(left, right, scale):
    def times(first, second):
        return jnp.dot(
            first, second, precision=lax.Precision.HIGHEST, preferred_element_type=jnp.float32
        )

    real = times(left[0], right[0]) - times(left[1], right[1])
    imag = times(left[0], right[1]) + times(left[1], right[0])
    return real * scale, imag * scale


def last_kernel(moved_ref, state_ref, costate_ref, rows, copy_sems):
    half = moved_ref.shape[1] // 2
    copies = []
    for block in range(rows.shape[1] // 2):
        pieces = swap_groups([moved_ref[block * 4 + index] for index in range(4)])
        for vector, ref in enumerate((state_ref, costate_ref)):
            for part in range(2):
                column = block * 2 + part
                for bit in range(2):
                    piece = pieces[2 * vector + bit][part * half : (part + 1) * half]
                    rows[vector, column, bit * half : (bit + 1) * half] = piece
                copy = pltpu.make_async_copy(
                    rows.at[vector, column], ref.at[:, column, 0], copy_sems.at[vector, column]
                )
                copy.start()
                copies.append(copy)
    wait_all(copies)


def gather_kernel(*refs, distance):
    *part_refs, out_ref, copy_sems = refs
    place = lax.rem(lax.axis_index("amp") // distance, len(part_refs))
    copies = [
        pltpu.make_async_copy(ref, out_ref.at[place ^ index], copy_sems.at[index])
        for index, ref in enumerate(part_refs)
    ]
    for copy in copies:
        copy.start()
    wait_all(copies)


def tree_sum(parts):
    while len(parts) > 1:
        parts = [parts[i] + parts[i + 1] for i in range(0, len(parts), 2)]
    return parts[0]


def reversed_bits(index, count):
    result = 0
    while count > 1:
        result, index, count = result * 2 + index % 2, index // 2, count // 2
    return result


def exchange_all(field):
    devices = lax.axis_size("amp")
    group = [reversed_bits(i, devices) for i in range(devices)]
    return lax.all_to_all(field, "amp", 0, 0, axis_index_groups=[group], tiled=True)


def exchange(part, distance):
    devices = lax.axis_size("amp")
    return lax.ppermute(part, "amp", [(i, i ^ distance) for i in range(devices)])


def scattered_sum(value):
    devices = lax.axis_size("amp")
    inner = min(8, devices)
    own = lax.axis_index("amp") % inner
    blocks = value.reshape(inner, -1, value.shape[-1])

    def pick(index):
        return lax.dynamic_index_in_dim(blocks, index, 0, keepdims=False)

    part = tree_sum([pick(own)] + [exchange(pick(own ^ k), k) for k in range(1, inner)])
    distance = inner
    while distance < devices:
        part = part + exchange(part, distance)
        distance *= 2
    return part


def gathered(part, shape):
    inner = min(8, lax.axis_size("amp"))
    other = exchange(part, 1)
    upper = lax.axis_index("amp") % 2 == 1
    pair = jnp.stack([jnp.where(upper, other, part), jnp.where(upper, part, other)], axis=0)
    pairs = [pair] + [exchange(pair, k) for k in range(2, inner, 2)]
    out = pl.pallas_call(
        functools.partial(gather_kernel, distance=2),
        in_specs=[pl.BlockSpec(memory_space=pl.ANY)] * len(pairs),
        out_specs=IN_HBM,
        out_shape=jax.ShapeDtypeStruct((len(pairs),) + pair.shape, part.dtype),
        scratch_shapes=[pltpu.SemaphoreType.DMA((len(pairs),))],
        compiler_params=PARAMS,
    )(*pairs)
    return out.reshape(shape)


def to_rows(field, lanes):
    return field.reshape(2, -1, lanes).swapaxes(0, 1).reshape(-1, lanes)


def from_rows(rows):
    return rows.reshape(-1, 2, rows.shape[-1]).swapaxes(0, 1).reshape(2, -1)


IN_HBM = pl.BlockSpec(memory_space=pltpu.HBM)
IN_VMEM = pl.BlockSpec(memory_space=pltpu.VMEM)
PARAMS = pltpu.CompilerParams(vmem_limit_bytes=VMEM_BYTES)
HBM_PARAMS = pltpu.CompilerParams(vmem_limit_bytes=60 * 1024 * 1024)


def cost(layers, amplitudes, order):
    flops = layers * 3 * 8 * amplitudes * order
    return pl.CostEstimate(flops=flops, bytes_accessed=32 * amplitudes, transcendentals=0)


def on_device_lanes(state, costate, gates, devices, order, columns):
    lanes = 4 * columns // devices
    steps = devices // 4
    rows = 2 * columns // lanes
    scale = 1.0 / math.sqrt(devices * columns)
    field_shape = (devices, order, lanes)
    sum_shape = (order, 2 * order)
    amplitudes = 2 * order * columns

    def array(shape, kind=jnp.float32):
        return jax.ShapeDtypeStruct(shape, kind)

    sent = pl.pallas_call(
        first_kernel,
        in_specs=[IN_HBM, IN_HBM, IN_HBM],
        out_specs=IN_HBM,
        out_shape=array(field_shape),
        scratch_shapes=[
            pltpu.VMEM((2, order, order), jnp.float32),
            pltpu.VMEM((2, rows * order, lanes), jnp.float32),
            pltpu.VMEM(field_shape, jnp.float32),
            pltpu.SemaphoreType.DMA,
            pltpu.SemaphoreType.DMA((2, 4)),
            pltpu.SemaphoreType.DMA((steps,)),
        ],
        compiler_params=HBM_PARAMS,
        cost_estimate=cost(1, amplitudes, order),
    )(to_rows(state, lanes), to_rows(costate, lanes), gates)
    moved = exchange_all(sent)
    early, matrices = pl.pallas_call(
        early_kernel,
        in_specs=[IN_VMEM, IN_VMEM],
        out_specs=[IN_VMEM, IN_VMEM],
        out_shape=[array(sum_shape), array((2, 4 * order, 2 * order), jnp.bfloat16)],
        compiler_params=PARAMS,
        cost_estimate=cost(1, amplitudes, order),
    )(sent, gates)
    moved = moved.reshape(2, steps, 2, order, lanes)
    last = pl.pallas_call(
        middle_kernel,
        in_specs=[IN_HBM, IN_HBM],
        out_specs=IN_HBM,
        out_shape=array(field_shape),
        scratch_shapes=[
            pltpu.VMEM((2, steps, 2, order, lanes), jnp.float32),
            pltpu.VMEM(matrices.shape, jnp.bfloat16),
            pltpu.VMEM((devices * order, lanes), jnp.float32),
            pltpu.VMEM(field_shape, jnp.float32),
            pltpu.SemaphoreType.DMA,
            pltpu.SemaphoreType.DMA((steps,)),
            pltpu.SemaphoreType.DMA((steps,)),
        ],
        compiler_params=HBM_PARAMS,
        cost_estimate=cost(2, amplitudes, order),
    )(moved, matrices)
    arrived = exchange_all(last)
    gradients = pl.pallas_call(
        functools.partial(late_kernel, scale=scale),
        in_specs=[IN_VMEM, IN_VMEM, IN_VMEM, IN_VMEM],
        out_specs=IN_VMEM,
        out_shape=array(gates.shape),
        scratch_shapes=[pltpu.VMEM((3,) + sum_shape, jnp.float32)],
        compiler_params=PARAMS,
        cost_estimate=cost(2, amplitudes, order),
    )(moved, last, early, gates)
    part, arrived = lax.optimization_barrier((scattered_sum(gradients), arrived))
    gradients = gathered(part, gates.shape)
    state_rows, costate_rows = pl.pallas_call(
        last_kernel,
        in_specs=[IN_VMEM],
        out_specs=[IN_HBM, IN_HBM],
        out_shape=[array((order, rows, 1, lanes))] * 2,
        scratch_shapes=[
            pltpu.VMEM((2, rows, order, lanes), jnp.float32),
            pltpu.SemaphoreType.DMA((2, rows)),
        ],
        compiler_params=PARAMS,
        cost_estimate=cost(1, amplitudes, order),
    )(arrived)
    return from_rows(state_rows), from_rows(costate_rows), gradients


def undo_gate(field, gate):
    high = lax.Precision.HIGHEST
    shape = field.shape
    parts = field.reshape(shape[:-1] + (2, 2, -1))
    real, imag = parts[..., 0, :], parts[..., 1, :]

    def contract(matrix, operand):
        return jnp.einsum("ts,btvc->bsvc", matrix, operand, precision=high)

    new_real = contract(gate[0], real) + contract(gate[1], imag)
    new_imag = contract(gate[0], imag) - contract(gate[1], real)
    return jnp.stack([new_real, new_imag], axis=-2).reshape(shape)


def gate_gradient(before, after):
    high = lax.Precision.HIGHEST
    lam = before.reshape(before.shape[:-1] + (2, 2, -1))[..., 1, :, :]
    psi = after.reshape(after.shape[:-1] + (2, 2, -1))[..., 0, :, :]
    real = jnp.einsum("btpc,bspc->ts", lam, psi, precision=high)
    imag = jnp.einsum("btc,bsc->ts", lam[..., 1, :], psi[..., 0, :], precision=high) - jnp.einsum(
        "btc,bsc->ts", lam[..., 0, :], psi[..., 1, :], precision=high
    )
    return jnp.stack([real, imag], axis=0)


def on_device_plain(state, costate, gates, devices, order, columns):
    own = columns // devices
    both = jnp.stack([state, costate], axis=0).reshape(2, 2, order, devices, own)
    field = both.transpose(3, 2, 0, 1, 4).reshape(devices, order, 4 * own)
    field = lax.all_to_all(field, "amp", 0, 0, tiled=True)
    after = undo_gate(field, gates[0])
    terms = [gate_gradient(field, after)]
    field = after.reshape(2, devices // 4, 2, 2, 2, order // 4, 4 * own)
    field = field.transpose(3, 1, 4, 0, 2, 5, 6).reshape(devices, order, 4 * own)
    after = undo_gate(field, gates[1])
    terms.append(gate_gradient(field, after))
    field = after.reshape(devices, order // devices, devices, 4 * own)
    field = field.transpose(2, 1, 0, 3).reshape(devices, order, 4 * own)
    after = undo_gate(field, gates[2])
    terms.append(gate_gradient(field, after))
    terms = jnp.stack(terms, axis=0) / math.sqrt(devices * columns)
    gradients = gathered(scattered_sum(terms), gates.shape)
    field = lax.all_to_all(after, "amp", 0, 0, tiled=True)
    field = field.reshape(devices, order, 2, 2, own).transpose(2, 3, 1, 0, 4)
    field = field.reshape(2, 2, order * columns)
    return field[0], field[1], gradients


def on_device(state, costate, gates):
    devices = lax.axis_size("amp")
    order = gates.shape[2]
    columns = state.shape[1] // order
    filled = 4 * columns == 128 * devices and order == 4 * devices
    form = on_device_lanes if filled else on_device_plain
    return form(state, costate, gates, devices, order, columns)


def solution(mesh):
    return jax.shard_map(
        on_device,
        mesh=mesh,
        in_specs=(P(None, "amp"), P(None, "amp"), P()),
        out_specs=(P(None, "amp"), P(None, "amp"), P()),
        check_vma=False,
    )
```

```python
import functools
import math

import jax
import jax.numpy as jnp
from jax import lax
from jax.experimental import pallas as pl
from jax.experimental.pallas import tpu as pltpu
from jax.sharding import PartitionSpec as P

VMEM_BYTES = 24 * 1024 * 1024


def split(value):
    high = value.astype(jnp.bfloat16)
    low = (value - high.astype(jnp.float32)).astype(jnp.bfloat16)
    return high, low


def left_parts(value):
    high, low = split(value)
    return jnp.concatenate([high, low, high], axis=1)


def dot_parts(left, right):
    high, low = split(right)
    return jnp.dot(
        left, jnp.concatenate([high, high, low], axis=0), preferred_element_type=jnp.float32
    )


def dot_parts_rows(left, right):
    high, low = split(right)
    return lax.dot_general(
        left,
        jnp.concatenate([high, high, low], axis=1),
        (((1,), (1,)), ((), ())),
        preferred_element_type=jnp.float32,
    )


def lane_index(shape):
    return lax.broadcasted_iota(jnp.int32, shape, len(shape) - 1)


def swap_groups(values):
    lanes = values[0].shape[-1]
    group = lane_index(values[0].shape) // (lanes // 4)
    for bit in (2, 1):
        width = bit * (lanes // 4)
        fresh = list(values)
        for index in range(4):
            if index & bit == 0:
                low, high = values[index], values[index | bit]
                upper = group & bit != 0
                fresh[index] = jnp.where(upper, pltpu.roll(high, width, 1), low)
                fresh[index | bit] = jnp.where(upper, high, pltpu.roll(low, lanes - width, 1))
        values = fresh
    return values


def swap_bit(low, high):
    lanes = low.shape[-1]
    width = lanes // 4
    upper = (lane_index(low.shape) // width) % 2 == 1
    first = jnp.where(upper, pltpu.roll(high, width, 1), low)
    second = jnp.where(upper, high, pltpu.roll(low, lanes - width, 1))
    return first, second


def row_halves(value, groups):
    rows, lanes = value.shape
    parts = value.reshape(groups, 2, rows // groups // 2, lanes)
    return parts[:, 0].reshape(rows // 2, lanes), parts[:, 1].reshape(rows // 2, lanes)


def wait_all(copies):
    for copy in copies:
        copy.wait()


def undo_matrix(gate):
    real, imag = gate[0].T, gate[1].T
    top = jnp.concatenate([real, imag], axis=1)
    low = jnp.concatenate([-imag, real], axis=1)
    return left_parts(jnp.concatenate([top, low], axis=0))


def first_kernel(
    state_ref, costate_ref, gates_ref, out_ref, gate, rows, field_ref, gate_sem, row_sems, out_sems
):
    order = gate.shape[1]
    lanes = rows.shape[2]
    stride = rows.shape[1] // order
    chunks = row_sems.shape[1]
    chunk = rows.shape[1] // chunks
    copies = [pltpu.make_async_copy(gates_ref.at[0], gate, gate_sem)]
    for index in range(chunks):
        part = pl.ds(index * chunk, chunk)
        for vector, ref in enumerate((state_ref, costate_ref)):
            copies.append(
                pltpu.make_async_copy(ref.at[part], rows.at[vector, part], row_sems.at[vector, index])
            )
    for copy in copies:
        copy.start()
    copies[0].wait()
    matrix = undo_matrix(gate)
    wait_all(copies[1:])

    def column(vector, block):
        parts = [rows[vector, pl.ds(block * 2 + part, order, stride=stride), :] for part in range(2)]
        return jnp.concatenate(parts, axis=0)

    out_copies = []
    for block in range(stride // 2):
        field = jnp.concatenate([column(0, block), column(1, block)], axis=1)
        undone = dot_parts(matrix, field)
        pieces = []
        for vector in range(2):
            pieces += row_halves(undone[:, vector * lanes : (vector + 1) * lanes], 2)
        for index, piece in enumerate(swap_groups(pieces)):
            field_ref[block * 4 + index] = piece
        part = pl.ds(block * 4, 4)
        copy = pltpu.make_async_copy(field_ref.at[part], out_ref.at[part], out_sems.at[block])
        copy.start()
        out_copies.append(copy)
    wait_all(out_copies)


def outer_product(lam, psi):
    order = lam.shape[0] // 2
    left = jnp.concatenate([lam[:order], lam[order:]], axis=1)
    plain = jnp.concatenate([psi[:order], psi[order:]], axis=1)
    other = jnp.concatenate([-psi[order:], psi[:order]], axis=1)
    return dot_parts_rows(left_parts(left), jnp.concatenate([plain, other], axis=0))


def four_products(fields, groups):
    pieces = swap_groups(fields)
    rows, lanes = pieces[0].shape

    def joined(vector):
        parts = [
            piece.reshape(groups, 1, rows // groups, lanes)
            for piece in pieces[2 * vector : 2 * vector + 2]
        ]
        return jnp.concatenate(parts, axis=1).reshape(2 * rows, lanes)

    return outer_product(joined(1), joined(0))


def early_kernel(sent_ref, gates_ref, out_ref, matrix_ref):
    devices = sent_ref.shape[0]
    for index in range(2):
        matrix_ref[index] = undo_matrix(gates_ref[index + 1])
    out_ref[...] = jnp.zeros_like(out_ref)

    @pl.loop(0, devices // 4)
    def _(step):
        out_ref[...] += four_products([sent_ref[step * 4 + index] for index in range(4)], 2)


def middle_kernel(
    moved_ref, matrix_ref, out_ref, moved, matrix, kept, last, matrix_sem, in_sems, out_sems
):
    _, steps, _, order, lanes = moved.shape
    batches = 2 * steps
    in_copies = [
        pltpu.make_async_copy(moved_ref.at[:, step], moved.at[:, step], in_sems.at[step])
        for step in range(steps)
    ]
    matrix_copy = pltpu.make_async_copy(matrix_ref, matrix, matrix_sem)
    matrix_copy.start()
    for copy in in_copies:
        copy.start()
    matrix_copy.wait()
    out_copies = []

    def undo(which, fields):
        result = dot_parts(matrix[which], jnp.concatenate(fields, axis=1))
        return [result[:, index * lanes : (index + 1) * lanes] for index in range(len(fields))]

    for step in range(steps):
        in_copies[step].wait()
        fields = [mixed_rows(moved, step, bit) for bit in range(2)]
        for bit, result in enumerate(undo(0, fields)):
            for top, piece in enumerate(swap_bit(*row_halves(result, 8))):
                place = (top * steps + step) * 2 + bit
                kept[pl.ds(place * order, order), :] = piece

    for step in range(steps):
        fields = [regrouped(kept, step * 2 + index, order) for index in range(2)]
        for index, result in enumerate(undo(1, fields)):
            for bit, piece in enumerate(swap_bit(*row_halves(result, 2))):
                last[bit * batches + step * 2 + index] = piece
        for bit in range(2):
            part = pl.ds(bit * batches + step * 2, 2)
            copy = pltpu.make_async_copy(last.at[part], out_ref.at[part], out_sems.at[bit, step])
            copy.start()
            out_copies.append(copy)
    wait_all(out_copies)


def regrouped(kept_ref, batch, order):
    devices = kept_ref.shape[0] // order
    parts = [
        kept_ref[pl.ds(row * (devices // 2) + batch, devices, stride=order), :] for row in range(8)
    ]
    return jnp.concatenate(parts, axis=0)


def mixed_rows(moved_ref, step, bit):
    low_rows = moved_ref.shape[3] // 4
    parts = [
        moved_ref[top, step, low, pl.ds((part * 2 + bit) * low_rows, low_rows), :]
        for part in range(2)
        for top in range(2)
        for low in range(2)
    ]
    return jnp.concatenate(parts, axis=0)


def late_kernel(moved_ref, last_ref, early_ref, gates_ref, out_ref, sum_ref, *, scale):
    order = early_ref.shape[0]
    steps = moved_ref.shape[1]
    sum_ref[0] = early_ref[...]
    sum_ref[1:3] = jnp.zeros((2,) + early_ref.shape, jnp.float32)

    @pl.loop(0, steps)
    def _(step):
        first, second = (mixed_rows(moved_ref, step, bit) for bit in range(2))
        half = first.shape[-1] // 2
        lower = lane_index(first.shape) < half
        psi = jnp.where(lower, first, pltpu.roll(second, half, 1))
        lam = jnp.where(lower, pltpu.roll(first, half, 1), second)
        sum_ref[1] += outer_product(lam, psi)
        sum_ref[2] += four_products([last_ref[step * 4 + index] for index in range(4)], 2)

    for index in range(3):
        total = (sum_ref[index, :, :order], sum_ref[index, :, order:])
        gate = (gates_ref[index, 0], gates_ref[index, 1])
        left, right = (total, gate) if index == 1 else (gate, total)
        out_ref[index, 0], out_ref[index, 1] = complex_product(left, right, scale)


def complex_product(left, right, scale):
    def times(first, second):
        return jnp.dot(
            first, second, precision=lax.Precision.HIGHEST, preferred_element_type=jnp.float32
        )

    real = times(left[0], right[0]) - times(left[1], right[1])
    imag = times(left[0], right[1]) + times(left[1], right[0])
    return real * scale, imag * scale


def last_kernel(moved_ref, state_ref, costate_ref, rows, copy_sems):
    half = moved_ref.shape[1] // 2
    copies = []
    for block in range(rows.shape[1] // 2):
        pieces = swap_groups([moved_ref[block * 4 + index] for index in range(4)])
        for vector, ref in enumerate((state_ref, costate_ref)):
            for part in range(2):
                column = block * 2 + part
                for bit in range(2):
                    piece = pieces[2 * vector + bit][part * half : (part + 1) * half]
                    rows[vector, column, bit * half : (bit + 1) * half] = piece
                copy = pltpu.make_async_copy(
                    rows.at[vector, column], ref.at[:, column, 0], copy_sems.at[vector, column]
                )
                copy.start()
                copies.append(copy)
    wait_all(copies)


def gather_kernel(*refs):
    *part_refs, out_ref, copy_sems = refs
    place = lax.rem(lax.axis_index("amp"), len(part_refs))
    copies = [
        pltpu.make_async_copy(ref, out_ref.at[place ^ index], copy_sems.at[index])
        for index, ref in enumerate(part_refs)
    ]
    for copy in copies:
        copy.start()
    wait_all(copies)


def tree_sum(parts):
    while len(parts) > 1:
        parts = [parts[i] + parts[i + 1] for i in range(0, len(parts), 2)]
    return parts[0]


def exchange(part, distance):
    devices = lax.axis_size("amp")
    return lax.ppermute(part, "amp", [(i, i ^ distance) for i in range(devices)])


def scattered_sum(value):
    devices = lax.axis_size("amp")
    inner = min(8, devices)
    own = lax.axis_index("amp") % inner
    blocks = value.reshape(inner, -1, value.shape[-1])

    def pick(index):
        return lax.dynamic_index_in_dim(blocks, index, 0, keepdims=False)

    part = tree_sum([pick(own)] + [exchange(pick(own ^ k), k) for k in range(1, inner)])
    distance = inner
    while distance < devices:
        part = part + exchange(part, distance)
        distance *= 2
    return part


def gathered(part, shape):
    inner = min(8, lax.axis_size("amp"))
    own = [part] + [exchange(part, k) for k in range(2, inner, 2)]
    others = [exchange(found, 1) for found in own]
    parts = [found for pair in zip(own, others) for found in pair]
    out = pl.pallas_call(
        gather_kernel,
        in_specs=[pl.BlockSpec(memory_space=pl.ANY)] * inner,
        out_specs=IN_HBM,
        out_shape=jax.ShapeDtypeStruct((inner,) + part.shape, part.dtype),
        scratch_shapes=[pltpu.SemaphoreType.DMA((inner,))],
        compiler_params=PARAMS,
    )(*parts)
    return out.reshape(shape)


def to_rows(field, lanes):
    return field.reshape(2, -1, lanes).swapaxes(0, 1).reshape(-1, lanes)


def from_rows(rows):
    return rows.reshape(-1, 2, rows.shape[-1]).swapaxes(0, 1).reshape(2, -1)


IN_HBM = pl.BlockSpec(memory_space=pltpu.HBM)
IN_VMEM = pl.BlockSpec(memory_space=pltpu.VMEM)
PARAMS = pltpu.CompilerParams(vmem_limit_bytes=VMEM_BYTES)
HBM_PARAMS = pltpu.CompilerParams(vmem_limit_bytes=60 * 1024 * 1024)


def cost(layers, amplitudes, order):
    flops = layers * 3 * 8 * amplitudes * order
    return pl.CostEstimate(flops=flops, bytes_accessed=32 * amplitudes, transcendentals=0)


def on_device_lanes(state, costate, gates, devices, order, columns):
    lanes = 4 * columns // devices
    steps = devices // 4
    rows = 2 * columns // lanes
    scale = 1.0 / math.sqrt(devices * columns)
    field_shape = (devices, order, lanes)
    sum_shape = (order, 2 * order)
    amplitudes = 2 * order * columns

    def array(shape, kind=jnp.float32):
        return jax.ShapeDtypeStruct(shape, kind)

    sent = pl.pallas_call(
        first_kernel,
        in_specs=[IN_HBM, IN_HBM, IN_HBM],
        out_specs=IN_HBM,
        out_shape=array(field_shape),
        scratch_shapes=[
            pltpu.VMEM((2, order, order), jnp.float32),
            pltpu.VMEM((2, rows * order, lanes), jnp.float32),
            pltpu.VMEM(field_shape, jnp.float32),
            pltpu.SemaphoreType.DMA,
            pltpu.SemaphoreType.DMA((2, 4)),
            pltpu.SemaphoreType.DMA((steps,)),
        ],
        compiler_params=HBM_PARAMS,
        cost_estimate=cost(1, amplitudes, order),
    )(to_rows(state, lanes), to_rows(costate, lanes), gates)
    moved = lax.all_to_all(sent, "amp", 0, 0, tiled=True)
    early, matrices = pl.pallas_call(
        early_kernel,
        in_specs=[IN_VMEM, IN_VMEM],
        out_specs=[IN_VMEM, IN_VMEM],
        out_shape=[array(sum_shape), array((2, 2 * order, 6 * order), jnp.bfloat16)],
        compiler_params=PARAMS,
        cost_estimate=cost(1, amplitudes, order),
    )(sent, gates)
    moved = moved.reshape(2, steps, 2, order, lanes)
    last = pl.pallas_call(
        middle_kernel,
        in_specs=[IN_HBM, IN_HBM],
        out_specs=IN_HBM,
        out_shape=array(field_shape),
        scratch_shapes=[
            pltpu.VMEM((2, steps, 2, order, lanes), jnp.float32),
            pltpu.VMEM(matrices.shape, jnp.bfloat16),
            pltpu.VMEM((devices * order, lanes), jnp.float32),
            pltpu.VMEM(field_shape, jnp.float32),
            pltpu.SemaphoreType.DMA,
            pltpu.SemaphoreType.DMA((steps,)),
            pltpu.SemaphoreType.DMA((2, steps)),
        ],
        compiler_params=HBM_PARAMS,
        cost_estimate=cost(2, amplitudes, order),
    )(moved, matrices)
    arrived = lax.all_to_all(last, "amp", 0, 0, tiled=True)
    gradients = pl.pallas_call(
        functools.partial(late_kernel, scale=scale),
        in_specs=[IN_VMEM, IN_VMEM, IN_VMEM, IN_VMEM],
        out_specs=IN_VMEM,
        out_shape=array(gates.shape),
        scratch_shapes=[pltpu.VMEM((3,) + sum_shape, jnp.float32)],
        compiler_params=PARAMS,
        cost_estimate=cost(2, amplitudes, order),
    )(moved, last, early, gates)
    part, arrived = lax.optimization_barrier((scattered_sum(gradients), arrived))
    gradients = gathered(part, gates.shape)
    state_rows, costate_rows = pl.pallas_call(
        last_kernel,
        in_specs=[IN_VMEM],
        out_specs=[IN_HBM, IN_HBM],
        out_shape=[array((order, rows, 1, lanes))] * 2,
        scratch_shapes=[
            pltpu.VMEM((2, rows, order, lanes), jnp.float32),
            pltpu.SemaphoreType.DMA((2, rows)),
        ],
        compiler_params=PARAMS,
        cost_estimate=cost(1, amplitudes, order),
    )(arrived)
    return from_rows(state_rows), from_rows(costate_rows), gradients


def undo_gate(field, gate):
    high = lax.Precision.HIGHEST
    shape = field.shape
    parts = field.reshape(shape[:-1] + (2, 2, -1))
    real, imag = parts[..., 0, :], parts[..., 1, :]

    def contract(matrix, operand):
        return jnp.einsum("ts,btvc->bsvc", matrix, operand, precision=high)

    new_real = contract(gate[0], real) + contract(gate[1], imag)
    new_imag = contract(gate[0], imag) - contract(gate[1], real)
    return jnp.stack([new_real, new_imag], axis=-2).reshape(shape)


def gate_gradient(before, after):
    high = lax.Precision.HIGHEST
    lam = before.reshape(before.shape[:-1] + (2, 2, -1))[..., 1, :, :]
    psi = after.reshape(after.shape[:-1] + (2, 2, -1))[..., 0, :, :]
    real = jnp.einsum("btpc,bspc->ts", lam, psi, precision=high)
    imag = jnp.einsum("btc,bsc->ts", lam[..., 1, :], psi[..., 0, :], precision=high) - jnp.einsum(
        "btc,bsc->ts", lam[..., 0, :], psi[..., 1, :], precision=high
    )
    return jnp.stack([real, imag], axis=0)


def on_device_plain(state, costate, gates, devices, order, columns):
    own = columns // devices
    both = jnp.stack([state, costate], axis=0).reshape(2, 2, order, devices, own)
    field = both.transpose(3, 2, 0, 1, 4).reshape(devices, order, 4 * own)
    field = lax.all_to_all(field, "amp", 0, 0, tiled=True)
    after = undo_gate(field, gates[0])
    terms = [gate_gradient(field, after)]
    field = after.reshape(2, devices // 4, 2, 2, 2, order // 4, 4 * own)
    field = field.transpose(3, 1, 4, 0, 2, 5, 6).reshape(devices, order, 4 * own)
    after = undo_gate(field, gates[1])
    terms.append(gate_gradient(field, after))
    field = after.reshape(devices, order // devices, devices, 4 * own)
    field = field.transpose(2, 1, 0, 3).reshape(devices, order, 4 * own)
    after = undo_gate(field, gates[2])
    terms.append(gate_gradient(field, after))
    terms = jnp.stack(terms, axis=0) / math.sqrt(devices * columns)
    gradients = gathered(scattered_sum(terms), gates.shape)
    field = lax.all_to_all(after, "amp", 0, 0, tiled=True)
    field = field.reshape(devices, order, 2, 2, own).transpose(2, 3, 1, 0, 4)
    field = field.reshape(2, 2, order * columns)
    return field[0], field[1], gradients


def on_device(state, costate, gates):
    devices = lax.axis_size("amp")
    order = gates.shape[2]
    columns = state.shape[1] // order
    filled = 4 * columns == 128 * devices and order == 4 * devices
    form = on_device_lanes if filled else on_device_plain
    return form(state, costate, gates, devices, order, columns)


def solution(mesh):
    return jax.shard_map(
        on_device,
        mesh=mesh,
        in_specs=(P(None, "amp"), P(None, "amp"), P()),
        out_specs=(P(None, "amp"), P(None, "amp"), P()),
        check_vma=False,
    )
```

```python
import functools
import math

import jax
import jax.numpy as jnp
from jax import lax
from jax.experimental import pallas as pl
from jax.experimental.pallas import tpu as pltpu
from jax.sharding import PartitionSpec as P

VMEM_BYTES = 24 * 1024 * 1024


def split(value):
    high = value.astype(jnp.bfloat16)
    low = (value - high.astype(jnp.float32)).astype(jnp.bfloat16)
    return high, low


def left_parts(value):
    high, low = split(value)
    return jnp.concatenate([high, low, high], axis=1)


def dot_parts(left, right):
    high, low = split(right)
    return jnp.dot(
        left, jnp.concatenate([high, high, low], axis=0), preferred_element_type=jnp.float32
    )


def dot_parts_rows(left, right):
    high, low = split(right)
    return lax.dot_general(
        left,
        jnp.concatenate([high, high, low], axis=1),
        (((1,), (1,)), ((), ())),
        preferred_element_type=jnp.float32,
    )


def lane_index(shape):
    return lax.broadcasted_iota(jnp.int32, shape, len(shape) - 1)


def swap_groups(values):
    lanes = values[0].shape[-1]
    group = lane_index(values[0].shape) // (lanes // 4)
    for bit in (2, 1):
        width = bit * (lanes // 4)
        fresh = list(values)
        for index in range(4):
            if index & bit == 0:
                low, high = values[index], values[index | bit]
                upper = group & bit != 0
                fresh[index] = jnp.where(upper, pltpu.roll(high, width, 1), low)
                fresh[index | bit] = jnp.where(upper, high, pltpu.roll(low, lanes - width, 1))
        values = fresh
    return values


def swap_bit(low, high):
    lanes = low.shape[-1]
    width = lanes // 4
    upper = (lane_index(low.shape) // width) % 2 == 1
    first = jnp.where(upper, pltpu.roll(high, width, 1), low)
    second = jnp.where(upper, high, pltpu.roll(low, lanes - width, 1))
    return first, second


def row_halves(value, groups):
    rows, lanes = value.shape
    parts = value.reshape(groups, 2, rows // groups // 2, lanes)
    return parts[:, 0].reshape(rows // 2, lanes), parts[:, 1].reshape(rows // 2, lanes)


def wait_all(copies):
    for copy in copies:
        copy.wait()


def undo_matrix(gate):
    real, imag = gate[0].T, gate[1].T
    top = jnp.concatenate([real, imag], axis=1)
    low = jnp.concatenate([-imag, real], axis=1)
    return left_parts(jnp.concatenate([top, low], axis=0))


def first_kernel(
    state_ref, costate_ref, gates_ref, out_ref, gate, rows, field_ref, gate_sem, row_sems, out_sems
):
    order = gate.shape[1]
    lanes = rows.shape[2]
    stride = rows.shape[1] // order
    chunks = row_sems.shape[1]
    chunk = rows.shape[1] // chunks
    copies = [pltpu.make_async_copy(gates_ref.at[0], gate, gate_sem)]
    for index in range(chunks):
        part = pl.ds(index * chunk, chunk)
        for vector, ref in enumerate((state_ref, costate_ref)):
            copies.append(
                pltpu.make_async_copy(ref.at[part], rows.at[vector, part], row_sems.at[vector, index])
            )
    for copy in copies:
        copy.start()
    copies[0].wait()
    matrix = undo_matrix(gate)
    wait_all(copies[1:])

    def column(vector, block):
        parts = [rows[vector, pl.ds(block * 2 + part, order, stride=stride), :] for part in range(2)]
        return jnp.concatenate(parts, axis=0)

    out_copies = []
    for block in range(stride // 2):
        field = jnp.concatenate([column(0, block), column(1, block)], axis=1)
        undone = dot_parts(matrix, field)
        pieces = []
        for vector in range(2):
            pieces += row_halves(undone[:, vector * lanes : (vector + 1) * lanes], 2)
        for index, piece in enumerate(swap_groups(pieces)):
            field_ref[block * 4 + index] = piece
        part = pl.ds(block * 4, 4)
        copy = pltpu.make_async_copy(field_ref.at[part], out_ref.at[part], out_sems.at[block])
        copy.start()
        out_copies.append(copy)
    wait_all(out_copies)


def outer_product(lam, psi):
    order = lam.shape[0] // 2
    left = jnp.concatenate([lam[:order], lam[order:]], axis=1)
    plain = jnp.concatenate([psi[:order], psi[order:]], axis=1)
    other = jnp.concatenate([-psi[order:], psi[:order]], axis=1)
    return dot_parts_rows(left_parts(left), jnp.concatenate([plain, other], axis=0))


def four_products(fields, groups):
    pieces = swap_groups(fields)
    rows, lanes = pieces[0].shape

    def joined(vector):
        parts = [
            piece.reshape(groups, 1, rows // groups, lanes)
            for piece in pieces[2 * vector : 2 * vector + 2]
        ]
        return jnp.concatenate(parts, axis=1).reshape(2 * rows, lanes)

    return outer_product(joined(1), joined(0))


def early_kernel(sent_ref, gates_ref, out_ref, matrix_ref):
    devices = sent_ref.shape[0]
    for index in range(2):
        matrix_ref[index] = undo_matrix(gates_ref[index + 1])
    out_ref[...] = jnp.zeros_like(out_ref)

    @pl.loop(0, devices // 4)
    def _(step):
        out_ref[...] += four_products([sent_ref[step * 4 + index] for index in range(4)], 2)


def middle_kernel(moved_ref, matrix_ref, out_ref, kept):
    _, steps, _, order, lanes = moved_ref.shape
    batches = 2 * steps

    def undo(which, fields):
        result = dot_parts(matrix_ref[which], jnp.concatenate(fields, axis=1))
        return [result[:, index * lanes : (index + 1) * lanes] for index in range(len(fields))]

    for step in range(steps):
        fields = [mixed_rows(moved_ref, step, bit) for bit in range(2)]
        for bit, result in enumerate(undo(0, fields)):
            for top, piece in enumerate(swap_bit(*row_halves(result, 8))):
                place = (top * steps + step) * 2 + bit
                kept[pl.ds(place * order, order), :] = piece

    for step in range(steps):
        fields = [regrouped(kept, step * 2 + index, order) for index in range(2)]
        for index, result in enumerate(undo(1, fields)):
            for bit, piece in enumerate(swap_bit(*row_halves(result, 2))):
                out_ref[bit * batches + step * 2 + index] = piece


def regrouped(kept_ref, batch, order):
    devices = kept_ref.shape[0] // order
    parts = [
        kept_ref[pl.ds(row * (devices // 2) + batch, devices, stride=order), :] for row in range(8)
    ]
    return jnp.concatenate(parts, axis=0)


def mixed_rows(moved_ref, step, bit):
    low_rows = moved_ref.shape[3] // 4
    parts = [
        moved_ref[top, step, low, pl.ds((part * 2 + bit) * low_rows, low_rows), :]
        for part in range(2)
        for top in range(2)
        for low in range(2)
    ]
    return jnp.concatenate(parts, axis=0)


def late_kernel(moved_ref, last_ref, early_ref, gates_ref, out_ref, sum_ref, *, scale):
    order = early_ref.shape[0]
    steps = moved_ref.shape[1]
    sum_ref[0] = early_ref[...]
    sum_ref[1:3] = jnp.zeros((2,) + early_ref.shape, jnp.float32)

    @pl.loop(0, steps)
    def _(step):
        first, second = (mixed_rows(moved_ref, step, bit) for bit in range(2))
        half = first.shape[-1] // 2
        lower = lane_index(first.shape) < half
        psi = jnp.where(lower, first, pltpu.roll(second, half, 1))
        lam = jnp.where(lower, pltpu.roll(first, half, 1), second)
        sum_ref[1] += outer_product(lam, psi)
        sum_ref[2] += four_products([last_ref[step * 4 + index] for index in range(4)], 2)

    for index in range(3):
        total = (sum_ref[index, :, :order], sum_ref[index, :, order:])
        gate = (gates_ref[index, 0], gates_ref[index, 1])
        left, right = (total, gate) if index == 1 else (gate, total)
        out_ref[index, 0], out_ref[index, 1] = complex_product(left, right, scale)


def complex_product(left, right, scale):
    def times(first, second):
        return jnp.dot(
            first, second, precision=lax.Precision.HIGHEST, preferred_element_type=jnp.float32
        )

    real = times(left[0], right[0]) - times(left[1], right[1])
    imag = times(left[0], right[1]) + times(left[1], right[0])
    return real * scale, imag * scale


def last_kernel(moved_ref, state_ref, costate_ref, rows, copy_sems):
    half = moved_ref.shape[1] // 2
    copies = []
    for block in range(rows.shape[1] // 2):
        pieces = swap_groups([moved_ref[block * 4 + index] for index in range(4)])
        for vector, ref in enumerate((state_ref, costate_ref)):
            for part in range(2):
                column = block * 2 + part
                for bit in range(2):
                    piece = pieces[2 * vector + bit][part * half : (part + 1) * half]
                    rows[vector, column, bit * half : (bit + 1) * half] = piece
                copy = pltpu.make_async_copy(
                    rows.at[vector, column], ref.at[:, column, 0], copy_sems.at[vector, column]
                )
                copy.start()
                copies.append(copy)
    wait_all(copies)


def gather_kernel(*refs):
    *part_refs, out_ref, copy_sems = refs
    place = lax.rem(lax.axis_index("amp"), len(part_refs))
    copies = [
        pltpu.make_async_copy(ref, out_ref.at[place ^ index], copy_sems.at[index])
        for index, ref in enumerate(part_refs)
    ]
    for copy in copies:
        copy.start()
    wait_all(copies)


def tree_sum(parts):
    while len(parts) > 1:
        parts = [parts[i] + parts[i + 1] for i in range(0, len(parts), 2)]
    return parts[0]


def exchange(part, distance):
    devices = lax.axis_size("amp")
    return lax.ppermute(part, "amp", [(i, i ^ distance) for i in range(devices)])


def scattered_sum(value):
    devices = lax.axis_size("amp")
    inner = min(8, devices)
    own = lax.axis_index("amp") % inner
    blocks = value.reshape(inner, -1, value.shape[-1])

    def pick(index):
        return lax.dynamic_index_in_dim(blocks, index, 0, keepdims=False)

    part = tree_sum([pick(own)] + [exchange(pick(own ^ k), k) for k in range(1, inner)])
    distance = inner
    while distance < devices:
        part = part + exchange(part, distance)
        distance *= 2
    return part


def gathered(part, shape):
    inner = min(8, lax.axis_size("amp"))
    own = [part] + [exchange(part, k) for k in range(2, inner, 2)]
    others = [exchange(found, 1) for found in own]
    parts = [found for pair in zip(own, others) for found in pair]
    out = pl.pallas_call(
        gather_kernel,
        in_specs=[pl.BlockSpec(memory_space=pl.ANY)] * inner,
        out_specs=IN_HBM,
        out_shape=jax.ShapeDtypeStruct((inner,) + part.shape, part.dtype),
        scratch_shapes=[pltpu.SemaphoreType.DMA((inner,))],
        compiler_params=PARAMS,
    )(*parts)
    return out.reshape(shape)


def to_rows(field, lanes):
    return field.reshape(2, -1, lanes).swapaxes(0, 1).reshape(-1, lanes)


def from_rows(rows):
    return rows.reshape(-1, 2, rows.shape[-1]).swapaxes(0, 1).reshape(2, -1)


IN_HBM = pl.BlockSpec(memory_space=pltpu.HBM)
IN_VMEM = pl.BlockSpec(memory_space=pltpu.VMEM)
PARAMS = pltpu.CompilerParams(vmem_limit_bytes=VMEM_BYTES)
HBM_PARAMS = pltpu.CompilerParams(vmem_limit_bytes=60 * 1024 * 1024)


def cost(layers, amplitudes, order):
    flops = layers * 3 * 8 * amplitudes * order
    return pl.CostEstimate(flops=flops, bytes_accessed=32 * amplitudes, transcendentals=0)


def on_device_lanes(state, costate, gates, devices, order, columns):
    lanes = 4 * columns // devices
    steps = devices // 4
    rows = 2 * columns // lanes
    scale = 1.0 / math.sqrt(devices * columns)
    field_shape = (devices, order, lanes)
    sum_shape = (order, 2 * order)
    amplitudes = 2 * order * columns

    def array(shape, kind=jnp.float32):
        return jax.ShapeDtypeStruct(shape, kind)

    sent = pl.pallas_call(
        first_kernel,
        in_specs=[IN_HBM, IN_HBM, IN_HBM],
        out_specs=IN_HBM,
        out_shape=array(field_shape),
        scratch_shapes=[
            pltpu.VMEM((2, order, order), jnp.float32),
            pltpu.VMEM((2, rows * order, lanes), jnp.float32),
            pltpu.VMEM(field_shape, jnp.float32),
            pltpu.SemaphoreType.DMA,
            pltpu.SemaphoreType.DMA((2, 4)),
            pltpu.SemaphoreType.DMA((steps,)),
        ],
        compiler_params=HBM_PARAMS,
        cost_estimate=cost(1, amplitudes, order),
    )(to_rows(state, lanes), to_rows(costate, lanes), gates)
    moved = lax.all_to_all(sent, "amp", 0, 0, tiled=True)
    early, matrices = pl.pallas_call(
        early_kernel,
        in_specs=[IN_VMEM, IN_VMEM],
        out_specs=[IN_VMEM, IN_VMEM],
        out_shape=[array(sum_shape), array((2, 2 * order, 6 * order), jnp.bfloat16)],
        compiler_params=PARAMS,
        cost_estimate=cost(1, amplitudes, order),
    )(sent, gates)
    moved = moved.reshape(2, steps, 2, order, lanes)
    last = pl.pallas_call(
        middle_kernel,
        in_specs=[IN_VMEM, IN_VMEM],
        out_specs=IN_VMEM,
        out_shape=array(field_shape),
        scratch_shapes=[pltpu.VMEM((devices * order, lanes), jnp.float32)],
        compiler_params=PARAMS,
        cost_estimate=cost(2, amplitudes, order),
    )(moved, matrices)
    arrived = lax.all_to_all(last, "amp", 0, 0, tiled=True)
    gradients = pl.pallas_call(
        functools.partial(late_kernel, scale=scale),
        in_specs=[IN_VMEM, IN_VMEM, IN_VMEM, IN_VMEM],
        out_specs=IN_VMEM,
        out_shape=array(gates.shape),
        scratch_shapes=[pltpu.VMEM((3,) + sum_shape, jnp.float32)],
        compiler_params=PARAMS,
        cost_estimate=cost(2, amplitudes, order),
    )(moved, last, early, gates)
    part, arrived = lax.optimization_barrier((scattered_sum(gradients), arrived))
    gradients = gathered(part, gates.shape)
    state_rows, costate_rows = pl.pallas_call(
        last_kernel,
        in_specs=[IN_VMEM],
        out_specs=[IN_HBM, IN_HBM],
        out_shape=[array((order, rows, 1, lanes))] * 2,
        scratch_shapes=[
            pltpu.VMEM((2, rows, order, lanes), jnp.float32),
            pltpu.SemaphoreType.DMA((2, rows)),
        ],
        compiler_params=PARAMS,
        cost_estimate=cost(1, amplitudes, order),
    )(arrived)
    return from_rows(state_rows), from_rows(costate_rows), gradients


def undo_gate(field, gate):
    high = lax.Precision.HIGHEST
    shape = field.shape
    parts = field.reshape(shape[:-1] + (2, 2, -1))
    real, imag = parts[..., 0, :], parts[..., 1, :]

    def contract(matrix, operand):
        return jnp.einsum("ts,btvc->bsvc", matrix, operand, precision=high)

    new_real = contract(gate[0], real) + contract(gate[1], imag)
    new_imag = contract(gate[0], imag) - contract(gate[1], real)
    return jnp.stack([new_real, new_imag], axis=-2).reshape(shape)


def gate_gradient(before, after):
    high = lax.Precision.HIGHEST
    lam = before.reshape(before.shape[:-1] + (2, 2, -1))[..., 1, :, :]
    psi = after.reshape(after.shape[:-1] + (2, 2, -1))[..., 0, :, :]
    real = jnp.einsum("btpc,bspc->ts", lam, psi, precision=high)
    imag = jnp.einsum("btc,bsc->ts", lam[..., 1, :], psi[..., 0, :], precision=high) - jnp.einsum(
        "btc,bsc->ts", lam[..., 0, :], psi[..., 1, :], precision=high
    )
    return jnp.stack([real, imag], axis=0)


def on_device_plain(state, costate, gates, devices, order, columns):
    own = columns // devices
    both = jnp.stack([state, costate], axis=0).reshape(2, 2, order, devices, own)
    field = both.transpose(3, 2, 0, 1, 4).reshape(devices, order, 4 * own)
    field = lax.all_to_all(field, "amp", 0, 0, tiled=True)
    after = undo_gate(field, gates[0])
    terms = [gate_gradient(field, after)]
    field = after.reshape(2, devices // 4, 2, 2, 2, order // 4, 4 * own)
    field = field.transpose(3, 1, 4, 0, 2, 5, 6).reshape(devices, order, 4 * own)
    after = undo_gate(field, gates[1])
    terms.append(gate_gradient(field, after))
    field = after.reshape(devices, order // devices, devices, 4 * own)
    field = field.transpose(2, 1, 0, 3).reshape(devices, order, 4 * own)
    after = undo_gate(field, gates[2])
    terms.append(gate_gradient(field, after))
    terms = jnp.stack(terms, axis=0) / math.sqrt(devices * columns)
    gradients = gathered(scattered_sum(terms), gates.shape)
    field = lax.all_to_all(after, "amp", 0, 0, tiled=True)
    field = field.reshape(devices, order, 2, 2, own).transpose(2, 3, 1, 0, 4)
    field = field.reshape(2, 2, order * columns)
    return field[0], field[1], gradients


def on_device(state, costate, gates):
    devices = lax.axis_size("amp")
    order = gates.shape[2]
    columns = state.shape[1] // order
    filled = 4 * columns == 128 * devices and order == 4 * devices
    form = on_device_lanes if filled else on_device_plain
    return form(state, costate, gates, devices, order, columns)


def solution(mesh):
    return jax.shard_map(
        on_device,
        mesh=mesh,
        in_specs=(P(None, "amp"), P(None, "amp"), P()),
        out_specs=(P(None, "amp"), P(None, "amp"), P()),
        check_vma=False,
    )
```

```python
import functools
import math

import jax
import jax.numpy as jnp
from jax import lax
from jax.experimental import pallas as pl
from jax.experimental.pallas import tpu as pltpu
from jax.sharding import PartitionSpec as P

VMEM_BYTES = 24 * 1024 * 1024


def split(value):
    high = value.astype(jnp.bfloat16)
    low = (value - high.astype(jnp.float32)).astype(jnp.bfloat16)
    return high, low


def left_parts(value):
    high, low = split(value)
    return jnp.concatenate([high, low, high], axis=1)


def dot_parts(left, right):
    high, low = split(right)
    return jnp.dot(
        left, jnp.concatenate([high, high, low], axis=0), preferred_element_type=jnp.float32
    )


def dot_parts_rows(left, right):
    high, low = split(right)
    return lax.dot_general(
        left,
        jnp.concatenate([high, high, low], axis=1),
        (((1,), (1,)), ((), ())),
        preferred_element_type=jnp.float32,
    )


def lane_index(shape):
    return lax.broadcasted_iota(jnp.int32, shape, len(shape) - 1)


def swap_groups(values):
    lanes = values[0].shape[-1]
    group = lane_index(values[0].shape) // (lanes // 4)
    for bit in (2, 1):
        width = bit * (lanes // 4)
        fresh = list(values)
        for index in range(4):
            if index & bit == 0:
                low, high = values[index], values[index | bit]
                upper = group & bit != 0
                fresh[index] = jnp.where(upper, pltpu.roll(high, width, 1), low)
                fresh[index | bit] = jnp.where(upper, high, pltpu.roll(low, lanes - width, 1))
        values = fresh
    return values


def swap_bit(low, high):
    lanes = low.shape[-1]
    width = lanes // 4
    upper = (lane_index(low.shape) // width) % 2 == 1
    first = jnp.where(upper, pltpu.roll(high, width, 1), low)
    second = jnp.where(upper, high, pltpu.roll(low, lanes - width, 1))
    return first, second


def row_halves(value, groups):
    rows, lanes = value.shape
    parts = value.reshape(groups, 2, rows // groups // 2, lanes)
    return parts[:, 0].reshape(rows // 2, lanes), parts[:, 1].reshape(rows // 2, lanes)


def wait_all(copies):
    for copy in copies:
        copy.wait()


def undo_matrix(gate):
    real, imag = gate[0].T, gate[1].T
    top = jnp.concatenate([real, imag], axis=1)
    low = jnp.concatenate([-imag, real], axis=1)
    return left_parts(jnp.concatenate([top, low], axis=0))


def reordered(pieces, offset):
    bit = 1
    while bit < len(pieces):
        swap = (offset & bit) != 0
        pieces = [jnp.where(swap, pieces[i ^ bit], piece) for i, piece in enumerate(pieces)]
        bit *= 2
    return pieces


def column(rows, block, order):
    stride = rows.shape[0] // order
    parts = [rows[pl.ds(block * 2 + part, order, stride=stride), :] for part in range(2)]
    return jnp.concatenate(parts, axis=0)


def first_kernel(state_ref, costate_ref, gates_ref, *refs):
    *out_refs, gate, rows, field_ref, gate_sem, row_sems, out_sems = refs
    own_ref, *cross_refs = out_refs
    order = gate.shape[1]
    lanes = rows.shape[2]
    blocks = field_ref.shape[0] // 4
    chunks = row_sems.shape[1]
    chunk = rows.shape[1] // chunks
    place = lax.axis_index("amp")
    copies = [pltpu.make_async_copy(gates_ref.at[0], gate, gate_sem)]
    for index in range(chunks):
        part = pl.ds(index * chunk, chunk)
        for vector, ref in enumerate((state_ref, costate_ref)):
            copies.append(
                pltpu.make_async_copy(ref.at[part], rows.at[vector, part], row_sems.at[vector, index])
            )
    for copy in copies:
        copy.start()
    copies[0].wait()
    matrix = undo_matrix(gate)
    wait_all(copies[1:])

    out_copies = []
    for apart in list(range(blocks // 2, blocks)) + list(range(blocks // 2)):
        block = (place // 4) ^ apart
        field = jnp.concatenate([column(rows.at[v], block, order) for v in range(2)], axis=1)
        undone = dot_parts(matrix, field)
        pieces = []
        for vector in range(2):
            pieces += row_halves(undone[:, vector * lanes : (vector + 1) * lanes], 2)
        pieces = swap_groups(pieces)
        crosses = apart >= blocks // 2
        if crosses:
            pieces = reordered(pieces, place % 4)
        for index, piece in enumerate(pieces):
            field_ref[apart * 4 + index] = piece
        if crosses:
            for index in range(4):
                number = (apart - blocks // 2) * 4 + index
                out_copies.append(
                    pltpu.make_async_copy(
                        field_ref.at[apart * 4 + index], cross_refs[number], out_sems.at[number]
                    )
                )
                out_copies[-1].start()
        else:
            target = own_ref.at[pl.ds(lax.rem(block, blocks // 2) * 4, 4)]
            out_copies.append(
                pltpu.make_async_copy(
                    field_ref.at[pl.ds(apart * 4, 4)], target, out_sems.at[2 * blocks + apart]
                )
            )
            out_copies[-1].start()
    wait_all(out_copies)


def outer_product(lam, psi):
    order = lam.shape[0] // 2
    left = jnp.concatenate([lam[:order], lam[order:]], axis=1)
    plain = jnp.concatenate([psi[:order], psi[order:]], axis=1)
    other = jnp.concatenate([-psi[order:], psi[:order]], axis=1)
    return dot_parts_rows(left_parts(left), jnp.concatenate([plain, other], axis=0))


def four_products(fields, groups):
    pieces = swap_groups(fields)
    rows, lanes = pieces[0].shape

    def joined(vector):
        parts = [
            piece.reshape(groups, 1, rows // groups, lanes)
            for piece in pieces[2 * vector : 2 * vector + 2]
        ]
        return jnp.concatenate(parts, axis=1).reshape(2 * rows, lanes)

    return outer_product(joined(1), joined(0))


def early_kernel(state_ref, costate_ref, gates_ref, out_ref, matrix_ref):
    order = gates_ref.shape[2]
    for index in range(2):
        matrix_ref[index] = undo_matrix(gates_ref[index + 1])
    out_ref[...] = jnp.zeros_like(out_ref)

    @pl.loop(0, state_ref.shape[0] // order // 2)
    def _(block):
        out_ref[...] += outer_product(
            column(costate_ref, block, order), column(state_ref, block, order)
        )


def middle_kernel(matrix_ref, own_ref, *refs):
    *cross_refs, out_ref, moved_ref, kept, sems = refs
    _, steps, _, order, lanes = moved_ref.shape
    batches = 2 * steps
    place = lax.axis_index("amp")
    top, inner = place // batches, lax.rem(place, batches)
    copies = [pltpu.make_async_copy(own_ref, moved_ref.at[top], sems.at[batches])]
    for index, ref in enumerate(cross_refs):
        source = inner ^ index
        target = moved_ref.at[1 - top, source // 2, lax.rem(source, 2)]
        copies.append(pltpu.make_async_copy(ref, target, sems.at[index]))
    for copy in copies:
        copy.start()
    wait_all(copies)

    def undo(which, fields):
        result = dot_parts(matrix_ref[which], jnp.concatenate(fields, axis=1))
        return [result[:, index * lanes : (index + 1) * lanes] for index in range(len(fields))]

    for step in range(steps):
        fields = [mixed_rows(moved_ref, step, bit) for bit in range(2)]
        for bit, result in enumerate(undo(0, fields)):
            for top, piece in enumerate(swap_bit(*row_halves(result, 8))):
                place = (top * steps + step) * 2 + bit
                kept[pl.ds(place * order, order), :] = piece

    for step in range(steps):
        fields = [regrouped(kept, step * 2 + index, order) for index in range(2)]
        for index, result in enumerate(undo(1, fields)):
            for bit, piece in enumerate(swap_bit(*row_halves(result, 2))):
                out_ref[bit * batches + step * 2 + index] = piece


def regrouped(kept_ref, batch, order):
    devices = kept_ref.shape[0] // order
    parts = [
        kept_ref[pl.ds(row * (devices // 2) + batch, devices, stride=order), :] for row in range(8)
    ]
    return jnp.concatenate(parts, axis=0)


def mixed_rows(moved_ref, step, bit):
    low_rows = moved_ref.shape[3] // 4
    parts = [
        moved_ref[top, step, low, pl.ds((part * 2 + bit) * low_rows, low_rows), :]
        for part in range(2)
        for top in range(2)
        for low in range(2)
    ]
    return jnp.concatenate(parts, axis=0)


def late_kernel(moved_ref, last_ref, early_ref, gates_ref, out_ref, sum_ref, *, scale):
    order = early_ref.shape[0]
    steps = moved_ref.shape[1]
    sum_ref[0] = early_ref[...]
    sum_ref[1:3] = jnp.zeros((2,) + early_ref.shape, jnp.float32)

    @pl.loop(0, steps)
    def _(step):
        first, second = (mixed_rows(moved_ref, step, bit) for bit in range(2))
        half = first.shape[-1] // 2
        lower = lane_index(first.shape) < half
        psi = jnp.where(lower, first, pltpu.roll(second, half, 1))
        lam = jnp.where(lower, pltpu.roll(first, half, 1), second)
        sum_ref[1] += outer_product(lam, psi)
        sum_ref[2] += four_products([last_ref[step * 4 + index] for index in range(4)], 2)

    for index in range(3):
        total = (sum_ref[index, :, :order], sum_ref[index, :, order:])
        gate = (gates_ref[index, 0], gates_ref[index, 1])
        left, right = (gate, total) if index == 2 else (total, gate)
        out_ref[index, 0], out_ref[index, 1] = complex_product(left, right, scale)


def complex_product(left, right, scale):
    def times(first, second):
        return jnp.dot(
            first, second, precision=lax.Precision.HIGHEST, preferred_element_type=jnp.float32
        )

    real = times(left[0], right[0]) - times(left[1], right[1])
    imag = times(left[0], right[1]) + times(left[1], right[0])
    return real * scale, imag * scale


def last_kernel(moved_ref, state_ref, costate_ref, rows, copy_sems):
    half = moved_ref.shape[1] // 2
    copies = []
    for block in range(rows.shape[1] // 2):
        pieces = swap_groups([moved_ref[block * 4 + index] for index in range(4)])
        for vector, ref in enumerate((state_ref, costate_ref)):
            for part in range(2):
                column = block * 2 + part
                for bit in range(2):
                    piece = pieces[2 * vector + bit][part * half : (part + 1) * half]
                    rows[vector, column, bit * half : (bit + 1) * half] = piece
                copy = pltpu.make_async_copy(
                    rows.at[vector, column], ref.at[:, column, 0], copy_sems.at[vector, column]
                )
                copy.start()
                copies.append(copy)
    wait_all(copies)


def gather_kernel(*refs):
    *part_refs, out_ref, copy_sems = refs
    place = lax.rem(lax.axis_index("amp"), len(part_refs))
    copies = [
        pltpu.make_async_copy(ref, out_ref.at[place ^ index], copy_sems.at[index])
        for index, ref in enumerate(part_refs)
    ]
    for copy in copies:
        copy.start()
    wait_all(copies)


def tree_sum(parts):
    while len(parts) > 1:
        parts = [parts[i] + parts[i + 1] for i in range(0, len(parts), 2)]
    return parts[0]


def exchange(part, distance):
    devices = lax.axis_size("amp")
    return lax.ppermute(part, "amp", [(i, i ^ distance) for i in range(devices)])


def scattered_sum(value):
    devices = lax.axis_size("amp")
    inner = min(8, devices)
    own = lax.axis_index("amp") % inner
    blocks = value.reshape(inner, -1, value.shape[-1])

    def pick(index):
        return lax.dynamic_index_in_dim(blocks, index, 0, keepdims=False)

    part = tree_sum([pick(own)] + [exchange(pick(own ^ k), k) for k in range(1, inner)])
    distance = inner
    while distance < devices:
        part = part + exchange(part, distance)
        distance *= 2
    return part


def gathered(part, shape):
    inner = min(8, lax.axis_size("amp"))
    own = [part] + [exchange(part, k) for k in range(2, inner, 2)]
    others = [exchange(found, 1) for found in own]
    parts = [found for pair in zip(own, others) for found in pair]
    out = pl.pallas_call(
        gather_kernel,
        in_specs=[pl.BlockSpec(memory_space=pl.ANY)] * inner,
        out_specs=IN_HBM,
        out_shape=jax.ShapeDtypeStruct((inner,) + part.shape, part.dtype),
        scratch_shapes=[pltpu.SemaphoreType.DMA((inner,))],
        compiler_params=PARAMS,
    )(*parts)
    return out.reshape(shape)


def to_rows(field, lanes):
    return field.reshape(2, -1, lanes).swapaxes(0, 1).reshape(-1, lanes)


def from_rows(rows):
    return rows.reshape(-1, 2, rows.shape[-1]).swapaxes(0, 1).reshape(2, -1)


IN_HBM = pl.BlockSpec(memory_space=pltpu.HBM)
IN_VMEM = pl.BlockSpec(memory_space=pltpu.VMEM)
PARAMS = pltpu.CompilerParams(vmem_limit_bytes=VMEM_BYTES)
HBM_PARAMS = pltpu.CompilerParams(vmem_limit_bytes=60 * 1024 * 1024)


def cost(layers, amplitudes, order):
    flops = layers * 3 * 8 * amplitudes * order
    return pl.CostEstimate(flops=flops, bytes_accessed=32 * amplitudes, transcendentals=0)


def on_device_lanes(state, costate, gates, devices, order, columns):
    lanes = 4 * columns // devices
    steps = devices // 4
    rows = 2 * columns // lanes
    scale = 1.0 / math.sqrt(devices * columns)
    field_shape = (devices, order, lanes)
    sum_shape = (order, 2 * order)
    amplitudes = 2 * order * columns

    def array(shape, kind=jnp.float32):
        return jax.ShapeDtypeStruct(shape, kind)

    half = devices // 2
    groups = [list(range(half)), list(range(half, devices))]
    block = array((order, lanes))
    state, costate = to_rows(state, lanes), to_rows(costate, lanes)
    own, *cross = pl.pallas_call(
        first_kernel,
        in_specs=[IN_HBM, IN_HBM, IN_HBM],
        out_specs=[IN_HBM] * (1 + half),
        out_shape=[array((half, order, lanes))] + [block] * half,
        scratch_shapes=[
            pltpu.VMEM((2, order, order), jnp.float32),
            pltpu.VMEM((2, rows * order, lanes), jnp.float32),
            pltpu.VMEM(field_shape, jnp.float32),
            pltpu.SemaphoreType.DMA,
            pltpu.SemaphoreType.DMA((2, 4)),
            pltpu.SemaphoreType.DMA((devices,)),
        ],
        compiler_params=HBM_PARAMS,
        cost_estimate=cost(1, amplitudes, order),
    )(state, costate, gates)
    cross = [exchange(part, half + index) for index, part in enumerate(cross)]
    own = lax.all_to_all(own, "amp", 0, 0, axis_index_groups=groups, tiled=True)
    early, matrices = pl.pallas_call(
        early_kernel,
        in_specs=[IN_VMEM, IN_VMEM, IN_VMEM],
        out_specs=[IN_VMEM, IN_VMEM],
        out_shape=[array(sum_shape), array((2, 2 * order, 6 * order), jnp.bfloat16)],
        compiler_params=PARAMS,
        cost_estimate=cost(1, amplitudes, order),
    )(state, costate, gates)
    last, moved = pl.pallas_call(
        middle_kernel,
        in_specs=[IN_VMEM] + [pl.BlockSpec(memory_space=pl.ANY)] * (1 + half),
        out_specs=[IN_VMEM, IN_VMEM],
        out_shape=[array(field_shape), array((2, steps, 2, order, lanes))],
        scratch_shapes=[
            pltpu.VMEM((devices * order, lanes), jnp.float32),
            pltpu.SemaphoreType.DMA((half + 1,)),
        ],
        compiler_params=PARAMS,
        cost_estimate=cost(2, amplitudes, order),
    )(matrices, own.reshape(steps, 2, order, lanes), *cross)
    arrived = lax.all_to_all(last, "amp", 0, 0, tiled=True)
    gradients = pl.pallas_call(
        functools.partial(late_kernel, scale=scale),
        in_specs=[IN_VMEM, IN_VMEM, IN_VMEM, IN_VMEM],
        out_specs=IN_VMEM,
        out_shape=array(gates.shape),
        scratch_shapes=[pltpu.VMEM((3,) + sum_shape, jnp.float32)],
        compiler_params=PARAMS,
        cost_estimate=cost(2, amplitudes, order),
    )(moved, last, early, gates)
    part, arrived = lax.optimization_barrier((scattered_sum(gradients), arrived))
    gradients = gathered(part, gates.shape)
    state_rows, costate_rows = pl.pallas_call(
        last_kernel,
        in_specs=[IN_VMEM],
        out_specs=[IN_HBM, IN_HBM],
        out_shape=[array((order, rows, 1, lanes))] * 2,
        scratch_shapes=[
            pltpu.VMEM((2, rows, order, lanes), jnp.float32),
            pltpu.SemaphoreType.DMA((2, rows)),
        ],
        compiler_params=PARAMS,
        cost_estimate=cost(1, amplitudes, order),
    )(arrived)
    return from_rows(state_rows), from_rows(costate_rows), gradients


def undo_gate(field, gate):
    high = lax.Precision.HIGHEST
    shape = field.shape
    parts = field.reshape(shape[:-1] + (2, 2, -1))
    real, imag = parts[..., 0, :], parts[..., 1, :]

    def contract(matrix, operand):
        return jnp.einsum("ts,btvc->bsvc", matrix, operand, precision=high)

    new_real = contract(gate[0], real) + contract(gate[1], imag)
    new_imag = contract(gate[0], imag) - contract(gate[1], real)
    return jnp.stack([new_real, new_imag], axis=-2).reshape(shape)


def gate_gradient(before, after):
    high = lax.Precision.HIGHEST
    lam = before.reshape(before.shape[:-1] + (2, 2, -1))[..., 1, :, :]
    psi = after.reshape(after.shape[:-1] + (2, 2, -1))[..., 0, :, :]
    real = jnp.einsum("btpc,bspc->ts", lam, psi, precision=high)
    imag = jnp.einsum("btc,bsc->ts", lam[..., 1, :], psi[..., 0, :], precision=high) - jnp.einsum(
        "btc,bsc->ts", lam[..., 0, :], psi[..., 1, :], precision=high
    )
    return jnp.stack([real, imag], axis=0)


def on_device_plain(state, costate, gates, devices, order, columns):
    own = columns // devices
    both = jnp.stack([state, costate], axis=0).reshape(2, 2, order, devices, own)
    field = both.transpose(3, 2, 0, 1, 4).reshape(devices, order, 4 * own)
    field = lax.all_to_all(field, "amp", 0, 0, tiled=True)
    after = undo_gate(field, gates[0])
    terms = [gate_gradient(field, after)]
    field = after.reshape(2, devices // 4, 2, 2, 2, order // 4, 4 * own)
    field = field.transpose(3, 1, 4, 0, 2, 5, 6).reshape(devices, order, 4 * own)
    after = undo_gate(field, gates[1])
    terms.append(gate_gradient(field, after))
    field = after.reshape(devices, order // devices, devices, 4 * own)
    field = field.transpose(2, 1, 0, 3).reshape(devices, order, 4 * own)
    after = undo_gate(field, gates[2])
    terms.append(gate_gradient(field, after))
    terms = jnp.stack(terms, axis=0) / math.sqrt(devices * columns)
    gradients = gathered(scattered_sum(terms), gates.shape)
    field = lax.all_to_all(after, "amp", 0, 0, tiled=True)
    field = field.reshape(devices, order, 2, 2, own).transpose(2, 3, 1, 0, 4)
    field = field.reshape(2, 2, order * columns)
    return field[0], field[1], gradients


def on_device(state, costate, gates):
    devices = lax.axis_size("amp")
    order = gates.shape[2]
    columns = state.shape[1] // order
    filled = 4 * columns == 128 * devices and order == 4 * devices
    form = on_device_lanes if filled else on_device_plain
    return form(state, costate, gates, devices, order, columns)


def solution(mesh):
    return jax.shard_map(
        on_device,
        mesh=mesh,
        in_specs=(P(None, "amp"), P(None, "amp"), P()),
        out_specs=(P(None, "amp"), P(None, "amp"), P()),
        check_vma=False,
    )
```

```python
import functools
import math

import jax
import jax.numpy as jnp
from jax import lax
from jax.experimental import pallas as pl
from jax.experimental.pallas import tpu as pltpu
from jax.sharding import PartitionSpec as P

VMEM_BYTES = 24 * 1024 * 1024


def split(value):
    high = value.astype(jnp.bfloat16)
    low = (value - high.astype(jnp.float32)).astype(jnp.bfloat16)
    return high, low


def left_parts(value):
    high, low = split(value)
    return jnp.concatenate([high, low, high], axis=1)


def dot_parts(left, right):
    high, low = split(right)
    return jnp.dot(
        left, jnp.concatenate([high, high, low], axis=0), preferred_element_type=jnp.float32
    )


def dot_parts_rows(left, right):
    high, low = split(right)
    return lax.dot_general(
        left,
        jnp.concatenate([high, high, low], axis=1),
        (((1,), (1,)), ((), ())),
        preferred_element_type=jnp.float32,
    )


def lane_index(shape):
    return lax.broadcasted_iota(jnp.int32, shape, len(shape) - 1)


def swap_groups(values):
    lanes = values[0].shape[-1]
    group = lane_index(values[0].shape) // (lanes // 4)
    for bit in (2, 1):
        width = bit * (lanes // 4)
        fresh = list(values)
        for index in range(4):
            if index & bit == 0:
                low, high = values[index], values[index | bit]
                upper = group & bit != 0
                fresh[index] = jnp.where(upper, pltpu.roll(high, width, 1), low)
                fresh[index | bit] = jnp.where(upper, high, pltpu.roll(low, lanes - width, 1))
        values = fresh
    return values


def swap_bit(low, high):
    lanes = low.shape[-1]
    width = lanes // 4
    upper = (lane_index(low.shape) // width) % 2 == 1
    first = jnp.where(upper, pltpu.roll(high, width, 1), low)
    second = jnp.where(upper, high, pltpu.roll(low, lanes - width, 1))
    return first, second


def row_halves(value, groups):
    rows, lanes = value.shape
    parts = value.reshape(groups, 2, rows // groups // 2, lanes)
    return parts[:, 0].reshape(rows // 2, lanes), parts[:, 1].reshape(rows // 2, lanes)


def wait_all(copies):
    for copy in copies:
        copy.wait()


def undo_matrix(gate):
    real, imag = gate[0].T, gate[1].T
    top = jnp.concatenate([real, imag], axis=1)
    low = jnp.concatenate([-imag, real], axis=1)
    return left_parts(jnp.concatenate([top, low], axis=0))


def column(rows, block, order):
    stride = rows.shape[0] // order
    parts = [rows[pl.ds(block * 2 + part, order, stride=stride), :] for part in range(2)]
    return jnp.concatenate(parts, axis=0)


def first_kernel(
    state_ref, costate_ref, gates_ref, out_ref, gate, rows, field_ref, gate_sem, row_sems, out_sems
):
    order = gate.shape[1]
    lanes = rows.shape[2]
    blocks = field_ref.shape[0] // 4
    chunks = row_sems.shape[1]
    chunk = rows.shape[1] // chunks
    gate_copy = pltpu.make_async_copy(gates_ref.at[0], gate, gate_sem)
    row_copies = []
    for vector, ref in enumerate((state_ref, costate_ref)):
        for index in range(chunks):
            part = pl.ds(index * chunk, chunk)
            row_copies.append(
                pltpu.make_async_copy(ref.at[part], rows.at[vector, part], row_sems.at[vector, index])
            )
    gate_copy.start()
    for copy in row_copies:
        copy.start()
    gate_copy.wait()
    matrix = undo_matrix(gate)

    def undone(vector, block):
        pair = [column(rows.at[vector], block + index, order) for index in range(2)]
        result = dot_parts(matrix, jnp.concatenate(pair, axis=1))
        return [row_halves(result[:, i * lanes : (i + 1) * lanes], 2) for i in range(2)]

    wait_all(row_copies[:chunks])
    for block in range(0, blocks, 2):
        for index, halves in enumerate(undone(0, block)):
            for bit in range(2):
                field_ref[(block + index) * 4 + bit] = halves[bit]
    wait_all(row_copies[chunks:])
    out_copies = []
    for block in range(0, blocks, 2):
        for index, halves in enumerate(undone(1, block)):
            place = (block + index) * 4
            pieces = [field_ref[place], field_ref[place + 1], *halves]
            for number, piece in enumerate(swap_groups(pieces)):
                field_ref[place + number] = piece
        part = pl.ds(block * 4, 8)
        out_copies.append(
            pltpu.make_async_copy(field_ref.at[part], out_ref.at[part], out_sems.at[block // 2])
        )
        out_copies[-1].start()
    wait_all(out_copies)


def outer_product(lam, psi):
    order = lam.shape[0] // 2
    left = jnp.concatenate([lam[:order], lam[order:]], axis=1)
    plain = jnp.concatenate([psi[:order], psi[order:]], axis=1)
    other = jnp.concatenate([-psi[order:], psi[:order]], axis=1)
    return dot_parts_rows(left_parts(left), jnp.concatenate([plain, other], axis=0))


def four_products(fields, groups):
    pieces = swap_groups(fields)
    rows, lanes = pieces[0].shape

    def joined(vector):
        parts = [
            piece.reshape(groups, 1, rows // groups, lanes)
            for piece in pieces[2 * vector : 2 * vector + 2]
        ]
        return jnp.concatenate(parts, axis=1).reshape(2 * rows, lanes)

    return outer_product(joined(1), joined(0))


def early_kernel(state_ref, costate_ref, gates_ref, out_ref, matrix_ref):
    order = gates_ref.shape[2]
    for index in range(2):
        matrix_ref[index] = undo_matrix(gates_ref[index + 1])
    out_ref[...] = jnp.zeros_like(out_ref)

    @pl.loop(0, state_ref.shape[0] // order // 2)
    def _(block):
        out_ref[...] += outer_product(
            column(costate_ref, block, order), column(state_ref, block, order)
        )


def middle_kernel(moved_ref, matrix_ref, spent_ref, out_ref, kept, last, sems):
    del spent_ref
    _, steps, _, order, lanes = moved_ref.shape
    batches = 2 * steps
    copies = []

    def undo(which, fields):
        result = dot_parts(matrix_ref[which], jnp.concatenate(fields, axis=1))
        return [result[:, index * lanes : (index + 1) * lanes] for index in range(len(fields))]

    for step in range(steps):
        fields = [mixed_rows(moved_ref, step, bit) for bit in range(2)]
        for bit, result in enumerate(undo(0, fields)):
            for top, piece in enumerate(swap_bit(*row_halves(result, 8))):
                place = (top * steps + step) * 2 + bit
                kept[pl.ds(place * order, order), :] = piece

    for step in range(steps):
        fields = [regrouped(kept, step * 2 + index, order) for index in range(2)]
        for index, result in enumerate(undo(1, fields)):
            for bit, piece in enumerate(swap_bit(*row_halves(result, 2))):
                last[bit * batches + step * 2 + index] = piece
        for bit in range(2):
            part = pl.ds(bit * batches + step * 2, 2)
            copy = pltpu.make_async_copy(last.at[part], out_ref.at[part], sems.at[bit, step])
            copy.start()
            copies.append(copy)
    wait_all(copies)


def regrouped(kept_ref, batch, order):
    devices = kept_ref.shape[0] // order
    parts = [
        kept_ref[pl.ds(row * (devices // 2) + batch, devices, stride=order), :] for row in range(8)
    ]
    return jnp.concatenate(parts, axis=0)


def mixed_rows(moved_ref, step, bit):
    low_rows = moved_ref.shape[3] // 4
    parts = [
        moved_ref[top, step, low, pl.ds((part * 2 + bit) * low_rows, low_rows), :]
        for part in range(2)
        for top in range(2)
        for low in range(2)
    ]
    return jnp.concatenate(parts, axis=0)


def late_kernel(moved_ref, last_ref, early_ref, gates_ref, out_ref, sum_ref, *, scale):
    order = early_ref.shape[0]
    steps = moved_ref.shape[1]
    sum_ref[0] = early_ref[...]
    sum_ref[1:3] = jnp.zeros((2,) + early_ref.shape, jnp.float32)

    @pl.loop(0, steps)
    def _(step):
        first, second = (mixed_rows(moved_ref, step, bit) for bit in range(2))
        half = first.shape[-1] // 2
        lower = lane_index(first.shape) < half
        psi = jnp.where(lower, first, pltpu.roll(second, half, 1))
        lam = jnp.where(lower, pltpu.roll(first, half, 1), second)
        sum_ref[1] += outer_product(lam, psi)
        sum_ref[2] += four_products([last_ref[step * 4 + index] for index in range(4)], 2)

    for index in range(3):
        total = (sum_ref[index, :, :order], sum_ref[index, :, order:])
        gate = (gates_ref[index, 0], gates_ref[index, 1])
        left, right = (gate, total) if index == 2 else (total, gate)
        out_ref[index, 0], out_ref[index, 1] = complex_product(left, right, scale)


def complex_product(left, right, scale):
    def times(first, second):
        return jnp.dot(
            first, second, precision=lax.Precision.HIGHEST, preferred_element_type=jnp.float32
        )

    real = times(left[0], right[0]) - times(left[1], right[1])
    imag = times(left[0], right[1]) + times(left[1], right[0])
    return real * scale, imag * scale


def last_kernel(moved_ref, state_ref, costate_ref, rows, copy_sems):
    half = moved_ref.shape[1] // 2
    copies = []
    for block in range(rows.shape[1] // 2):
        pieces = swap_groups([moved_ref[block * 4 + index] for index in range(4)])
        for vector, ref in enumerate((state_ref, costate_ref)):
            for part in range(2):
                column = block * 2 + part
                for bit in range(2):
                    piece = pieces[2 * vector + bit][part * half : (part + 1) * half]
                    rows[vector, column, bit * half : (bit + 1) * half] = piece
                copy = pltpu.make_async_copy(
                    rows.at[vector, column], ref.at[:, column, 0], copy_sems.at[vector, column]
                )
                copy.start()
                copies.append(copy)
    wait_all(copies)


def gather_kernel(*refs):
    *part_refs, out_ref, copy_sems = refs
    place = lax.rem(lax.axis_index("amp"), len(part_refs))
    copies = [
        pltpu.make_async_copy(ref, out_ref.at[place ^ index], copy_sems.at[index])
        for index, ref in enumerate(part_refs)
    ]
    for copy in copies:
        copy.start()
    wait_all(copies)


def tree_sum(parts):
    while len(parts) > 1:
        parts = [parts[i] + parts[i + 1] for i in range(0, len(parts), 2)]
    return parts[0]


def exchange(part, distance):
    devices = lax.axis_size("amp")
    return lax.ppermute(part, "amp", [(i, i ^ distance) for i in range(devices)])


def scattered_sum(value):
    devices = lax.axis_size("amp")
    inner = min(8, devices)
    own = lax.axis_index("amp") % inner
    blocks = value.reshape(inner, -1, value.shape[-1])

    def pick(index):
        return lax.dynamic_index_in_dim(blocks, index, 0, keepdims=False)

    part = tree_sum([pick(own)] + [exchange(pick(own ^ k), k) for k in range(1, inner)])
    distance = inner
    while distance < devices:
        part = part + exchange(part, distance)
        distance *= 2
    return part


def gathered_chips(part):
    inner = min(8, lax.axis_size("amp"))
    return [part] + [exchange(part, k) for k in range(2, inner, 2)]


def gathered_cores(own, shape):
    others = [exchange(found, 1) for found in own]
    parts = [found for pair in zip(own, others) for found in pair]
    out = pl.pallas_call(
        gather_kernel,
        in_specs=[pl.BlockSpec(memory_space=pl.ANY)] * len(parts),
        out_specs=IN_HBM,
        out_shape=jax.ShapeDtypeStruct((len(parts),) + parts[0].shape, parts[0].dtype),
        scratch_shapes=[pltpu.SemaphoreType.DMA((len(parts),))],
        compiler_params=PARAMS,
    )(*parts)
    return out.reshape(shape)


def to_rows(field, lanes):
    return field.reshape(2, -1, lanes).swapaxes(0, 1).reshape(-1, lanes)


def from_rows(rows):
    return rows.reshape(-1, 2, rows.shape[-1]).swapaxes(0, 1).reshape(2, -1)


IN_HBM = pl.BlockSpec(memory_space=pltpu.HBM)
IN_VMEM = pl.BlockSpec(memory_space=pltpu.VMEM)
PARAMS = pltpu.CompilerParams(vmem_limit_bytes=VMEM_BYTES)
HBM_PARAMS = pltpu.CompilerParams(vmem_limit_bytes=60 * 1024 * 1024)


def cost(layers, amplitudes, order):
    flops = layers * 3 * 8 * amplitudes * order
    return pl.CostEstimate(flops=flops, bytes_accessed=32 * amplitudes, transcendentals=0)


def on_device_lanes(state, costate, gates, devices, order, columns):
    lanes = 4 * columns // devices
    steps = devices // 4
    rows = 2 * columns // lanes
    scale = 1.0 / math.sqrt(devices * columns)
    field_shape = (devices, order, lanes)
    sum_shape = (order, 2 * order)
    amplitudes = 2 * order * columns

    def array(shape, kind=jnp.float32):
        return jax.ShapeDtypeStruct(shape, kind)

    state, costate = to_rows(state, lanes), to_rows(costate, lanes)
    sent = pl.pallas_call(
        first_kernel,
        in_specs=[IN_HBM, IN_HBM, IN_HBM],
        out_specs=IN_HBM,
        out_shape=array(field_shape),
        scratch_shapes=[
            pltpu.VMEM((2, order, order), jnp.float32),
            pltpu.VMEM((2, rows * order, lanes), jnp.float32),
            pltpu.VMEM(field_shape, jnp.float32),
            pltpu.SemaphoreType.DMA,
            pltpu.SemaphoreType.DMA((2, 4)),
            pltpu.SemaphoreType.DMA((steps // 2,)),
        ],
        compiler_params=HBM_PARAMS,
        cost_estimate=cost(1, amplitudes, order),
    )(state, costate, gates)
    state, costate, sent = lax.optimization_barrier((state, costate, sent))
    moved = lax.all_to_all(sent, "amp", 0, 0, tiled=True)
    early, matrices = pl.pallas_call(
        early_kernel,
        in_specs=[IN_VMEM, IN_VMEM, IN_VMEM],
        out_specs=[IN_VMEM, IN_VMEM],
        out_shape=[array(sum_shape), array((2, 2 * order, 6 * order), jnp.bfloat16)],
        compiler_params=PARAMS,
        cost_estimate=cost(1, amplitudes, order),
    )(state, costate, gates)
    moved = moved.reshape(2, steps, 2, order, lanes)
    last = pl.pallas_call(
        middle_kernel,
        in_specs=[IN_VMEM, IN_VMEM, IN_HBM],
        out_specs=IN_HBM,
        out_shape=array(field_shape),
        input_output_aliases={2: 0},
        scratch_shapes=[
            pltpu.VMEM((devices * order, lanes), jnp.float32),
            pltpu.VMEM(field_shape, jnp.float32),
            pltpu.SemaphoreType.DMA((2, steps)),
        ],
        compiler_params=PARAMS,
        cost_estimate=cost(2, amplitudes, order),
    )(moved, matrices, sent)
    arrived = lax.all_to_all(last, "amp", 0, 0, tiled=True)
    gradients = pl.pallas_call(
        functools.partial(late_kernel, scale=scale),
        in_specs=[IN_VMEM, IN_VMEM, IN_VMEM, IN_VMEM],
        out_specs=IN_VMEM,
        out_shape=array(gates.shape),
        scratch_shapes=[pltpu.VMEM((3,) + sum_shape, jnp.float32)],
        compiler_params=PARAMS,
        cost_estimate=cost(2, amplitudes, order),
    )(moved, last, early, gates)
    part, arrived = lax.optimization_barrier((scattered_sum(gradients), arrived))
    parts = gathered_chips(part)
    state_rows, costate_rows = pl.pallas_call(
        last_kernel,
        in_specs=[IN_VMEM],
        out_specs=[IN_HBM, IN_HBM],
        out_shape=[array((order, rows, 1, lanes))] * 2,
        scratch_shapes=[
            pltpu.VMEM((2, rows, order, lanes), jnp.float32),
            pltpu.SemaphoreType.DMA((2, rows)),
        ],
        compiler_params=PARAMS,
        cost_estimate=cost(1, amplitudes, order),
    )(arrived)
    parts, state_rows, costate_rows = lax.optimization_barrier((parts, state_rows, costate_rows))
    gradients = gathered_cores(parts, gates.shape)
    return from_rows(state_rows), from_rows(costate_rows), gradients


def undo_gate(field, gate):
    high = lax.Precision.HIGHEST
    shape = field.shape
    parts = field.reshape(shape[:-1] + (2, 2, -1))
    real, imag = parts[..., 0, :], parts[..., 1, :]

    def contract(matrix, operand):
        return jnp.einsum("ts,btvc->bsvc", matrix, operand, precision=high)

    new_real = contract(gate[0], real) + contract(gate[1], imag)
    new_imag = contract(gate[0], imag) - contract(gate[1], real)
    return jnp.stack([new_real, new_imag], axis=-2).reshape(shape)


def gate_gradient(before, after):
    high = lax.Precision.HIGHEST
    lam = before.reshape(before.shape[:-1] + (2, 2, -1))[..., 1, :, :]
    psi = after.reshape(after.shape[:-1] + (2, 2, -1))[..., 0, :, :]
    real = jnp.einsum("btpc,bspc->ts", lam, psi, precision=high)
    imag = jnp.einsum("btc,bsc->ts", lam[..., 1, :], psi[..., 0, :], precision=high) - jnp.einsum(
        "btc,bsc->ts", lam[..., 0, :], psi[..., 1, :], precision=high
    )
    return jnp.stack([real, imag], axis=0)


def on_device_plain(state, costate, gates, devices, order, columns):
    own = columns // devices
    both = jnp.stack([state, costate], axis=0).reshape(2, 2, order, devices, own)
    field = both.transpose(3, 2, 0, 1, 4).reshape(devices, order, 4 * own)
    field = lax.all_to_all(field, "amp", 0, 0, tiled=True)
    after = undo_gate(field, gates[0])
    terms = [gate_gradient(field, after)]
    field = after.reshape(2, devices // 4, 2, 2, 2, order // 4, 4 * own)
    field = field.transpose(3, 1, 4, 0, 2, 5, 6).reshape(devices, order, 4 * own)
    after = undo_gate(field, gates[1])
    terms.append(gate_gradient(field, after))
    field = after.reshape(devices, order // devices, devices, 4 * own)
    field = field.transpose(2, 1, 0, 3).reshape(devices, order, 4 * own)
    after = undo_gate(field, gates[2])
    terms.append(gate_gradient(field, after))
    terms = jnp.stack(terms, axis=0) / math.sqrt(devices * columns)
    gradients = gathered_cores(gathered_chips(scattered_sum(terms)), gates.shape)
    field = lax.all_to_all(after, "amp", 0, 0, tiled=True)
    field = field.reshape(devices, order, 2, 2, own).transpose(2, 3, 1, 0, 4)
    field = field.reshape(2, 2, order * columns)
    return field[0], field[1], gradients


def on_device(state, costate, gates):
    devices = lax.axis_size("amp")
    order = gates.shape[2]
    columns = state.shape[1] // order
    filled = 4 * columns == 128 * devices and order == 4 * devices
    form = on_device_lanes if filled else on_device_plain
    return form(state, costate, gates, devices, order, columns)


def solution(mesh):
    return jax.shard_map(
        on_device,
        mesh=mesh,
        in_specs=(P(None, "amp"), P(None, "amp"), P()),
        out_specs=(P(None, "amp"), P(None, "amp"), P()),
        check_vma=False,
    )
```

```python
import functools
import math

import jax
import jax.numpy as jnp
from jax import lax
from jax.experimental import pallas as pl
from jax.experimental.pallas import tpu as pltpu
from jax.sharding import PartitionSpec as P

VMEM_BYTES = 12 * 1024 * 1024


def split(value):
    high = value.astype(jnp.bfloat16)
    low = (value - high.astype(jnp.float32)).astype(jnp.bfloat16)
    return high, low


def both_parts(value):
    return jnp.concatenate(split(value), axis=0)


def left_parts(both):
    rows = both.shape[0] // 2
    high, low = both[:rows], both[rows:]
    return jnp.concatenate([high, low, high], axis=1)


def dot_parts(left, right):
    high, low = split(right)
    return jnp.dot(
        left_parts(left),
        jnp.concatenate([high, high, low], axis=0),
        preferred_element_type=jnp.float32,
    )


def dot_parts_rows(left, right):
    high, low = split(right)
    return lax.dot_general(
        left_parts(left),
        jnp.concatenate([high, high, low], axis=1),
        (((1,), (1,)), ((), ())),
        preferred_element_type=jnp.float32,
    )


def lane_index(shape):
    return lax.broadcasted_iota(jnp.int32, shape, len(shape) - 1)


def swap_groups(values):
    lanes = values[0].shape[-1]
    group = lane_index(values[0].shape) // (lanes // 4)
    for bit in (2, 1):
        width = bit * (lanes // 4)
        fresh = list(values)
        for index in range(4):
            if index & bit == 0:
                low, high = values[index], values[index | bit]
                upper = group & bit != 0
                fresh[index] = jnp.where(upper, pltpu.roll(high, width, 1), low)
                fresh[index | bit] = jnp.where(upper, high, pltpu.roll(low, lanes - width, 1))
        values = fresh
    return values


def swap_bit(low, high):
    lanes = low.shape[-1]
    width = lanes // 4
    upper = (lane_index(low.shape) // width) % 2 == 1
    first = jnp.where(upper, pltpu.roll(high, width, 1), low)
    second = jnp.where(upper, high, pltpu.roll(low, lanes - width, 1))
    return first, second


def row_halves(value, groups):
    rows, lanes = value.shape
    parts = value.reshape(groups, 2, rows // groups // 2, lanes)
    return parts[:, 0].reshape(rows // 2, lanes), parts[:, 1].reshape(rows // 2, lanes)


def wait_all(copies):
    for copy in copies:
        copy.wait()


def undo_matrix(gate):
    real, imag = gate[0].T, gate[1].T
    top = jnp.concatenate([real, imag], axis=1)
    low = jnp.concatenate([-imag, real], axis=1)
    return both_parts(jnp.concatenate([top, low], axis=0))


def column(rows, block, order):
    stride = rows.shape[0] // order
    parts = [rows[pl.ds(block * 2 + part, order, stride=stride), :] for part in range(2)]
    return jnp.concatenate(parts, axis=0)


def first_kernel(
    state_ref, costate_ref, gates_ref, out_ref, gate, rows, field_ref, gate_sem, row_sems, out_sems
):
    order = gate.shape[1]
    lanes = rows.shape[2]
    stride = rows.shape[1] // order
    chunks = row_sems.shape[1]
    chunk = rows.shape[1] // chunks
    copies = [pltpu.make_async_copy(gates_ref.at[0], gate, gate_sem)]
    for index in range(chunks):
        part = pl.ds(index * chunk, chunk)
        for vector, ref in enumerate((state_ref, costate_ref)):
            copies.append(
                pltpu.make_async_copy(ref.at[part], rows.at[vector, part], row_sems.at[vector, index])
            )
    for copy in copies:
        copy.start()
    copies[0].wait()
    matrix = undo_matrix(gate)
    wait_all(copies[1:])

    def column(vector, block):
        parts = [rows[vector, pl.ds(block * 2 + part, order, stride=stride), :] for part in range(2)]
        return jnp.concatenate(parts, axis=0)

    out_copies = []
    for block in range(stride // 2):
        field = jnp.concatenate([column(0, block), column(1, block)], axis=1)
        undone = dot_parts(matrix, field)
        pieces = []
        for vector in range(2):
            pieces += row_halves(undone[:, vector * lanes : (vector + 1) * lanes], 2)
        for index, piece in enumerate(swap_groups(pieces)):
            field_ref[block * 4 + index] = piece
        part = pl.ds(block * 4, 4)
        copy = pltpu.make_async_copy(field_ref.at[part], out_ref.at[part], out_sems.at[block])
        copy.start()
        out_copies.append(copy)
    wait_all(out_copies)


def outer_product(lam, psi):
    order = lam.shape[0] // 2
    left = jnp.concatenate([lam[:order], lam[order:]], axis=1)
    plain = jnp.concatenate([psi[:order], psi[order:]], axis=1)
    other = jnp.concatenate([-psi[order:], psi[:order]], axis=1)
    return dot_parts_rows(both_parts(left), jnp.concatenate([plain, other], axis=0))


def four_products(fields, groups):
    pieces = swap_groups(fields)
    rows, lanes = pieces[0].shape

    def joined(vector):
        parts = [
            piece.reshape(groups, 1, rows // groups, lanes)
            for piece in pieces[2 * vector : 2 * vector + 2]
        ]
        return jnp.concatenate(parts, axis=1).reshape(2 * rows, lanes)

    return outer_product(joined(1), joined(0))


def early_kernel(state_ref, costate_ref, gates_ref, out_ref, matrix_ref):
    order = gates_ref.shape[2]
    for index in range(2):
        matrix_ref[index] = undo_matrix(gates_ref[index + 1])
    out_ref[...] = jnp.zeros_like(out_ref)

    @pl.loop(0, state_ref.shape[0] // order // 2)
    def _(block):
        out_ref[...] += outer_product(
            column(costate_ref, block, order), column(state_ref, block, order)
        )


def middle_kernel(moved_ref, matrix_ref, spent_ref, out_ref, kept, last, sems):
    del spent_ref
    _, steps, _, order, lanes = moved_ref.shape
    batches = 2 * steps
    copies = []

    def undo(which, fields):
        result = dot_parts(matrix_ref[which], jnp.concatenate(fields, axis=1))
        return [result[:, index * lanes : (index + 1) * lanes] for index in range(len(fields))]

    for step in range(steps):
        fields = [mixed_rows(moved_ref, step, bit) for bit in range(2)]
        for bit, result in enumerate(undo(0, fields)):
            for top, piece in enumerate(swap_bit(*row_halves(result, 8))):
                place = (top * steps + step) * 2 + bit
                kept[pl.ds(place * order, order), :] = piece

    for step in range(steps):
        fields = [regrouped(kept, step * 2 + index, order) for index in range(2)]
        for index, result in enumerate(undo(1, fields)):
            for bit, piece in enumerate(swap_bit(*row_halves(result, 2))):
                last[bit * batches + step * 2 + index] = piece
        for bit in range(2):
            part = pl.ds(bit * batches + step * 2, 2)
            copy = pltpu.make_async_copy(last.at[part], out_ref.at[part], sems.at[bit, step])
            copy.start()
            copies.append(copy)
    wait_all(copies)


def regrouped(kept_ref, batch, order):
    devices = kept_ref.shape[0] // order
    parts = [
        kept_ref[pl.ds(row * (devices // 2) + batch, devices, stride=order), :] for row in range(8)
    ]
    return jnp.concatenate(parts, axis=0)


def mixed_rows(moved_ref, step, bit):
    low_rows = moved_ref.shape[3] // 4
    parts = [
        moved_ref[top, step, low, pl.ds((part * 2 + bit) * low_rows, low_rows), :]
        for part in range(2)
        for top in range(2)
        for low in range(2)
    ]
    return jnp.concatenate(parts, axis=0)


def late_kernel(moved_ref, last_ref, early_ref, gates_ref, out_ref, sum_ref, *, scale):
    order = early_ref.shape[0]
    steps = moved_ref.shape[1]
    sum_ref[0] = early_ref[...]
    sum_ref[1:3] = jnp.zeros((2,) + early_ref.shape, jnp.float32)

    @pl.loop(0, steps)
    def _(step):
        first, second = (mixed_rows(moved_ref, step, bit) for bit in range(2))
        half = first.shape[-1] // 2
        lower = lane_index(first.shape) < half
        psi = jnp.where(lower, first, pltpu.roll(second, half, 1))
        lam = jnp.where(lower, pltpu.roll(first, half, 1), second)
        sum_ref[1] += outer_product(lam, psi)
        sum_ref[2] += four_products([last_ref[step * 4 + index] for index in range(4)], 2)

    for index in range(3):
        total = (sum_ref[index, :, :order], sum_ref[index, :, order:])
        gate = (gates_ref[index, 0], gates_ref[index, 1])
        left, right = (gate, total) if index == 2 else (total, gate)
        out_ref[index, 0], out_ref[index, 1] = complex_product(left, right, scale)


def complex_product(left, right, scale):
    def times(first, second):
        return jnp.dot(
            first, second, precision=lax.Precision.HIGHEST, preferred_element_type=jnp.float32
        )

    real = times(left[0], right[0]) - times(left[1], right[1])
    imag = times(left[0], right[1]) + times(left[1], right[0])
    return real * scale, imag * scale


def last_kernel(moved_ref, state_ref, costate_ref, rows, copy_sems):
    half = moved_ref.shape[1] // 2
    copies = []
    for block in range(rows.shape[1] // 2):
        pieces = swap_groups([moved_ref[block * 4 + index] for index in range(4)])
        for vector, ref in enumerate((state_ref, costate_ref)):
            for part in range(2):
                column = block * 2 + part
                for bit in range(2):
                    piece = pieces[2 * vector + bit][part * half : (part + 1) * half]
                    rows[vector, column, bit * half : (bit + 1) * half] = piece
                copy = pltpu.make_async_copy(
                    rows.at[vector, column], ref.at[:, column, 0], copy_sems.at[vector, column]
                )
                copy.start()
                copies.append(copy)
    wait_all(copies)


def gather_kernel(*refs):
    *part_refs, out_ref, copy_sems = refs
    place = lax.rem(lax.axis_index("amp"), len(part_refs))
    copies = [
        pltpu.make_async_copy(ref, out_ref.at[place ^ index], copy_sems.at[index])
        for index, ref in enumerate(part_refs)
    ]
    for copy in copies:
        copy.start()
    wait_all(copies)


def tree_sum(parts):
    while len(parts) > 1:
        parts = [parts[i] + parts[i + 1] for i in range(0, len(parts), 2)]
    return parts[0]


def exchange(part, distance):
    devices = lax.axis_size("amp")
    return lax.ppermute(part, "amp", [(i, i ^ distance) for i in range(devices)])


def scattered_sum(value):
    devices = lax.axis_size("amp")
    inner = min(8, devices)
    own = lax.axis_index("amp") % inner
    blocks = value.reshape(inner, -1, value.shape[-1])

    def pick(index):
        return lax.dynamic_index_in_dim(blocks, index, 0, keepdims=False)

    part = tree_sum([pick(own)] + [exchange(pick(own ^ k), k) for k in range(1, inner)])
    distance = inner
    while distance < devices:
        part = part + exchange(part, distance)
        distance *= 2
    return part


def gathered_chips(part):
    inner = min(8, lax.axis_size("amp"))
    return [part] + [exchange(part, k) for k in range(2, inner, 2)]


def gathered_cores(own, shape):
    others = [exchange(found, 1) for found in own]
    parts = [found for pair in zip(own, others) for found in pair]
    out = pl.pallas_call(
        gather_kernel,
        in_specs=[pl.BlockSpec(memory_space=pl.ANY)] * len(parts),
        out_specs=IN_HBM,
        out_shape=jax.ShapeDtypeStruct((len(parts),) + parts[0].shape, parts[0].dtype),
        scratch_shapes=[pltpu.SemaphoreType.DMA((len(parts),))],
        compiler_params=PARAMS,
    )(*parts)
    return out.reshape(shape)


def to_rows(field, lanes):
    return field.reshape(2, -1, lanes).swapaxes(0, 1).reshape(-1, lanes)


def from_rows(rows):
    return rows.reshape(-1, 2, rows.shape[-1]).swapaxes(0, 1).reshape(2, -1)


IN_HBM = pl.BlockSpec(memory_space=pltpu.HBM)
IN_VMEM = pl.BlockSpec(memory_space=pltpu.VMEM)
PARAMS = pltpu.CompilerParams(vmem_limit_bytes=VMEM_BYTES)
HBM_PARAMS = pltpu.CompilerParams(vmem_limit_bytes=60 * 1024 * 1024)


def cost(layers, amplitudes, order):
    flops = layers * 3 * 8 * amplitudes * order
    return pl.CostEstimate(flops=flops, bytes_accessed=32 * amplitudes, transcendentals=0)


def on_device_lanes(state, costate, gates, devices, order, columns):
    lanes = 4 * columns // devices
    steps = devices // 4
    rows = 2 * columns // lanes
    scale = 1.0 / math.sqrt(devices * columns)
    field_shape = (devices, order, lanes)
    sum_shape = (order, 2 * order)
    amplitudes = 2 * order * columns

    def array(shape, kind=jnp.float32):
        return jax.ShapeDtypeStruct(shape, kind)

    state, costate = to_rows(state, lanes), to_rows(costate, lanes)
    sent = pl.pallas_call(
        first_kernel,
        in_specs=[IN_HBM, IN_HBM, IN_HBM],
        out_specs=IN_HBM,
        out_shape=array(field_shape),
        scratch_shapes=[
            pltpu.VMEM((2, order, order), jnp.float32),
            pltpu.VMEM((2, rows * order, lanes), jnp.float32),
            pltpu.VMEM(field_shape, jnp.float32),
            pltpu.SemaphoreType.DMA,
            pltpu.SemaphoreType.DMA((2, 4)),
            pltpu.SemaphoreType.DMA((steps,)),
        ],
        compiler_params=HBM_PARAMS,
        cost_estimate=cost(1, amplitudes, order),
    )(state, costate, gates)
    state, costate, sent = lax.optimization_barrier((state, costate, sent))
    moved = lax.all_to_all(sent, "amp", 0, 0, tiled=True)
    early, matrices = pl.pallas_call(
        early_kernel,
        in_specs=[IN_VMEM, IN_VMEM, IN_VMEM],
        out_specs=[IN_VMEM, IN_VMEM],
        out_shape=[array(sum_shape), array((2, 4 * order, 2 * order), jnp.bfloat16)],
        compiler_params=PARAMS,
        cost_estimate=cost(1, amplitudes, order),
    )(state, costate, gates)
    moved = moved.reshape(2, steps, 2, order, lanes)
    last = pl.pallas_call(
        middle_kernel,
        in_specs=[IN_VMEM, IN_VMEM, IN_HBM],
        out_specs=IN_HBM,
        out_shape=array(field_shape),
        input_output_aliases={2: 0},
        scratch_shapes=[
            pltpu.VMEM((devices * order, lanes), jnp.float32),
            pltpu.VMEM(field_shape, jnp.float32),
            pltpu.SemaphoreType.DMA((2, steps)),
        ],
        compiler_params=PARAMS,
        cost_estimate=cost(2, amplitudes, order),
    )(moved, matrices, sent)
    arrived = lax.all_to_all(last, "amp", 0, 0, tiled=True)
    gradients = pl.pallas_call(
        functools.partial(late_kernel, scale=scale),
        in_specs=[IN_VMEM, IN_VMEM, IN_VMEM, IN_VMEM],
        out_specs=IN_VMEM,
        out_shape=array(gates.shape),
        scratch_shapes=[pltpu.VMEM((3,) + sum_shape, jnp.float32)],
        compiler_params=PARAMS,
        cost_estimate=cost(2, amplitudes, order),
    )(moved, last, early, gates)
    part, arrived = lax.optimization_barrier((scattered_sum(gradients), arrived))
    parts = gathered_chips(part)
    state_rows, costate_rows = pl.pallas_call(
        last_kernel,
        in_specs=[IN_VMEM],
        out_specs=[IN_HBM, IN_HBM],
        out_shape=[array((order, rows, 1, lanes))] * 2,
        scratch_shapes=[
            pltpu.VMEM((2, rows, order, lanes), jnp.float32),
            pltpu.SemaphoreType.DMA((2, rows)),
        ],
        compiler_params=PARAMS,
        cost_estimate=cost(1, amplitudes, order),
    )(arrived)
    parts, state_rows, costate_rows = lax.optimization_barrier((parts, state_rows, costate_rows))
    gradients = gathered_cores(parts, gates.shape)
    return from_rows(state_rows), from_rows(costate_rows), gradients


def undo_gate(field, gate):
    high = lax.Precision.HIGHEST
    shape = field.shape
    parts = field.reshape(shape[:-1] + (2, 2, -1))
    real, imag = parts[..., 0, :], parts[..., 1, :]

    def contract(matrix, operand):
        return jnp.einsum("ts,btvc->bsvc", matrix, operand, precision=high)

    new_real = contract(gate[0], real) + contract(gate[1], imag)
    new_imag = contract(gate[0], imag) - contract(gate[1], real)
    return jnp.stack([new_real, new_imag], axis=-2).reshape(shape)


def gate_gradient(before, after):
    high = lax.Precision.HIGHEST
    lam = before.reshape(before.shape[:-1] + (2, 2, -1))[..., 1, :, :]
    psi = after.reshape(after.shape[:-1] + (2, 2, -1))[..., 0, :, :]
    real = jnp.einsum("btpc,bspc->ts", lam, psi, precision=high)
    imag = jnp.einsum("btc,bsc->ts", lam[..., 1, :], psi[..., 0, :], precision=high) - jnp.einsum(
        "btc,bsc->ts", lam[..., 0, :], psi[..., 1, :], precision=high
    )
    return jnp.stack([real, imag], axis=0)


def on_device_plain(state, costate, gates, devices, order, columns):
    own = columns // devices
    both = jnp.stack([state, costate], axis=0).reshape(2, 2, order, devices, own)
    field = both.transpose(3, 2, 0, 1, 4).reshape(devices, order, 4 * own)
    field = lax.all_to_all(field, "amp", 0, 0, tiled=True)
    after = undo_gate(field, gates[0])
    terms = [gate_gradient(field, after)]
    field = after.reshape(2, devices // 4, 2, 2, 2, order // 4, 4 * own)
    field = field.transpose(3, 1, 4, 0, 2, 5, 6).reshape(devices, order, 4 * own)
    after = undo_gate(field, gates[1])
    terms.append(gate_gradient(field, after))
    field = after.reshape(devices, order // devices, devices, 4 * own)
    field = field.transpose(2, 1, 0, 3).reshape(devices, order, 4 * own)
    after = undo_gate(field, gates[2])
    terms.append(gate_gradient(field, after))
    terms = jnp.stack(terms, axis=0) / math.sqrt(devices * columns)
    gradients = gathered_cores(gathered_chips(scattered_sum(terms)), gates.shape)
    field = lax.all_to_all(after, "amp", 0, 0, tiled=True)
    field = field.reshape(devices, order, 2, 2, own).transpose(2, 3, 1, 0, 4)
    field = field.reshape(2, 2, order * columns)
    return field[0], field[1], gradients


def on_device(state, costate, gates):
    devices = lax.axis_size("amp")
    order = gates.shape[2]
    columns = state.shape[1] // order
    filled = 4 * columns == 128 * devices and order == 4 * devices
    form = on_device_lanes if filled else on_device_plain
    return form(state, costate, gates, devices, order, columns)


def solution(mesh):
    return jax.shard_map(
        on_device,
        mesh=mesh,
        in_specs=(P(None, "amp"), P(None, "amp"), P()),
        out_specs=(P(None, "amp"), P(None, "amp"), P()),
        check_vma=False,
    )
```

```python
import functools
import math

import jax
import jax.numpy as jnp
from jax import lax
from jax.experimental import pallas as pl
from jax.experimental.pallas import tpu as pltpu
from jax.sharding import PartitionSpec as P

VMEM_BYTES = 12 * 1024 * 1024


def split(value):
    high = value.astype(jnp.bfloat16)
    low = (value - high.astype(jnp.float32)).astype(jnp.bfloat16)
    return high, low


def both_parts(value):
    return jnp.concatenate(split(value), axis=0)


def left_parts(both):
    rows = both.shape[0] // 2
    high, low = both[:rows], both[rows:]
    return jnp.concatenate([high, low, high], axis=1)


def dot_parts(left, right):
    high, low = split(right)
    return jnp.dot(
        left_parts(left),
        jnp.concatenate([high, high, low], axis=0),
        preferred_element_type=jnp.float32,
    )


def dot_parts_rows(left, right):
    high, low = split(right)
    return lax.dot_general(
        left_parts(left),
        jnp.concatenate([high, high, low], axis=1),
        (((1,), (1,)), ((), ())),
        preferred_element_type=jnp.float32,
    )


def lane_index(shape):
    return lax.broadcasted_iota(jnp.int32, shape, len(shape) - 1)


def swap_groups(values):
    lanes = values[0].shape[-1]
    group = lane_index(values[0].shape) // (lanes // 4)
    for bit in (2, 1):
        width = bit * (lanes // 4)
        fresh = list(values)
        for index in range(4):
            if index & bit == 0:
                low, high = values[index], values[index | bit]
                upper = group & bit != 0
                fresh[index] = jnp.where(upper, pltpu.roll(high, width, 1), low)
                fresh[index | bit] = jnp.where(upper, high, pltpu.roll(low, lanes - width, 1))
        values = fresh
    return values


def swap_bit(low, high):
    lanes = low.shape[-1]
    width = lanes // 4
    upper = (lane_index(low.shape) // width) % 2 == 1
    first = jnp.where(upper, pltpu.roll(high, width, 1), low)
    second = jnp.where(upper, high, pltpu.roll(low, lanes - width, 1))
    return first, second


def row_halves(value, groups):
    rows, lanes = value.shape
    parts = value.reshape(groups, 2, rows // groups // 2, lanes)
    return parts[:, 0].reshape(rows // 2, lanes), parts[:, 1].reshape(rows // 2, lanes)


def wait_all(copies):
    for copy in copies:
        copy.wait()


def undo_matrix(gate):
    real, imag = gate[0].T, gate[1].T
    top = jnp.concatenate([real, imag], axis=1)
    low = jnp.concatenate([-imag, real], axis=1)
    return both_parts(jnp.concatenate([top, low], axis=0))


def column(rows, block, order):
    stride = rows.shape[0] // order
    parts = [rows[pl.ds(block * 2 + part, order, stride=stride), :] for part in range(2)]
    return jnp.concatenate(parts, axis=0)


def first_kernel(
    state_ref, costate_ref, gates_ref, out_ref, gate, rows, field_ref, gate_sem, row_sems, out_sems
):
    order = gate.shape[1]
    lanes = rows.shape[2]
    stride = rows.shape[1] // order
    chunks = row_sems.shape[1]
    chunk = rows.shape[1] // chunks
    copies = [pltpu.make_async_copy(gates_ref.at[0], gate, gate_sem)]
    for index in range(chunks):
        part = pl.ds(index * chunk, chunk)
        for vector, ref in enumerate((state_ref, costate_ref)):
            copies.append(
                pltpu.make_async_copy(ref.at[part], rows.at[vector, part], row_sems.at[vector, index])
            )
    for copy in copies:
        copy.start()
    copies[0].wait()
    matrix = undo_matrix(gate)
    wait_all(copies[1:])

    def column(vector, block):
        parts = [rows[vector, pl.ds(block * 2 + part, order, stride=stride), :] for part in range(2)]
        return jnp.concatenate(parts, axis=0)

    out_copies = []
    for block in range(stride // 2):
        field = jnp.concatenate([column(0, block), column(1, block)], axis=1)
        undone = dot_parts(matrix, field)
        pieces = []
        for vector in range(2):
            pieces += row_halves(undone[:, vector * lanes : (vector + 1) * lanes], 2)
        for index, piece in enumerate(swap_groups(pieces)):
            field_ref[block * 4 + index] = piece
        part = pl.ds(block * 4, 4)
        copy = pltpu.make_async_copy(field_ref.at[part], out_ref.at[part], out_sems.at[block])
        copy.start()
        out_copies.append(copy)
    wait_all(out_copies)


def outer_product(lam, psi):
    order = lam.shape[0] // 2
    left = jnp.concatenate([lam[:order], lam[order:]], axis=1)
    plain = jnp.concatenate([psi[:order], psi[order:]], axis=1)
    other = jnp.concatenate([-psi[order:], psi[:order]], axis=1)
    return dot_parts_rows(both_parts(left), jnp.concatenate([plain, other], axis=0))


def four_products(fields, groups):
    pieces = swap_groups(fields)
    rows, lanes = pieces[0].shape

    def joined(vector):
        parts = [
            piece.reshape(groups, 1, rows // groups, lanes)
            for piece in pieces[2 * vector : 2 * vector + 2]
        ]
        return jnp.concatenate(parts, axis=1).reshape(2 * rows, lanes)

    return outer_product(joined(1), joined(0))


def early_kernel(state_ref, costate_ref, out_ref):
    order = out_ref.shape[0]
    out_ref[...] = jnp.zeros_like(out_ref)

    @pl.loop(0, state_ref.shape[0] // order // 2)
    def _(block):
        out_ref[...] += outer_product(
            column(costate_ref, block, order), column(state_ref, block, order)
        )


def middle_kernel(moved_ref, gates_ref, spent_ref, out_ref, kept, last, sems):
    del spent_ref
    _, steps, _, order, lanes = moved_ref.shape
    batches = 2 * steps
    copies = []

    def undo(matrix, fields):
        result = dot_parts(matrix, jnp.concatenate(fields, axis=1))
        return [result[:, index * lanes : (index + 1) * lanes] for index in range(len(fields))]

    matrices = [undo_matrix(gates_ref[index + 1]) for index in range(2)]
    for step in range(steps):
        fields = [mixed_rows(moved_ref, step, bit) for bit in range(2)]
        for bit, result in enumerate(undo(matrices[0], fields)):
            for top, piece in enumerate(swap_bit(*row_halves(result, 8))):
                place = (top * steps + step) * 2 + bit
                kept[pl.ds(place * order, order), :] = piece

    for step in range(steps):
        fields = [regrouped(kept, step * 2 + index, order) for index in range(2)]
        for index, result in enumerate(undo(matrices[1], fields)):
            for bit, piece in enumerate(swap_bit(*row_halves(result, 2))):
                last[bit * batches + step * 2 + index] = piece
        for bit in range(2):
            part = pl.ds(bit * batches + step * 2, 2)
            copy = pltpu.make_async_copy(last.at[part], out_ref.at[part], sems.at[bit, step])
            copy.start()
            copies.append(copy)
    wait_all(copies)


def regrouped(kept_ref, batch, order):
    devices = kept_ref.shape[0] // order
    parts = [
        kept_ref[pl.ds(row * (devices // 2) + batch, devices, stride=order), :] for row in range(8)
    ]
    return jnp.concatenate(parts, axis=0)


def mixed_rows(moved_ref, step, bit):
    low_rows = moved_ref.shape[3] // 4
    parts = [
        moved_ref[top, step, low, pl.ds((part * 2 + bit) * low_rows, low_rows), :]
        for part in range(2)
        for top in range(2)
        for low in range(2)
    ]
    return jnp.concatenate(parts, axis=0)


def late_kernel(moved_ref, last_ref, early_ref, gates_ref, out_ref, sum_ref, *, scale):
    order = early_ref.shape[0]
    steps = moved_ref.shape[1]
    sum_ref[0] = early_ref[...]
    sum_ref[1:3] = jnp.zeros((2,) + early_ref.shape, jnp.float32)

    @pl.loop(0, steps)
    def _(step):
        first, second = (mixed_rows(moved_ref, step, bit) for bit in range(2))
        half = first.shape[-1] // 2
        lower = lane_index(first.shape) < half
        psi = jnp.where(lower, first, pltpu.roll(second, half, 1))
        lam = jnp.where(lower, pltpu.roll(first, half, 1), second)
        sum_ref[1] += outer_product(lam, psi)
        sum_ref[2] += four_products([last_ref[step * 4 + index] for index in range(4)], 2)

    for index in range(3):
        total = (sum_ref[index, :, :order], sum_ref[index, :, order:])
        gate = (gates_ref[index, 0], gates_ref[index, 1])
        left, right = (gate, total) if index == 2 else (total, gate)
        out_ref[index, 0], out_ref[index, 1] = complex_product(left, right, scale)


def complex_product(left, right, scale):
    def times(first, second):
        return jnp.dot(
            first, second, precision=lax.Precision.HIGHEST, preferred_element_type=jnp.float32
        )

    real = times(left[0], right[0]) - times(left[1], right[1])
    imag = times(left[0], right[1]) + times(left[1], right[0])
    return real * scale, imag * scale


def last_kernel(moved_ref, state_ref, costate_ref, moved, rows, in_sems, copy_sems):
    half = moved.shape[1] // 2
    blocks = rows.shape[1] // 2
    in_copies = []
    for block in range(blocks):
        part = pl.ds(block * 4, 4)
        in_copies.append(
            pltpu.make_async_copy(moved_ref.at[part], moved.at[part], in_sems.at[block])
        )
        in_copies[-1].start()
    copies = []
    for block in range(blocks):
        in_copies[block].wait()
        pieces = swap_groups([moved[block * 4 + index] for index in range(4)])
        for vector, ref in enumerate((state_ref, costate_ref)):
            for part in range(2):
                place = block * 2 + part
                for bit in range(2):
                    piece = pieces[2 * vector + bit][part * half : (part + 1) * half]
                    rows[vector, place, bit * half : (bit + 1) * half] = piece
                copy = pltpu.make_async_copy(
                    rows.at[vector, place], ref.at[:, place, 0], copy_sems.at[vector, place]
                )
                copy.start()
                copies.append(copy)
    wait_all(copies)


def gather_kernel(*refs):
    *part_refs, out_ref, copy_sems = refs
    place = lax.rem(lax.axis_index("amp"), len(part_refs))
    copies = [
        pltpu.make_async_copy(ref, out_ref.at[place ^ index], copy_sems.at[index])
        for index, ref in enumerate(part_refs)
    ]
    for copy in copies:
        copy.start()
    wait_all(copies)


def tree_sum(parts):
    while len(parts) > 1:
        parts = [parts[i] + parts[i + 1] for i in range(0, len(parts), 2)]
    return parts[0]


def exchange(part, distance):
    devices = lax.axis_size("amp")
    return lax.ppermute(part, "amp", [(i, i ^ distance) for i in range(devices)])


def scattered_sum(value):
    devices = lax.axis_size("amp")
    inner = min(8, devices)
    own = lax.axis_index("amp") % inner
    blocks = value.reshape(inner, -1, value.shape[-1])

    def pick(index):
        return lax.dynamic_index_in_dim(blocks, index, 0, keepdims=False)

    part = tree_sum([pick(own)] + [exchange(pick(own ^ k), k) for k in range(1, inner)])
    distance = inner
    while distance < devices:
        part = part + exchange(part, distance)
        distance *= 2
    return part


def gathered_chips(part):
    inner = min(8, lax.axis_size("amp"))
    return [part] + [exchange(part, k) for k in range(2, inner, 2)]


def gathered_cores(own, shape):
    others = [exchange(found, 1) for found in own]
    parts = [found for pair in zip(own, others) for found in pair]
    out = pl.pallas_call(
        gather_kernel,
        in_specs=[pl.BlockSpec(memory_space=pl.ANY)] * len(parts),
        out_specs=IN_HBM,
        out_shape=jax.ShapeDtypeStruct((len(parts),) + parts[0].shape, parts[0].dtype),
        scratch_shapes=[pltpu.SemaphoreType.DMA((len(parts),))],
        compiler_params=PARAMS,
    )(*parts)
    return out.reshape(shape)


def to_rows(field, lanes):
    return field.reshape(2, -1, lanes).swapaxes(0, 1).reshape(-1, lanes)


def from_rows(rows):
    return rows.reshape(-1, 2, rows.shape[-1]).swapaxes(0, 1).reshape(2, -1)


IN_HBM = pl.BlockSpec(memory_space=pltpu.HBM)
IN_VMEM = pl.BlockSpec(memory_space=pltpu.VMEM)
PARAMS = pltpu.CompilerParams(vmem_limit_bytes=VMEM_BYTES)
HBM_PARAMS = pltpu.CompilerParams(vmem_limit_bytes=60 * 1024 * 1024)


def cost(layers, amplitudes, order):
    flops = layers * 3 * 8 * amplitudes * order
    return pl.CostEstimate(flops=flops, bytes_accessed=32 * amplitudes, transcendentals=0)


def on_device_lanes(state, costate, gates, devices, order, columns):
    lanes = 4 * columns // devices
    steps = devices // 4
    rows = 2 * columns // lanes
    scale = 1.0 / math.sqrt(devices * columns)
    field_shape = (devices, order, lanes)
    sum_shape = (order, 2 * order)
    amplitudes = 2 * order * columns

    def array(shape, kind=jnp.float32):
        return jax.ShapeDtypeStruct(shape, kind)

    state, costate = to_rows(state, lanes), to_rows(costate, lanes)
    sent = pl.pallas_call(
        first_kernel,
        in_specs=[IN_HBM, IN_HBM, IN_HBM],
        out_specs=IN_HBM,
        out_shape=array(field_shape),
        scratch_shapes=[
            pltpu.VMEM((2, order, order), jnp.float32),
            pltpu.VMEM((2, rows * order, lanes), jnp.float32),
            pltpu.VMEM(field_shape, jnp.float32),
            pltpu.SemaphoreType.DMA,
            pltpu.SemaphoreType.DMA((2, 4)),
            pltpu.SemaphoreType.DMA((steps,)),
        ],
        compiler_params=HBM_PARAMS,
        cost_estimate=cost(1, amplitudes, order),
    )(state, costate, gates)
    state, costate, sent = lax.optimization_barrier((state, costate, sent))
    moved = lax.all_to_all(sent, "amp", 0, 0, tiled=True)
    early = pl.pallas_call(
        early_kernel,
        in_specs=[IN_VMEM, IN_VMEM],
        out_specs=IN_VMEM,
        out_shape=array(sum_shape),
        compiler_params=PARAMS,
        cost_estimate=cost(1, amplitudes, order),
    )(state, costate)
    moved = moved.reshape(2, steps, 2, order, lanes)
    last = pl.pallas_call(
        middle_kernel,
        in_specs=[IN_VMEM, IN_VMEM, IN_HBM],
        out_specs=IN_HBM,
        out_shape=array(field_shape),
        input_output_aliases={2: 0},
        scratch_shapes=[
            pltpu.VMEM((devices * order, lanes), jnp.float32),
            pltpu.VMEM(field_shape, jnp.float32),
            pltpu.SemaphoreType.DMA((2, steps)),
        ],
        compiler_params=PARAMS,
        cost_estimate=cost(2, amplitudes, order),
    )(moved, gates, sent)
    arrived = lax.all_to_all(last, "amp", 0, 0, tiled=True)
    gradients = pl.pallas_call(
        functools.partial(late_kernel, scale=scale),
        in_specs=[IN_VMEM, IN_VMEM, IN_VMEM, IN_VMEM],
        out_specs=IN_VMEM,
        out_shape=array(gates.shape),
        scratch_shapes=[pltpu.VMEM((3,) + sum_shape, jnp.float32)],
        compiler_params=PARAMS,
        cost_estimate=cost(2, amplitudes, order),
    )(moved, last, early, gates)
    part, arrived = lax.optimization_barrier((scattered_sum(gradients), arrived))
    parts = gathered_chips(part)
    state_rows, costate_rows = pl.pallas_call(
        last_kernel,
        in_specs=[IN_HBM],
        out_specs=[IN_HBM, IN_HBM],
        out_shape=[array((order, rows, 1, lanes))] * 2,
        scratch_shapes=[
            pltpu.VMEM(field_shape, jnp.float32),
            pltpu.VMEM((2, rows, order, lanes), jnp.float32),
            pltpu.SemaphoreType.DMA((rows // 2,)),
            pltpu.SemaphoreType.DMA((2, rows)),
        ],
        compiler_params=PARAMS,
        cost_estimate=cost(1, amplitudes, order),
    )(arrived)
    parts, state_rows, costate_rows = lax.optimization_barrier((parts, state_rows, costate_rows))
    gradients = gathered_cores(parts, gates.shape)
    return from_rows(state_rows), from_rows(costate_rows), gradients


def undo_gate(field, gate):
    high = lax.Precision.HIGHEST
    shape = field.shape
    parts = field.reshape(shape[:-1] + (2, 2, -1))
    real, imag = parts[..., 0, :], parts[..., 1, :]

    def contract(matrix, operand):
        return jnp.einsum("ts,btvc->bsvc", matrix, operand, precision=high)

    new_real = contract(gate[0], real) + contract(gate[1], imag)
    new_imag = contract(gate[0], imag) - contract(gate[1], real)
    return jnp.stack([new_real, new_imag], axis=-2).reshape(shape)


def gate_gradient(before, after):
    high = lax.Precision.HIGHEST
    lam = before.reshape(before.shape[:-1] + (2, 2, -1))[..., 1, :, :]
    psi = after.reshape(after.shape[:-1] + (2, 2, -1))[..., 0, :, :]
    real = jnp.einsum("btpc,bspc->ts", lam, psi, precision=high)
    imag = jnp.einsum("btc,bsc->ts", lam[..., 1, :], psi[..., 0, :], precision=high) - jnp.einsum(
        "btc,bsc->ts", lam[..., 0, :], psi[..., 1, :], precision=high
    )
    return jnp.stack([real, imag], axis=0)


def on_device_plain(state, costate, gates, devices, order, columns):
    own = columns // devices
    both = jnp.stack([state, costate], axis=0).reshape(2, 2, order, devices, own)
    field = both.transpose(3, 2, 0, 1, 4).reshape(devices, order, 4 * own)
    field = lax.all_to_all(field, "amp", 0, 0, tiled=True)
    after = undo_gate(field, gates[0])
    terms = [gate_gradient(field, after)]
    field = after.reshape(2, devices // 4, 2, 2, 2, order // 4, 4 * own)
    field = field.transpose(3, 1, 4, 0, 2, 5, 6).reshape(devices, order, 4 * own)
    after = undo_gate(field, gates[1])
    terms.append(gate_gradient(field, after))
    field = after.reshape(devices, order // devices, devices, 4 * own)
    field = field.transpose(2, 1, 0, 3).reshape(devices, order, 4 * own)
    after = undo_gate(field, gates[2])
    terms.append(gate_gradient(field, after))
    terms = jnp.stack(terms, axis=0) / math.sqrt(devices * columns)
    gradients = gathered_cores(gathered_chips(scattered_sum(terms)), gates.shape)
    field = lax.all_to_all(after, "amp", 0, 0, tiled=True)
    field = field.reshape(devices, order, 2, 2, own).transpose(2, 3, 1, 0, 4)
    field = field.reshape(2, 2, order * columns)
    return field[0], field[1], gradients


def on_device(state, costate, gates):
    devices = lax.axis_size("amp")
    order = gates.shape[2]
    columns = state.shape[1] // order
    filled = 4 * columns == 128 * devices and order == 4 * devices
    form = on_device_lanes if filled else on_device_plain
    return form(state, costate, gates, devices, order, columns)


def solution(mesh):
    return jax.shard_map(
        on_device,
        mesh=mesh,
        in_specs=(P(None, "amp"), P(None, "amp"), P()),
        out_specs=(P(None, "amp"), P(None, "amp"), P()),
        check_vma=False,
    )
```

```python
import functools
import math

import jax
import jax.numpy as jnp
from jax import lax
from jax.experimental import pallas as pl
from jax.experimental.pallas import tpu as pltpu
from jax.sharding import PartitionSpec as P

VMEM_BYTES = 12 * 1024 * 1024


def split(value):
    high = value.astype(jnp.bfloat16)
    low = (value - high.astype(jnp.float32)).astype(jnp.bfloat16)
    return high, low


def both_parts(value):
    return jnp.concatenate(split(value), axis=0)


def left_parts(both):
    rows = both.shape[0] // 2
    high, low = both[:rows], both[rows:]
    return jnp.concatenate([high, low, high], axis=1)


def dot_parts(left, right):
    high, low = split(right)
    return jnp.dot(
        left_parts(left),
        jnp.concatenate([high, high, low], axis=0),
        preferred_element_type=jnp.float32,
    )


def dot_parts_rows(left, right):
    high, low = split(right)
    return lax.dot_general(
        left_parts(left),
        jnp.concatenate([high, high, low], axis=1),
        (((1,), (1,)), ((), ())),
        preferred_element_type=jnp.float32,
    )


def lane_index(shape):
    return lax.broadcasted_iota(jnp.int32, shape, len(shape) - 1)


def swap_groups(values):
    lanes = values[0].shape[-1]
    group = lane_index(values[0].shape) // (lanes // 4)
    for bit in (2, 1):
        width = bit * (lanes // 4)
        fresh = list(values)
        for index in range(4):
            if index & bit == 0:
                low, high = values[index], values[index | bit]
                upper = group & bit != 0
                fresh[index] = jnp.where(upper, pltpu.roll(high, width, 1), low)
                fresh[index | bit] = jnp.where(upper, high, pltpu.roll(low, lanes - width, 1))
        values = fresh
    return values


def swap_bit(low, high):
    lanes = low.shape[-1]
    width = lanes // 4
    upper = (lane_index(low.shape) // width) % 2 == 1
    first = jnp.where(upper, pltpu.roll(high, width, 1), low)
    second = jnp.where(upper, high, pltpu.roll(low, lanes - width, 1))
    return first, second


def row_halves(value, groups):
    rows, lanes = value.shape
    parts = value.reshape(groups, 2, rows // groups // 2, lanes)
    return parts[:, 0].reshape(rows // 2, lanes), parts[:, 1].reshape(rows // 2, lanes)


def wait_all(copies):
    for copy in copies:
        copy.wait()


def undo_matrix(gate):
    real, imag = gate[0].T, gate[1].T
    top = jnp.concatenate([real, imag], axis=1)
    low = jnp.concatenate([-imag, real], axis=1)
    return both_parts(jnp.concatenate([top, low], axis=0))


def column(rows, block, order):
    stride = rows.shape[0] // order
    parts = [rows[pl.ds(block * 2 + part, order, stride=stride), :] for part in range(2)]
    return jnp.concatenate(parts, axis=0)


def first_kernel(
    state_ref, costate_ref, gates_ref, out_ref, gate, rows, field_ref, gate_sem, row_sems, out_sems
):
    order = gate.shape[1]
    lanes = rows.shape[2]
    stride = rows.shape[1] // order
    chunks = row_sems.shape[1]
    chunk = rows.shape[1] // chunks
    copies = [pltpu.make_async_copy(gates_ref.at[0], gate, gate_sem)]
    for index in range(chunks):
        part = pl.ds(index * chunk, chunk)
        for vector, ref in enumerate((state_ref, costate_ref)):
            copies.append(
                pltpu.make_async_copy(ref.at[part], rows.at[vector, part], row_sems.at[vector, index])
            )
    for copy in copies:
        copy.start()
    copies[0].wait()
    matrix = undo_matrix(gate)
    wait_all(copies[1:])

    def column(vector, block):
        parts = [rows[vector, pl.ds(block * 2 + part, order, stride=stride), :] for part in range(2)]
        return jnp.concatenate(parts, axis=0)

    out_copies = []
    for block in range(stride // 2):
        field = jnp.concatenate([column(0, block), column(1, block)], axis=1)
        undone = dot_parts(matrix, field)
        pieces = []
        for vector in range(2):
            pieces += row_halves(undone[:, vector * lanes : (vector + 1) * lanes], 2)
        for index, piece in enumerate(swap_groups(pieces)):
            field_ref[block * 4 + index] = piece
        part = pl.ds(block * 4, 4)
        copy = pltpu.make_async_copy(field_ref.at[part], out_ref.at[part], out_sems.at[block])
        copy.start()
        out_copies.append(copy)
    wait_all(out_copies)


def outer_product(lam, psi):
    order = lam.shape[0] // 2
    left = jnp.concatenate([lam[:order], lam[order:]], axis=1)
    plain = jnp.concatenate([psi[:order], psi[order:]], axis=1)
    other = jnp.concatenate([-psi[order:], psi[:order]], axis=1)
    return dot_parts_rows(both_parts(left), jnp.concatenate([plain, other], axis=0))


def four_products(fields, groups):
    pieces = swap_groups(fields)
    rows, lanes = pieces[0].shape

    def joined(vector):
        parts = [
            piece.reshape(groups, 1, rows // groups, lanes)
            for piece in pieces[2 * vector : 2 * vector + 2]
        ]
        return jnp.concatenate(parts, axis=1).reshape(2 * rows, lanes)

    return outer_product(joined(1), joined(0))


def early_kernel(state_ref, costate_ref, out_ref):
    order = out_ref.shape[0]
    out_ref[...] = jnp.zeros_like(out_ref)

    @pl.loop(0, state_ref.shape[0] // order // 2)
    def _(block):
        out_ref[...] += outer_product(
            column(costate_ref, block, order), column(state_ref, block, order)
        )


def middle_kernel(moved_ref, gates_ref, spent_ref, out_ref, kept, last, sems):
    del spent_ref
    _, _, half_steps, _, order, lanes = moved_ref.shape
    steps, batches = 2 * half_steps, 4 * half_steps
    copies = []

    def block(bit, batch):
        high, rest = divmod(batch, batches // 2)
        return (high * 2 + bit) * (batches // 2) + rest


    def undo(matrix, fields):
        result = dot_parts(matrix, jnp.concatenate(fields, axis=1))
        return [result[:, index * lanes : (index + 1) * lanes] for index in range(len(fields))]

    matrices = [undo_matrix(gates_ref[index + 1]) for index in range(2)]
    for step in range(steps):
        fields = [mixed_rows(moved_ref, step, bit) for bit in range(2)]
        for bit, result in enumerate(undo(matrices[0], fields)):
            for top, piece in enumerate(swap_bit(*row_halves(result, 8))):
                place = (top * steps + step) * 2 + bit
                kept[pl.ds(place * order, order), :] = piece

    for step in range(steps):
        fields = [regrouped(kept, step * 2 + index, order) for index in range(2)]
        for index, result in enumerate(undo(matrices[1], fields)):
            for bit, piece in enumerate(swap_bit(*row_halves(result, 2))):
                last[block(bit, step * 2 + index)] = piece
        for bit in range(2):
            part = pl.ds(block(bit, step * 2), 2)
            copy = pltpu.make_async_copy(last.at[part], out_ref.at[part], sems.at[bit, step])
            copy.start()
            copies.append(copy)
    wait_all(copies)


def regrouped(kept_ref, batch, order):
    devices = kept_ref.shape[0] // order
    parts = [
        kept_ref[pl.ds(row * (devices // 2) + batch, devices, stride=order), :] for row in range(8)
    ]
    return jnp.concatenate(parts, axis=0)


def mixed_rows(moved_ref, step, bit):
    _, _, half_steps, _, order, _ = moved_ref.shape
    low_rows = order // 4
    high, rest = lax.div(step, half_steps), lax.rem(step, half_steps)
    parts = [
        moved_ref[high, top, rest, low, pl.ds((part * 2 + bit) * low_rows, low_rows), :]
        for part in range(2)
        for top in range(2)
        for low in range(2)
    ]
    return jnp.concatenate(parts, axis=0)


def late_kernel(moved_ref, last_ref, early_ref, gates_ref, out_ref, sum_ref, *, scale):
    order = early_ref.shape[0]
    steps = 2 * moved_ref.shape[2]
    sum_ref[0] = early_ref[...]
    sum_ref[1:3] = jnp.zeros((2,) + early_ref.shape, jnp.float32)

    @pl.loop(0, steps)
    def _(step):
        first, second = (mixed_rows(moved_ref, step, bit) for bit in range(2))
        half = first.shape[-1] // 2
        lower = lane_index(first.shape) < half
        psi = jnp.where(lower, first, pltpu.roll(second, half, 1))
        lam = jnp.where(lower, pltpu.roll(first, half, 1), second)
        sum_ref[1] += outer_product(lam, psi)
        sum_ref[2] += four_products([last_ref[step * 4 + index] for index in range(4)], 2)

    for index in range(3):
        total = (sum_ref[index, :, :order], sum_ref[index, :, order:])
        gate = (gates_ref[index, 0], gates_ref[index, 1])
        left, right = (gate, total) if index == 2 else (total, gate)
        out_ref[index, 0], out_ref[index, 1] = complex_product(left, right, scale)


def complex_product(left, right, scale):
    def times(first, second):
        return jnp.dot(
            first, second, precision=lax.Precision.HIGHEST, preferred_element_type=jnp.float32
        )

    real = times(left[0], right[0]) - times(left[1], right[1])
    imag = times(left[0], right[1]) + times(left[1], right[0])
    return real * scale, imag * scale


def last_kernel(moved_ref, state_ref, costate_ref, moved, rows, in_sems, copy_sems):
    half = moved.shape[1] // 2
    blocks = rows.shape[1] // 2
    in_copies = []
    for block in range(blocks):
        part = pl.ds(block * 4, 4)
        in_copies.append(
            pltpu.make_async_copy(moved_ref.at[part], moved.at[part], in_sems.at[block])
        )
        in_copies[-1].start()
    copies = []
    for block in range(blocks):
        in_copies[block].wait()
        pieces = swap_groups([moved[block * 4 + index] for index in range(4)])
        for vector, ref in enumerate((state_ref, costate_ref)):
            for part in range(2):
                place = block * 2 + part
                for bit in range(2):
                    piece = pieces[2 * vector + bit][part * half : (part + 1) * half]
                    rows[vector, place, bit * half : (bit + 1) * half] = piece
                copy = pltpu.make_async_copy(
                    rows.at[vector, place], ref.at[:, place, 0], copy_sems.at[vector, place]
                )
                copy.start()
                copies.append(copy)
    wait_all(copies)


def gather_kernel(*refs):
    *part_refs, out_ref, copy_sems = refs
    place = lax.rem(lax.axis_index("amp"), len(part_refs))
    copies = [
        pltpu.make_async_copy(ref, out_ref.at[place ^ index], copy_sems.at[index])
        for index, ref in enumerate(part_refs)
    ]
    for copy in copies:
        copy.start()
    wait_all(copies)


def tree_sum(parts):
    while len(parts) > 1:
        parts = [parts[i] + parts[i + 1] for i in range(0, len(parts), 2)]
    return parts[0]


def exchange_all(field):
    quarter = lax.axis_size("amp") // 4
    group = [part * quarter + i for part in (0, 2, 1, 3) for i in range(quarter)]
    return lax.all_to_all(field, "amp", 0, 0, axis_index_groups=[group], tiled=True)


def exchange(part, distance):
    devices = lax.axis_size("amp")
    return lax.ppermute(part, "amp", [(i, i ^ distance) for i in range(devices)])


def scattered_sum(value):
    devices = lax.axis_size("amp")
    inner = min(8, devices)
    own = lax.axis_index("amp") % inner
    blocks = value.reshape(inner, -1, value.shape[-1])

    def pick(index):
        return lax.dynamic_index_in_dim(blocks, index, 0, keepdims=False)

    part = tree_sum([pick(own)] + [exchange(pick(own ^ k), k) for k in range(1, inner)])
    distance = inner
    while distance < devices:
        part = part + exchange(part, distance)
        distance *= 2
    return part


def gathered_chips(part):
    inner = min(8, lax.axis_size("amp"))
    return [part] + [exchange(part, k) for k in range(2, inner, 2)]


def gathered_cores(own, shape):
    others = [exchange(found, 1) for found in own]
    parts = [found for pair in zip(own, others) for found in pair]
    out = pl.pallas_call(
        gather_kernel,
        in_specs=[pl.BlockSpec(memory_space=pl.ANY)] * len(parts),
        out_specs=IN_HBM,
        out_shape=jax.ShapeDtypeStruct((len(parts),) + parts[0].shape, parts[0].dtype),
        scratch_shapes=[pltpu.SemaphoreType.DMA((len(parts),))],
        compiler_params=PARAMS,
    )(*parts)
    return out.reshape(shape)


def to_rows(field, lanes):
    return field.reshape(2, -1, lanes).swapaxes(0, 1).reshape(-1, lanes)


def from_rows(rows):
    return rows.reshape(-1, 2, rows.shape[-1]).swapaxes(0, 1).reshape(2, -1)


IN_HBM = pl.BlockSpec(memory_space=pltpu.HBM)
IN_VMEM = pl.BlockSpec(memory_space=pltpu.VMEM)
PARAMS = pltpu.CompilerParams(vmem_limit_bytes=VMEM_BYTES)
HBM_PARAMS = pltpu.CompilerParams(vmem_limit_bytes=60 * 1024 * 1024)


def cost(layers, amplitudes, order):
    flops = layers * 3 * 8 * amplitudes * order
    return pl.CostEstimate(flops=flops, bytes_accessed=32 * amplitudes, transcendentals=0)


def on_device_lanes(state, costate, gates, devices, order, columns):
    lanes = 4 * columns // devices
    steps = devices // 4
    rows = 2 * columns // lanes
    scale = 1.0 / math.sqrt(devices * columns)
    field_shape = (devices, order, lanes)
    sum_shape = (order, 2 * order)
    amplitudes = 2 * order * columns

    def array(shape, kind=jnp.float32):
        return jax.ShapeDtypeStruct(shape, kind)

    state, costate = to_rows(state, lanes), to_rows(costate, lanes)
    sent = pl.pallas_call(
        first_kernel,
        in_specs=[IN_HBM, IN_HBM, IN_HBM],
        out_specs=IN_HBM,
        out_shape=array(field_shape),
        scratch_shapes=[
            pltpu.VMEM((2, order, order), jnp.float32),
            pltpu.VMEM((2, rows * order, lanes), jnp.float32),
            pltpu.VMEM(field_shape, jnp.float32),
            pltpu.SemaphoreType.DMA,
            pltpu.SemaphoreType.DMA((2, 4)),
            pltpu.SemaphoreType.DMA((steps,)),
        ],
        compiler_params=HBM_PARAMS,
        cost_estimate=cost(1, amplitudes, order),
    )(state, costate, gates)
    state, costate, sent = lax.optimization_barrier((state, costate, sent))
    moved = exchange_all(sent)
    early = pl.pallas_call(
        early_kernel,
        in_specs=[IN_VMEM, IN_VMEM],
        out_specs=IN_VMEM,
        out_shape=array(sum_shape),
        compiler_params=PARAMS,
        cost_estimate=cost(1, amplitudes, order),
    )(state, costate)
    moved = moved.reshape(2, 2, steps // 2, 2, order, lanes)
    last = pl.pallas_call(
        middle_kernel,
        in_specs=[IN_VMEM, IN_VMEM, IN_HBM],
        out_specs=IN_HBM,
        out_shape=array(field_shape),
        input_output_aliases={2: 0},
        scratch_shapes=[
            pltpu.VMEM((devices * order, lanes), jnp.float32),
            pltpu.VMEM(field_shape, jnp.float32),
            pltpu.SemaphoreType.DMA((2, steps)),
        ],
        compiler_params=PARAMS,
        cost_estimate=cost(2, amplitudes, order),
    )(moved, gates, sent)
    arrived = exchange_all(last)
    gradients = pl.pallas_call(
        functools.partial(late_kernel, scale=scale),
        in_specs=[IN_VMEM, IN_VMEM, IN_VMEM, IN_VMEM],
        out_specs=IN_VMEM,
        out_shape=array(gates.shape),
        scratch_shapes=[pltpu.VMEM((3,) + sum_shape, jnp.float32)],
        compiler_params=PARAMS,
        cost_estimate=cost(2, amplitudes, order),
    )(moved, last, early, gates)
    part, arrived = lax.optimization_barrier((scattered_sum(gradients), arrived))
    parts = gathered_chips(part)
    state_rows, costate_rows = pl.pallas_call(
        last_kernel,
        in_specs=[IN_HBM],
        out_specs=[IN_HBM, IN_HBM],
        out_shape=[array((order, rows, 1, lanes))] * 2,
        scratch_shapes=[
            pltpu.VMEM(field_shape, jnp.float32),
            pltpu.VMEM((2, rows, order, lanes), jnp.float32),
            pltpu.SemaphoreType.DMA((rows // 2,)),
            pltpu.SemaphoreType.DMA((2, rows)),
        ],
        compiler_params=PARAMS,
        cost_estimate=cost(1, amplitudes, order),
    )(arrived)
    parts, state_rows, costate_rows = lax.optimization_barrier((parts, state_rows, costate_rows))
    gradients = gathered_cores(parts, gates.shape)
    return from_rows(state_rows), from_rows(costate_rows), gradients


def undo_gate(field, gate):
    high = lax.Precision.HIGHEST
    shape = field.shape
    parts = field.reshape(shape[:-1] + (2, 2, -1))
    real, imag = parts[..., 0, :], parts[..., 1, :]

    def contract(matrix, operand):
        return jnp.einsum("ts,btvc->bsvc", matrix, operand, precision=high)

    new_real = contract(gate[0], real) + contract(gate[1], imag)
    new_imag = contract(gate[0], imag) - contract(gate[1], real)
    return jnp.stack([new_real, new_imag], axis=-2).reshape(shape)


def gate_gradient(before, after):
    high = lax.Precision.HIGHEST
    lam = before.reshape(before.shape[:-1] + (2, 2, -1))[..., 1, :, :]
    psi = after.reshape(after.shape[:-1] + (2, 2, -1))[..., 0, :, :]
    real = jnp.einsum("btpc,bspc->ts", lam, psi, precision=high)
    imag = jnp.einsum("btc,bsc->ts", lam[..., 1, :], psi[..., 0, :], precision=high) - jnp.einsum(
        "btc,bsc->ts", lam[..., 0, :], psi[..., 1, :], precision=high
    )
    return jnp.stack([real, imag], axis=0)


def on_device_plain(state, costate, gates, devices, order, columns):
    own = columns // devices
    both = jnp.stack([state, costate], axis=0).reshape(2, 2, order, devices, own)
    field = both.transpose(3, 2, 0, 1, 4).reshape(devices, order, 4 * own)
    field = lax.all_to_all(field, "amp", 0, 0, tiled=True)
    after = undo_gate(field, gates[0])
    terms = [gate_gradient(field, after)]
    field = after.reshape(2, devices // 4, 2, 2, 2, order // 4, 4 * own)
    field = field.transpose(3, 1, 4, 0, 2, 5, 6).reshape(devices, order, 4 * own)
    after = undo_gate(field, gates[1])
    terms.append(gate_gradient(field, after))
    field = after.reshape(devices, order // devices, devices, 4 * own)
    field = field.transpose(2, 1, 0, 3).reshape(devices, order, 4 * own)
    after = undo_gate(field, gates[2])
    terms.append(gate_gradient(field, after))
    terms = jnp.stack(terms, axis=0) / math.sqrt(devices * columns)
    gradients = gathered_cores(gathered_chips(scattered_sum(terms)), gates.shape)
    field = lax.all_to_all(after, "amp", 0, 0, tiled=True)
    field = field.reshape(devices, order, 2, 2, own).transpose(2, 3, 1, 0, 4)
    field = field.reshape(2, 2, order * columns)
    return field[0], field[1], gradients


def on_device(state, costate, gates):
    devices = lax.axis_size("amp")
    order = gates.shape[2]
    columns = state.shape[1] // order
    filled = 4 * columns == 128 * devices and order == 4 * devices
    form = on_device_lanes if filled else on_device_plain
    return form(state, costate, gates, devices, order, columns)


def solution(mesh):
    return jax.shard_map(
        on_device,
        mesh=mesh,
        in_specs=(P(None, "amp"), P(None, "amp"), P()),
        out_specs=(P(None, "amp"), P(None, "amp"), P()),
        check_vma=False,
    )
```

```python
import functools
import math

import jax
import jax.numpy as jnp
from jax import lax
from jax.experimental import pallas as pl
from jax.experimental.pallas import tpu as pltpu
from jax.sharding import PartitionSpec as P

VMEM_BYTES = 12 * 1024 * 1024


def split(value):
    high = value.astype(jnp.bfloat16)
    low = (value - high.astype(jnp.float32)).astype(jnp.bfloat16)
    return high, low


def both_parts(value):
    return jnp.concatenate(split(value), axis=0)


def left_parts(both):
    rows = both.shape[0] // 2
    high, low = both[:rows], both[rows:]
    return jnp.concatenate([high, low, high], axis=1)


def dot_parts(left, right):
    high, low = split(right)
    return jnp.dot(
        left_parts(left),
        jnp.concatenate([high, high, low], axis=0),
        preferred_element_type=jnp.float32,
    )


def dot_parts_rows(left, right):
    high, low = split(right)
    return lax.dot_general(
        left_parts(left),
        jnp.concatenate([high, high, low], axis=1),
        (((1,), (1,)), ((), ())),
        preferred_element_type=jnp.float32,
    )


def lane_index(shape):
    return lax.broadcasted_iota(jnp.int32, shape, len(shape) - 1)


def swap_groups(values):
    lanes = values[0].shape[-1]
    group = lane_index(values[0].shape) // (lanes // 4)
    for bit in (2, 1):
        width = bit * (lanes // 4)
        fresh = list(values)
        for index in range(4):
            if index & bit == 0:
                low, high = values[index], values[index | bit]
                upper = group & bit != 0
                fresh[index] = jnp.where(upper, pltpu.roll(high, width, 1), low)
                fresh[index | bit] = jnp.where(upper, high, pltpu.roll(low, lanes - width, 1))
        values = fresh
    return values


def swap_bit(low, high):
    lanes = low.shape[-1]
    width = lanes // 4
    upper = (lane_index(low.shape) // width) % 2 == 1
    first = jnp.where(upper, pltpu.roll(high, width, 1), low)
    second = jnp.where(upper, high, pltpu.roll(low, lanes - width, 1))
    return first, second


def row_halves(value, groups):
    rows, lanes = value.shape
    parts = value.reshape(groups, 2, rows // groups // 2, lanes)
    return parts[:, 0].reshape(rows // 2, lanes), parts[:, 1].reshape(rows // 2, lanes)


def wait_all(copies):
    for copy in copies:
        copy.wait()


def undo_matrix(gate):
    real, imag = gate[0].T, gate[1].T
    top = jnp.concatenate([real, imag], axis=1)
    low = jnp.concatenate([-imag, real], axis=1)
    return both_parts(jnp.concatenate([top, low], axis=0))


def column(rows, block, order):
    stride = rows.shape[0] // order
    parts = [rows[pl.ds(block * 2 + part, order, stride=stride), :] for part in range(2)]
    return jnp.concatenate(parts, axis=0)


def first_kernel(
    state_ref, costate_ref, gates_ref, out_ref, gate, rows, field_ref, gate_sem, row_sems, out_sems
):
    order = gate.shape[1]
    lanes = rows.shape[2]
    stride = rows.shape[1] // order
    chunks = row_sems.shape[1]
    chunk = rows.shape[1] // chunks
    copies = [pltpu.make_async_copy(gates_ref.at[0], gate, gate_sem)]
    for index in range(chunks):
        part = pl.ds(index * chunk, chunk)
        for vector, ref in enumerate((state_ref, costate_ref)):
            copies.append(
                pltpu.make_async_copy(ref.at[part], rows.at[vector, part], row_sems.at[vector, index])
            )
    for copy in copies:
        copy.start()
    copies[0].wait()
    matrix = undo_matrix(gate)
    wait_all(copies[1:])

    def column(vector, block):
        parts = [rows[vector, pl.ds(block * 2 + part, order, stride=stride), :] for part in range(2)]
        return jnp.concatenate(parts, axis=0)

    out_copies = []
    for block in range(stride // 2):
        field = jnp.concatenate([column(0, block), column(1, block)], axis=1)
        undone = dot_parts(matrix, field)
        pieces = []
        for vector in range(2):
            pieces += row_halves(undone[:, vector * lanes : (vector + 1) * lanes], 2)
        for index, piece in enumerate(swap_groups(pieces)):
            field_ref[block * 4 + index] = piece
        part = pl.ds(block * 4, 4)
        copy = pltpu.make_async_copy(field_ref.at[part], out_ref.at[part], out_sems.at[block])
        copy.start()
        out_copies.append(copy)
    wait_all(out_copies)


def outer_product(lam, psi):
    order = lam.shape[0] // 2
    left = jnp.concatenate([lam[:order], lam[order:]], axis=1)
    plain = jnp.concatenate([psi[:order], psi[order:]], axis=1)
    other = jnp.concatenate([-psi[order:], psi[:order]], axis=1)
    return dot_parts_rows(both_parts(left), jnp.concatenate([plain, other], axis=0))


def four_products(fields, groups):
    pieces = swap_groups(fields)
    rows, lanes = pieces[0].shape

    def joined(vector):
        parts = [
            piece.reshape(groups, 1, rows // groups, lanes)
            for piece in pieces[2 * vector : 2 * vector + 2]
        ]
        return jnp.concatenate(parts, axis=1).reshape(2 * rows, lanes)

    return outer_product(joined(1), joined(0))


def early_kernel(state_ref, costate_ref, out_ref):
    order = out_ref.shape[0]
    out_ref[...] = jnp.zeros_like(out_ref)

    @pl.loop(0, state_ref.shape[0] // order // 2)
    def _(block):
        out_ref[...] += outer_product(
            column(costate_ref, block, order), column(state_ref, block, order)
        )


def middle_kernel(moved_ref, gates_ref, spent_ref, out_ref, kept, last, sems):
    del spent_ref
    _, _, half_steps, _, order, lanes = moved_ref.shape
    steps, batches = 2 * half_steps, 4 * half_steps
    copies = []

    def block(bit, batch):
        high, rest = divmod(batch, batches // 2)
        return (high * 2 + bit) * (batches // 2) + rest


    def undo(matrix, fields):
        result = dot_parts(matrix, jnp.concatenate(fields, axis=1))
        return [result[:, index * lanes : (index + 1) * lanes] for index in range(len(fields))]

    matrices = [undo_matrix(gates_ref[index + 1]) for index in range(2)]
    for step in range(steps):
        fields = [mixed_rows(moved_ref, step, bit) for bit in range(2)]
        for bit, result in enumerate(undo(matrices[0], fields)):
            for top, piece in enumerate(swap_bit(*row_halves(result, 8))):
                place = (top * steps + step) * 2 + bit
                kept[pl.ds(place * order, order), :] = piece

    for step in range(steps):
        fields = [regrouped(kept, step * 2 + index, order) for index in range(2)]
        for index, result in enumerate(undo(matrices[1], fields)):
            for bit, piece in enumerate(swap_bit(*row_halves(result, 2))):
                last[block(bit, step * 2 + index)] = piece
        for bit in range(2):
            part = pl.ds(block(bit, step * 2), 2)
            copy = pltpu.make_async_copy(last.at[part], out_ref.at[part], sems.at[bit, step])
            copy.start()
            copies.append(copy)
    wait_all(copies)


def regrouped(kept_ref, batch, order):
    devices = kept_ref.shape[0] // order
    parts = [
        kept_ref[pl.ds(row * (devices // 2) + batch, devices, stride=order), :] for row in range(8)
    ]
    return jnp.concatenate(parts, axis=0)


def mixed_rows(moved_ref, step, bit):
    _, _, half_steps, _, order, _ = moved_ref.shape
    low_rows = order // 4
    high, rest = lax.div(step, half_steps), lax.rem(step, half_steps)
    parts = [
        moved_ref[high, top, rest, low, pl.ds((part * 2 + bit) * low_rows, low_rows), :]
        for part in range(2)
        for top in range(2)
        for low in range(2)
    ]
    return jnp.concatenate(parts, axis=0)


def late_kernel(moved_ref, last_ref, early_ref, gates_ref, out_ref, sum_ref, *, scale):
    order = early_ref.shape[0]
    steps = 2 * moved_ref.shape[2]
    sum_ref[0] = early_ref[...]
    sum_ref[1:3] = jnp.zeros((2,) + early_ref.shape, jnp.float32)

    @pl.loop(0, steps)
    def _(step):
        first, second = (mixed_rows(moved_ref, step, bit) for bit in range(2))
        half = first.shape[-1] // 2
        lower = lane_index(first.shape) < half
        psi = jnp.where(lower, first, pltpu.roll(second, half, 1))
        lam = jnp.where(lower, pltpu.roll(first, half, 1), second)
        sum_ref[1] += outer_product(lam, psi)
        sum_ref[2] += four_products([last_ref[step * 4 + index] for index in range(4)], 2)

    for index in range(3):
        total = (sum_ref[index, :, :order], sum_ref[index, :, order:])
        gate = (gates_ref[index, 0], gates_ref[index, 1])
        left, right = (gate, total) if index == 2 else (total, gate)
        out_ref[index, 0], out_ref[index, 1] = complex_product(left, right, scale)


def complex_product(left, right, scale):
    def times(first, second):
        return jnp.dot(
            first, second, precision=lax.Precision.HIGHEST, preferred_element_type=jnp.float32
        )

    real = times(left[0], right[0]) - times(left[1], right[1])
    imag = times(left[0], right[1]) + times(left[1], right[0])
    return real * scale, imag * scale


def last_kernel(moved_ref, state_ref, costate_ref, moved, rows, in_sems, copy_sems):
    half = moved.shape[1] // 2
    blocks = rows.shape[1] // 2
    in_copies = []
    for block in range(blocks):
        part = pl.ds(block * 4, 4)
        in_copies.append(
            pltpu.make_async_copy(moved_ref.at[part], moved.at[part], in_sems.at[block])
        )
    ahead = 4
    for copy in in_copies[:ahead]:
        copy.start()
    copies = []
    for block in range(blocks):
        in_copies[block].wait()
        if block + ahead < blocks:
            in_copies[block + ahead].start()
        pieces = swap_groups([moved[block * 4 + index] for index in range(4)])
        for vector, ref in enumerate((state_ref, costate_ref)):
            for part in range(2):
                place = block * 2 + part
                for bit in range(2):
                    piece = pieces[2 * vector + bit][part * half : (part + 1) * half]
                    rows[vector, place, bit * half : (bit + 1) * half] = piece
                copy = pltpu.make_async_copy(
                    rows.at[vector, place], ref.at[:, place, 0], copy_sems.at[vector, place]
                )
                copy.start()
                copies.append(copy)
    wait_all(copies)


def gather_kernel(*refs):
    *part_refs, out_ref, copy_sems = refs
    place = lax.rem(lax.axis_index("amp"), len(part_refs))
    copies = [
        pltpu.make_async_copy(ref, out_ref.at[place ^ index], copy_sems.at[index])
        for index, ref in enumerate(part_refs)
    ]
    for copy in copies:
        copy.start()
    wait_all(copies)


def tree_sum(parts):
    while len(parts) > 1:
        parts = [parts[i] + parts[i + 1] for i in range(0, len(parts), 2)]
    return parts[0]


def exchange_all(field):
    quarter = lax.axis_size("amp") // 4
    group = [part * quarter + i for part in (0, 2, 1, 3) for i in range(quarter)]
    return lax.all_to_all(field, "amp", 0, 0, axis_index_groups=[group], tiled=True)


def exchange(part, distance):
    devices = lax.axis_size("amp")
    return lax.ppermute(part, "amp", [(i, i ^ distance) for i in range(devices)])


def scattered_sum(value):
    devices = lax.axis_size("amp")
    half = devices // 2
    inner = min(8, half)
    place = lax.axis_index("amp")
    own = place % inner
    blocks = value.reshape(inner, -1, value.shape[-1])

    def pick(index):
        return lax.dynamic_index_in_dim(blocks, index, 0, keepdims=False)

    part = tree_sum([pick(own)] + [exchange(pick(own ^ k), k) for k in range(1, inner)])
    distance = inner
    while distance < half:
        part = part + exchange(part, distance)
        distance *= 2

    def away(device):
        group = device % half // inner
        return half // inner - 1 - group if device < half else group

    pairs = [(i, i + inner) for i in range(half - inner, half)]
    part = part + lax.ppermute(part, "amp", pairs + [(j, i) for i, j in pairs])
    own_away = jnp.where(place < half, half // inner - 1 - place % half // inner, place % half // inner)
    reach = 1
    while reach < half // inner:
        outwards = [-reach * inner, reach * inner]
        pairs = [(i, i + outwards[i // half]) for i in range(devices) if away(i) < reach]
        pairs = [(i, j) for i, j in pairs if 0 <= j < devices]
        part = jnp.where(own_away < reach, part, lax.ppermute(part, "amp", pairs))
        reach *= 2
    return part


def gathered_chips(part):
    inner = min(8, lax.axis_size("amp"))
    return [part] + [exchange(part, k) for k in range(2, inner, 2)]


def gathered_cores(own, shape):
    others = [exchange(found, 1) for found in own]
    parts = [found for pair in zip(own, others) for found in pair]
    out = pl.pallas_call(
        gather_kernel,
        in_specs=[pl.BlockSpec(memory_space=pl.ANY)] * len(parts),
        out_specs=IN_HBM,
        out_shape=jax.ShapeDtypeStruct((len(parts),) + parts[0].shape, parts[0].dtype),
        scratch_shapes=[pltpu.SemaphoreType.DMA((len(parts),))],
        compiler_params=PARAMS,
    )(*parts)
    return out.reshape(shape)


def to_rows(field, lanes):
    return field.reshape(2, -1, lanes).swapaxes(0, 1).reshape(-1, lanes)


def from_rows(rows):
    return rows.reshape(-1, 2, rows.shape[-1]).swapaxes(0, 1).reshape(2, -1)


IN_HBM = pl.BlockSpec(memory_space=pltpu.HBM)
IN_VMEM = pl.BlockSpec(memory_space=pltpu.VMEM)
PARAMS = pltpu.CompilerParams(vmem_limit_bytes=VMEM_BYTES)
HBM_PARAMS = pltpu.CompilerParams(vmem_limit_bytes=60 * 1024 * 1024)


def cost(layers, amplitudes, order):
    flops = layers * 3 * 8 * amplitudes * order
    return pl.CostEstimate(flops=flops, bytes_accessed=32 * amplitudes, transcendentals=0)


def on_device_lanes(state, costate, gates, devices, order, columns):
    lanes = 4 * columns // devices
    steps = devices // 4
    rows = 2 * columns // lanes
    scale = 1.0 / math.sqrt(devices * columns)
    field_shape = (devices, order, lanes)
    sum_shape = (order, 2 * order)
    amplitudes = 2 * order * columns

    def array(shape, kind=jnp.float32):
        return jax.ShapeDtypeStruct(shape, kind)

    state, costate = to_rows(state, lanes), to_rows(costate, lanes)
    sent = pl.pallas_call(
        first_kernel,
        in_specs=[IN_HBM, IN_HBM, IN_HBM],
        out_specs=IN_HBM,
        out_shape=array(field_shape),
        scratch_shapes=[
            pltpu.VMEM((2, order, order), jnp.float32),
            pltpu.VMEM((2, rows * order, lanes), jnp.float32),
            pltpu.VMEM(field_shape, jnp.float32),
            pltpu.SemaphoreType.DMA,
            pltpu.SemaphoreType.DMA((2, 4)),
            pltpu.SemaphoreType.DMA((steps,)),
        ],
        compiler_params=HBM_PARAMS,
        cost_estimate=cost(1, amplitudes, order),
    )(state, costate, gates)
    state, costate, sent = lax.optimization_barrier((state, costate, sent))
    moved = exchange_all(sent)
    early = pl.pallas_call(
        early_kernel,
        in_specs=[IN_VMEM, IN_VMEM],
        out_specs=IN_VMEM,
        out_shape=array(sum_shape),
        compiler_params=PARAMS,
        cost_estimate=cost(1, amplitudes, order),
    )(state, costate)
    moved = moved.reshape(2, 2, steps // 2, 2, order, lanes)
    last = pl.pallas_call(
        middle_kernel,
        in_specs=[IN_VMEM, IN_VMEM, IN_HBM],
        out_specs=IN_HBM,
        out_shape=array(field_shape),
        input_output_aliases={2: 0},
        scratch_shapes=[
            pltpu.VMEM((devices * order, lanes), jnp.float32),
            pltpu.VMEM(field_shape, jnp.float32),
            pltpu.SemaphoreType.DMA((2, steps)),
        ],
        compiler_params=PARAMS,
        cost_estimate=cost(2, amplitudes, order),
    )(moved, gates, sent)
    arrived = exchange_all(last)
    gradients = pl.pallas_call(
        functools.partial(late_kernel, scale=scale),
        in_specs=[IN_VMEM, IN_VMEM, IN_VMEM, IN_VMEM],
        out_specs=IN_VMEM,
        out_shape=array(gates.shape),
        scratch_shapes=[pltpu.VMEM((3,) + sum_shape, jnp.float32)],
        compiler_params=PARAMS,
        cost_estimate=cost(2, amplitudes, order),
    )(moved, last, early, gates)
    parts = gathered_chips(scattered_sum(gradients))
    state_rows, costate_rows = pl.pallas_call(
        last_kernel,
        in_specs=[IN_HBM],
        out_specs=[IN_HBM, IN_HBM],
        out_shape=[array((order, rows, 1, lanes))] * 2,
        scratch_shapes=[
            pltpu.VMEM(field_shape, jnp.float32),
            pltpu.VMEM((2, rows, order, lanes), jnp.float32),
            pltpu.SemaphoreType.DMA((rows // 2,)),
            pltpu.SemaphoreType.DMA((2, rows)),
        ],
        compiler_params=PARAMS,
        cost_estimate=cost(1, amplitudes, order),
    )(arrived)
    parts, state_rows, costate_rows = lax.optimization_barrier((parts, state_rows, costate_rows))
    gradients = gathered_cores(parts, gates.shape)
    return from_rows(state_rows), from_rows(costate_rows), gradients


def undo_gate(field, gate):
    high = lax.Precision.HIGHEST
    shape = field.shape
    parts = field.reshape(shape[:-1] + (2, 2, -1))
    real, imag = parts[..., 0, :], parts[..., 1, :]

    def contract(matrix, operand):
        return jnp.einsum("ts,btvc->bsvc", matrix, operand, precision=high)

    new_real = contract(gate[0], real) + contract(gate[1], imag)
    new_imag = contract(gate[0], imag) - contract(gate[1], real)
    return jnp.stack([new_real, new_imag], axis=-2).reshape(shape)


def gate_gradient(before, after):
    high = lax.Precision.HIGHEST
    lam = before.reshape(before.shape[:-1] + (2, 2, -1))[..., 1, :, :]
    psi = after.reshape(after.shape[:-1] + (2, 2, -1))[..., 0, :, :]
    real = jnp.einsum("btpc,bspc->ts", lam, psi, precision=high)
    imag = jnp.einsum("btc,bsc->ts", lam[..., 1, :], psi[..., 0, :], precision=high) - jnp.einsum(
        "btc,bsc->ts", lam[..., 0, :], psi[..., 1, :], precision=high
    )
    return jnp.stack([real, imag], axis=0)


def on_device_plain(state, costate, gates, devices, order, columns):
    own = columns // devices
    both = jnp.stack([state, costate], axis=0).reshape(2, 2, order, devices, own)
    field = both.transpose(3, 2, 0, 1, 4).reshape(devices, order, 4 * own)
    field = lax.all_to_all(field, "amp", 0, 0, tiled=True)
    after = undo_gate(field, gates[0])
    terms = [gate_gradient(field, after)]
    field = after.reshape(2, devices // 4, 2, 2, 2, order // 4, 4 * own)
    field = field.transpose(3, 1, 4, 0, 2, 5, 6).reshape(devices, order, 4 * own)
    after = undo_gate(field, gates[1])
    terms.append(gate_gradient(field, after))
    field = after.reshape(devices, order // devices, devices, 4 * own)
    field = field.transpose(2, 1, 0, 3).reshape(devices, order, 4 * own)
    after = undo_gate(field, gates[2])
    terms.append(gate_gradient(field, after))
    terms = jnp.stack(terms, axis=0) / math.sqrt(devices * columns)
    gradients = gathered_cores(gathered_chips(scattered_sum(terms)), gates.shape)
    field = lax.all_to_all(after, "amp", 0, 0, tiled=True)
    field = field.reshape(devices, order, 2, 2, own).transpose(2, 3, 1, 0, 4)
    field = field.reshape(2, 2, order * columns)
    return field[0], field[1], gradients


def on_device(state, costate, gates):
    devices = lax.axis_size("amp")
    order = gates.shape[2]
    columns = state.shape[1] // order
    filled = 4 * columns == 128 * devices and order == 4 * devices
    form = on_device_lanes if filled else on_device_plain
    return form(state, costate, gates, devices, order, columns)


def solution(mesh):
    return jax.shard_map(
        on_device,
        mesh=mesh,
        in_specs=(P(None, "amp"), P(None, "amp"), P()),
        out_specs=(P(None, "amp"), P(None, "amp"), P()),
        check_vma=False,
    )
```

```python
import functools
import math

import jax
import jax.numpy as jnp
from jax import lax
from jax.experimental import pallas as pl
from jax.experimental.pallas import tpu as pltpu
from jax.sharding import PartitionSpec as P

VMEM_BYTES = 12 * 1024 * 1024


def split(value):
    high = value.astype(jnp.bfloat16)
    low = (value - high.astype(jnp.float32)).astype(jnp.bfloat16)
    return high, low


def both_parts(value):
    return jnp.concatenate(split(value), axis=0)


def left_parts(both):
    rows = both.shape[0] // 2
    high, low = both[:rows], both[rows:]
    return jnp.concatenate([high, low, high], axis=1)


def dot_parts(left, right):
    high, low = split(right)
    return jnp.dot(
        left_parts(left),
        jnp.concatenate([high, high, low], axis=0),
        preferred_element_type=jnp.float32,
    )


def dot_parts_rows(left, right):
    high, low = split(right)
    return lax.dot_general(
        left_parts(left),
        jnp.concatenate([high, high, low], axis=1),
        (((1,), (1,)), ((), ())),
        preferred_element_type=jnp.float32,
    )


def lane_index(shape):
    return lax.broadcasted_iota(jnp.int32, shape, len(shape) - 1)


def swap_groups(values):
    lanes = values[0].shape[-1]
    group = lane_index(values[0].shape) // (lanes // 4)
    for bit in (2, 1):
        width = bit * (lanes // 4)
        fresh = list(values)
        for index in range(4):
            if index & bit == 0:
                low, high = values[index], values[index | bit]
                upper = group & bit != 0
                fresh[index] = jnp.where(upper, pltpu.roll(high, width, 1), low)
                fresh[index | bit] = jnp.where(upper, high, pltpu.roll(low, lanes - width, 1))
        values = fresh
    return values


def swap_bit(low, high):
    lanes = low.shape[-1]
    width = lanes // 4
    upper = (lane_index(low.shape) // width) % 2 == 1
    first = jnp.where(upper, pltpu.roll(high, width, 1), low)
    second = jnp.where(upper, high, pltpu.roll(low, lanes - width, 1))
    return first, second


def row_halves(value, groups):
    rows, lanes = value.shape
    parts = value.reshape(groups, 2, rows // groups // 2, lanes)
    return parts[:, 0].reshape(rows // 2, lanes), parts[:, 1].reshape(rows // 2, lanes)


def wait_all(copies):
    for copy in copies:
        copy.wait()


def undo_matrix(gate):
    real, imag = gate[0].T, gate[1].T
    top = jnp.concatenate([real, imag], axis=1)
    low = jnp.concatenate([-imag, real], axis=1)
    return both_parts(jnp.concatenate([top, low], axis=0))


def column(rows, block, order):
    stride = rows.shape[0] // order
    parts = [rows[pl.ds(block * 2 + part, order, stride=stride), :] for part in range(2)]
    return jnp.concatenate(parts, axis=0)


def first_kernel(
    state_ref,
    costate_ref,
    gates_ref,
    out_ref,
    gate,
    rows,
    half_ref,
    field_ref,
    gate_sem,
    row_sems,
    out_sems,
):
    order = gate.shape[1]
    lanes = rows.shape[2]
    blocks = field_ref.shape[0] // 4
    chunks = row_sems.shape[1]
    chunk = rows.shape[1] // chunks
    gate_copy = pltpu.make_async_copy(gates_ref.at[0], gate, gate_sem)
    copies = [
        [
            pltpu.make_async_copy(
                ref.at[pl.ds(index * chunk, chunk)],
                rows.at[vector, pl.ds(index * chunk, chunk)],
                row_sems.at[vector, index],
            )
            for index in range(chunks)
        ]
        for vector, ref in enumerate((state_ref, costate_ref))
    ]
    gate_copy.start()
    for copy in copies[0]:
        copy.start()
    gate_copy.wait()
    matrix = undo_matrix(gate)
    wait_all(copies[0])
    for copy in copies[1]:
        copy.start()

    def undone(vector, block):
        pair = [column(rows.at[vector], block + index, order) for index in range(2)]
        return dot_parts(matrix, jnp.concatenate(pair, axis=1))

    for block in range(0, blocks, 2):
        half_ref[block // 2] = undone(0, block)
    wait_all(copies[1])
    out_copies = []
    for block in range(0, blocks, 2):
        results = [half_ref[block // 2], undone(1, block)]
        for index in range(2):
            part = slice(index * lanes, (index + 1) * lanes)
            pieces = []
            for result in results:
                pieces += row_halves(result[:, part], 2)
            for number, piece in enumerate(swap_groups(pieces)):
                field_ref[(block + index) * 4 + number] = piece
        part = pl.ds(block * 4, 8)
        out_copies.append(
            pltpu.make_async_copy(field_ref.at[part], out_ref.at[part], out_sems.at[block // 2])
        )
        out_copies[-1].start()
    wait_all(out_copies)


def outer_product(lam, psi):
    order = lam.shape[0] // 2
    left = jnp.concatenate([lam[:order], lam[order:]], axis=1)
    plain = jnp.concatenate([psi[:order], psi[order:]], axis=1)
    other = jnp.concatenate([-psi[order:], psi[:order]], axis=1)
    return dot_parts_rows(both_parts(left), jnp.concatenate([plain, other], axis=0))


def four_products(fields, groups):
    pieces = swap_groups(fields)
    rows, lanes = pieces[0].shape

    def joined(vector):
        parts = [
            piece.reshape(groups, 1, rows // groups, lanes)
            for piece in pieces[2 * vector : 2 * vector + 2]
        ]
        return jnp.concatenate(parts, axis=1).reshape(2 * rows, lanes)

    return outer_product(joined(1), joined(0))


def early_kernel(state_ref, costate_ref, out_ref):
    order = out_ref.shape[0]
    out_ref[...] = jnp.zeros_like(out_ref)

    @pl.loop(0, state_ref.shape[0] // order // 2)
    def _(block):
        out_ref[...] += outer_product(
            column(costate_ref, block, order), column(state_ref, block, order)
        )


def middle_kernel(moved_ref, gates_ref, spent_ref, out_ref, kept, last, sems):
    del spent_ref
    _, steps, _, order, lanes = moved_ref.shape
    batches = 2 * steps
    copies = []

    def undo(matrix, fields):
        result = dot_parts(matrix, jnp.concatenate(fields, axis=1))
        return [result[:, index * lanes : (index + 1) * lanes] for index in range(len(fields))]

    matrices = [undo_matrix(gates_ref[index + 1]) for index in range(2)]
    for step in range(steps):
        fields = [mixed_rows(moved_ref, step, bit) for bit in range(2)]
        for bit, result in enumerate(undo(matrices[0], fields)):
            for top, piece in enumerate(swap_bit(*row_halves(result, 8))):
                place = (top * steps + step) * 2 + bit
                kept[pl.ds(place * order, order), :] = piece

    for step in range(steps):
        fields = [regrouped(kept, step * 2 + index, order) for index in range(2)]
        for index, result in enumerate(undo(matrices[1], fields)):
            for bit, piece in enumerate(swap_bit(*row_halves(result, 2))):
                last[bit * batches + step * 2 + index] = piece
        for bit in range(2):
            part = pl.ds(bit * batches + step * 2, 2)
            copy = pltpu.make_async_copy(last.at[part], out_ref.at[part], sems.at[bit, step])
            copy.start()
            copies.append(copy)
    wait_all(copies)


def regrouped(kept_ref, batch, order):
    devices = kept_ref.shape[0] // order
    parts = [
        kept_ref[pl.ds(row * (devices // 2) + batch, devices, stride=order), :] for row in range(8)
    ]
    return jnp.concatenate(parts, axis=0)


def mixed_rows(moved_ref, step, bit):
    low_rows = moved_ref.shape[3] // 4
    parts = [
        moved_ref[top, step, low, pl.ds((part * 2 + bit) * low_rows, low_rows), :]
        for part in range(2)
        for top in range(2)
        for low in range(2)
    ]
    return jnp.concatenate(parts, axis=0)


def late_kernel(moved_ref, last_ref, early_ref, gates_ref, out_ref, sum_ref, *, scale):
    order = early_ref.shape[0]
    steps = moved_ref.shape[1]
    sum_ref[0] = early_ref[...]
    sum_ref[1:3] = jnp.zeros((2,) + early_ref.shape, jnp.float32)

    @pl.loop(0, steps)
    def _(step):
        first, second = (mixed_rows(moved_ref, step, bit) for bit in range(2))
        half = first.shape[-1] // 2
        lower = lane_index(first.shape) < half
        psi = jnp.where(lower, first, pltpu.roll(second, half, 1))
        lam = jnp.where(lower, pltpu.roll(first, half, 1), second)
        sum_ref[1] += outer_product(lam, psi)
        sum_ref[2] += four_products([last_ref[step * 4 + index] for index in range(4)], 2)

    for index in range(3):
        total = (sum_ref[index, :, :order], sum_ref[index, :, order:])
        gate = (gates_ref[index, 0], gates_ref[index, 1])
        left, right = (gate, total) if index == 2 else (total, gate)
        out_ref[index, 0], out_ref[index, 1] = complex_product(left, right, scale)


def complex_product(left, right, scale):
    def times(first, second):
        return jnp.dot(
            first, second, precision=lax.Precision.HIGHEST, preferred_element_type=jnp.float32
        )

    real = times(left[0], right[0]) - times(left[1], right[1])
    imag = times(left[0], right[1]) + times(left[1], right[0])
    return real * scale, imag * scale


def last_kernel(moved_ref, state_ref, costate_ref, rows, copy_sems):
    half = moved_ref.shape[1] // 2
    copies = []
    for block in range(rows.shape[1] // 2):
        pieces = swap_groups([moved_ref[block * 4 + index] for index in range(4)])
        for vector, ref in enumerate((state_ref, costate_ref)):
            for part in range(2):
                column = block * 2 + part
                for bit in range(2):
                    piece = pieces[2 * vector + bit][part * half : (part + 1) * half]
                    rows[vector, column, bit * half : (bit + 1) * half] = piece
                copy = pltpu.make_async_copy(
                    rows.at[vector, column], ref.at[:, column, 0], copy_sems.at[vector, column]
                )
                copy.start()
                copies.append(copy)
    wait_all(copies)


def gather_kernel(*refs):
    *part_refs, out_ref, copy_sems = refs
    place = lax.rem(lax.axis_index("amp"), len(part_refs))
    copies = [
        pltpu.make_async_copy(ref, out_ref.at[place ^ index], copy_sems.at[index])
        for index, ref in enumerate(part_refs)
    ]
    for copy in copies:
        copy.start()
    wait_all(copies)


def tree_sum(parts):
    while len(parts) > 1:
        parts = [parts[i] + parts[i + 1] for i in range(0, len(parts), 2)]
    return parts[0]


def exchange(part, distance):
    devices = lax.axis_size("amp")
    return lax.ppermute(part, "amp", [(i, i ^ distance) for i in range(devices)])


def scattered_sum(value):
    devices = lax.axis_size("amp")
    inner = min(8, devices)
    own = lax.axis_index("amp") % inner
    blocks = value.reshape(inner, -1, value.shape[-1])

    def pick(index):
        return lax.dynamic_index_in_dim(blocks, index, 0, keepdims=False)

    part = tree_sum([pick(own)] + [exchange(pick(own ^ k), k) for k in range(1, inner)])
    distance = inner
    while distance < devices:
        part = part + exchange(part, distance)
        distance *= 2
    return part


def gathered_chips(part):
    inner = min(8, lax.axis_size("amp"))
    return [part] + [exchange(part, k) for k in range(2, inner, 2)]


def gathered_cores(own, shape):
    others = [exchange(found, 1) for found in own]
    parts = [found for pair in zip(own, others) for found in pair]
    out = pl.pallas_call(
        gather_kernel,
        in_specs=[pl.BlockSpec(memory_space=pl.ANY)] * len(parts),
        out_specs=IN_HBM,
        out_shape=jax.ShapeDtypeStruct((len(parts),) + parts[0].shape, parts[0].dtype),
        scratch_shapes=[pltpu.SemaphoreType.DMA((len(parts),))],
        compiler_params=PARAMS,
    )(*parts)
    return out.reshape(shape)


def to_rows(field, lanes):
    return field.reshape(2, -1, lanes).swapaxes(0, 1).reshape(-1, lanes)


def from_rows(rows):
    return rows.reshape(-1, 2, rows.shape[-1]).swapaxes(0, 1).reshape(2, -1)


IN_HBM = pl.BlockSpec(memory_space=pltpu.HBM)
IN_VMEM = pl.BlockSpec(memory_space=pltpu.VMEM)
PARAMS = pltpu.CompilerParams(vmem_limit_bytes=VMEM_BYTES)
HBM_PARAMS = pltpu.CompilerParams(vmem_limit_bytes=60 * 1024 * 1024)


def cost(layers, amplitudes, order):
    flops = layers * 3 * 8 * amplitudes * order
    return pl.CostEstimate(flops=flops, bytes_accessed=32 * amplitudes, transcendentals=0)


def on_device_lanes(state, costate, gates, devices, order, columns):
    lanes = 4 * columns // devices
    steps = devices // 4
    rows = 2 * columns // lanes
    scale = 1.0 / math.sqrt(devices * columns)
    field_shape = (devices, order, lanes)
    sum_shape = (order, 2 * order)
    amplitudes = 2 * order * columns

    def array(shape, kind=jnp.float32):
        return jax.ShapeDtypeStruct(shape, kind)

    state, costate = to_rows(state, lanes), to_rows(costate, lanes)
    sent = pl.pallas_call(
        first_kernel,
        in_specs=[IN_HBM, IN_HBM, IN_HBM],
        out_specs=IN_HBM,
        out_shape=array(field_shape),
        scratch_shapes=[
            pltpu.VMEM((2, order, order), jnp.float32),
            pltpu.VMEM((2, rows * order, lanes), jnp.float32),
            pltpu.VMEM((steps // 2, 2 * order, 2 * lanes), jnp.float32),
            pltpu.VMEM(field_shape, jnp.float32),
            pltpu.SemaphoreType.DMA,
            pltpu.SemaphoreType.DMA((2, 4)),
            pltpu.SemaphoreType.DMA((steps // 2,)),
        ],
        compiler_params=HBM_PARAMS,
        cost_estimate=cost(1, amplitudes, order),
    )(state, costate, gates)
    state, costate, sent = lax.optimization_barrier((state, costate, sent))
    moved = lax.all_to_all(sent, "amp", 0, 0, tiled=True)
    early = pl.pallas_call(
        early_kernel,
        in_specs=[IN_VMEM, IN_VMEM],
        out_specs=IN_VMEM,
        out_shape=array(sum_shape),
        compiler_params=PARAMS,
        cost_estimate=cost(1, amplitudes, order),
    )(state, costate)
    moved = moved.reshape(2, steps, 2, order, lanes)
    last = pl.pallas_call(
        middle_kernel,
        in_specs=[IN_VMEM, IN_VMEM, IN_HBM],
        out_specs=IN_HBM,
        out_shape=array(field_shape),
        input_output_aliases={2: 0},
        scratch_shapes=[
            pltpu.VMEM((devices * order, lanes), jnp.float32),
            pltpu.VMEM(field_shape, jnp.float32),
            pltpu.SemaphoreType.DMA((2, steps)),
        ],
        compiler_params=PARAMS,
        cost_estimate=cost(2, amplitudes, order),
    )(moved, gates, sent)
    arrived = lax.all_to_all(last, "amp", 0, 0, tiled=True)
    gradients = pl.pallas_call(
        functools.partial(late_kernel, scale=scale),
        in_specs=[IN_VMEM, IN_VMEM, IN_VMEM, IN_VMEM],
        out_specs=IN_VMEM,
        out_shape=array(gates.shape),
        scratch_shapes=[pltpu.VMEM((3,) + sum_shape, jnp.float32)],
        compiler_params=PARAMS,
        cost_estimate=cost(2, amplitudes, order),
    )(moved, last, early, gates)
    part, arrived = lax.optimization_barrier((scattered_sum(gradients), arrived))
    parts = gathered_chips(part)
    state_rows, costate_rows = pl.pallas_call(
        last_kernel,
        in_specs=[IN_VMEM],
        out_specs=[IN_HBM, IN_HBM],
        out_shape=[array((order, rows, 1, lanes))] * 2,
        scratch_shapes=[
            pltpu.VMEM((2, rows, order, lanes), jnp.float32),
            pltpu.SemaphoreType.DMA((2, rows)),
        ],
        compiler_params=PARAMS,
        cost_estimate=cost(1, amplitudes, order),
    )(arrived)
    gradients = gathered_cores(parts, gates.shape)
    return from_rows(state_rows), from_rows(costate_rows), gradients


def undo_gate(field, gate):
    high = lax.Precision.HIGHEST
    shape = field.shape
    parts = field.reshape(shape[:-1] + (2, 2, -1))
    real, imag = parts[..., 0, :], parts[..., 1, :]

    def contract(matrix, operand):
        return jnp.einsum("ts,btvc->bsvc", matrix, operand, precision=high)

    new_real = contract(gate[0], real) + contract(gate[1], imag)
    new_imag = contract(gate[0], imag) - contract(gate[1], real)
    return jnp.stack([new_real, new_imag], axis=-2).reshape(shape)


def gate_gradient(before, after):
    high = lax.Precision.HIGHEST
    lam = before.reshape(before.shape[:-1] + (2, 2, -1))[..., 1, :, :]
    psi = after.reshape(after.shape[:-1] + (2, 2, -1))[..., 0, :, :]
    real = jnp.einsum("btpc,bspc->ts", lam, psi, precision=high)
    imag = jnp.einsum("btc,bsc->ts", lam[..., 1, :], psi[..., 0, :], precision=high) - jnp.einsum(
        "btc,bsc->ts", lam[..., 0, :], psi[..., 1, :], precision=high
    )
    return jnp.stack([real, imag], axis=0)


def on_device_plain(state, costate, gates, devices, order, columns):
    own = columns // devices
    both = jnp.stack([state, costate], axis=0).reshape(2, 2, order, devices, own)
    field = both.transpose(3, 2, 0, 1, 4).reshape(devices, order, 4 * own)
    field = lax.all_to_all(field, "amp", 0, 0, tiled=True)
    after = undo_gate(field, gates[0])
    terms = [gate_gradient(field, after)]
    field = after.reshape(2, devices // 4, 2, 2, 2, order // 4, 4 * own)
    field = field.transpose(3, 1, 4, 0, 2, 5, 6).reshape(devices, order, 4 * own)
    after = undo_gate(field, gates[1])
    terms.append(gate_gradient(field, after))
    field = after.reshape(devices, order // devices, devices, 4 * own)
    field = field.transpose(2, 1, 0, 3).reshape(devices, order, 4 * own)
    after = undo_gate(field, gates[2])
    terms.append(gate_gradient(field, after))
    terms = jnp.stack(terms, axis=0) / math.sqrt(devices * columns)
    gradients = gathered_cores(gathered_chips(scattered_sum(terms)), gates.shape)
    field = lax.all_to_all(after, "amp", 0, 0, tiled=True)
    field = field.reshape(devices, order, 2, 2, own).transpose(2, 3, 1, 0, 4)
    field = field.reshape(2, 2, order * columns)
    return field[0], field[1], gradients


def on_device(state, costate, gates):
    devices = lax.axis_size("amp")
    order = gates.shape[2]
    columns = state.shape[1] // order
    filled = 4 * columns == 128 * devices and order == 4 * devices
    form = on_device_lanes if filled else on_device_plain
    return form(state, costate, gates, devices, order, columns)


def solution(mesh):
    return jax.shard_map(
        on_device,
        mesh=mesh,
        in_specs=(P(None, "amp"), P(None, "amp"), P()),
        out_specs=(P(None, "amp"), P(None, "amp"), P()),
        check_vma=False,
    )
```

```python
import functools
import math

import jax
import jax.numpy as jnp
from jax import lax
from jax.experimental import pallas as pl
from jax.experimental.pallas import tpu as pltpu
from jax.sharding import PartitionSpec as P

VMEM_BYTES = 12 * 1024 * 1024


def split(value):
    high = value.astype(jnp.bfloat16)
    low = (value - high.astype(jnp.float32)).astype(jnp.bfloat16)
    return high, low


def both_parts(value):
    return jnp.concatenate(split(value), axis=0)


def left_parts(both):
    rows = both.shape[0] // 2
    high, low = both[:rows], both[rows:]
    return jnp.concatenate([high, low, high], axis=1)


def dot_parts(left, right):
    high, low = split(right)
    return jnp.dot(
        left_parts(left),
        jnp.concatenate([high, high, low], axis=0),
        preferred_element_type=jnp.float32,
    )


def dot_parts_rows(left, right):
    high, low = split(right)
    return lax.dot_general(
        left_parts(left),
        jnp.concatenate([high, high, low], axis=1),
        (((1,), (1,)), ((), ())),
        preferred_element_type=jnp.float32,
    )


def lane_index(shape):
    return lax.broadcasted_iota(jnp.int32, shape, len(shape) - 1)


def swap_groups(values):
    lanes = values[0].shape[-1]
    group = lane_index(values[0].shape) // (lanes // 4)
    for bit in (2, 1):
        width = bit * (lanes // 4)
        fresh = list(values)
        for index in range(4):
            if index & bit == 0:
                low, high = values[index], values[index | bit]
                upper = group & bit != 0
                fresh[index] = jnp.where(upper, pltpu.roll(high, width, 1), low)
                fresh[index | bit] = jnp.where(upper, high, pltpu.roll(low, lanes - width, 1))
        values = fresh
    return values


def swap_bit(low, high):
    lanes = low.shape[-1]
    width = lanes // 4
    upper = (lane_index(low.shape) // width) % 2 == 1
    first = jnp.where(upper, pltpu.roll(high, width, 1), low)
    second = jnp.where(upper, high, pltpu.roll(low, lanes - width, 1))
    return first, second


def row_halves(value, groups):
    rows, lanes = value.shape
    parts = value.reshape(groups, 2, rows // groups // 2, lanes)
    return parts[:, 0].reshape(rows // 2, lanes), parts[:, 1].reshape(rows // 2, lanes)


def wait_all(copies):
    for copy in copies:
        copy.wait()


def undo_matrix(gate):
    real, imag = gate[0].T, gate[1].T
    top = jnp.concatenate([real, imag], axis=1)
    low = jnp.concatenate([-imag, real], axis=1)
    return both_parts(jnp.concatenate([top, low], axis=0))


def column(rows, block, order):
    stride = rows.shape[0] // order
    parts = [rows[pl.ds(block * 2 + part, order, stride=stride), :] for part in range(2)]
    return jnp.concatenate(parts, axis=0)


def first_kernel(
    state_ref, costate_ref, gates_ref, out_ref, gate, rows, field_ref, gate_sem, row_sems, out_sems
):
    order = gate.shape[1]
    lanes = rows.shape[2]
    stride = rows.shape[1] // order
    chunks = row_sems.shape[1]
    chunk = rows.shape[1] // chunks
    copies = [pltpu.make_async_copy(gates_ref.at[0], gate, gate_sem)]
    for index in range(chunks):
        part = pl.ds(index * chunk, chunk)
        for vector, ref in enumerate((state_ref, costate_ref)):
            copies.append(
                pltpu.make_async_copy(ref.at[part], rows.at[vector, part], row_sems.at[vector, index])
            )
    for copy in copies:
        copy.start()
    copies[0].wait()
    matrix = undo_matrix(gate)
    wait_all(copies[1:])

    def column(vector, block):
        parts = [rows[vector, pl.ds(block * 2 + part, order, stride=stride), :] for part in range(2)]
        return jnp.concatenate(parts, axis=0)

    out_copies = []
    for block in range(stride // 2):
        field = jnp.concatenate([column(0, block), column(1, block)], axis=1)
        undone = dot_parts(matrix, field)
        pieces = []
        for vector in range(2):
            pieces += row_halves(undone[:, vector * lanes : (vector + 1) * lanes], 2)
        for index, piece in enumerate(swap_groups(pieces)):
            field_ref[block * 4 + index] = piece
        part = pl.ds(block * 4, 4)
        copy = pltpu.make_async_copy(field_ref.at[part], out_ref.at[part], out_sems.at[block])
        copy.start()
        out_copies.append(copy)
    wait_all(out_copies)


def outer_product(lam, psi):
    order = lam.shape[0] // 2
    left = jnp.concatenate([lam[:order], lam[order:]], axis=1)
    plain = jnp.concatenate([psi[:order], psi[order:]], axis=1)
    other = jnp.concatenate([-psi[order:], psi[:order]], axis=1)
    return dot_parts_rows(both_parts(left), jnp.concatenate([plain, other], axis=0))


def four_products(fields, groups):
    pieces = swap_groups(fields)
    rows, lanes = pieces[0].shape

    def joined(vector):
        parts = [
            piece.reshape(groups, 1, rows // groups, lanes)
            for piece in pieces[2 * vector : 2 * vector + 2]
        ]
        return jnp.concatenate(parts, axis=1).reshape(2 * rows, lanes)

    return outer_product(joined(1), joined(0))


def early_kernel(state_ref, costate_ref, out_ref):
    order = out_ref.shape[0]
    out_ref[...] = jnp.zeros_like(out_ref)

    @pl.loop(0, state_ref.shape[0] // order // 2)
    def _(block):
        out_ref[...] += outer_product(
            column(costate_ref, block, order), column(state_ref, block, order)
        )


def middle_kernel(moved_ref, gates_ref, out_ref, kept, last, sems):
    _, steps, _, order, lanes = moved_ref.shape
    batches = 2 * steps
    copies = []

    def undo(matrix, fields):
        result = dot_parts(matrix, jnp.concatenate(fields, axis=1))
        return [result[:, index * lanes : (index + 1) * lanes] for index in range(len(fields))]

    matrices = [undo_matrix(gates_ref[index + 1]) for index in range(2)]
    for step in range(steps):
        fields = [mixed_rows(moved_ref, step, bit) for bit in range(2)]
        for bit, result in enumerate(undo(matrices[0], fields)):
            for top, piece in enumerate(swap_bit(*row_halves(result, 8))):
                place = (top * steps + step) * 2 + bit
                kept[pl.ds(place * order, order), :] = piece

    for step in range(steps):
        fields = [regrouped(kept, step * 2 + index, order) for index in range(2)]
        for index, result in enumerate(undo(matrices[1], fields)):
            for bit, piece in enumerate(swap_bit(*row_halves(result, 2))):
                last[bit * batches + step * 2 + index] = piece
        for bit in range(2):
            part = pl.ds(bit * batches + step * 2, 2)
            copy = pltpu.make_async_copy(last.at[part], out_ref.at[part], sems.at[bit, step])
            copy.start()
            copies.append(copy)
    wait_all(copies)


def regrouped(kept_ref, batch, order):
    devices = kept_ref.shape[0] // order
    parts = [
        kept_ref[pl.ds(row * (devices // 2) + batch, devices, stride=order), :] for row in range(8)
    ]
    return jnp.concatenate(parts, axis=0)


def mixed_rows(moved_ref, step, bit):
    low_rows = moved_ref.shape[3] // 4
    parts = [
        moved_ref[top, step, low, pl.ds((part * 2 + bit) * low_rows, low_rows), :]
        for part in range(2)
        for top in range(2)
        for low in range(2)
    ]
    return jnp.concatenate(parts, axis=0)


def late_kernel(moved_ref, last_ref, early_ref, gates_ref, out_ref, sum_ref, *, scale):
    order = early_ref.shape[0]
    steps = moved_ref.shape[1]
    sum_ref[0] = early_ref[...]
    sum_ref[1:3] = jnp.zeros((2,) + early_ref.shape, jnp.float32)

    @pl.loop(0, steps)
    def _(step):
        first, second = (mixed_rows(moved_ref, step, bit) for bit in range(2))
        half = first.shape[-1] // 2
        lower = lane_index(first.shape) < half
        psi = jnp.where(lower, first, pltpu.roll(second, half, 1))
        lam = jnp.where(lower, pltpu.roll(first, half, 1), second)
        sum_ref[1] += outer_product(lam, psi)
        sum_ref[2] += four_products([last_ref[step * 4 + index] for index in range(4)], 2)

    for index in range(3):
        total = (sum_ref[index, :, :order], sum_ref[index, :, order:])
        gate = (gates_ref[index, 0], gates_ref[index, 1])
        left, right = (gate, total) if index == 2 else (total, gate)
        out_ref[index, 0], out_ref[index, 1] = complex_product(left, right, scale)


def complex_product(left, right, scale):
    def times(first, second):
        return jnp.dot(
            first, second, precision=lax.Precision.HIGHEST, preferred_element_type=jnp.float32
        )

    real = times(left[0], right[0]) - times(left[1], right[1])
    imag = times(left[0], right[1]) + times(left[1], right[0])
    return real * scale, imag * scale


def last_kernel(moved_ref, state_ref, costate_ref, rows, copy_sems):
    half = moved_ref.shape[1] // 2
    copies = []
    for block in range(rows.shape[1] // 2):
        pieces = swap_groups([moved_ref[block * 4 + index] for index in range(4)])
        for vector, ref in enumerate((state_ref, costate_ref)):
            for part in range(2):
                column = block * 2 + part
                for bit in range(2):
                    piece = pieces[2 * vector + bit][part * half : (part + 1) * half]
                    rows[vector, column, bit * half : (bit + 1) * half] = piece
                copy = pltpu.make_async_copy(
                    rows.at[vector, column], ref.at[:, column, 0], copy_sems.at[vector, column]
                )
                copy.start()
                copies.append(copy)
    wait_all(copies)


def gather_kernel(*refs):
    *part_refs, out_ref, copy_sems = refs
    place = lax.rem(lax.axis_index("amp"), len(part_refs))
    copies = [
        pltpu.make_async_copy(ref, out_ref.at[place ^ index], copy_sems.at[index])
        for index, ref in enumerate(part_refs)
    ]
    for copy in copies:
        copy.start()
    wait_all(copies)


def tree_sum(parts):
    while len(parts) > 1:
        parts = [parts[i] + parts[i + 1] for i in range(0, len(parts), 2)]
    return parts[0]


def exchange(part, distance):
    devices = lax.axis_size("amp")
    return lax.ppermute(part, "amp", [(i, i ^ distance) for i in range(devices)])


def scattered_sum(value):
    devices = lax.axis_size("amp")
    inner = min(8, devices)
    own = lax.axis_index("amp") % inner
    blocks = value.reshape(inner, -1, value.shape[-1])

    def pick(index):
        return lax.dynamic_index_in_dim(blocks, index, 0, keepdims=False)

    part = tree_sum([pick(own)] + [exchange(pick(own ^ k), k) for k in range(1, inner)])
    distance = inner
    while distance < devices:
        part = part + exchange(part, distance)
        distance *= 2
    return part


def gathered_chips(part):
    inner = min(8, lax.axis_size("amp"))
    return [part] + [exchange(part, k) for k in range(2, inner, 2)]


def gathered_cores(own, shape):
    others = [exchange(found, 1) for found in own]
    parts = [found for pair in zip(own, others) for found in pair]
    out = pl.pallas_call(
        gather_kernel,
        in_specs=[pl.BlockSpec(memory_space=pl.ANY)] * len(parts),
        out_specs=IN_HBM,
        out_shape=jax.ShapeDtypeStruct((len(parts),) + parts[0].shape, parts[0].dtype),
        scratch_shapes=[pltpu.SemaphoreType.DMA((len(parts),))],
        compiler_params=PARAMS,
    )(*parts)
    return out.reshape(shape)


def to_rows(field, lanes):
    return field.reshape(2, -1, lanes).swapaxes(0, 1).reshape(-1, lanes)


def from_rows(rows):
    return rows.reshape(-1, 2, rows.shape[-1]).swapaxes(0, 1).reshape(2, -1)


IN_HBM = pl.BlockSpec(memory_space=pltpu.HBM)
IN_VMEM = pl.BlockSpec(memory_space=pltpu.VMEM)
PARAMS = pltpu.CompilerParams(vmem_limit_bytes=VMEM_BYTES)
HBM_PARAMS = pltpu.CompilerParams(vmem_limit_bytes=60 * 1024 * 1024)


def cost(layers, amplitudes, order):
    flops = layers * 3 * 8 * amplitudes * order
    return pl.CostEstimate(flops=flops, bytes_accessed=32 * amplitudes, transcendentals=0)


def on_device_lanes(state, costate, gates, devices, order, columns):
    lanes = 4 * columns // devices
    steps = devices // 4
    rows = 2 * columns // lanes
    scale = 1.0 / math.sqrt(devices * columns)
    field_shape = (devices, order, lanes)
    sum_shape = (order, 2 * order)
    amplitudes = 2 * order * columns

    def array(shape, kind=jnp.float32):
        return jax.ShapeDtypeStruct(shape, kind)

    state, costate = to_rows(state, lanes), to_rows(costate, lanes)
    sent = pl.pallas_call(
        first_kernel,
        in_specs=[IN_HBM, IN_HBM, IN_HBM],
        out_specs=IN_HBM,
        out_shape=array(field_shape),
        scratch_shapes=[
            pltpu.VMEM((2, order, order), jnp.float32),
            pltpu.VMEM((2, rows * order, lanes), jnp.float32),
            pltpu.VMEM(field_shape, jnp.float32),
            pltpu.SemaphoreType.DMA,
            pltpu.SemaphoreType.DMA((2, 4)),
            pltpu.SemaphoreType.DMA((steps,)),
        ],
        compiler_params=HBM_PARAMS,
        cost_estimate=cost(1, amplitudes, order),
    )(state, costate, gates)
    state, costate, sent = lax.optimization_barrier((state, costate, sent))
    moved = lax.all_to_all(sent, "amp", 0, 0, tiled=True)
    early = pl.pallas_call(
        early_kernel,
        in_specs=[IN_VMEM, IN_VMEM],
        out_specs=IN_VMEM,
        out_shape=array(sum_shape),
        compiler_params=PARAMS,
        cost_estimate=cost(1, amplitudes, order),
    )(state, costate)
    moved = moved.reshape(2, steps, 2, order, lanes)
    last = pl.pallas_call(
        middle_kernel,
        in_specs=[IN_VMEM, IN_VMEM],
        out_specs=IN_HBM,
        out_shape=pltpu.HBM(field_shape, jnp.float32),
        scratch_shapes=[
            pltpu.VMEM((devices * order, lanes), jnp.float32),
            pltpu.VMEM(field_shape, jnp.float32),
            pltpu.SemaphoreType.DMA((2, steps)),
        ],
        compiler_params=PARAMS,
        cost_estimate=cost(2, amplitudes, order),
    )(moved, gates)
    arrived = lax.all_to_all(last, "amp", 0, 0, tiled=True)
    gradients = pl.pallas_call(
        functools.partial(late_kernel, scale=scale),
        in_specs=[IN_VMEM, IN_VMEM, IN_VMEM, IN_VMEM],
        out_specs=IN_VMEM,
        out_shape=array(gates.shape),
        scratch_shapes=[pltpu.VMEM((3,) + sum_shape, jnp.float32)],
        compiler_params=PARAMS,
        cost_estimate=cost(2, amplitudes, order),
    )(moved, last, early, gates)
    part, arrived = lax.optimization_barrier((scattered_sum(gradients), arrived))
    parts = gathered_chips(part)
    state_rows, costate_rows = pl.pallas_call(
        last_kernel,
        in_specs=[IN_VMEM],
        out_specs=[IN_HBM, IN_HBM],
        out_shape=[array((order, rows, 1, lanes))] * 2,
        scratch_shapes=[
            pltpu.VMEM((2, rows, order, lanes), jnp.float32),
            pltpu.SemaphoreType.DMA((2, rows)),
        ],
        compiler_params=PARAMS,
        cost_estimate=cost(1, amplitudes, order),
    )(arrived)
    parts, state_rows, costate_rows = lax.optimization_barrier((parts, state_rows, costate_rows))
    gradients = gathered_cores(parts, gates.shape)
    return from_rows(state_rows), from_rows(costate_rows), gradients


def undo_gate(field, gate):
    high = lax.Precision.HIGHEST
    shape = field.shape
    parts = field.reshape(shape[:-1] + (2, 2, -1))
    real, imag = parts[..., 0, :], parts[..., 1, :]

    def contract(matrix, operand):
        return jnp.einsum("ts,btvc->bsvc", matrix, operand, precision=high)

    new_real = contract(gate[0], real) + contract(gate[1], imag)
    new_imag = contract(gate[0], imag) - contract(gate[1], real)
    return jnp.stack([new_real, new_imag], axis=-2).reshape(shape)


def gate_gradient(before, after):
    high = lax.Precision.HIGHEST
    lam = before.reshape(before.shape[:-1] + (2, 2, -1))[..., 1, :, :]
    psi = after.reshape(after.shape[:-1] + (2, 2, -1))[..., 0, :, :]
    real = jnp.einsum("btpc,bspc->ts", lam, psi, precision=high)
    imag = jnp.einsum("btc,bsc->ts", lam[..., 1, :], psi[..., 0, :], precision=high) - jnp.einsum(
        "btc,bsc->ts", lam[..., 0, :], psi[..., 1, :], precision=high
    )
    return jnp.stack([real, imag], axis=0)


def on_device_plain(state, costate, gates, devices, order, columns):
    own = columns // devices
    both = jnp.stack([state, costate], axis=0).reshape(2, 2, order, devices, own)
    field = both.transpose(3, 2, 0, 1, 4).reshape(devices, order, 4 * own)
    field = lax.all_to_all(field, "amp", 0, 0, tiled=True)
    after = undo_gate(field, gates[0])
    terms = [gate_gradient(field, after)]
    field = after.reshape(2, devices // 4, 2, 2, 2, order // 4, 4 * own)
    field = field.transpose(3, 1, 4, 0, 2, 5, 6).reshape(devices, order, 4 * own)
    after = undo_gate(field, gates[1])
    terms.append(gate_gradient(field, after))
    field = after.reshape(devices, order // devices, devices, 4 * own)
    field = field.transpose(2, 1, 0, 3).reshape(devices, order, 4 * own)
    after = undo_gate(field, gates[2])
    terms.append(gate_gradient(field, after))
    terms = jnp.stack(terms, axis=0) / math.sqrt(devices * columns)
    gradients = gathered_cores(gathered_chips(scattered_sum(terms)), gates.shape)
    field = lax.all_to_all(after, "amp", 0, 0, tiled=True)
    field = field.reshape(devices, order, 2, 2, own).transpose(2, 3, 1, 0, 4)
    field = field.reshape(2, 2, order * columns)
    return field[0], field[1], gradients


def on_device(state, costate, gates):
    devices = lax.axis_size("amp")
    order = gates.shape[2]
    columns = state.shape[1] // order
    filled = 4 * columns == 128 * devices and order == 4 * devices
    form = on_device_lanes if filled else on_device_plain
    return form(state, costate, gates, devices, order, columns)


def solution(mesh):
    return jax.shard_map(
        on_device,
        mesh=mesh,
        in_specs=(P(None, "amp"), P(None, "amp"), P()),
        out_specs=(P(None, "amp"), P(None, "amp"), P()),
        check_vma=False,
    )
```

```python
import functools
import math

import jax
import jax.numpy as jnp
from jax import lax
from jax.experimental import pallas as pl
from jax.experimental.pallas import tpu as pltpu
from jax.sharding import PartitionSpec as P

VMEM_BYTES = 12 * 1024 * 1024


def split(value):
    high = value.astype(jnp.bfloat16)
    low = (value - high.astype(jnp.float32)).astype(jnp.bfloat16)
    return high, low


def both_parts(value):
    return jnp.concatenate(split(value), axis=0)


def left_parts(both):
    rows = both.shape[0] // 2
    high, low = both[:rows], both[rows:]
    return jnp.concatenate([high, low, high], axis=1)


def dot_parts(left, right):
    high, low = split(right)
    return jnp.dot(
        left_parts(left),
        jnp.concatenate([high, high, low], axis=0),
        preferred_element_type=jnp.float32,
    )


def dot_parts_rows(left, right):
    high, low = split(right)
    return lax.dot_general(
        left_parts(left),
        jnp.concatenate([high, high, low], axis=1),
        (((1,), (1,)), ((), ())),
        preferred_element_type=jnp.float32,
    )


def lane_index(shape):
    return lax.broadcasted_iota(jnp.int32, shape, len(shape) - 1)


def swap_groups(values):
    lanes = values[0].shape[-1]
    group = lane_index(values[0].shape) // (lanes // 4)
    for bit in (2, 1):
        width = bit * (lanes // 4)
        fresh = list(values)
        for index in range(4):
            if index & bit == 0:
                low, high = values[index], values[index | bit]
                upper = group & bit != 0
                fresh[index] = jnp.where(upper, pltpu.roll(high, width, 1), low)
                fresh[index | bit] = jnp.where(upper, high, pltpu.roll(low, lanes - width, 1))
        values = fresh
    return values


def swap_bit(low, high):
    lanes = low.shape[-1]
    width = lanes // 4
    upper = (lane_index(low.shape) // width) % 2 == 1
    first = jnp.where(upper, pltpu.roll(high, width, 1), low)
    second = jnp.where(upper, high, pltpu.roll(low, lanes - width, 1))
    return first, second


def row_halves(value, groups):
    rows, lanes = value.shape
    parts = value.reshape(groups, 2, rows // groups // 2, lanes)
    return parts[:, 0].reshape(rows // 2, lanes), parts[:, 1].reshape(rows // 2, lanes)


def wait_all(copies):
    for copy in copies:
        copy.wait()


def undo_matrix(gate):
    real, imag = gate[0].T, gate[1].T
    top = jnp.concatenate([real, imag], axis=1)
    low = jnp.concatenate([-imag, real], axis=1)
    return both_parts(jnp.concatenate([top, low], axis=0))


def column(rows, block, order):
    stride = rows.shape[0] // order
    parts = [rows[pl.ds(block * 2 + part, order, stride=stride), :] for part in range(2)]
    return jnp.concatenate(parts, axis=0)


def first_kernel(
    state_ref, costate_ref, gates_ref, out_ref, gate, rows, field_ref, gate_sem, row_sems, out_sems
):
    order = gate.shape[1]
    lanes = rows.shape[2]
    stride = rows.shape[1] // order
    chunks = row_sems.shape[1]
    chunk = rows.shape[1] // chunks
    copies = [pltpu.make_async_copy(gates_ref.at[0], gate, gate_sem)]
    for index in range(chunks):
        part = pl.ds(index * chunk, chunk)
        for vector, ref in enumerate((state_ref, costate_ref)):
            copies.append(
                pltpu.make_async_copy(ref.at[part], rows.at[vector, part], row_sems.at[vector, index])
            )
    for copy in copies:
        copy.start()
    copies[0].wait()
    matrix = undo_matrix(gate)
    wait_all(copies[1:])

    def column(vector, block):
        parts = [rows[vector, pl.ds(block * 2 + part, order, stride=stride), :] for part in range(2)]
        return jnp.concatenate(parts, axis=0)

    out_copies = []
    for block in range(stride // 2):
        field = jnp.concatenate([column(0, block), column(1, block)], axis=1)
        undone = dot_parts(matrix, field)
        pieces = []
        for vector in range(2):
            pieces += row_halves(undone[:, vector * lanes : (vector + 1) * lanes], 2)
        for index, piece in enumerate(swap_groups(pieces)):
            field_ref[block * 4 + index] = piece
        part = pl.ds(block * 4, 4)
        copy = pltpu.make_async_copy(field_ref.at[part], out_ref.at[part], out_sems.at[block])
        copy.start()
        out_copies.append(copy)
    wait_all(out_copies)


def outer_product(lam, psi):
    order = lam.shape[0] // 2
    left = jnp.concatenate([lam[:order], lam[order:]], axis=1)
    plain = jnp.concatenate([psi[:order], psi[order:]], axis=1)
    other = jnp.concatenate([-psi[order:], psi[:order]], axis=1)
    return dot_parts_rows(both_parts(left), jnp.concatenate([plain, other], axis=0))


def four_products(fields, groups):
    pieces = swap_groups(fields)
    rows, lanes = pieces[0].shape

    def joined(vector):
        parts = [
            piece.reshape(groups, 1, rows // groups, lanes)
            for piece in pieces[2 * vector : 2 * vector + 2]
        ]
        return jnp.concatenate(parts, axis=1).reshape(2 * rows, lanes)

    return outer_product(joined(1), joined(0))


def early_kernel(state_ref, costate_ref, gates_ref, out_ref, matrix_ref):
    order = out_ref.shape[0]
    for index in range(2):
        matrix_ref[index] = undo_matrix(gates_ref[index + 1])
    out_ref[...] = jnp.zeros_like(out_ref)

    @pl.loop(0, state_ref.shape[0] // order // 2)
    def _(block):
        out_ref[...] += outer_product(
            column(costate_ref, block, order), column(state_ref, block, order)
        )


def middle_kernel(moved_ref, matrix_ref, out_ref, kept, last, sems):
    _, steps, _, order, lanes = moved_ref.shape
    batches = 2 * steps
    copies = []

    def undo(matrix, fields):
        result = dot_parts(matrix, jnp.concatenate(fields, axis=1))
        return [result[:, index * lanes : (index + 1) * lanes] for index in range(len(fields))]

    for step in range(steps):
        fields = [mixed_rows(moved_ref, step, bit) for bit in range(2)]
        for bit, result in enumerate(undo(matrix_ref[0], fields)):
            for top, piece in enumerate(swap_bit(*row_halves(result, 8))):
                place = (top * steps + step) * 2 + bit
                kept[pl.ds(place * order, order), :] = piece

    for step in range(steps):
        fields = [regrouped(kept, step * 2 + index, order) for index in range(2)]
        for index, result in enumerate(undo(matrix_ref[1], fields)):
            for bit, piece in enumerate(swap_bit(*row_halves(result, 2))):
                last[bit * batches + step * 2 + index] = piece
        for bit in range(2):
            part = pl.ds(bit * batches + step * 2, 2)
            copy = pltpu.make_async_copy(last.at[part], out_ref.at[part], sems.at[bit, step])
            copy.start()
            copies.append(copy)
    wait_all(copies)


def regrouped(kept_ref, batch, order):
    devices = kept_ref.shape[0] // order
    parts = [
        kept_ref[pl.ds(row * (devices // 2) + batch, devices, stride=order), :] for row in range(8)
    ]
    return jnp.concatenate(parts, axis=0)


def mixed_rows(moved_ref, step, bit):
    low_rows = moved_ref.shape[3] // 4
    parts = [
        moved_ref[top, step, low, pl.ds((part * 2 + bit) * low_rows, low_rows), :]
        for part in range(2)
        for top in range(2)
        for low in range(2)
    ]
    return jnp.concatenate(parts, axis=0)


def late_kernel(moved_ref, last_ref, early_ref, gates_ref, out_ref, sum_ref, *, scale):
    order = early_ref.shape[0]
    steps = moved_ref.shape[1]
    sum_ref[0] = early_ref[...]
    sum_ref[1:3] = jnp.zeros((2,) + early_ref.shape, jnp.float32)

    @pl.loop(0, steps)
    def _(step):
        first, second = (mixed_rows(moved_ref, step, bit) for bit in range(2))
        half = first.shape[-1] // 2
        lower = lane_index(first.shape) < half
        psi = jnp.where(lower, first, pltpu.roll(second, half, 1))
        lam = jnp.where(lower, pltpu.roll(first, half, 1), second)
        sum_ref[1] += outer_product(lam, psi)
        sum_ref[2] += four_products([last_ref[step * 4 + index] for index in range(4)], 2)

    for index in range(3):
        total = (sum_ref[index, :, :order], sum_ref[index, :, order:])
        gate = (gates_ref[index, 0], gates_ref[index, 1])
        left, right = (gate, total) if index == 2 else (total, gate)
        out_ref[index, 0], out_ref[index, 1] = complex_product(left, right, scale)


def complex_product(left, right, scale):
    def times(first, second):
        return jnp.dot(
            first, second, precision=lax.Precision.HIGHEST, preferred_element_type=jnp.float32
        )

    real = times(left[0], right[0]) - times(left[1], right[1])
    imag = times(left[0], right[1]) + times(left[1], right[0])
    return real * scale, imag * scale


def last_kernel(moved_ref, state_ref, costate_ref, rows, copy_sems):
    half = moved_ref.shape[1] // 2
    copies = []
    for block in range(rows.shape[1] // 2):
        pieces = swap_groups([moved_ref[block * 4 + index] for index in range(4)])
        for vector, ref in enumerate((state_ref, costate_ref)):
            for part in range(2):
                column = block * 2 + part
                for bit in range(2):
                    piece = pieces[2 * vector + bit][part * half : (part + 1) * half]
                    rows[vector, column, bit * half : (bit + 1) * half] = piece
                copy = pltpu.make_async_copy(
                    rows.at[vector, column], ref.at[:, column, 0], copy_sems.at[vector, column]
                )
                copy.start()
                copies.append(copy)
    wait_all(copies)


def gather_kernel(*refs):
    *part_refs, out_ref, copy_sems = refs
    place = lax.rem(lax.axis_index("amp"), len(part_refs))
    copies = [
        pltpu.make_async_copy(ref, out_ref.at[place ^ index], copy_sems.at[index])
        for index, ref in enumerate(part_refs)
    ]
    for copy in copies:
        copy.start()
    wait_all(copies)


def tree_sum(parts):
    while len(parts) > 1:
        parts = [parts[i] + parts[i + 1] for i in range(0, len(parts), 2)]
    return parts[0]


def exchange(part, distance):
    devices = lax.axis_size("amp")
    return lax.ppermute(part, "amp", [(i, i ^ distance) for i in range(devices)])


def scattered_sum(value):
    devices = lax.axis_size("amp")
    inner = min(8, devices)
    own = lax.axis_index("amp") % inner
    blocks = value.reshape(inner, -1, value.shape[-1])

    def pick(index):
        return lax.dynamic_index_in_dim(blocks, index, 0, keepdims=False)

    part = tree_sum([pick(own)] + [exchange(pick(own ^ k), k) for k in range(1, inner)])
    distance = inner
    while distance < devices:
        part = part + exchange(part, distance)
        distance *= 2
    return part


def gathered_chips(part):
    inner = min(8, lax.axis_size("amp"))
    return [part] + [exchange(part, k) for k in range(2, inner, 2)]


def gathered_cores(own, shape):
    others = [exchange(found, 1) for found in own]
    parts = [found for pair in zip(own, others) for found in pair]
    out = pl.pallas_call(
        gather_kernel,
        in_specs=[pl.BlockSpec(memory_space=pl.ANY)] * len(parts),
        out_specs=IN_HBM,
        out_shape=jax.ShapeDtypeStruct((len(parts),) + parts[0].shape, parts[0].dtype),
        scratch_shapes=[pltpu.SemaphoreType.DMA((len(parts),))],
        compiler_params=PARAMS,
    )(*parts)
    return out.reshape(shape)


def to_rows(field, lanes):
    return field.reshape(2, -1, lanes).swapaxes(0, 1).reshape(-1, lanes)


def from_rows(rows):
    return rows.reshape(-1, 2, rows.shape[-1]).swapaxes(0, 1).reshape(2, -1)


IN_HBM = pl.BlockSpec(memory_space=pltpu.HBM)
IN_VMEM = pl.BlockSpec(memory_space=pltpu.VMEM)
PARAMS = pltpu.CompilerParams(vmem_limit_bytes=VMEM_BYTES)
HBM_PARAMS = pltpu.CompilerParams(vmem_limit_bytes=60 * 1024 * 1024)


def cost(layers, amplitudes, order):
    flops = layers * 3 * 8 * amplitudes * order
    return pl.CostEstimate(flops=flops, bytes_accessed=32 * amplitudes, transcendentals=0)


def on_device_lanes(state, costate, gates, devices, order, columns):
    lanes = 4 * columns // devices
    steps = devices // 4
    rows = 2 * columns // lanes
    scale = 1.0 / math.sqrt(devices * columns)
    field_shape = (devices, order, lanes)
    sum_shape = (order, 2 * order)
    amplitudes = 2 * order * columns

    def array(shape, kind=jnp.float32):
        return jax.ShapeDtypeStruct(shape, kind)

    state, costate = to_rows(state, lanes), to_rows(costate, lanes)
    sent = pl.pallas_call(
        first_kernel,
        in_specs=[IN_HBM, IN_HBM, IN_HBM],
        out_specs=IN_HBM,
        out_shape=array(field_shape),
        scratch_shapes=[
            pltpu.VMEM((2, order, order), jnp.float32),
            pltpu.VMEM((2, rows * order, lanes), jnp.float32),
            pltpu.VMEM(field_shape, jnp.float32),
            pltpu.SemaphoreType.DMA,
            pltpu.SemaphoreType.DMA((2, 4)),
            pltpu.SemaphoreType.DMA((steps,)),
        ],
        compiler_params=HBM_PARAMS,
        cost_estimate=cost(1, amplitudes, order),
    )(state, costate, gates)
    state, costate, sent = lax.optimization_barrier((state, costate, sent))
    moved = lax.all_to_all(sent, "amp", 0, 0, tiled=True)
    early, matrices = pl.pallas_call(
        early_kernel,
        in_specs=[IN_VMEM, IN_VMEM, IN_VMEM],
        out_specs=[IN_VMEM, IN_VMEM],
        out_shape=[
            pltpu.VMEM(sum_shape, jnp.float32),
            pltpu.VMEM((2, 4 * order, 2 * order), jnp.bfloat16),
        ],
        compiler_params=PARAMS,
        cost_estimate=cost(1, amplitudes, order),
    )(state, costate, gates)
    moved = moved.reshape(2, steps, 2, order, lanes)
    last = pl.pallas_call(
        middle_kernel,
        in_specs=[IN_VMEM, IN_VMEM],
        out_specs=IN_HBM,
        out_shape=pltpu.HBM(field_shape, jnp.float32),
        scratch_shapes=[
            pltpu.VMEM((devices * order, lanes), jnp.float32),
            pltpu.VMEM(field_shape, jnp.float32),
            pltpu.SemaphoreType.DMA((2, steps)),
        ],
        compiler_params=PARAMS,
        cost_estimate=cost(2, amplitudes, order),
    )(moved, matrices)
    arrived = lax.all_to_all(last, "amp", 0, 0, tiled=True)
    gradients = pl.pallas_call(
        functools.partial(late_kernel, scale=scale),
        in_specs=[IN_VMEM, IN_VMEM, IN_VMEM, IN_VMEM],
        out_specs=IN_VMEM,
        out_shape=array(gates.shape),
        scratch_shapes=[pltpu.VMEM((3,) + sum_shape, jnp.float32)],
        compiler_params=PARAMS,
        cost_estimate=cost(2, amplitudes, order),
    )(moved, last, early, gates)
    part, arrived = lax.optimization_barrier((scattered_sum(gradients), arrived))
    parts = gathered_chips(part)
    state_rows, costate_rows = pl.pallas_call(
        last_kernel,
        in_specs=[IN_VMEM],
        out_specs=[IN_HBM, IN_HBM],
        out_shape=[array((order, rows, 1, lanes))] * 2,
        scratch_shapes=[
            pltpu.VMEM((2, rows, order, lanes), jnp.float32),
            pltpu.SemaphoreType.DMA((2, rows)),
        ],
        compiler_params=PARAMS,
        cost_estimate=cost(1, amplitudes, order),
    )(arrived)
    for index in range(1, len(parts)):
        parts[index], state_rows = lax.optimization_barrier((parts[index], state_rows))
    gradients = gathered_cores(parts, gates.shape)
    return from_rows(state_rows), from_rows(costate_rows), gradients


def undo_gate(field, gate):
    high = lax.Precision.HIGHEST
    shape = field.shape
    parts = field.reshape(shape[:-1] + (2, 2, -1))
    real, imag = parts[..., 0, :], parts[..., 1, :]

    def contract(matrix, operand):
        return jnp.einsum("ts,btvc->bsvc", matrix, operand, precision=high)

    new_real = contract(gate[0], real) + contract(gate[1], imag)
    new_imag = contract(gate[0], imag) - contract(gate[1], real)
    return jnp.stack([new_real, new_imag], axis=-2).reshape(shape)


def gate_gradient(before, after):
    high = lax.Precision.HIGHEST
    lam = before.reshape(before.shape[:-1] + (2, 2, -1))[..., 1, :, :]
    psi = after.reshape(after.shape[:-1] + (2, 2, -1))[..., 0, :, :]
    real = jnp.einsum("btpc,bspc->ts", lam, psi, precision=high)
    imag = jnp.einsum("btc,bsc->ts", lam[..., 1, :], psi[..., 0, :], precision=high) - jnp.einsum(
        "btc,bsc->ts", lam[..., 0, :], psi[..., 1, :], precision=high
    )
    return jnp.stack([real, imag], axis=0)


def on_device_plain(state, costate, gates, devices, order, columns):
    own = columns // devices
    both = jnp.stack([state, costate], axis=0).reshape(2, 2, order, devices, own)
    field = both.transpose(3, 2, 0, 1, 4).reshape(devices, order, 4 * own)
    field = lax.all_to_all(field, "amp", 0, 0, tiled=True)
    after = undo_gate(field, gates[0])
    terms = [gate_gradient(field, after)]
    field = after.reshape(2, devices // 4, 2, 2, 2, order // 4, 4 * own)
    field = field.transpose(3, 1, 4, 0, 2, 5, 6).reshape(devices, order, 4 * own)
    after = undo_gate(field, gates[1])
    terms.append(gate_gradient(field, after))
    field = after.reshape(devices, order // devices, devices, 4 * own)
    field = field.transpose(2, 1, 0, 3).reshape(devices, order, 4 * own)
    after = undo_gate(field, gates[2])
    terms.append(gate_gradient(field, after))
    terms = jnp.stack(terms, axis=0) / math.sqrt(devices * columns)
    gradients = gathered_cores(gathered_chips(scattered_sum(terms)), gates.shape)
    field = lax.all_to_all(after, "amp", 0, 0, tiled=True)
    field = field.reshape(devices, order, 2, 2, own).transpose(2, 3, 1, 0, 4)
    field = field.reshape(2, 2, order * columns)
    return field[0], field[1], gradients


def on_device(state, costate, gates):
    devices = lax.axis_size("amp")
    order = gates.shape[2]
    columns = state.shape[1] // order
    filled = 4 * columns == 128 * devices and order == 4 * devices
    form = on_device_lanes if filled else on_device_plain
    return form(state, costate, gates, devices, order, columns)


def solution(mesh):
    return jax.shard_map(
        on_device,
        mesh=mesh,
        in_specs=(P(None, "amp"), P(None, "amp"), P()),
        out_specs=(P(None, "amp"), P(None, "amp"), P()),
        check_vma=False,
    )
```

```python
import functools
import math

import jax
import jax.numpy as jnp
from jax import lax
from jax.experimental import pallas as pl
from jax.experimental.pallas import tpu as pltpu
from jax.sharding import PartitionSpec as P

VMEM_BYTES = 12 * 1024 * 1024


def split(value):
    high = value.astype(jnp.bfloat16)
    low = (value - high.astype(jnp.float32)).astype(jnp.bfloat16)
    return high, low


def both_parts(value):
    return jnp.concatenate(split(value), axis=0)


def left_parts(both):
    rows = both.shape[0] // 2
    high, low = both[:rows], both[rows:]
    return jnp.concatenate([high, low, high], axis=1)


def dot_parts(left, right):
    high, low = split(right)
    return jnp.dot(
        left_parts(left),
        jnp.concatenate([high, high, low], axis=0),
        preferred_element_type=jnp.float32,
    )


def dot_parts_rows(left, right):
    high, low = split(right)
    return lax.dot_general(
        left_parts(left),
        jnp.concatenate([high, high, low], axis=1),
        (((1,), (1,)), ((), ())),
        preferred_element_type=jnp.float32,
    )


def lane_index(shape):
    return lax.broadcasted_iota(jnp.int32, shape, len(shape) - 1)


def swap_groups(values):
    lanes = values[0].shape[-1]
    group = lane_index(values[0].shape) // (lanes // 4)
    for bit in (2, 1):
        width = bit * (lanes // 4)
        fresh = list(values)
        for index in range(4):
            if index & bit == 0:
                low, high = values[index], values[index | bit]
                upper = group & bit != 0
                fresh[index] = jnp.where(upper, pltpu.roll(high, width, 1), low)
                fresh[index | bit] = jnp.where(upper, high, pltpu.roll(low, lanes - width, 1))
        values = fresh
    return values


def swap_bit(low, high):
    lanes = low.shape[-1]
    width = lanes // 4
    upper = (lane_index(low.shape) // width) % 2 == 1
    first = jnp.where(upper, pltpu.roll(high, width, 1), low)
    second = jnp.where(upper, high, pltpu.roll(low, lanes - width, 1))
    return first, second


def row_halves(value, groups):
    rows, lanes = value.shape
    parts = value.reshape(groups, 2, rows // groups // 2, lanes)
    return parts[:, 0].reshape(rows // 2, lanes), parts[:, 1].reshape(rows // 2, lanes)


def wait_all(copies):
    for copy in copies:
        copy.wait()


def undo_matrix(gate):
    real, imag = gate[0].T, gate[1].T
    top = jnp.concatenate([real, imag], axis=1)
    low = jnp.concatenate([-imag, real], axis=1)
    return both_parts(jnp.concatenate([top, low], axis=0))


def column(rows, block, order):
    stride = rows.shape[0] // order
    parts = [rows[pl.ds(block * 2 + part, order, stride=stride), :] for part in range(2)]
    return jnp.concatenate(parts, axis=0)


def first_kernel(
    state_ref, costate_ref, gates_ref, out_ref, gate, rows, field_ref, gate_sem, row_sems, out_sems
):
    order = gate.shape[1]
    lanes = rows.shape[2]
    stride = rows.shape[1] // order
    chunks = row_sems.shape[1]
    chunk = rows.shape[1] // chunks
    copies = [pltpu.make_async_copy(gates_ref.at[0], gate, gate_sem)]
    for index in range(chunks):
        part = pl.ds(index * chunk, chunk)
        for vector, ref in enumerate((state_ref, costate_ref)):
            copies.append(
                pltpu.make_async_copy(ref.at[part], rows.at[vector, part], row_sems.at[vector, index])
            )
    for copy in copies:
        copy.start()
    copies[0].wait()
    matrix = undo_matrix(gate)
    wait_all(copies[1:])

    def column(vector, block):
        parts = [rows[vector, pl.ds(block * 2 + part, order, stride=stride), :] for part in range(2)]
        return jnp.concatenate(parts, axis=0)

    out_copies = []
    for block in range(stride // 2):
        field = jnp.concatenate([column(0, block), column(1, block)], axis=1)
        undone = dot_parts(matrix, field)
        pieces = []
        for vector in range(2):
            pieces += row_halves(undone[:, vector * lanes : (vector + 1) * lanes], 2)
        for index, piece in enumerate(swap_groups(pieces)):
            field_ref[block * 4 + index] = piece
        part = pl.ds(block * 4, 4)
        copy = pltpu.make_async_copy(field_ref.at[part], out_ref.at[part], out_sems.at[block])
        copy.start()
        out_copies.append(copy)
    wait_all(out_copies)


def outer_product(lam, psi):
    order = lam.shape[0] // 2
    left = jnp.concatenate([lam[:order], lam[order:]], axis=1)
    plain = jnp.concatenate([psi[:order], psi[order:]], axis=1)
    other = jnp.concatenate([-psi[order:], psi[:order]], axis=1)
    return dot_parts_rows(both_parts(left), jnp.concatenate([plain, other], axis=0))


def four_products(fields, groups):
    pieces = swap_groups(fields)
    rows, lanes = pieces[0].shape

    def joined(vector):
        parts = [
            piece.reshape(groups, 1, rows // groups, lanes)
            for piece in pieces[2 * vector : 2 * vector + 2]
        ]
        return jnp.concatenate(parts, axis=1).reshape(2 * rows, lanes)

    return outer_product(joined(1), joined(0))


def early_kernel(state_ref, costate_ref, out_ref):
    order = out_ref.shape[0]
    out_ref[...] = jnp.zeros_like(out_ref)

    @pl.loop(0, state_ref.shape[0] // order // 2)
    def _(block):
        out_ref[...] += outer_product(
            column(costate_ref, block, order), column(state_ref, block, order)
        )


def middle_kernel(moved_ref, gates_ref, out_ref, kept, last, sems):
    _, steps, _, order, lanes = moved_ref.shape
    batches = 2 * steps
    copies = []

    def undo(matrix, fields):
        result = dot_parts(matrix, jnp.concatenate(fields, axis=1))
        return [result[:, index * lanes : (index + 1) * lanes] for index in range(len(fields))]

    matrices = [undo_matrix(gates_ref[index + 1]) for index in range(2)]
    for step in range(steps):
        fields = [mixed_rows(moved_ref, step, bit) for bit in range(2)]
        for bit, result in enumerate(undo(matrices[0], fields)):
            for top, piece in enumerate(swap_bit(*row_halves(result, 8))):
                place = (top * steps + step) * 2 + bit
                kept[pl.ds(place * order, order), :] = piece

    for step in range(steps):
        fields = [regrouped(kept, step * 2 + index, order) for index in range(2)]
        for index, result in enumerate(undo(matrices[1], fields)):
            for bit, piece in enumerate(swap_bit(*row_halves(result, 2))):
                last[bit * batches + step * 2 + index] = piece
        for bit in range(2):
            part = pl.ds(bit * batches + step * 2, 2)
            copy = pltpu.make_async_copy(last.at[part], out_ref.at[part], sems.at[bit, step])
            copy.start()
            copies.append(copy)
    wait_all(copies)


def regrouped(kept_ref, batch, order):
    devices = kept_ref.shape[0] // order
    parts = [
        kept_ref[pl.ds(row * (devices // 2) + batch, devices, stride=order), :] for row in range(8)
    ]
    return jnp.concatenate(parts, axis=0)


def mixed_rows(moved_ref, step, bit):
    low_rows = moved_ref.shape[3] // 4
    parts = [
        moved_ref[top, step, low, pl.ds((part * 2 + bit) * low_rows, low_rows), :]
        for part in range(2)
        for top in range(2)
        for low in range(2)
    ]
    return jnp.concatenate(parts, axis=0)


def late_kernel(moved_ref, last_ref, early_ref, gates_ref, out_ref, sum_ref, *, scale):
    order = early_ref.shape[0]
    steps = moved_ref.shape[1]
    sum_ref[0] = early_ref[...]
    sum_ref[1:3] = jnp.zeros((2,) + early_ref.shape, jnp.float32)

    @pl.loop(0, steps)
    def _(step):
        first, second = (mixed_rows(moved_ref, step, bit) for bit in range(2))
        half = first.shape[-1] // 2
        lower = lane_index(first.shape) < half
        psi = jnp.where(lower, first, pltpu.roll(second, half, 1))
        lam = jnp.where(lower, pltpu.roll(first, half, 1), second)
        sum_ref[1] += outer_product(lam, psi)
        sum_ref[2] += four_products([last_ref[step * 4 + index] for index in range(4)], 2)

    for index in range(3):
        total = (sum_ref[index, :, :order], sum_ref[index, :, order:])
        gate = (gates_ref[index, 0], gates_ref[index, 1])
        left, right = (gate, total) if index == 2 else (total, gate)
        out_ref[index, 0], out_ref[index, 1] = complex_product(left, right, scale)


def complex_product(left, right, scale):
    def times(first, second):
        return jnp.dot(
            first, second, precision=lax.Precision.HIGHEST, preferred_element_type=jnp.float32
        )

    real = times(left[0], right[0]) - times(left[1], right[1])
    imag = times(left[0], right[1]) + times(left[1], right[0])
    return real * scale, imag * scale


def last_kernel(moved_ref, state_ref, costate_ref, rows, copy_sems):
    half = moved_ref.shape[1] // 2
    copies = []
    for block in range(rows.shape[1] // 2):
        pieces = swap_groups([moved_ref[block * 4 + index] for index in range(4)])
        for vector, ref in enumerate((state_ref, costate_ref)):
            for part in range(2):
                column = block * 2 + part
                for bit in range(2):
                    piece = pieces[2 * vector + bit][part * half : (part + 1) * half]
                    rows[vector, column, bit * half : (bit + 1) * half] = piece
                copy = pltpu.make_async_copy(
                    rows.at[vector, column], ref.at[:, column, 0], copy_sems.at[vector, column]
                )
                copy.start()
                copies.append(copy)
    wait_all(copies)


def gather_kernel(*refs):
    *part_refs, out_ref, copy_sems = refs
    place = lax.rem(lax.axis_index("amp"), len(part_refs))
    copies = [
        pltpu.make_async_copy(ref, out_ref.at[place ^ index], copy_sems.at[index])
        for index, ref in enumerate(part_refs)
    ]
    for copy in copies:
        copy.start()
    wait_all(copies)


def tree_sum(parts):
    while len(parts) > 1:
        parts = [parts[i] + parts[i + 1] for i in range(0, len(parts), 2)]
    return parts[0]


def exchange(part, distance):
    devices = lax.axis_size("amp")
    return lax.ppermute(part, "amp", [(i, i ^ distance) for i in range(devices)])


def scattered_sum(value):
    devices = lax.axis_size("amp")
    inner = min(8, devices)
    own = lax.axis_index("amp") % inner
    blocks = value.reshape(inner, -1, value.shape[-1])

    def pick(index):
        return lax.dynamic_index_in_dim(blocks, index, 0, keepdims=False)

    part = tree_sum([pick(own)] + [exchange(pick(own ^ k), k) for k in range(1, inner)])
    distance = inner
    while distance < devices:
        part = part + exchange(part, distance)
        distance *= 2
    return part


def gathered_chips(part):
    inner = min(8, lax.axis_size("amp"))
    return [part] + [exchange(part, k) for k in range(2, inner, 2)]


def gathered_cores(own, shape):
    others = [exchange(found, 1) for found in own]
    parts = [found for pair in zip(own, others) for found in pair]
    out = pl.pallas_call(
        gather_kernel,
        in_specs=[pl.BlockSpec(memory_space=pl.ANY)] * len(parts),
        out_specs=IN_HBM,
        out_shape=jax.ShapeDtypeStruct((len(parts),) + parts[0].shape, parts[0].dtype),
        scratch_shapes=[pltpu.SemaphoreType.DMA((len(parts),))],
        compiler_params=PARAMS,
    )(*parts)
    return out.reshape(shape)


def to_rows(field, lanes):
    return field.reshape(2, -1, lanes).swapaxes(0, 1).reshape(-1, lanes)


def from_rows(rows):
    return rows.reshape(-1, 2, rows.shape[-1]).swapaxes(0, 1).reshape(2, -1)


IN_HBM = pl.BlockSpec(memory_space=pltpu.HBM)
IN_VMEM = pl.BlockSpec(memory_space=pltpu.VMEM)
PARAMS = pltpu.CompilerParams(vmem_limit_bytes=VMEM_BYTES)
HBM_PARAMS = pltpu.CompilerParams(vmem_limit_bytes=60 * 1024 * 1024)


def cost(layers, amplitudes, order):
    flops = layers * 3 * 8 * amplitudes * order
    return pl.CostEstimate(flops=flops, bytes_accessed=32 * amplitudes, transcendentals=0)


def on_device_lanes(state, costate, gates, devices, order, columns):
    lanes = 4 * columns // devices
    steps = devices // 4
    rows = 2 * columns // lanes
    scale = 1.0 / math.sqrt(devices * columns)
    field_shape = (devices, order, lanes)
    sum_shape = (order, 2 * order)
    amplitudes = 2 * order * columns

    def array(shape, kind=jnp.float32):
        return jax.ShapeDtypeStruct(shape, kind)

    state, costate = to_rows(state, lanes), to_rows(costate, lanes)
    sent = pl.pallas_call(
        first_kernel,
        in_specs=[IN_HBM, IN_HBM, IN_HBM],
        out_specs=IN_HBM,
        out_shape=array(field_shape),
        scratch_shapes=[
            pltpu.VMEM((2, order, order), jnp.float32),
            pltpu.VMEM((2, rows * order, lanes), jnp.float32),
            pltpu.VMEM(field_shape, jnp.float32),
            pltpu.SemaphoreType.DMA,
            pltpu.SemaphoreType.DMA((2, 4)),
            pltpu.SemaphoreType.DMA((steps,)),
        ],
        compiler_params=HBM_PARAMS,
        cost_estimate=cost(1, amplitudes, order),
    )(state, costate, gates)
    state, costate, sent = lax.optimization_barrier((state, costate, sent))
    moved = lax.all_to_all(sent, "amp", 0, 0, tiled=True)
    early = pl.pallas_call(
        early_kernel,
        in_specs=[IN_VMEM, IN_VMEM],
        out_specs=IN_VMEM,
        out_shape=array(sum_shape),
        compiler_params=PARAMS,
        cost_estimate=cost(1, amplitudes, order),
    )(state, costate)
    moved = moved.reshape(2, steps, 2, order, lanes)
    last = pl.pallas_call(
        middle_kernel,
        in_specs=[IN_VMEM, IN_VMEM],
        out_specs=IN_HBM,
        out_shape=pltpu.HBM(field_shape, jnp.float32),
        scratch_shapes=[
            pltpu.VMEM((devices * order, lanes), jnp.float32),
            pltpu.VMEM(field_shape, jnp.float32),
            pltpu.SemaphoreType.DMA((2, steps)),
        ],
        compiler_params=PARAMS,
        cost_estimate=cost(2, amplitudes, order),
    )(moved, gates)
    arrived = lax.all_to_all(last, "amp", 0, 0, tiled=True)
    gradients = pl.pallas_call(
        functools.partial(late_kernel, scale=scale),
        in_specs=[IN_VMEM, IN_VMEM, IN_VMEM, IN_VMEM],
        out_specs=IN_VMEM,
        out_shape=array(gates.shape),
        scratch_shapes=[pltpu.VMEM((3,) + sum_shape, jnp.float32)],
        compiler_params=PARAMS,
        cost_estimate=cost(2, amplitudes, order),
    )(moved, last, early, gates)
    part, arrived = lax.optimization_barrier((scattered_sum(gradients), arrived))
    parts = gathered_chips(part)
    state_rows, costate_rows = pl.pallas_call(
        last_kernel,
        in_specs=[IN_VMEM],
        out_specs=[IN_HBM, IN_HBM],
        out_shape=[array((order, rows, 1, lanes))] * 2,
        scratch_shapes=[
            pltpu.VMEM((2, rows, order, lanes), jnp.float32),
            pltpu.SemaphoreType.DMA((2, rows)),
        ],
        compiler_params=PARAMS,
        cost_estimate=cost(1, amplitudes, order),
    )(arrived)
    for index in range(1, len(parts)):
        parts[index], state_rows = lax.optimization_barrier((parts[index], state_rows))
    gradients = gathered_cores(parts, gates.shape)
    return from_rows(state_rows), from_rows(costate_rows), gradients


def undo_gate(field, gate):
    high = lax.Precision.HIGHEST
    shape = field.shape
    parts = field.reshape(shape[:-1] + (2, 2, -1))
    real, imag = parts[..., 0, :], parts[..., 1, :]

    def contract(matrix, operand):
        return jnp.einsum("ts,btvc->bsvc", matrix, operand, precision=high)

    new_real = contract(gate[0], real) + contract(gate[1], imag)
    new_imag = contract(gate[0], imag) - contract(gate[1], real)
    return jnp.stack([new_real, new_imag], axis=-2).reshape(shape)


def gate_gradient(before, after):
    high = lax.Precision.HIGHEST
    lam = before.reshape(before.shape[:-1] + (2, 2, -1))[..., 1, :, :]
    psi = after.reshape(after.shape[:-1] + (2, 2, -1))[..., 0, :, :]
    real = jnp.einsum("btpc,bspc->ts", lam, psi, precision=high)
    imag = jnp.einsum("btc,bsc->ts", lam[..., 1, :], psi[..., 0, :], precision=high) - jnp.einsum(
        "btc,bsc->ts", lam[..., 0, :], psi[..., 1, :], precision=high
    )
    return jnp.stack([real, imag], axis=0)


def on_device_plain(state, costate, gates, devices, order, columns):
    own = columns // devices
    both = jnp.stack([state, costate], axis=0).reshape(2, 2, order, devices, own)
    field = both.transpose(3, 2, 0, 1, 4).reshape(devices, order, 4 * own)
    field = lax.all_to_all(field, "amp", 0, 0, tiled=True)
    after = undo_gate(field, gates[0])
    terms = [gate_gradient(field, after)]
    field = after.reshape(2, devices // 4, 2, 2, 2, order // 4, 4 * own)
    field = field.transpose(3, 1, 4, 0, 2, 5, 6).reshape(devices, order, 4 * own)
    after = undo_gate(field, gates[1])
    terms.append(gate_gradient(field, after))
    field = after.reshape(devices, order // devices, devices, 4 * own)
    field = field.transpose(2, 1, 0, 3).reshape(devices, order, 4 * own)
    after = undo_gate(field, gates[2])
    terms.append(gate_gradient(field, after))
    terms = jnp.stack(terms, axis=0) / math.sqrt(devices * columns)
    gradients = gathered_cores(gathered_chips(scattered_sum(terms)), gates.shape)
    field = lax.all_to_all(after, "amp", 0, 0, tiled=True)
    field = field.reshape(devices, order, 2, 2, own).transpose(2, 3, 1, 0, 4)
    field = field.reshape(2, 2, order * columns)
    return field[0], field[1], gradients


def on_device(state, costate, gates):
    devices = lax.axis_size("amp")
    order = gates.shape[2]
    columns = state.shape[1] // order
    filled = 4 * columns == 128 * devices and order == 4 * devices
    form = on_device_lanes if filled else on_device_plain
    return form(state, costate, gates, devices, order, columns)


def solution(mesh):
    return jax.shard_map(
        on_device,
        mesh=mesh,
        in_specs=(P(None, "amp"), P(None, "amp"), P()),
        out_specs=(P(None, "amp"), P(None, "amp"), P()),
        check_vma=False,
    )
```

```python
import functools
import math

import jax
import jax.numpy as jnp
from jax import lax
from jax.experimental import pallas as pl
from jax.experimental.pallas import tpu as pltpu
from jax.sharding import PartitionSpec as P

VMEM_BYTES = 12 * 1024 * 1024


def split(value):
    high = value.astype(jnp.bfloat16)
    low = (value - high.astype(jnp.float32)).astype(jnp.bfloat16)
    return high, low


def both_parts(value):
    return jnp.concatenate(split(value), axis=0)


def left_parts(both):
    rows = both.shape[0] // 2
    high, low = both[:rows], both[rows:]
    return jnp.concatenate([high, low, high], axis=1)


def dot_parts(left, right):
    high, low = split(right)
    return jnp.dot(
        left_parts(left),
        jnp.concatenate([high, high, low], axis=0),
        preferred_element_type=jnp.float32,
    )


def dot_parts_rows(left, right):
    high, low = split(right)
    return lax.dot_general(
        left_parts(left),
        jnp.concatenate([high, high, low], axis=1),
        (((1,), (1,)), ((), ())),
        preferred_element_type=jnp.float32,
    )


def lane_index(shape):
    return lax.broadcasted_iota(jnp.int32, shape, len(shape) - 1)


def swap_groups(values):
    lanes = values[0].shape[-1]
    group = lane_index(values[0].shape) // (lanes // 4)
    for bit in (2, 1):
        width = bit * (lanes // 4)
        fresh = list(values)
        for index in range(4):
            if index & bit == 0:
                low, high = values[index], values[index | bit]
                upper = group & bit != 0
                fresh[index] = jnp.where(upper, pltpu.roll(high, width, 1), low)
                fresh[index | bit] = jnp.where(upper, high, pltpu.roll(low, lanes - width, 1))
        values = fresh
    return values


def swap_bit(low, high):
    lanes = low.shape[-1]
    width = lanes // 4
    upper = (lane_index(low.shape) // width) % 2 == 1
    first = jnp.where(upper, pltpu.roll(high, width, 1), low)
    second = jnp.where(upper, high, pltpu.roll(low, lanes - width, 1))
    return first, second


def row_halves(value, groups):
    rows, lanes = value.shape
    parts = value.reshape(groups, 2, rows // groups // 2, lanes)
    return parts[:, 0].reshape(rows // 2, lanes), parts[:, 1].reshape(rows // 2, lanes)


def wait_all(copies):
    for copy in copies:
        copy.wait()


def undo_matrix(gate):
    real, imag = gate[0].T, gate[1].T
    top = jnp.concatenate([real, imag], axis=1)
    low = jnp.concatenate([-imag, real], axis=1)
    return both_parts(jnp.concatenate([top, low], axis=0))


def column(rows, block, order):
    stride = rows.shape[0] // order
    parts = [rows[pl.ds(block * 2 + part, order, stride=stride), :] for part in range(2)]
    return jnp.concatenate(parts, axis=0)


def first_kernel(
    state_ref, costate_ref, gates_ref, out_ref, gate, rows, field_ref, gate_sem, row_sems, out_sems
):
    order = gate.shape[1]
    lanes = rows.shape[2]
    stride = rows.shape[1] // order
    chunks = row_sems.shape[1]
    chunk = rows.shape[1] // chunks
    copies = [pltpu.make_async_copy(gates_ref.at[0], gate, gate_sem)]
    for index in range(chunks):
        part = pl.ds(index * chunk, chunk)
        for vector, ref in enumerate((state_ref, costate_ref)):
            copies.append(
                pltpu.make_async_copy(ref.at[part], rows.at[vector, part], row_sems.at[vector, index])
            )
    for copy in copies:
        copy.start()
    copies[0].wait()
    matrix = undo_matrix(gate)
    wait_all(copies[1:])

    def column(vector, block):
        parts = [rows[vector, pl.ds(block * 2 + part, order, stride=stride), :] for part in range(2)]
        return jnp.concatenate(parts, axis=0)

    out_copies = []
    for block in range(stride // 2):
        field = jnp.concatenate([column(0, block), column(1, block)], axis=1)
        undone = dot_parts(matrix, field)
        pieces = []
        for vector in range(2):
            pieces += row_halves(undone[:, vector * lanes : (vector + 1) * lanes], 2)
        for index, piece in enumerate(swap_groups(pieces)):
            field_ref[block * 4 + index] = piece
        part = pl.ds(block * 4, 4)
        copy = pltpu.make_async_copy(field_ref.at[part], out_ref.at[part], out_sems.at[block])
        copy.start()
        out_copies.append(copy)
    wait_all(out_copies)


def outer_product(lam, psi):
    order = lam.shape[0] // 2
    left = jnp.concatenate([lam[:order], lam[order:]], axis=1)
    plain = jnp.concatenate([psi[:order], psi[order:]], axis=1)
    other = jnp.concatenate([-psi[order:], psi[:order]], axis=1)
    return dot_parts_rows(both_parts(left), jnp.concatenate([plain, other], axis=0))


def four_products(fields, groups):
    pieces = swap_groups(fields)
    rows, lanes = pieces[0].shape

    def joined(vector):
        parts = [
            piece.reshape(groups, 1, rows // groups, lanes)
            for piece in pieces[2 * vector : 2 * vector + 2]
        ]
        return jnp.concatenate(parts, axis=1).reshape(2 * rows, lanes)

    return outer_product(joined(1), joined(0))


def early_kernel(state_ref, costate_ref, out_ref):
    order = out_ref.shape[0]
    out_ref[...] = jnp.zeros_like(out_ref)

    @pl.loop(0, state_ref.shape[0] // order // 2)
    def _(block):
        out_ref[...] += outer_product(
            column(costate_ref, block, order), column(state_ref, block, order)
        )


def middle_kernel(moved_ref, gates_ref, out_ref, kept, last, sems):
    _, steps, _, order, lanes = moved_ref.shape
    batches = 2 * steps
    copies = []

    def undo(matrix, fields):
        result = dot_parts(matrix, jnp.concatenate(fields, axis=1))
        return [result[:, index * lanes : (index + 1) * lanes] for index in range(len(fields))]

    matrices = [undo_matrix(gates_ref[index + 1]) for index in range(2)]
    for step in range(steps):
        fields = [mixed_rows(moved_ref, step, bit) for bit in range(2)]
        for bit, result in enumerate(undo(matrices[0], fields)):
            for top, piece in enumerate(swap_bit(*row_halves(result, 8))):
                place = (top * steps + step) * 2 + bit
                kept[pl.ds(place * order, order), :] = piece

    for step in range(steps):
        fields = [regrouped(kept, step * 2 + index, order) for index in range(2)]
        for index, result in enumerate(undo(matrices[1], fields)):
            for bit, piece in enumerate(swap_bit(*row_halves(result, 2))):
                last[2 * batches - 1 - (bit * batches + step * 2 + index)] = piece
        for bit in range(2):
            part = pl.ds(2 * batches - 2 - (bit * batches + step * 2), 2)
            copy = pltpu.make_async_copy(last.at[part], out_ref.at[part], sems.at[bit, step])
            copy.start()
            copies.append(copy)
    wait_all(copies)


def regrouped(kept_ref, batch, order):
    devices = kept_ref.shape[0] // order
    parts = [
        kept_ref[pl.ds(row * (devices // 2) + batch, devices, stride=order), :] for row in range(8)
    ]
    return jnp.concatenate(parts, axis=0)


def mixed_rows(moved_ref, step, bit):
    low_rows = moved_ref.shape[3] // 4
    last_step = moved_ref.shape[1] - 1
    parts = [
        moved_ref[1 - top, last_step - step, 1 - low, pl.ds((part * 2 + bit) * low_rows, low_rows), :]
        for part in range(2)
        for top in range(2)
        for low in range(2)
    ]
    return jnp.concatenate(parts, axis=0)


def late_kernel(moved_ref, last_ref, early_ref, gates_ref, out_ref, sum_ref, *, scale):
    order = early_ref.shape[0]
    steps = moved_ref.shape[1]
    sum_ref[0] = early_ref[...]
    sum_ref[1:3] = jnp.zeros((2,) + early_ref.shape, jnp.float32)

    @pl.loop(0, steps)
    def _(step):
        first, second = (mixed_rows(moved_ref, step, bit) for bit in range(2))
        half = first.shape[-1] // 2
        lower = lane_index(first.shape) < half
        psi = jnp.where(lower, first, pltpu.roll(second, half, 1))
        lam = jnp.where(lower, pltpu.roll(first, half, 1), second)
        sum_ref[1] += outer_product(lam, psi)
        sum_ref[2] += four_products([last_ref[step * 4 + index] for index in range(4)], 2)

    for index in range(3):
        total = (sum_ref[index, :, :order], sum_ref[index, :, order:])
        gate = (gates_ref[index, 0], gates_ref[index, 1])
        left, right = (gate, total) if index == 2 else (total, gate)
        out_ref[index, 0], out_ref[index, 1] = complex_product(left, right, scale)


def complex_product(left, right, scale):
    def times(first, second):
        return jnp.dot(
            first, second, precision=lax.Precision.HIGHEST, preferred_element_type=jnp.float32
        )

    real = times(left[0], right[0]) - times(left[1], right[1])
    imag = times(left[0], right[1]) + times(left[1], right[0])
    return real * scale, imag * scale


def last_kernel(moved_ref, state_ref, costate_ref, rows, copy_sems):
    half = moved_ref.shape[1] // 2
    copies = []
    for block in range(rows.shape[1] // 2):
        pieces = swap_groups([moved_ref[block * 4 + index] for index in range(4)])
        for vector, ref in enumerate((state_ref, costate_ref)):
            for part in range(2):
                column = block * 2 + part
                for bit in range(2):
                    piece = pieces[2 * vector + bit][part * half : (part + 1) * half]
                    rows[vector, column, bit * half : (bit + 1) * half] = piece
                copy = pltpu.make_async_copy(
                    rows.at[vector, column], ref.at[:, column, 0], copy_sems.at[vector, column]
                )
                copy.start()
                copies.append(copy)
    wait_all(copies)


def gather_kernel(*refs):
    *part_refs, out_ref, copy_sems = refs
    place = lax.rem(lax.axis_index("amp"), len(part_refs))
    copies = [
        pltpu.make_async_copy(ref, out_ref.at[place ^ index], copy_sems.at[index])
        for index, ref in enumerate(part_refs)
    ]
    for copy in copies:
        copy.start()
    wait_all(copies)


def tree_sum(parts):
    while len(parts) > 1:
        parts = [parts[i] + parts[i + 1] for i in range(0, len(parts), 2)]
    return parts[0]


def exchange_all(field):
    group = list(reversed(range(lax.axis_size("amp"))))
    return lax.all_to_all(field, "amp", 0, 0, axis_index_groups=[group], tiled=True)


def exchange(part, distance):
    devices = lax.axis_size("amp")
    return lax.ppermute(part, "amp", [(i, i ^ distance) for i in range(devices)])


def scattered_sum(value):
    devices = lax.axis_size("amp")
    inner = min(8, devices)
    own = lax.axis_index("amp") % inner
    blocks = value.reshape(inner, -1, value.shape[-1])

    def pick(index):
        return lax.dynamic_index_in_dim(blocks, index, 0, keepdims=False)

    part = tree_sum([pick(own)] + [exchange(pick(own ^ k), k) for k in range(1, inner)])
    distance = inner
    while distance < devices:
        part = part + exchange(part, distance)
        distance *= 2
    return part


def gathered_chips(part):
    inner = min(8, lax.axis_size("amp"))
    return [part] + [exchange(part, k) for k in range(2, inner, 2)]


def gathered_cores(own, shape):
    others = [exchange(found, 1) for found in own]
    parts = [found for pair in zip(own, others) for found in pair]
    out = pl.pallas_call(
        gather_kernel,
        in_specs=[pl.BlockSpec(memory_space=pl.ANY)] * len(parts),
        out_specs=IN_HBM,
        out_shape=jax.ShapeDtypeStruct((len(parts),) + parts[0].shape, parts[0].dtype),
        scratch_shapes=[pltpu.SemaphoreType.DMA((len(parts),))],
        compiler_params=PARAMS,
    )(*parts)
    return out.reshape(shape)


def to_rows(field, lanes):
    return field.reshape(2, -1, lanes).swapaxes(0, 1).reshape(-1, lanes)


def from_rows(rows):
    return rows.reshape(-1, 2, rows.shape[-1]).swapaxes(0, 1).reshape(2, -1)


IN_HBM = pl.BlockSpec(memory_space=pltpu.HBM)
IN_VMEM = pl.BlockSpec(memory_space=pltpu.VMEM)
PARAMS = pltpu.CompilerParams(vmem_limit_bytes=VMEM_BYTES)
HBM_PARAMS = pltpu.CompilerParams(vmem_limit_bytes=60 * 1024 * 1024)


def cost(layers, amplitudes, order):
    flops = layers * 3 * 8 * amplitudes * order
    return pl.CostEstimate(flops=flops, bytes_accessed=32 * amplitudes, transcendentals=0)


def on_device_lanes(state, costate, gates, devices, order, columns):
    lanes = 4 * columns // devices
    steps = devices // 4
    rows = 2 * columns // lanes
    scale = 1.0 / math.sqrt(devices * columns)
    field_shape = (devices, order, lanes)
    sum_shape = (order, 2 * order)
    amplitudes = 2 * order * columns

    def array(shape, kind=jnp.float32):
        return jax.ShapeDtypeStruct(shape, kind)

    state, costate = to_rows(state, lanes), to_rows(costate, lanes)
    sent = pl.pallas_call(
        first_kernel,
        in_specs=[IN_HBM, IN_HBM, IN_HBM],
        out_specs=IN_HBM,
        out_shape=array(field_shape),
        scratch_shapes=[
            pltpu.VMEM((2, order, order), jnp.float32),
            pltpu.VMEM((2, rows * order, lanes), jnp.float32),
            pltpu.VMEM(field_shape, jnp.float32),
            pltpu.SemaphoreType.DMA,
            pltpu.SemaphoreType.DMA((2, 4)),
            pltpu.SemaphoreType.DMA((steps,)),
        ],
        compiler_params=HBM_PARAMS,
        cost_estimate=cost(1, amplitudes, order),
    )(state, costate, gates)
    state, costate, sent = lax.optimization_barrier((state, costate, sent))
    moved = exchange_all(sent)
    early = pl.pallas_call(
        early_kernel,
        in_specs=[IN_VMEM, IN_VMEM],
        out_specs=IN_VMEM,
        out_shape=array(sum_shape),
        compiler_params=PARAMS,
        cost_estimate=cost(1, amplitudes, order),
    )(state, costate)
    moved = moved.reshape(2, steps, 2, order, lanes)
    last = pl.pallas_call(
        middle_kernel,
        in_specs=[IN_VMEM, IN_VMEM],
        out_specs=IN_HBM,
        out_shape=pltpu.HBM(field_shape, jnp.float32),
        scratch_shapes=[
            pltpu.VMEM((devices * order, lanes), jnp.float32),
            pltpu.VMEM(field_shape, jnp.float32),
            pltpu.SemaphoreType.DMA((2, steps)),
        ],
        compiler_params=PARAMS,
        cost_estimate=cost(2, amplitudes, order),
    )(moved, gates)
    arrived = exchange_all(last)
    gradients = pl.pallas_call(
        functools.partial(late_kernel, scale=scale),
        in_specs=[IN_VMEM, IN_VMEM, IN_VMEM, IN_VMEM],
        out_specs=IN_VMEM,
        out_shape=array(gates.shape),
        scratch_shapes=[pltpu.VMEM((3,) + sum_shape, jnp.float32)],
        compiler_params=PARAMS,
        cost_estimate=cost(2, amplitudes, order),
    )(moved, last, early, gates)
    part, arrived = lax.optimization_barrier((scattered_sum(gradients), arrived))
    parts = gathered_chips(part)
    state_rows, costate_rows = pl.pallas_call(
        last_kernel,
        in_specs=[IN_VMEM],
        out_specs=[IN_HBM, IN_HBM],
        out_shape=[array((order, rows, 1, lanes))] * 2,
        scratch_shapes=[
            pltpu.VMEM((2, rows, order, lanes), jnp.float32),
            pltpu.SemaphoreType.DMA((2, rows)),
        ],
        compiler_params=PARAMS,
        cost_estimate=cost(1, amplitudes, order),
    )(arrived)
    for index in range(1, len(parts)):
        parts[index], state_rows = lax.optimization_barrier((parts[index], state_rows))
    gradients = gathered_cores(parts, gates.shape)
    return from_rows(state_rows), from_rows(costate_rows), gradients


def undo_gate(field, gate):
    high = lax.Precision.HIGHEST
    shape = field.shape
    parts = field.reshape(shape[:-1] + (2, 2, -1))
    real, imag = parts[..., 0, :], parts[..., 1, :]

    def contract(matrix, operand):
        return jnp.einsum("ts,btvc->bsvc", matrix, operand, precision=high)

    new_real = contract(gate[0], real) + contract(gate[1], imag)
    new_imag = contract(gate[0], imag) - contract(gate[1], real)
    return jnp.stack([new_real, new_imag], axis=-2).reshape(shape)


def gate_gradient(before, after):
    high = lax.Precision.HIGHEST
    lam = before.reshape(before.shape[:-1] + (2, 2, -1))[..., 1, :, :]
    psi = after.reshape(after.shape[:-1] + (2, 2, -1))[..., 0, :, :]
    real = jnp.einsum("btpc,bspc->ts", lam, psi, precision=high)
    imag = jnp.einsum("btc,bsc->ts", lam[..., 1, :], psi[..., 0, :], precision=high) - jnp.einsum(
        "btc,bsc->ts", lam[..., 0, :], psi[..., 1, :], precision=high
    )
    return jnp.stack([real, imag], axis=0)


def on_device_plain(state, costate, gates, devices, order, columns):
    own = columns // devices
    both = jnp.stack([state, costate], axis=0).reshape(2, 2, order, devices, own)
    field = both.transpose(3, 2, 0, 1, 4).reshape(devices, order, 4 * own)
    field = lax.all_to_all(field, "amp", 0, 0, tiled=True)
    after = undo_gate(field, gates[0])
    terms = [gate_gradient(field, after)]
    field = after.reshape(2, devices // 4, 2, 2, 2, order // 4, 4 * own)
    field = field.transpose(3, 1, 4, 0, 2, 5, 6).reshape(devices, order, 4 * own)
    after = undo_gate(field, gates[1])
    terms.append(gate_gradient(field, after))
    field = after.reshape(devices, order // devices, devices, 4 * own)
    field = field.transpose(2, 1, 0, 3).reshape(devices, order, 4 * own)
    after = undo_gate(field, gates[2])
    terms.append(gate_gradient(field, after))
    terms = jnp.stack(terms, axis=0) / math.sqrt(devices * columns)
    gradients = gathered_cores(gathered_chips(scattered_sum(terms)), gates.shape)
    field = lax.all_to_all(after, "amp", 0, 0, tiled=True)
    field = field.reshape(devices, order, 2, 2, own).transpose(2, 3, 1, 0, 4)
    field = field.reshape(2, 2, order * columns)
    return field[0], field[1], gradients


def on_device(state, costate, gates):
    devices = lax.axis_size("amp")
    order = gates.shape[2]
    columns = state.shape[1] // order
    filled = 4 * columns == 128 * devices and order == 4 * devices
    form = on_device_lanes if filled else on_device_plain
    return form(state, costate, gates, devices, order, columns)


def solution(mesh):
    return jax.shard_map(
        on_device,
        mesh=mesh,
        in_specs=(P(None, "amp"), P(None, "amp"), P()),
        out_specs=(P(None, "amp"), P(None, "amp"), P()),
        check_vma=False,
    )
```

```python
import functools
import math

import jax
import jax.numpy as jnp
from jax import lax
from jax.experimental import pallas as pl
from jax.experimental.pallas import tpu as pltpu
from jax.sharding import PartitionSpec as P

VMEM_BYTES = 12 * 1024 * 1024


def split(value):
    high = value.astype(jnp.bfloat16)
    low = (value - high.astype(jnp.float32)).astype(jnp.bfloat16)
    return high, low


def both_parts(value):
    return jnp.concatenate(split(value), axis=0)


def left_parts(both):
    rows = both.shape[0] // 2
    high, low = both[:rows], both[rows:]
    return jnp.concatenate([high, low, high], axis=1)


def dot_parts(left, right):
    high, low = split(right)
    return jnp.dot(
        left_parts(left),
        jnp.concatenate([high, high, low], axis=0),
        preferred_element_type=jnp.float32,
    )


def dot_parts_rows(left, right):
    high, low = split(right)
    return lax.dot_general(
        left_parts(left),
        jnp.concatenate([high, high, low], axis=1),
        (((1,), (1,)), ((), ())),
        preferred_element_type=jnp.float32,
    )


def lane_index(shape):
    return lax.broadcasted_iota(jnp.int32, shape, len(shape) - 1)


def swap_groups(values):
    lanes = values[0].shape[-1]
    group = lane_index(values[0].shape) // (lanes // 4)
    for bit in (2, 1):
        width = bit * (lanes // 4)
        fresh = list(values)
        for index in range(4):
            if index & bit == 0:
                low, high = values[index], values[index | bit]
                upper = group & bit != 0
                fresh[index] = jnp.where(upper, pltpu.roll(high, width, 1), low)
                fresh[index | bit] = jnp.where(upper, high, pltpu.roll(low, lanes - width, 1))
        values = fresh
    return values


def swap_bit(low, high):
    lanes = low.shape[-1]
    width = lanes // 4
    upper = (lane_index(low.shape) // width) % 2 == 1
    first = jnp.where(upper, pltpu.roll(high, width, 1), low)
    second = jnp.where(upper, high, pltpu.roll(low, lanes - width, 1))
    return first, second


def row_halves(value, groups):
    rows, lanes = value.shape
    parts = value.reshape(groups, 2, rows // groups // 2, lanes)
    return parts[:, 0].reshape(rows // 2, lanes), parts[:, 1].reshape(rows // 2, lanes)


def wait_all(copies):
    for copy in copies:
        copy.wait()


def undo_matrix(gate):
    real, imag = gate[0].T, gate[1].T
    top = jnp.concatenate([real, imag], axis=1)
    low = jnp.concatenate([-imag, real], axis=1)
    return both_parts(jnp.concatenate([top, low], axis=0))


def column(rows, block, order):
    stride = rows.shape[0] // order
    parts = [rows[pl.ds(block * 2 + part, order, stride=stride), :] for part in range(2)]
    return jnp.concatenate(parts, axis=0)


def first_kernel(
    state_ref, costate_ref, gates_ref, out_ref, gate, rows, field_ref, gate_sem, row_sems, out_sems
):
    order = gate.shape[1]
    lanes = rows.shape[2]
    stride = rows.shape[1] // order
    chunks = row_sems.shape[1]
    chunk = rows.shape[1] // chunks
    copies = [pltpu.make_async_copy(gates_ref.at[0], gate, gate_sem)]
    for index in range(chunks):
        part = pl.ds(index * chunk, chunk)
        for vector, ref in enumerate((state_ref, costate_ref)):
            copies.append(
                pltpu.make_async_copy(ref.at[part], rows.at[vector, part], row_sems.at[vector, index])
            )
    for copy in copies:
        copy.start()
    copies[0].wait()
    matrix = undo_matrix(gate)
    wait_all(copies[1:])

    def column(vector, block):
        parts = [rows[vector, pl.ds(block * 2 + part, order, stride=stride), :] for part in range(2)]
        return jnp.concatenate(parts, axis=0)

    out_copies = []
    for block in range(stride // 2):
        field = jnp.concatenate([column(0, block), column(1, block)], axis=1)
        undone = dot_parts(matrix, field)
        pieces = []
        for vector in range(2):
            pieces += row_halves(undone[:, vector * lanes : (vector + 1) * lanes], 2)
        for index, piece in enumerate(swap_groups(pieces)):
            field_ref[block * 4 + index] = piece
        part = pl.ds(block * 4, 4)
        copy = pltpu.make_async_copy(field_ref.at[part], out_ref.at[part], out_sems.at[block])
        copy.start()
        out_copies.append(copy)
    wait_all(out_copies)


def outer_product(lam, psi):
    order = lam.shape[0] // 2
    left = jnp.concatenate([lam[:order], lam[order:]], axis=1)
    plain = jnp.concatenate([psi[:order], psi[order:]], axis=1)
    other = jnp.concatenate([-psi[order:], psi[:order]], axis=1)
    return dot_parts_rows(both_parts(left), jnp.concatenate([plain, other], axis=0))


def four_products(fields, groups):
    pieces = swap_groups(fields)
    rows, lanes = pieces[0].shape

    def joined(vector):
        parts = [
            piece.reshape(groups, 1, rows // groups, lanes)
            for piece in pieces[2 * vector : 2 * vector + 2]
        ]
        return jnp.concatenate(parts, axis=1).reshape(2 * rows, lanes)

    return outer_product(joined(1), joined(0))


def early_kernel(state_ref, costate_ref, out_ref):
    order = out_ref.shape[0]
    out_ref[...] = jnp.zeros_like(out_ref)

    @pl.loop(0, state_ref.shape[0] // order // 2)
    def _(block):
        out_ref[...] += outer_product(
            column(costate_ref, block, order), column(state_ref, block, order)
        )


def middle_kernel(moved_ref, gates_ref, out_ref, kept, last, sems):
    _, steps, _, order, lanes = moved_ref.shape
    batches = 2 * steps
    copies = []

    def undo(matrix, fields):
        result = dot_parts(matrix, jnp.concatenate(fields, axis=1))
        return [result[:, index * lanes : (index + 1) * lanes] for index in range(len(fields))]

    matrices = [undo_matrix(gates_ref[index + 1]) for index in range(2)]
    for step in range(steps):
        fields = [mixed_rows(moved_ref, step, bit) for bit in range(2)]
        for bit, result in enumerate(undo(matrices[0], fields)):
            for top, piece in enumerate(swap_bit(*row_halves(result, 8))):
                place = (top * steps + step) * 2 + bit
                kept[pl.ds(place * order, order), :] = piece

    for step in range(steps):
        fields = [regrouped(kept, step * 2 + index, order) for index in range(2)]
        for index, result in enumerate(undo(matrices[1], fields)):
            for bit, piece in enumerate(swap_bit(*row_halves(result, 2))):
                last[bit * batches + step * 2 + index] = piece
        for bit in range(2):
            part = pl.ds(bit * batches + step * 2, 2)
            copy = pltpu.make_async_copy(last.at[part], out_ref.at[part], sems.at[bit, step])
            copy.start()
            copies.append(copy)
    wait_all(copies)


def regrouped(kept_ref, batch, order):
    devices = kept_ref.shape[0] // order
    parts = [
        kept_ref[pl.ds(row * (devices // 2) + batch, devices, stride=order), :] for row in range(8)
    ]
    return jnp.concatenate(parts, axis=0)


def mixed_rows(moved_ref, step, bit):
    low_rows = moved_ref.shape[3] // 4
    parts = [
        moved_ref[top, step, low, pl.ds((part * 2 + bit) * low_rows, low_rows), :]
        for part in range(2)
        for top in range(2)
        for low in range(2)
    ]
    return jnp.concatenate(parts, axis=0)


def late_kernel(moved_ref, last_ref, early_ref, gates_ref, out_ref, sum_ref, *, scale):
    order = early_ref.shape[0]
    steps = moved_ref.shape[1]
    sum_ref[0] = early_ref[...]
    sum_ref[1:3] = jnp.zeros((2,) + early_ref.shape, jnp.float32)

    @pl.loop(0, steps)
    def _(step):
        first, second = (mixed_rows(moved_ref, step, bit) for bit in range(2))
        half = first.shape[-1] // 2
        lower = lane_index(first.shape) < half
        psi = jnp.where(lower, first, pltpu.roll(second, half, 1))
        lam = jnp.where(lower, pltpu.roll(first, half, 1), second)
        sum_ref[1] += outer_product(lam, psi)
        sum_ref[2] += four_products([last_ref[step * 4 + index] for index in range(4)], 2)

    for index in range(3):
        total = (sum_ref[index, :, :order], sum_ref[index, :, order:])
        gate = (gates_ref[index, 0], gates_ref[index, 1])
        left, right = (gate, total) if index == 2 else (total, gate)
        out_ref[index, 0], out_ref[index, 1] = complex_product(left, right, scale)


def complex_product(left, right, scale):
    def times(first, second):
        return jnp.dot(
            first, second, precision=lax.Precision.HIGHEST, preferred_element_type=jnp.float32
        )

    real = times(left[0], right[0]) - times(left[1], right[1])
    imag = times(left[0], right[1]) + times(left[1], right[0])
    return real * scale, imag * scale


def last_kernel(moved_ref, state_ref, costate_ref, rows, copy_sems):
    half = moved_ref.shape[1] // 2
    copies = []
    for block in range(rows.shape[1] // 2):
        pieces = swap_groups([moved_ref[block * 4 + index] for index in range(4)])
        for vector, ref in enumerate((state_ref, costate_ref)):
            for part in range(2):
                column = block * 2 + part
                for bit in range(2):
                    piece = pieces[2 * vector + bit][part * half : (part + 1) * half]
                    rows[vector, column, bit * half : (bit + 1) * half] = piece
                copy = pltpu.make_async_copy(
                    rows.at[vector, column], ref.at[:, column, 0], copy_sems.at[vector, column]
                )
                copy.start()
                copies.append(copy)
    wait_all(copies)


def gather_kernel(*refs):
    *part_refs, out_ref, copy_sems = refs
    place = lax.rem(lax.axis_index("amp"), len(part_refs))
    copies = [
        pltpu.make_async_copy(ref, out_ref.at[place ^ index], copy_sems.at[index])
        for index, ref in enumerate(part_refs)
    ]
    for copy in copies:
        copy.start()
    wait_all(copies)


def tree_sum(parts):
    while len(parts) > 1:
        parts = [parts[i] + parts[i + 1] for i in range(0, len(parts), 2)]
    return parts[0]


def exchange(part, distance):
    devices = lax.axis_size("amp")
    return lax.ppermute(part, "amp", [(i, i ^ distance) for i in range(devices)])


def scattered_sum(value):
    devices = lax.axis_size("amp")
    inner = min(8, devices)
    own = lax.axis_index("amp") % inner
    blocks = value.reshape(inner, -1, value.shape[-1])

    def pick(index):
        return lax.dynamic_index_in_dim(blocks, index, 0, keepdims=False)

    part = tree_sum([pick(own)] + [exchange(pick(own ^ k), k) for k in range(1, inner)])
    distance = inner
    while distance < devices:
        part = part + exchange(part, distance)
        distance *= 2
    return part


def gathered_chips(part):
    inner = min(8, lax.axis_size("amp"))
    return [part] + [exchange(part, k) for k in range(2, inner, 2)]


def gathered_cores(own, shape):
    others = [exchange(found, 1) for found in own]
    parts = [found for pair in zip(own, others) for found in pair]
    out = pl.pallas_call(
        gather_kernel,
        in_specs=[pl.BlockSpec(memory_space=pl.ANY)] * len(parts),
        out_specs=IN_HBM,
        out_shape=jax.ShapeDtypeStruct((len(parts),) + parts[0].shape, parts[0].dtype),
        scratch_shapes=[pltpu.SemaphoreType.DMA((len(parts),))],
        compiler_params=PARAMS,
    )(*parts)
    return out.reshape(shape)


def to_rows(field, lanes):
    return field.reshape(2, -1, lanes).swapaxes(0, 1).reshape(-1, lanes)


def from_rows(rows):
    return rows.reshape(-1, 2, rows.shape[-1]).swapaxes(0, 1).reshape(2, -1)


IN_HBM = pl.BlockSpec(memory_space=pltpu.HBM)
IN_VMEM = pl.BlockSpec(memory_space=pltpu.VMEM)
PARAMS = pltpu.CompilerParams(vmem_limit_bytes=VMEM_BYTES)
HBM_PARAMS = pltpu.CompilerParams(vmem_limit_bytes=60 * 1024 * 1024)


def cost(layers, amplitudes, order):
    flops = layers * 3 * 8 * amplitudes * order
    return pl.CostEstimate(flops=flops, bytes_accessed=32 * amplitudes, transcendentals=0)


def on_device_lanes(state, costate, gates, devices, order, columns):
    lanes = 4 * columns // devices
    steps = devices // 4
    rows = 2 * columns // lanes
    scale = 1.0 / math.sqrt(devices * columns)
    field_shape = (devices, order, lanes)
    sum_shape = (order, 2 * order)
    amplitudes = 2 * order * columns

    def array(shape, kind=jnp.float32):
        return jax.ShapeDtypeStruct(shape, kind)

    state, costate = to_rows(state, lanes), to_rows(costate, lanes)
    sent = pl.pallas_call(
        first_kernel,
        in_specs=[IN_HBM, IN_HBM, IN_HBM],
        out_specs=IN_HBM,
        out_shape=array(field_shape),
        scratch_shapes=[
            pltpu.VMEM((2, order, order), jnp.float32),
            pltpu.VMEM((2, rows * order, lanes), jnp.float32),
            pltpu.VMEM(field_shape, jnp.float32),
            pltpu.SemaphoreType.DMA,
            pltpu.SemaphoreType.DMA((2, 16)),
            pltpu.SemaphoreType.DMA((steps,)),
        ],
        compiler_params=HBM_PARAMS,
        cost_estimate=cost(1, amplitudes, order),
    )(state, costate, gates)
    state, costate, sent = lax.optimization_barrier((state, costate, sent))
    moved = lax.all_to_all(sent, "amp", 0, 0, tiled=True)
    early = pl.pallas_call(
        early_kernel,
        in_specs=[IN_VMEM, IN_VMEM],
        out_specs=IN_VMEM,
        out_shape=array(sum_shape),
        compiler_params=PARAMS,
        cost_estimate=cost(1, amplitudes, order),
    )(state, costate)
    moved = moved.reshape(2, steps, 2, order, lanes)
    last = pl.pallas_call(
        middle_kernel,
        in_specs=[IN_VMEM, IN_VMEM],
        out_specs=IN_HBM,
        out_shape=pltpu.HBM(field_shape, jnp.float32),
        scratch_shapes=[
            pltpu.VMEM((devices * order, lanes), jnp.float32),
            pltpu.VMEM(field_shape, jnp.float32),
            pltpu.SemaphoreType.DMA((2, steps)),
        ],
        compiler_params=PARAMS,
        cost_estimate=cost(2, amplitudes, order),
    )(moved, gates)
    arrived = lax.all_to_all(last, "amp", 0, 0, tiled=True)
    gradients = pl.pallas_call(
        functools.partial(late_kernel, scale=scale),
        in_specs=[IN_VMEM, IN_VMEM, IN_VMEM, IN_VMEM],
        out_specs=IN_VMEM,
        out_shape=array(gates.shape),
        scratch_shapes=[pltpu.VMEM((3,) + sum_shape, jnp.float32)],
        compiler_params=PARAMS,
        cost_estimate=cost(2, amplitudes, order),
    )(moved, last, early, gates)
    part, arrived = lax.optimization_barrier((scattered_sum(gradients), arrived))
    parts = gathered_chips(part)
    state_rows, costate_rows = pl.pallas_call(
        last_kernel,
        in_specs=[IN_VMEM],
        out_specs=[IN_HBM, IN_HBM],
        out_shape=[array((order, rows, 1, lanes))] * 2,
        scratch_shapes=[
            pltpu.VMEM((2, rows, order, lanes), jnp.float32),
            pltpu.SemaphoreType.DMA((2, rows)),
        ],
        compiler_params=PARAMS,
        cost_estimate=cost(1, amplitudes, order),
    )(arrived)
    for index in range(1, len(parts)):
        parts[index], state_rows = lax.optimization_barrier((parts[index], state_rows))
    gradients = gathered_cores(parts, gates.shape)
    return from_rows(state_rows), from_rows(costate_rows), gradients


def undo_gate(field, gate):
    high = lax.Precision.HIGHEST
    shape = field.shape
    parts = field.reshape(shape[:-1] + (2, 2, -1))
    real, imag = parts[..., 0, :], parts[..., 1, :]

    def contract(matrix, operand):
        return jnp.einsum("ts,btvc->bsvc", matrix, operand, precision=high)

    new_real = contract(gate[0], real) + contract(gate[1], imag)
    new_imag = contract(gate[0], imag) - contract(gate[1], real)
    return jnp.stack([new_real, new_imag], axis=-2).reshape(shape)


def gate_gradient(before, after):
    high = lax.Precision.HIGHEST
    lam = before.reshape(before.shape[:-1] + (2, 2, -1))[..., 1, :, :]
    psi = after.reshape(after.shape[:-1] + (2, 2, -1))[..., 0, :, :]
    real = jnp.einsum("btpc,bspc->ts", lam, psi, precision=high)
    imag = jnp.einsum("btc,bsc->ts", lam[..., 1, :], psi[..., 0, :], precision=high) - jnp.einsum(
        "btc,bsc->ts", lam[..., 0, :], psi[..., 1, :], precision=high
    )
    return jnp.stack([real, imag], axis=0)


def on_device_plain(state, costate, gates, devices, order, columns):
    own = columns // devices
    both = jnp.stack([state, costate], axis=0).reshape(2, 2, order, devices, own)
    field = both.transpose(3, 2, 0, 1, 4).reshape(devices, order, 4 * own)
    field = lax.all_to_all(field, "amp", 0, 0, tiled=True)
    after = undo_gate(field, gates[0])
    terms = [gate_gradient(field, after)]
    field = after.reshape(2, devices // 4, 2, 2, 2, order // 4, 4 * own)
    field = field.transpose(3, 1, 4, 0, 2, 5, 6).reshape(devices, order, 4 * own)
    after = undo_gate(field, gates[1])
    terms.append(gate_gradient(field, after))
    field = after.reshape(devices, order // devices, devices, 4 * own)
    field = field.transpose(2, 1, 0, 3).reshape(devices, order, 4 * own)
    after = undo_gate(field, gates[2])
    terms.append(gate_gradient(field, after))
    terms = jnp.stack(terms, axis=0) / math.sqrt(devices * columns)
    gradients = gathered_cores(gathered_chips(scattered_sum(terms)), gates.shape)
    field = lax.all_to_all(after, "amp", 0, 0, tiled=True)
    field = field.reshape(devices, order, 2, 2, own).transpose(2, 3, 1, 0, 4)
    field = field.reshape(2, 2, order * columns)
    return field[0], field[1], gradients


def on_device(state, costate, gates):
    devices = lax.axis_size("amp")
    order = gates.shape[2]
    columns = state.shape[1] // order
    filled = 4 * columns == 128 * devices and order == 4 * devices
    form = on_device_lanes if filled else on_device_plain
    return form(state, costate, gates, devices, order, columns)


def solution(mesh):
    return jax.shard_map(
        on_device,
        mesh=mesh,
        in_specs=(P(None, "amp"), P(None, "amp"), P()),
        out_specs=(P(None, "amp"), P(None, "amp"), P()),
        check_vma=False,
    )
```

```python
import functools
import math

import jax
import jax.numpy as jnp
from jax import lax
from jax.experimental import pallas as pl
from jax.experimental.pallas import tpu as pltpu
from jax.sharding import PartitionSpec as P

VMEM_BYTES = 12 * 1024 * 1024


def split(value):
    high = value.astype(jnp.bfloat16)
    low = (value - high.astype(jnp.float32)).astype(jnp.bfloat16)
    return high, low


def both_parts(value):
    return jnp.concatenate(split(value), axis=0)


def left_parts(both):
    rows = both.shape[0] // 2
    high, low = both[:rows], both[rows:]
    return jnp.concatenate([high, low, high], axis=1)


def dot_parts(left, right):
    high, low = split(right)
    return jnp.dot(
        left_parts(left),
        jnp.concatenate([high, high, low], axis=0),
        preferred_element_type=jnp.float32,
    )


def dot_parts_rows(left, right):
    high, low = split(right)
    return lax.dot_general(
        left_parts(left),
        jnp.concatenate([high, high, low], axis=1),
        (((1,), (1,)), ((), ())),
        preferred_element_type=jnp.float32,
    )


def lane_index(shape):
    return lax.broadcasted_iota(jnp.int32, shape, len(shape) - 1)


def swap_groups(values):
    lanes = values[0].shape[-1]
    group = lane_index(values[0].shape) // (lanes // 4)
    for bit in (2, 1):
        width = bit * (lanes // 4)
        fresh = list(values)
        for index in range(4):
            if index & bit == 0:
                low, high = values[index], values[index | bit]
                upper = group & bit != 0
                fresh[index] = jnp.where(upper, pltpu.roll(high, width, 1), low)
                fresh[index | bit] = jnp.where(upper, high, pltpu.roll(low, lanes - width, 1))
        values = fresh
    return values


def swap_bit(low, high):
    lanes = low.shape[-1]
    width = lanes // 4
    upper = (lane_index(low.shape) // width) % 2 == 1
    first = jnp.where(upper, pltpu.roll(high, width, 1), low)
    second = jnp.where(upper, high, pltpu.roll(low, lanes - width, 1))
    return first, second


def row_halves(value, groups):
    rows, lanes = value.shape
    parts = value.reshape(groups, 2, rows // groups // 2, lanes)
    return parts[:, 0].reshape(rows // 2, lanes), parts[:, 1].reshape(rows // 2, lanes)


def wait_all(copies):
    for copy in copies:
        copy.wait()


def undo_matrix(gate):
    real, imag = gate[0].T, gate[1].T
    top = jnp.concatenate([real, imag], axis=1)
    low = jnp.concatenate([-imag, real], axis=1)
    return both_parts(jnp.concatenate([top, low], axis=0))


def column(rows, block, order):
    stride = rows.shape[0] // order
    parts = [rows[pl.ds(block * 2 + part, order, stride=stride), :] for part in range(2)]
    return jnp.concatenate(parts, axis=0)


def first_kernel(
    state_ref, costate_ref, gates_ref, out_ref, gate, rows, field_ref, gate_sem, row_sems, out_sems
):
    order = gate.shape[1]
    lanes = rows.shape[2]
    stride = rows.shape[1] // order
    chunks = row_sems.shape[1]
    chunk = rows.shape[1] // chunks
    copies = [pltpu.make_async_copy(gates_ref.at[0], gate, gate_sem)]
    for index in range(chunks):
        part = pl.ds(index * chunk, chunk)
        for vector, ref in enumerate((state_ref, costate_ref)):
            copies.append(
                pltpu.make_async_copy(ref.at[part], rows.at[vector, part], row_sems.at[vector, index])
            )
    for copy in copies:
        copy.start()
    copies[0].wait()
    matrix = undo_matrix(gate)
    wait_all(copies[1:])

    def column(vector, block):
        parts = [rows[vector, pl.ds(block * 2 + part, order, stride=stride), :] for part in range(2)]
        return jnp.concatenate(parts, axis=0)

    out_copies = []
    for block in range(stride // 2):
        field = jnp.concatenate([column(0, block), column(1, block)], axis=1)
        undone = dot_parts(matrix, field)
        pieces = []
        for vector in range(2):
            pieces += row_halves(undone[:, vector * lanes : (vector + 1) * lanes], 2)
        for index, piece in enumerate(swap_groups(pieces)):
            field_ref[block * 4 + index] = piece
        part = pl.ds(block * 4, 4)
        copy = pltpu.make_async_copy(field_ref.at[part], out_ref.at[part], out_sems.at[block])
        copy.start()
        out_copies.append(copy)
    wait_all(out_copies)


def outer_product(lam, psi):
    order = lam.shape[0] // 2
    left = jnp.concatenate([lam[:order], lam[order:]], axis=1)
    plain = jnp.concatenate([psi[:order], psi[order:]], axis=1)
    other = jnp.concatenate([-psi[order:], psi[:order]], axis=1)
    return dot_parts_rows(both_parts(left), jnp.concatenate([plain, other], axis=0))


def four_products(fields, groups):
    pieces = swap_groups(fields)
    rows, lanes = pieces[0].shape

    def joined(vector):
        parts = [
            piece.reshape(groups, 1, rows // groups, lanes)
            for piece in pieces[2 * vector : 2 * vector + 2]
        ]
        return jnp.concatenate(parts, axis=1).reshape(2 * rows, lanes)

    return outer_product(joined(1), joined(0))


def early_kernel(state_ref, costate_ref, out_ref):
    order = out_ref.shape[0]
    out_ref[...] = jnp.zeros_like(out_ref)

    @pl.loop(0, state_ref.shape[0] // order // 2)
    def _(block):
        out_ref[...] += outer_product(
            column(costate_ref, block, order), column(state_ref, block, order)
        )


def middle_kernel(moved_ref, gates_ref, out_ref, kept, last, sems):
    _, steps, _, order, lanes = moved_ref.shape
    batches = 2 * steps
    copies = []

    def undo(matrix, fields):
        result = dot_parts(matrix, jnp.concatenate(fields, axis=1))
        return [result[:, index * lanes : (index + 1) * lanes] for index in range(len(fields))]

    matrices = [undo_matrix(gates_ref[index + 1]) for index in range(2)]
    for step in range(steps):
        fields = [mixed_rows(moved_ref, step, bit) for bit in range(2)]
        for bit, result in enumerate(undo(matrices[0], fields)):
            for top, piece in enumerate(swap_bit(*row_halves(result, 8))):
                place = (top * steps + step) * 2 + bit
                kept[pl.ds(place * order, order), :] = piece

    for step in range(steps):
        fields = [regrouped(kept, step * 2 + index, order) for index in range(2)]
        for index, result in enumerate(undo(matrices[1], fields)):
            for bit, piece in enumerate(swap_bit(*row_halves(result, 2))):
                last[bit * batches + step * 2 + index] = piece
        for bit in range(2):
            part = pl.ds(bit * batches + step * 2, 2)
            copy = pltpu.make_async_copy(last.at[part], out_ref.at[part], sems.at[bit, step])
            copy.start()
            copies.append(copy)
    wait_all(copies)


def regrouped(kept_ref, batch, order):
    devices = kept_ref.shape[0] // order
    parts = [
        kept_ref[pl.ds(row * (devices // 2) + batch, devices, stride=order), :] for row in range(8)
    ]
    return jnp.concatenate(parts, axis=0)


def mixed_rows(moved_ref, step, bit):
    low_rows = moved_ref.shape[3] // 4
    parts = [
        moved_ref[top, step, low, pl.ds((part * 2 + bit) * low_rows, low_rows), :]
        for part in range(2)
        for top in range(2)
        for low in range(2)
    ]
    return jnp.concatenate(parts, axis=0)


def late_kernel(moved_ref, last_ref, early_ref, gates_ref, out_ref, sum_ref, *, scale):
    order = early_ref.shape[0]
    steps = moved_ref.shape[1]
    sum_ref[0] = early_ref[...]
    sum_ref[1:3] = jnp.zeros((2,) + early_ref.shape, jnp.float32)

    @pl.loop(0, steps)
    def _(step):
        first, second = (mixed_rows(moved_ref, step, bit) for bit in range(2))
        half = first.shape[-1] // 2
        lower = lane_index(first.shape) < half
        psi = jnp.where(lower, first, pltpu.roll(second, half, 1))
        lam = jnp.where(lower, pltpu.roll(first, half, 1), second)
        sum_ref[1] += outer_product(lam, psi)
        sum_ref[2] += four_products([last_ref[step * 4 + index] for index in range(4)], 2)

    for index in range(3):
        total = (sum_ref[index, :, :order], sum_ref[index, :, order:])
        gate = (gates_ref[index, 0], gates_ref[index, 1])
        left, right = (gate, total) if index == 2 else (total, gate)
        out_ref[index, 0], out_ref[index, 1] = complex_product(left, right, scale)


def complex_product(left, right, scale):
    def times(first, second):
        return jnp.dot(
            first, second, precision=lax.Precision.HIGHEST, preferred_element_type=jnp.float32
        )

    real = times(left[0], right[0]) - times(left[1], right[1])
    imag = times(left[0], right[1]) + times(left[1], right[0])
    return real * scale, imag * scale


def last_kernel(moved_ref, state_ref, costate_ref, rows, copy_sems):
    half = moved_ref.shape[1] // 2
    copies = []
    for block in range(rows.shape[1] // 2):
        pieces = swap_groups([moved_ref[block * 4 + index] for index in range(4)])
        for vector, ref in enumerate((state_ref, costate_ref)):
            for part in range(2):
                column = block * 2 + part
                for bit in range(2):
                    piece = pieces[2 * vector + bit][part * half : (part + 1) * half]
                    rows[vector, column, bit * half : (bit + 1) * half] = piece
                copy = pltpu.make_async_copy(
                    rows.at[vector, column], ref.at[:, column, 0], copy_sems.at[vector, column]
                )
                copy.start()
                copies.append(copy)
    wait_all(copies)


def gather_kernel(*refs):
    *part_refs, out_ref, copy_sems = refs
    place = lax.rem(lax.axis_index("amp"), len(part_refs))
    copies = [
        pltpu.make_async_copy(ref, out_ref.at[place ^ index], copy_sems.at[index])
        for index, ref in enumerate(part_refs)
    ]
    for copy in copies:
        copy.start()
    wait_all(copies)


def tree_sum(parts):
    while len(parts) > 1:
        parts = [parts[i] + parts[i + 1] for i in range(0, len(parts), 2)]
    return parts[0]


def exchange(part, distance):
    devices = lax.axis_size("amp")
    return lax.ppermute(part, "amp", [(i, i ^ distance) for i in range(devices)])


def scattered_sum(value):
    devices = lax.axis_size("amp")
    inner = min(8, devices)
    own = lax.axis_index("amp") % inner
    blocks = value.reshape(inner, -1, value.shape[-1])

    def pick(index):
        return lax.dynamic_index_in_dim(blocks, index, 0, keepdims=False)

    part = tree_sum([pick(own)] + [exchange(pick(own ^ k), k) for k in range(1, inner)])
    distance = inner
    while distance < devices:
        part = part + exchange(part, distance)
        distance *= 2
    return part


def gathered_chips(part):
    inner = min(8, lax.axis_size("amp"))
    return [part] + [exchange(part, k) for k in range(2, inner, 2)]


def gathered_cores(own, shape):
    others = [exchange(found, 1) for found in own]
    parts = [found for pair in zip(own, others) for found in pair]
    out = pl.pallas_call(
        gather_kernel,
        in_specs=[pl.BlockSpec(memory_space=pl.ANY)] * len(parts),
        out_specs=IN_HBM,
        out_shape=jax.ShapeDtypeStruct((len(parts),) + parts[0].shape, parts[0].dtype),
        scratch_shapes=[pltpu.SemaphoreType.DMA((len(parts),))],
        compiler_params=PARAMS,
    )(*parts)
    return out.reshape(shape)


def to_rows(field, lanes):
    return field.reshape(2, -1, lanes).swapaxes(0, 1).reshape(-1, lanes)


def from_rows(rows):
    return rows.reshape(-1, 2, rows.shape[-1]).swapaxes(0, 1).reshape(2, -1)


IN_HBM = pl.BlockSpec(memory_space=pltpu.HBM)
IN_VMEM = pl.BlockSpec(memory_space=pltpu.VMEM)
PARAMS = pltpu.CompilerParams(vmem_limit_bytes=VMEM_BYTES)
HBM_PARAMS = pltpu.CompilerParams(vmem_limit_bytes=60 * 1024 * 1024)


def cost(layers, amplitudes, order):
    flops = layers * 3 * 8 * amplitudes * order
    return pl.CostEstimate(flops=flops, bytes_accessed=32 * amplitudes, transcendentals=0)


def on_device_lanes(state, costate, gates, devices, order, columns):
    lanes = 4 * columns // devices
    steps = devices // 4
    rows = 2 * columns // lanes
    scale = 1.0 / math.sqrt(devices * columns)
    field_shape = (devices, order, lanes)
    sum_shape = (order, 2 * order)
    amplitudes = 2 * order * columns

    def array(shape, kind=jnp.float32):
        return jax.ShapeDtypeStruct(shape, kind)

    state, costate = to_rows(state, lanes), to_rows(costate, lanes)
    sent = pl.pallas_call(
        first_kernel,
        in_specs=[IN_HBM, IN_HBM, IN_HBM],
        out_specs=IN_HBM,
        out_shape=array(field_shape),
        scratch_shapes=[
            pltpu.VMEM((2, order, order), jnp.float32),
            pltpu.VMEM((2, rows * order, lanes), jnp.float32),
            pltpu.VMEM(field_shape, jnp.float32),
            pltpu.SemaphoreType.DMA,
            pltpu.SemaphoreType.DMA((2, 1)),
            pltpu.SemaphoreType.DMA((steps,)),
        ],
        compiler_params=HBM_PARAMS,
        cost_estimate=cost(1, amplitudes, order),
    )(state, costate, gates)
    state, costate, sent = lax.optimization_barrier((state, costate, sent))
    moved = lax.all_to_all(sent, "amp", 0, 0, tiled=True)
    early = pl.pallas_call(
        early_kernel,
        in_specs=[IN_VMEM, IN_VMEM],
        out_specs=IN_VMEM,
        out_shape=array(sum_shape),
        compiler_params=PARAMS,
        cost_estimate=cost(1, amplitudes, order),
    )(state, costate)
    moved = moved.reshape(2, steps, 2, order, lanes)
    last = pl.pallas_call(
        middle_kernel,
        in_specs=[IN_VMEM, IN_VMEM],
        out_specs=IN_HBM,
        out_shape=pltpu.HBM(field_shape, jnp.float32),
        scratch_shapes=[
            pltpu.VMEM((devices * order, lanes), jnp.float32),
            pltpu.VMEM(field_shape, jnp.float32),
            pltpu.SemaphoreType.DMA((2, steps)),
        ],
        compiler_params=PARAMS,
        cost_estimate=cost(2, amplitudes, order),
    )(moved, gates)
    arrived = lax.all_to_all(last, "amp", 0, 0, tiled=True)
    gradients = pl.pallas_call(
        functools.partial(late_kernel, scale=scale),
        in_specs=[IN_VMEM, IN_VMEM, IN_VMEM, IN_VMEM],
        out_specs=IN_VMEM,
        out_shape=array(gates.shape),
        scratch_shapes=[pltpu.VMEM((3,) + sum_shape, jnp.float32)],
        compiler_params=PARAMS,
        cost_estimate=cost(2, amplitudes, order),
    )(moved, last, early, gates)
    part, arrived = lax.optimization_barrier((scattered_sum(gradients), arrived))
    parts = gathered_chips(part)
    state_rows, costate_rows = pl.pallas_call(
        last_kernel,
        in_specs=[IN_VMEM],
        out_specs=[IN_HBM, IN_HBM],
        out_shape=[array((order, rows, 1, lanes))] * 2,
        scratch_shapes=[
            pltpu.VMEM((2, rows, order, lanes), jnp.float32),
            pltpu.SemaphoreType.DMA((2, rows)),
        ],
        compiler_params=PARAMS,
        cost_estimate=cost(1, amplitudes, order),
    )(arrived)
    for index in range(1, len(parts)):
        parts[index], state_rows = lax.optimization_barrier((parts[index], state_rows))
    gradients = gathered_cores(parts, gates.shape)
    return from_rows(state_rows), from_rows(costate_rows), gradients


def undo_gate(field, gate):
    high = lax.Precision.HIGHEST
    shape = field.shape
    parts = field.reshape(shape[:-1] + (2, 2, -1))
    real, imag = parts[..., 0, :], parts[..., 1, :]

    def contract(matrix, operand):
        return jnp.einsum("ts,btvc->bsvc", matrix, operand, precision=high)

    new_real = contract(gate[0], real) + contract(gate[1], imag)
    new_imag = contract(gate[0], imag) - contract(gate[1], real)
    return jnp.stack([new_real, new_imag], axis=-2).reshape(shape)


def gate_gradient(before, after):
    high = lax.Precision.HIGHEST
    lam = before.reshape(before.shape[:-1] + (2, 2, -1))[..., 1, :, :]
    psi = after.reshape(after.shape[:-1] + (2, 2, -1))[..., 0, :, :]
    real = jnp.einsum("btpc,bspc->ts", lam, psi, precision=high)
    imag = jnp.einsum("btc,bsc->ts", lam[..., 1, :], psi[..., 0, :], precision=high) - jnp.einsum(
        "btc,bsc->ts", lam[..., 0, :], psi[..., 1, :], precision=high
    )
    return jnp.stack([real, imag], axis=0)


def on_device_plain(state, costate, gates, devices, order, columns):
    own = columns // devices
    both = jnp.stack([state, costate], axis=0).reshape(2, 2, order, devices, own)
    field = both.transpose(3, 2, 0, 1, 4).reshape(devices, order, 4 * own)
    field = lax.all_to_all(field, "amp", 0, 0, tiled=True)
    after = undo_gate(field, gates[0])
    terms = [gate_gradient(field, after)]
    field = after.reshape(2, devices // 4, 2, 2, 2, order // 4, 4 * own)
    field = field.transpose(3, 1, 4, 0, 2, 5, 6).reshape(devices, order, 4 * own)
    after = undo_gate(field, gates[1])
    terms.append(gate_gradient(field, after))
    field = after.reshape(devices, order // devices, devices, 4 * own)
    field = field.transpose(2, 1, 0, 3).reshape(devices, order, 4 * own)
    after = undo_gate(field, gates[2])
    terms.append(gate_gradient(field, after))
    terms = jnp.stack(terms, axis=0) / math.sqrt(devices * columns)
    gradients = gathered_cores(gathered_chips(scattered_sum(terms)), gates.shape)
    field = lax.all_to_all(after, "amp", 0, 0, tiled=True)
    field = field.reshape(devices, order, 2, 2, own).transpose(2, 3, 1, 0, 4)
    field = field.reshape(2, 2, order * columns)
    return field[0], field[1], gradients


def on_device(state, costate, gates):
    devices = lax.axis_size("amp")
    order = gates.shape[2]
    columns = state.shape[1] // order
    filled = 4 * columns == 128 * devices and order == 4 * devices
    form = on_device_lanes if filled else on_device_plain
    return form(state, costate, gates, devices, order, columns)


def solution(mesh):
    return jax.shard_map(
        on_device,
        mesh=mesh,
        in_specs=(P(None, "amp"), P(None, "amp"), P()),
        out_specs=(P(None, "amp"), P(None, "amp"), P()),
        check_vma=False,
    )
```

```python
import functools
import math

import jax
import jax.numpy as jnp
from jax import lax
from jax.experimental import pallas as pl
from jax.experimental.pallas import tpu as pltpu
from jax.sharding import PartitionSpec as P

VMEM_BYTES = 12 * 1024 * 1024


def split(value):
    high = value.astype(jnp.bfloat16)
    low = (value - high.astype(jnp.float32)).astype(jnp.bfloat16)
    return high, low


def both_parts(value):
    return jnp.concatenate(split(value), axis=0)


def left_parts(both):
    rows = both.shape[0] // 2
    high, low = both[:rows], both[rows:]
    return jnp.concatenate([high, low, high], axis=1)


def dot_parts(left, right):
    high, low = split(right)
    return jnp.dot(
        left_parts(left),
        jnp.concatenate([high, high, low], axis=0),
        preferred_element_type=jnp.float32,
    )


def dot_parts_rows(left, right):
    high, low = split(right)
    return lax.dot_general(
        left_parts(left),
        jnp.concatenate([high, high, low], axis=1),
        (((1,), (1,)), ((), ())),
        preferred_element_type=jnp.float32,
    )


def lane_index(shape):
    return lax.broadcasted_iota(jnp.int32, shape, len(shape) - 1)


def swap_groups(values):
    lanes = values[0].shape[-1]
    group = lane_index(values[0].shape) // (lanes // 4)
    for bit in (2, 1):
        width = bit * (lanes // 4)
        fresh = list(values)
        for index in range(4):
            if index & bit == 0:
                low, high = values[index], values[index | bit]
                upper = group & bit != 0
                fresh[index] = jnp.where(upper, pltpu.roll(high, width, 1), low)
                fresh[index | bit] = jnp.where(upper, high, pltpu.roll(low, lanes - width, 1))
        values = fresh
    return values


def swap_bit(low, high):
    lanes = low.shape[-1]
    width = lanes // 4
    upper = (lane_index(low.shape) // width) % 2 == 1
    first = jnp.where(upper, pltpu.roll(high, width, 1), low)
    second = jnp.where(upper, high, pltpu.roll(low, lanes - width, 1))
    return first, second


def row_halves(value, groups):
    rows, lanes = value.shape
    parts = value.reshape(groups, 2, rows // groups // 2, lanes)
    return parts[:, 0].reshape(rows // 2, lanes), parts[:, 1].reshape(rows // 2, lanes)


def wait_all(copies):
    for copy in copies:
        copy.wait()


def undo_matrix(gate):
    real, imag = gate[0].T, gate[1].T
    top = jnp.concatenate([real, imag], axis=1)
    low = jnp.concatenate([-imag, real], axis=1)
    return both_parts(jnp.concatenate([top, low], axis=0))


def column(rows, block, order):
    stride = rows.shape[0] // order
    parts = [rows[pl.ds(block * 2 + part, order, stride=stride), :] for part in range(2)]
    return jnp.concatenate(parts, axis=0)


def first_kernel(
    state_ref, costate_ref, gates_ref, out_ref, gate, rows, field_ref, gate_sem, row_sems, out_sems
):
    order = gate.shape[1]
    lanes = rows.shape[2]
    stride = rows.shape[1] // order
    chunks = row_sems.shape[1]
    chunk = rows.shape[1] // chunks
    copies = [pltpu.make_async_copy(gates_ref.at[0], gate, gate_sem)]
    for index in range(chunks):
        part = pl.ds(index * chunk, chunk)
        for vector, ref in enumerate((state_ref, costate_ref)):
            copies.append(
                pltpu.make_async_copy(ref.at[part], rows.at[vector, part], row_sems.at[vector, index])
            )
    for copy in copies:
        copy.start()
    copies[0].wait()
    matrix = undo_matrix(gate)
    wait_all(copies[1:])

    def column(vector, block):
        parts = [rows[vector, pl.ds(block * 2 + part, order, stride=stride), :] for part in range(2)]
        return jnp.concatenate(parts, axis=0)

    out_copies = []
    for block in range(stride // 2):
        field = jnp.concatenate([column(0, block), column(1, block)], axis=1)
        undone = dot_parts(matrix, field)
        pieces = []
        for vector in range(2):
            pieces += row_halves(undone[:, vector * lanes : (vector + 1) * lanes], 2)
        for index, piece in enumerate(swap_groups(pieces)):
            field_ref[block * 4 + index] = piece
        part = pl.ds(block * 4, 4)
        copy = pltpu.make_async_copy(field_ref.at[part], out_ref.at[part], out_sems.at[block])
        copy.start()
        out_copies.append(copy)
    wait_all(out_copies)


def outer_product(lam, psi):
    order = lam.shape[0] // 2
    left = jnp.concatenate([lam[:order], lam[order:]], axis=1)
    plain = jnp.concatenate([psi[:order], psi[order:]], axis=1)
    other = jnp.concatenate([-psi[order:], psi[:order]], axis=1)
    return dot_parts_rows(both_parts(left), jnp.concatenate([plain, other], axis=0))


def four_products(fields, groups):
    pieces = swap_groups(fields)
    rows, lanes = pieces[0].shape

    def joined(vector):
        parts = [
            piece.reshape(groups, 1, rows // groups, lanes)
            for piece in pieces[2 * vector : 2 * vector + 2]
        ]
        return jnp.concatenate(parts, axis=1).reshape(2 * rows, lanes)

    return outer_product(joined(1), joined(0))


def early_kernel(state_ref, costate_ref, out_ref):
    order = out_ref.shape[0]
    out_ref[...] = jnp.zeros_like(out_ref)

    @pl.loop(0, state_ref.shape[0] // order // 2)
    def _(block):
        out_ref[...] += outer_product(
            column(costate_ref, block, order), column(state_ref, block, order)
        )


def middle_kernel(moved_ref, gates_ref, out_ref, kept, last, sems):
    _, steps, _, order, lanes = moved_ref.shape
    batches = 2 * steps
    copies = []

    def undo(matrix, fields):
        result = dot_parts(matrix, jnp.concatenate(fields, axis=1))
        return [result[:, index * lanes : (index + 1) * lanes] for index in range(len(fields))]

    matrix = undo_matrix(gates_ref[1])
    for step in range(steps):
        fields = [mixed_rows(moved_ref, step, bit) for bit in range(2)]
        for bit, result in enumerate(undo(matrix, fields)):
            for top, piece in enumerate(swap_bit(*row_halves(result, 8))):
                place = (top * steps + step) * 2 + bit
                kept[pl.ds(place * order, order), :] = piece

    matrix = undo_matrix(gates_ref[2])
    for step in range(steps):
        fields = [regrouped(kept, step * 2 + index, order) for index in range(2)]
        for index, result in enumerate(undo(matrix, fields)):
            for bit, piece in enumerate(swap_bit(*row_halves(result, 2))):
                last[bit * batches + step * 2 + index] = piece
        for bit in range(2):
            part = pl.ds(bit * batches + step * 2, 2)
            copy = pltpu.make_async_copy(last.at[part], out_ref.at[part], sems.at[bit, step])
            copy.start()
            copies.append(copy)
    wait_all(copies)


def regrouped(kept_ref, batch, order):
    devices = kept_ref.shape[0] // order
    parts = [
        kept_ref[pl.ds(row * (devices // 2) + batch, devices, stride=order), :] for row in range(8)
    ]
    return jnp.concatenate(parts, axis=0)


def mixed_rows(moved_ref, step, bit):
    low_rows = moved_ref.shape[3] // 4
    parts = [
        moved_ref[top, step, low, pl.ds((part * 2 + bit) * low_rows, low_rows), :]
        for part in range(2)
        for top in range(2)
        for low in range(2)
    ]
    return jnp.concatenate(parts, axis=0)


def late_kernel(moved_ref, last_ref, early_ref, gates_ref, out_ref, sum_ref, *, scale):
    order = early_ref.shape[0]
    steps = moved_ref.shape[1]
    sum_ref[0] = early_ref[...]
    sum_ref[1:3] = jnp.zeros((2,) + early_ref.shape, jnp.float32)

    @pl.loop(0, steps)
    def _(step):
        first, second = (mixed_rows(moved_ref, step, bit) for bit in range(2))
        half = first.shape[-1] // 2
        lower = lane_index(first.shape) < half
        psi = jnp.where(lower, first, pltpu.roll(second, half, 1))
        lam = jnp.where(lower, pltpu.roll(first, half, 1), second)
        sum_ref[1] += outer_product(lam, psi)
        sum_ref[2] += four_products([last_ref[step * 4 + index] for index in range(4)], 2)

    for index in range(3):
        total = (sum_ref[index, :, :order], sum_ref[index, :, order:])
        gate = (gates_ref[index, 0], gates_ref[index, 1])
        left, right = (gate, total) if index == 2 else (total, gate)
        out_ref[index, 0], out_ref[index, 1] = complex_product(left, right, scale)


def complex_product(left, right, scale):
    def times(first, second):
        return jnp.dot(
            first, second, precision=lax.Precision.HIGHEST, preferred_element_type=jnp.float32
        )

    real = times(left[0], right[0]) - times(left[1], right[1])
    imag = times(left[0], right[1]) + times(left[1], right[0])
    return real * scale, imag * scale


def last_kernel(moved_ref, state_ref, costate_ref, rows, copy_sems):
    half = moved_ref.shape[1] // 2
    copies = []
    for block in range(rows.shape[1] // 2):
        pieces = swap_groups([moved_ref[block * 4 + index] for index in range(4)])
        for vector, ref in enumerate((state_ref, costate_ref)):
            for part in range(2):
                column = block * 2 + part
                for bit in range(2):
                    piece = pieces[2 * vector + bit][part * half : (part + 1) * half]
                    rows[vector, column, bit * half : (bit + 1) * half] = piece
                copy = pltpu.make_async_copy(
                    rows.at[vector, column], ref.at[:, column, 0], copy_sems.at[vector, column]
                )
                copy.start()
                copies.append(copy)
    wait_all(copies)


def gather_kernel(*refs):
    *part_refs, out_ref, copy_sems = refs
    place = lax.rem(lax.axis_index("amp"), len(part_refs))
    copies = [
        pltpu.make_async_copy(ref, out_ref.at[place ^ index], copy_sems.at[index])
        for index, ref in enumerate(part_refs)
    ]
    for copy in copies:
        copy.start()
    wait_all(copies)


def tree_sum(parts):
    while len(parts) > 1:
        parts = [parts[i] + parts[i + 1] for i in range(0, len(parts), 2)]
    return parts[0]


def exchange(part, distance):
    devices = lax.axis_size("amp")
    return lax.ppermute(part, "amp", [(i, i ^ distance) for i in range(devices)])


def scattered_sum(value):
    devices = lax.axis_size("amp")
    inner = min(8, devices)
    own = lax.axis_index("amp") % inner
    blocks = value.reshape(inner, -1, value.shape[-1])

    def pick(index):
        return lax.dynamic_index_in_dim(blocks, index, 0, keepdims=False)

    part = tree_sum([pick(own)] + [exchange(pick(own ^ k), k) for k in range(1, inner)])
    distance = inner
    while distance < devices:
        part = part + exchange(part, distance)
        distance *= 2
    return part


def gathered_chips(part):
    inner = min(8, lax.axis_size("amp"))
    return [part] + [exchange(part, k) for k in range(2, inner, 2)]


def gathered_cores(own, shape):
    others = [exchange(found, 1) for found in own]
    parts = [found for pair in zip(own, others) for found in pair]
    out = pl.pallas_call(
        gather_kernel,
        in_specs=[pl.BlockSpec(memory_space=pl.ANY)] * len(parts),
        out_specs=IN_HBM,
        out_shape=jax.ShapeDtypeStruct((len(parts),) + parts[0].shape, parts[0].dtype),
        scratch_shapes=[pltpu.SemaphoreType.DMA((len(parts),))],
        compiler_params=PARAMS,
    )(*parts)
    return out.reshape(shape)


def to_rows(field, lanes):
    return field.reshape(2, -1, lanes).swapaxes(0, 1).reshape(-1, lanes)


def from_rows(rows):
    return rows.reshape(-1, 2, rows.shape[-1]).swapaxes(0, 1).reshape(2, -1)


IN_HBM = pl.BlockSpec(memory_space=pltpu.HBM)
IN_VMEM = pl.BlockSpec(memory_space=pltpu.VMEM)
PARAMS = pltpu.CompilerParams(vmem_limit_bytes=VMEM_BYTES)
HBM_PARAMS = pltpu.CompilerParams(vmem_limit_bytes=60 * 1024 * 1024)


def cost(layers, amplitudes, order):
    flops = layers * 3 * 8 * amplitudes * order
    return pl.CostEstimate(flops=flops, bytes_accessed=32 * amplitudes, transcendentals=0)


def on_device_lanes(state, costate, gates, devices, order, columns):
    lanes = 4 * columns // devices
    steps = devices // 4
    rows = 2 * columns // lanes
    scale = 1.0 / math.sqrt(devices * columns)
    field_shape = (devices, order, lanes)
    sum_shape = (order, 2 * order)
    amplitudes = 2 * order * columns

    def array(shape, kind=jnp.float32):
        return jax.ShapeDtypeStruct(shape, kind)

    state, costate = to_rows(state, lanes), to_rows(costate, lanes)
    sent = pl.pallas_call(
        first_kernel,
        in_specs=[IN_HBM, IN_HBM, IN_HBM],
        out_specs=IN_HBM,
        out_shape=array(field_shape),
        scratch_shapes=[
            pltpu.VMEM((2, order, order), jnp.float32),
            pltpu.VMEM((2, rows * order, lanes), jnp.float32),
            pltpu.VMEM(field_shape, jnp.float32),
            pltpu.SemaphoreType.DMA,
            pltpu.SemaphoreType.DMA((2, 1)),
            pltpu.SemaphoreType.DMA((steps,)),
        ],
        compiler_params=HBM_PARAMS,
        cost_estimate=cost(1, amplitudes, order),
    )(state, costate, gates)
    state, costate, sent = lax.optimization_barrier((state, costate, sent))
    moved = lax.all_to_all(sent, "amp", 0, 0, tiled=True)
    early = pl.pallas_call(
        early_kernel,
        in_specs=[IN_VMEM, IN_VMEM],
        out_specs=IN_VMEM,
        out_shape=array(sum_shape),
        compiler_params=PARAMS,
        cost_estimate=cost(1, amplitudes, order),
    )(state, costate)
    moved = moved.reshape(2, steps, 2, order, lanes)
    last = pl.pallas_call(
        middle_kernel,
        in_specs=[IN_VMEM, IN_VMEM],
        out_specs=IN_HBM,
        out_shape=pltpu.HBM(field_shape, jnp.float32),
        scratch_shapes=[
            pltpu.VMEM((devices * order, lanes), jnp.float32),
            pltpu.VMEM(field_shape, jnp.float32),
            pltpu.SemaphoreType.DMA((2, steps)),
        ],
        compiler_params=PARAMS,
        cost_estimate=cost(2, amplitudes, order),
    )(moved, gates)
    arrived = lax.all_to_all(last, "amp", 0, 0, tiled=True)
    gradients = pl.pallas_call(
        functools.partial(late_kernel, scale=scale),
        in_specs=[IN_VMEM, IN_VMEM, IN_VMEM, IN_VMEM],
        out_specs=IN_VMEM,
        out_shape=array(gates.shape),
        scratch_shapes=[pltpu.VMEM((3,) + sum_shape, jnp.float32)],
        compiler_params=PARAMS,
        cost_estimate=cost(2, amplitudes, order),
    )(moved, last, early, gates)
    part, arrived = lax.optimization_barrier((scattered_sum(gradients), arrived))
    parts = gathered_chips(part)
    state_rows, costate_rows = pl.pallas_call(
        last_kernel,
        in_specs=[IN_VMEM],
        out_specs=[IN_HBM, IN_HBM],
        out_shape=[array((order, rows, 1, lanes))] * 2,
        scratch_shapes=[
            pltpu.VMEM((2, rows, order, lanes), jnp.float32),
            pltpu.SemaphoreType.DMA((2, rows)),
        ],
        compiler_params=PARAMS,
        cost_estimate=cost(1, amplitudes, order),
    )(arrived)
    for index in range(1, len(parts)):
        parts[index], state_rows = lax.optimization_barrier((parts[index], state_rows))
    gradients = gathered_cores(parts, gates.shape)
    return from_rows(state_rows), from_rows(costate_rows), gradients


def undo_gate(field, gate):
    high = lax.Precision.HIGHEST
    shape = field.shape
    parts = field.reshape(shape[:-1] + (2, 2, -1))
    real, imag = parts[..., 0, :], parts[..., 1, :]

    def contract(matrix, operand):
        return jnp.einsum("ts,btvc->bsvc", matrix, operand, precision=high)

    new_real = contract(gate[0], real) + contract(gate[1], imag)
    new_imag = contract(gate[0], imag) - contract(gate[1], real)
    return jnp.stack([new_real, new_imag], axis=-2).reshape(shape)


def gate_gradient(before, after):
    high = lax.Precision.HIGHEST
    lam = before.reshape(before.shape[:-1] + (2, 2, -1))[..., 1, :, :]
    psi = after.reshape(after.shape[:-1] + (2, 2, -1))[..., 0, :, :]
    real = jnp.einsum("btpc,bspc->ts", lam, psi, precision=high)
    imag = jnp.einsum("btc,bsc->ts", lam[..., 1, :], psi[..., 0, :], precision=high) - jnp.einsum(
        "btc,bsc->ts", lam[..., 0, :], psi[..., 1, :], precision=high
    )
    return jnp.stack([real, imag], axis=0)


def on_device_plain(state, costate, gates, devices, order, columns):
    own = columns // devices
    both = jnp.stack([state, costate], axis=0).reshape(2, 2, order, devices, own)
    field = both.transpose(3, 2, 0, 1, 4).reshape(devices, order, 4 * own)
    field = lax.all_to_all(field, "amp", 0, 0, tiled=True)
    after = undo_gate(field, gates[0])
    terms = [gate_gradient(field, after)]
    field = after.reshape(2, devices // 4, 2, 2, 2, order // 4, 4 * own)
    field = field.transpose(3, 1, 4, 0, 2, 5, 6).reshape(devices, order, 4 * own)
    after = undo_gate(field, gates[1])
    terms.append(gate_gradient(field, after))
    field = after.reshape(devices, order // devices, devices, 4 * own)
    field = field.transpose(2, 1, 0, 3).reshape(devices, order, 4 * own)
    after = undo_gate(field, gates[2])
    terms.append(gate_gradient(field, after))
    terms = jnp.stack(terms, axis=0) / math.sqrt(devices * columns)
    gradients = gathered_cores(gathered_chips(scattered_sum(terms)), gates.shape)
    field = lax.all_to_all(after, "amp", 0, 0, tiled=True)
    field = field.reshape(devices, order, 2, 2, own).transpose(2, 3, 1, 0, 4)
    field = field.reshape(2, 2, order * columns)
    return field[0], field[1], gradients


def on_device(state, costate, gates):
    devices = lax.axis_size("amp")
    order = gates.shape[2]
    columns = state.shape[1] // order
    filled = 4 * columns == 128 * devices and order == 4 * devices
    form = on_device_lanes if filled else on_device_plain
    return form(state, costate, gates, devices, order, columns)


def solution(mesh):
    return jax.shard_map(
        on_device,
        mesh=mesh,
        in_specs=(P(None, "amp"), P(None, "amp"), P()),
        out_specs=(P(None, "amp"), P(None, "amp"), P()),
        check_vma=False,
    )
```

```python
import functools
import math

import jax
import jax.numpy as jnp
from jax import lax
from jax.experimental import pallas as pl
from jax.experimental.pallas import tpu as pltpu
from jax.sharding import PartitionSpec as P

VMEM_BYTES = 12 * 1024 * 1024


def split(value):
    high = value.astype(jnp.bfloat16)
    low = (value - high.astype(jnp.float32)).astype(jnp.bfloat16)
    return high, low


def both_parts(value):
    return jnp.concatenate(split(value), axis=0)


def left_parts(both):
    rows = both.shape[0] // 2
    high, low = both[:rows], both[rows:]
    return jnp.concatenate([high, low, high], axis=1)


def dot_parts(left, right):
    high, low = split(right)
    return jnp.dot(
        left_parts(left),
        jnp.concatenate([high, high, low], axis=0),
        preferred_element_type=jnp.float32,
    )


def dot_parts_rows(left, right):
    high, low = split(right)
    return lax.dot_general(
        left_parts(left),
        jnp.concatenate([high, high, low], axis=1),
        (((1,), (1,)), ((), ())),
        preferred_element_type=jnp.float32,
    )


def lane_index(shape):
    return lax.broadcasted_iota(jnp.int32, shape, len(shape) - 1)


def swap_groups(values):
    lanes = values[0].shape[-1]
    group = lane_index(values[0].shape) // (lanes // 4)
    for bit in (2, 1):
        width = bit * (lanes // 4)
        fresh = list(values)
        for index in range(4):
            if index & bit == 0:
                low, high = values[index], values[index | bit]
                upper = group & bit != 0
                fresh[index] = jnp.where(upper, pltpu.roll(high, width, 1), low)
                fresh[index | bit] = jnp.where(upper, high, pltpu.roll(low, lanes - width, 1))
        values = fresh
    return values


def swap_bit(low, high):
    lanes = low.shape[-1]
    width = lanes // 4
    upper = (lane_index(low.shape) // width) % 2 == 1
    first = jnp.where(upper, pltpu.roll(high, width, 1), low)
    second = jnp.where(upper, high, pltpu.roll(low, lanes - width, 1))
    return first, second


def row_halves(value, groups):
    rows, lanes = value.shape
    parts = value.reshape(groups, 2, rows // groups // 2, lanes)
    return parts[:, 0].reshape(rows // 2, lanes), parts[:, 1].reshape(rows // 2, lanes)


def wait_all(copies):
    for copy in copies:
        copy.wait()


def undo_matrix(gate):
    real, imag = gate[0].T, gate[1].T
    top = jnp.concatenate([real, imag], axis=1)
    low = jnp.concatenate([-imag, real], axis=1)
    return both_parts(jnp.concatenate([top, low], axis=0))


def column(rows, block, order):
    stride = rows.shape[0] // order
    parts = [rows[pl.ds(block * 2 + part, order, stride=stride), :] for part in range(2)]
    return jnp.concatenate(parts, axis=0)


def first_kernel(
    state_ref, costate_ref, gates_ref, out_ref, gate, rows, field_ref, gate_sem, row_sems, out_sems
):
    order = gate.shape[1]
    lanes = rows.shape[2]
    stride = rows.shape[1] // order
    chunks = row_sems.shape[1]
    chunk = rows.shape[1] // chunks
    copies = [pltpu.make_async_copy(gates_ref.at[0], gate, gate_sem)]
    for index in range(chunks):
        part = pl.ds(index * chunk, chunk)
        for vector, ref in enumerate((state_ref, costate_ref)):
            copies.append(
                pltpu.make_async_copy(ref.at[part], rows.at[vector, part], row_sems.at[vector, index])
            )
    for copy in copies:
        copy.start()
    copies[0].wait()
    matrix = undo_matrix(gate)
    wait_all(copies[1:])

    def column(vector, block):
        parts = [rows[vector, pl.ds(block * 2 + part, order, stride=stride), :] for part in range(2)]
        return jnp.concatenate(parts, axis=0)

    out_copies = []
    for block in range(stride // 2):
        field = jnp.concatenate([column(0, block), column(1, block)], axis=1)
        undone = dot_parts(matrix, field)
        pieces = []
        for vector in range(2):
            pieces += row_halves(undone[:, vector * lanes : (vector + 1) * lanes], 2)
        for index, piece in enumerate(swap_groups(pieces)):
            field_ref[block * 4 + index] = piece
        part = pl.ds(block * 4, 4)
        copy = pltpu.make_async_copy(field_ref.at[part], out_ref.at[part], out_sems.at[block])
        copy.start()
        out_copies.append(copy)
    wait_all(out_copies)


def outer_product(lam, psi):
    order = lam.shape[0] // 2
    left = jnp.concatenate([lam[:order], lam[order:]], axis=1)
    plain = jnp.concatenate([psi[:order], psi[order:]], axis=1)
    other = jnp.concatenate([-psi[order:], psi[:order]], axis=1)
    return dot_parts_rows(both_parts(left), jnp.concatenate([plain, other], axis=0))


def four_products(fields, groups):
    pieces = swap_groups(fields)
    rows, lanes = pieces[0].shape

    def joined(vector):
        parts = [
            piece.reshape(groups, 1, rows // groups, lanes)
            for piece in pieces[2 * vector : 2 * vector + 2]
        ]
        return jnp.concatenate(parts, axis=1).reshape(2 * rows, lanes)

    return outer_product(joined(1), joined(0))


def early_kernel(state_ref, costate_ref, out_ref):
    order = out_ref.shape[0]
    out_ref[...] = jnp.zeros_like(out_ref)

    @pl.loop(0, state_ref.shape[0] // order // 2)
    def _(block):
        out_ref[...] += outer_product(
            column(costate_ref, block, order), column(state_ref, block, order)
        )


def middle_kernel(moved_ref, gates_ref, out_ref, kept, last, sems):
    _, steps, _, order, lanes = moved_ref.shape
    batches = 2 * steps
    copies = []

    def undo(matrix, fields):
        result = dot_parts(matrix, jnp.concatenate(fields, axis=1))
        return [result[:, index * lanes : (index + 1) * lanes] for index in range(len(fields))]

    matrices = [undo_matrix(gates_ref[index + 1]) for index in range(2)]
    for step in range(steps):
        fields = [mixed_rows(moved_ref, step, bit) for bit in range(2)]
        for bit, result in enumerate(undo(matrices[0], fields)):
            for top, piece in enumerate(swap_bit(*row_halves(result, 8))):
                place = (top * steps + step) * 2 + bit
                kept[pl.ds(place * order, order), :] = piece

    for step in range(steps):
        fields = [regrouped(kept, step * 2 + index, order) for index in range(2)]
        for index, result in enumerate(undo(matrices[1], fields)):
            for bit, piece in enumerate(swap_bit(*row_halves(result, 2))):
                last[bit * batches + step * 2 + index] = piece
        for bit in range(2):
            part = pl.ds(bit * batches + step * 2, 2)
            copy = pltpu.make_async_copy(last.at[part], out_ref.at[part], sems.at[bit, step])
            copy.start()
            copies.append(copy)
    wait_all(copies)


def regrouped(kept_ref, batch, order):
    devices = kept_ref.shape[0] // order
    parts = [
        kept_ref[pl.ds(row * (devices // 2) + batch, devices, stride=order), :] for row in range(8)
    ]
    return jnp.concatenate(parts, axis=0)


def mixed_rows(moved_ref, step, bit):
    low_rows = moved_ref.shape[3] // 4
    parts = [
        moved_ref[top, step, low, pl.ds((part * 2 + bit) * low_rows, low_rows), :]
        for part in range(2)
        for top in range(2)
        for low in range(2)
    ]
    return jnp.concatenate(parts, axis=0)


def late_kernel(moved_ref, last_ref, early_ref, gates_ref, out_ref, sum_ref, *, scale):
    order = early_ref.shape[0]
    steps = moved_ref.shape[1]
    sum_ref[0] = early_ref[...]
    sum_ref[1:3] = jnp.zeros((2,) + early_ref.shape, jnp.float32)

    @pl.loop(0, steps)
    def _(step):
        first, second = (mixed_rows(moved_ref, step, bit) for bit in range(2))
        half = first.shape[-1] // 2
        lower = lane_index(first.shape) < half
        psi = jnp.where(lower, first, pltpu.roll(second, half, 1))
        lam = jnp.where(lower, pltpu.roll(first, half, 1), second)
        sum_ref[1] += outer_product(lam, psi)
        sum_ref[2] += four_products([last_ref[step * 4 + index] for index in range(4)], 2)

    for index in range(3):
        total = (sum_ref[index, :, :order], sum_ref[index, :, order:])
        gate = (gates_ref[index, 0], gates_ref[index, 1])
        left, right = (gate, total) if index == 2 else (total, gate)
        out_ref[index, 0], out_ref[index, 1] = complex_product(left, right, scale)


def complex_product(left, right, scale):
    def times(first, second):
        return jnp.dot(
            first, second, precision=lax.Precision.HIGHEST, preferred_element_type=jnp.float32
        )

    real = times(left[0], right[0]) - times(left[1], right[1])
    imag = times(left[0], right[1]) + times(left[1], right[0])
    return real * scale, imag * scale


def last_kernel(moved_ref, state_ref, costate_ref, rows, copy_sems):
    half = moved_ref.shape[1] // 2
    copies = []
    for block in range(rows.shape[1] // 2):
        pieces = swap_groups([moved_ref[block * 4 + index] for index in range(4)])
        for vector, ref in enumerate((state_ref, costate_ref)):
            for part in range(2):
                column = block * 2 + part
                for bit in range(2):
                    piece = pieces[2 * vector + bit][part * half : (part + 1) * half]
                    rows[vector, column, bit * half : (bit + 1) * half] = piece
                copy = pltpu.make_async_copy(
                    rows.at[vector, column], ref.at[:, column, 0], copy_sems.at[vector, column]
                )
                copy.start()
                copies.append(copy)
    wait_all(copies)


def gather_kernel(*refs):
    *part_refs, out_ref, copy_sems = refs
    place = lax.rem(lax.axis_index("amp"), len(part_refs))
    copies = [
        pltpu.make_async_copy(ref, out_ref.at[place ^ index], copy_sems.at[index])
        for index, ref in enumerate(part_refs)
    ]
    for copy in copies:
        copy.start()
    wait_all(copies)


def tree_sum(parts):
    while len(parts) > 1:
        parts = [parts[i] + parts[i + 1] for i in range(0, len(parts), 2)]
    return parts[0]


def exchange(part, distance):
    devices = lax.axis_size("amp")
    return lax.ppermute(part, "amp", [(i, i ^ distance) for i in range(devices)])


def scattered_sum(value):
    devices = lax.axis_size("amp")
    inner = min(8, devices)
    own = lax.axis_index("amp") % inner
    blocks = value.reshape(inner, -1, value.shape[-1])

    def pick(index):
        return lax.dynamic_index_in_dim(blocks, index, 0, keepdims=False)

    part = tree_sum([pick(own)] + [exchange(pick(own ^ k), k) for k in range(1, inner)])
    distance = inner
    while distance < devices:
        part = part + exchange(part, distance)
        distance *= 2
    return part


def gathered_chips(part):
    inner = min(8, lax.axis_size("amp"))
    return [part] + [exchange(part, k) for k in range(2, inner, 2)]


def gathered_cores(own, shape):
    others = [exchange(found, 1) for found in own]
    parts = [found for pair in zip(own, others) for found in pair]
    out = pl.pallas_call(
        gather_kernel,
        in_specs=[pl.BlockSpec(memory_space=pl.ANY)] * len(parts),
        out_specs=IN_HBM,
        out_shape=jax.ShapeDtypeStruct((len(parts),) + parts[0].shape, parts[0].dtype),
        scratch_shapes=[pltpu.SemaphoreType.DMA((len(parts),))],
        compiler_params=PARAMS,
    )(*parts)
    return out.reshape(shape)


def to_rows(field, lanes):
    return field.reshape(2, -1, lanes).swapaxes(0, 1).reshape(-1, lanes)


def from_rows(rows):
    return rows.reshape(-1, 2, rows.shape[-1]).swapaxes(0, 1).reshape(2, -1)


IN_HBM = pl.BlockSpec(memory_space=pltpu.HBM)
IN_VMEM = pl.BlockSpec(memory_space=pltpu.VMEM)
PARAMS = pltpu.CompilerParams(vmem_limit_bytes=VMEM_BYTES)
HBM_PARAMS = pltpu.CompilerParams(vmem_limit_bytes=60 * 1024 * 1024)


def cost(layers, amplitudes, order):
    flops = layers * 3 * 8 * amplitudes * order
    return pl.CostEstimate(flops=flops, bytes_accessed=32 * amplitudes, transcendentals=0)


def on_device_lanes(state, costate, gates, devices, order, columns):
    lanes = 4 * columns // devices
    steps = devices // 4
    rows = 2 * columns // lanes
    scale = 1.0 / math.sqrt(devices * columns)
    field_shape = (devices, order, lanes)
    sum_shape = (order, 2 * order)
    amplitudes = 2 * order * columns

    def array(shape, kind=jnp.float32):
        return jax.ShapeDtypeStruct(shape, kind)

    state, costate = to_rows(state, lanes), to_rows(costate, lanes)
    sent = pl.pallas_call(
        first_kernel,
        in_specs=[IN_HBM, IN_HBM, IN_HBM],
        out_specs=IN_HBM,
        out_shape=array(field_shape),
        scratch_shapes=[
            pltpu.VMEM((2, order, order), jnp.float32),
            pltpu.VMEM((2, rows * order, lanes), jnp.float32),
            pltpu.VMEM(field_shape, jnp.float32),
            pltpu.SemaphoreType.DMA,
            pltpu.SemaphoreType.DMA((2, 1)),
            pltpu.SemaphoreType.DMA((steps,)),
        ],
        compiler_params=HBM_PARAMS,
        cost_estimate=cost(1, amplitudes, order),
    )(state, costate, gates)
    state, costate, sent = lax.optimization_barrier((state, costate, sent))
    moved = lax.all_to_all(sent, "amp", 0, 0, tiled=True)
    early = pl.pallas_call(
        early_kernel,
        in_specs=[IN_VMEM, IN_VMEM],
        out_specs=IN_VMEM,
        out_shape=array(sum_shape),
        compiler_params=PARAMS,
        cost_estimate=cost(1, amplitudes, order),
    )(state, costate)
    moved = moved.reshape(2, steps, 2, order, lanes)
    last = pl.pallas_call(
        middle_kernel,
        in_specs=[IN_VMEM, IN_VMEM],
        out_specs=IN_HBM,
        out_shape=pltpu.HBM(field_shape, jnp.float32),
        scratch_shapes=[
            pltpu.VMEM((devices * order, lanes), jnp.float32),
            pltpu.VMEM(field_shape, jnp.float32),
            pltpu.SemaphoreType.DMA((2, steps)),
        ],
        compiler_params=PARAMS,
        cost_estimate=cost(2, amplitudes, order),
    )(moved, gates)
    arrived = lax.all_to_all(last, "amp", 0, 0, tiled=True)
    gradients = pl.pallas_call(
        functools.partial(late_kernel, scale=scale),
        in_specs=[IN_VMEM, IN_VMEM, IN_VMEM, IN_VMEM],
        out_specs=IN_VMEM,
        out_shape=array(gates.shape),
        scratch_shapes=[pltpu.VMEM((3,) + sum_shape, jnp.float32)],
        compiler_params=PARAMS,
        cost_estimate=cost(2, amplitudes, order),
    )(moved, last, early, gates)
    part, arrived = lax.optimization_barrier((scattered_sum(gradients), arrived))
    parts = gathered_chips(part)
    state_rows, costate_rows = pl.pallas_call(
        last_kernel,
        in_specs=[IN_VMEM],
        out_specs=[IN_HBM, IN_HBM],
        out_shape=[array((order, rows, 1, lanes))] * 2,
        scratch_shapes=[
            pltpu.VMEM((2, rows, order, lanes), jnp.float32),
            pltpu.SemaphoreType.DMA((2, rows)),
        ],
        compiler_params=PARAMS,
        cost_estimate=cost(1, amplitudes, order),
    )(arrived)
    for index in range(2, len(parts)):
        parts[index], state_rows = lax.optimization_barrier((parts[index], state_rows))
    gradients = gathered_cores(parts, gates.shape)
    return from_rows(state_rows), from_rows(costate_rows), gradients


def undo_gate(field, gate):
    high = lax.Precision.HIGHEST
    shape = field.shape
    parts = field.reshape(shape[:-1] + (2, 2, -1))
    real, imag = parts[..., 0, :], parts[..., 1, :]

    def contract(matrix, operand):
        return jnp.einsum("ts,btvc->bsvc", matrix, operand, precision=high)

    new_real = contract(gate[0], real) + contract(gate[1], imag)
    new_imag = contract(gate[0], imag) - contract(gate[1], real)
    return jnp.stack([new_real, new_imag], axis=-2).reshape(shape)


def gate_gradient(before, after):
    high = lax.Precision.HIGHEST
    lam = before.reshape(before.shape[:-1] + (2, 2, -1))[..., 1, :, :]
    psi = after.reshape(after.shape[:-1] + (2, 2, -1))[..., 0, :, :]
    real = jnp.einsum("btpc,bspc->ts", lam, psi, precision=high)
    imag = jnp.einsum("btc,bsc->ts", lam[..., 1, :], psi[..., 0, :], precision=high) - jnp.einsum(
        "btc,bsc->ts", lam[..., 0, :], psi[..., 1, :], precision=high
    )
    return jnp.stack([real, imag], axis=0)


def on_device_plain(state, costate, gates, devices, order, columns):
    own = columns // devices
    both = jnp.stack([state, costate], axis=0).reshape(2, 2, order, devices, own)
    field = both.transpose(3, 2, 0, 1, 4).reshape(devices, order, 4 * own)
    field = lax.all_to_all(field, "amp", 0, 0, tiled=True)
    after = undo_gate(field, gates[0])
    terms = [gate_gradient(field, after)]
    field = after.reshape(2, devices // 4, 2, 2, 2, order // 4, 4 * own)
    field = field.transpose(3, 1, 4, 0, 2, 5, 6).reshape(devices, order, 4 * own)
    after = undo_gate(field, gates[1])
    terms.append(gate_gradient(field, after))
    field = after.reshape(devices, order // devices, devices, 4 * own)
    field = field.transpose(2, 1, 0, 3).reshape(devices, order, 4 * own)
    after = undo_gate(field, gates[2])
    terms.append(gate_gradient(field, after))
    terms = jnp.stack(terms, axis=0) / math.sqrt(devices * columns)
    gradients = gathered_cores(gathered_chips(scattered_sum(terms)), gates.shape)
    field = lax.all_to_all(after, "amp", 0, 0, tiled=True)
    field = field.reshape(devices, order, 2, 2, own).transpose(2, 3, 1, 0, 4)
    field = field.reshape(2, 2, order * columns)
    return field[0], field[1], gradients


def on_device(state, costate, gates):
    devices = lax.axis_size("amp")
    order = gates.shape[2]
    columns = state.shape[1] // order
    filled = 4 * columns == 128 * devices and order == 4 * devices
    form = on_device_lanes if filled else on_device_plain
    return form(state, costate, gates, devices, order, columns)


def solution(mesh):
    return jax.shard_map(
        on_device,
        mesh=mesh,
        in_specs=(P(None, "amp"), P(None, "amp"), P()),
        out_specs=(P(None, "amp"), P(None, "amp"), P()),
        check_vma=False,
    )
```
